256 devices in a mesh: bx: 16 (over y, x), by: 8 (over z), cz: 2 (over core).
Axes of the slice: x: 4, y: 4, z: 8, core: 2. Of those that a mesh axis runs over, the one named last changes fastest.
Arguments:
- latents: bfloat16 [256, 16, 16, 16, 64], P(('bx', 'by', 'cz')), may hold values from -6 to 6
- target: bfloat16 [256, 16, 16, 16, 64], P(('bx', 'by', 'cz')), may hold values from -6 to 6
- block_coords: int32 [256, 3], P(('bx', 'by', 'cz')), may hold values from -1 to 1, as said below
- timestep: int32 [1], replicated, may hold values from 0 to 999
- conv_weight: bfloat16 [27, 64, 64], replicated, may hold values from -0.15625 to 0.15625
- coarse_weight: bfloat16 [27, 64, 64], replicated, may hold values from -0.15625 to 0.15625
- out_weight: bfloat16 [64, 64], replicated, may hold values from -0.75 to 0.75
- time_weight: bfloat16 [256, 64], replicated, may hold values from -0.5 to 0.5
- norm_gain: float32 [64], replicated, may hold values from 0.5 to 1.5
- norm_bias: float32 [64], replicated, may hold values from -3 to 3
Outputs:
- predicted: bfloat16 [256, 16, 16, 16, 64], P(('bx', 'by', 'cz'))
- mean_loss: float32 [1], replicated
- grad_conv: float32 [27, 64, 64], replicated
- grad_coarse: float32 [27, 64, 64], replicated
- grad_out: float32 [64, 64], replicated
- grad_time: float32 [256, 64], replicated
- grad_gain: float32 [64], replicated
- grad_bias: float32 [64], replicated
The draws below stay inside these ranges and needn't reach their ends.
Inputs may be any that keep to these rules, and one draw needn't show every extreme that they name: `block_coords`: each row is x, y, z of a block position within its region, x below 2, y below 2, z below 2; a device's live slots come first and hold distinct positions, its other slots are -1 in all three; every device has a live slot and some device fills all 1.
All inputs are finite; a program needn't handle non-finite values.
Results may differ from the reference program's by a relative error of at most 0.0045.
The reference program's roundings to bfloat16 on the way count: a program that leaves them out, or rounds other values in their place, can miss the bound.
Values may be sent and summed in bfloat16 or wider, within the bound.
No kernel may reach another device: no remote copies, remote signals or barrier semaphores. Data moves between devices by JAX's collectives and lax.ppermute only.
A program may use at most 128 MiB of HBM per device.

```python
import math
import jax
import jax.numpy as jnp
import numpy as np
from jax import lax

C = 64
BS = 16
G = 32
TE = 256
RX = 2
RY = 2
GZH = 2
BCAP = 1
SLOTS = 256
N_BX = 16
N_BY = 8
N_CZ = 2


def draw_block_coords(key, part):
    key = jax.random.fold_in(key, 7)
    devices = SLOTS // BCAP
    positions = RX * RY * GZH
    count_key, heavy_key, full_key, order_key = jax.random.split(key, 4)
    light = jax.random.randint(count_key, (devices,), 1, max(BCAP // 2, 1) + 1)
    heavy = jax.random.randint(heavy_key, (devices,), 0, 4) == 0
    counts = jnp.where(heavy, BCAP, light)
    fullest = jax.random.randint(full_key, (), 0, devices)
    counts = jnp.where(jnp.arange(devices) == fullest, BCAP, counts)
    orders = jax.vmap(lambda subkey: jax.random.permutation(subkey, positions))(jax.random.split(order_key, devices))
    chosen = orders[:, :BCAP]
    coord_x = chosen // (RY * GZH)
    coord_y = chosen // GZH % RY
    coord_z = chosen % GZH
    coords = jnp.stack([coord_x, coord_y, coord_z], axis=-1)
    keep_slot = jnp.arange(BCAP)[None, :] < counts[:, None]
    coords = jnp.where(keep_slot[:, :, None], coords, -1)
    return coords.reshape(SLOTS, 3).astype(jnp.int32)


def steps_of(stream_key, dims, cuts, smallest, high):
    factor_of = 1.0
    for dim, blocks in cuts:
        draws = jax.random.uniform(jax.random.fold_in(jax.random.fold_in(stream_key, 6), dim), (blocks,), jnp.float32, smallest / len(cuts), high / len(cuts))
        factor_of = factor_of * jnp.repeat(jnp.exp(draws), dims[dim] // blocks).reshape((-1,) + (1,) * (len(dims) - 1 - dim))
    return factor_of


def gaussian(rng, shape, scale, most, pieces=(), kind=jnp.bfloat16):
    entries = scale * jax.random.normal(rng, shape, jnp.float32)
    if pieces:
        entries = entries * steps_of(rng, shape, pieces, -0.22, 0.18)
    return jnp.clip(entries, -most, most).astype(kind)


def setup_inputs(seed: int = 0) -> dict:
    key_of = jax.random.split(jax.random.key(seed), 11)
    return {
        "latents": gaussian(key_of[0], (SLOTS, BS, BS, BS, C), 1.0, 6.0, ((0, 256),)),
        "target": gaussian(key_of[1], (SLOTS, BS, BS, BS, C), 1.0, 6.0, ((0, 256),)),
        "block_coords": draw_block_coords(jax.random.fold_in(key_of[10], 71), 0),
        "timestep": jax.random.randint(key_of[3], (1,), 0, 1000).astype(jnp.int32),
        "conv_weight": gaussian(key_of[4], (27, C, C), (27 * C) ** -0.5, 0.15625),
        "coarse_weight": gaussian(key_of[5], (27, C, C), (27 * C) ** -0.5, 0.15625),
        "out_weight": gaussian(key_of[6], (C, C), C ** -0.5, 0.75),
        "time_weight": gaussian(key_of[7], (TE, C), (TE // 2) ** -0.5, 0.5),
        "norm_gain": jnp.clip(1.0 + 0.1 * jax.random.normal(key_of[8], (C,), jnp.float32), 0.5, 1.5),
        "norm_bias": gaussian(key_of[9], (C,), 0.5, 3.0, (), jnp.float32),
    }


EPS = 1e-05
OFFSETS = np.array([[ox, oy, oz] for ox in (-1, 0, 1) for oy in (-1, 0, 1) for oz in (-1, 0, 1)], dtype=np.int32)

def time_embedding(timestep):
    halfway = TE // 2
    indices = jnp.arange(halfway).astype(jnp.float32)
    freqs = jnp.exp(indices * (-math.log(10000.0) / halfway))
    angles = timestep[0].astype(jnp.float32) * freqs
    return jnp.concatenate([jnp.sin(angles), jnp.cos(angles)])

def conv_taps(padded, weight):
    extent_x, extent_y, extent_z = (padded.shape[0] - 2, padded.shape[1] - 2, padded.shape[2] - 2)
    cells_all = extent_x * extent_y * extent_z
    running = jnp.zeros((cells_all, weight.shape[2]), jnp.float32)
    for tap_index in range(27):
        off_x, off_y, off_z = (tap_index // 9, tap_index // 3 % 3, tap_index % 3)
        shifted = padded[off_x:off_x + extent_x, off_y:off_y + extent_y, off_z:off_z + extent_z]
        shifted = shifted.reshape(cells_all, padded.shape[3])
        running = running + jnp.dot(shifted, weight[tap_index], preferred_element_type=jnp.float32)
    return running

def conv_grad(padded, upstream):
    extent_x, extent_y, extent_z = (padded.shape[0] - 2, padded.shape[1] - 2, padded.shape[2] - 2)
    cells_all = extent_x * extent_y * extent_z
    results = []
    for tap_index in range(27):
        off_x, off_y, off_z = (tap_index // 9, tap_index // 3 % 3, tap_index % 3)
        shifted = padded[off_x:off_x + extent_x, off_y:off_y + extent_y, off_z:off_z + extent_z]
        shifted = shifted.reshape(cells_all, padded.shape[3])
        results.append(lax.dot_general(shifted, upstream, (((0,), (0,)), ((), ())), preferred_element_type=jnp.float32))
    return jnp.stack(results)

def reference(latents, target, block_coords, timestep, conv_weight, coarse_weight, out_weight, time_weight, norm_gain, norm_bias):
    volume = BS ** 3
    half_edge = BS // 2
    per_group = C // G
    grid_x, grid_y, grid_z = (RX * N_BX, RY * N_BY, GZH * N_CZ)
    slot_ids = jnp.arange(SLOTS).astype(jnp.int32)
    device = slot_ids // BCAP
    occupied = block_coords[:, 0] >= 0
    global_x = device // (N_BY * N_CZ) * RX + block_coords[:, 0]
    global_y = device // N_CZ % N_BY * RY + block_coords[:, 1]
    global_z = device % N_CZ * GZH + block_coords[:, 2]
    lookup_size = grid_x * grid_y * grid_z
    cell_index = jnp.where(occupied, (global_x * grid_y + global_y) * grid_z + global_z, lookup_size)
    lookup = jnp.full((lookup_size,), -1, jnp.int32).at[cell_index].set(slot_ids, mode='drop')
    offsets = jnp.asarray(OFFSETS)

    def padded_block(slot_index):
        near_x = global_x[slot_index] + offsets[:, 0]
        near_y = global_y[slot_index] + offsets[:, 1]
        near_z = global_z[slot_index] + offsets[:, 2]
        inside = (near_x >= 0) & (near_x < grid_x) & (near_y >= 0) & (near_y < grid_y) & (near_z >= 0) & (near_z < grid_z)
        flat_near = jnp.clip((near_x * grid_y + near_y) * grid_z + near_z, 0, lookup_size - 1)
        source = jnp.where(inside, lookup[flat_near], -1)
        blocks = latents[jnp.maximum(source, 0)]
        blocks = jnp.where((source >= 0)[:, None, None, None, None], blocks, jnp.zeros((), jnp.bfloat16))
        joined = blocks.reshape(3, 3, 3, BS, BS, BS, C).transpose(0, 3, 1, 4, 2, 5, 6).reshape(3 * BS, 3 * BS, 3 * BS, C)
        return joined[BS - 1:2 * BS + 1, BS - 1:2 * BS + 1, BS - 1:2 * BS + 1]
    pooled = lax.optimization_barrier(jnp.sum(latents.reshape(SLOTS, 2, half_edge, 2, half_edge, 2, half_edge, C), axis=(2, 4, 6), dtype=jnp.float32))
    pooled = pooled * (1.0 / math.sqrt(half_edge ** 3))
    pair = jnp.arange(2).astype(jnp.int32)
    coarse_x = jnp.where(occupied, 2 * global_x, 2 * grid_x)[:, None, None, None] + pair[:, None, None]
    coarse_y = (2 * global_y)[:, None, None, None] + pair[None, :, None]
    coarse_z = (2 * global_z)[:, None, None, None] + pair[None, None, :]
    coarse_in = jnp.zeros((2 * grid_x, 2 * grid_y, 2 * grid_z, C), jnp.float32)
    coarse_in = coarse_in.at[coarse_x, coarse_y, coarse_z].set(pooled, mode='drop').astype(jnp.bfloat16)
    coarse_pad = jnp.pad(coarse_in, ((1, 1), (1, 1), (1, 1), (0, 0)))
    coarse_out = conv_taps(coarse_pad, coarse_weight).reshape(2 * grid_x, 2 * grid_y, 2 * grid_z, C).astype(jnp.bfloat16)
    temb = time_embedding(timestep)
    time_bias = lax.optimization_barrier(jnp.sum(temb[:, None] * time_weight.astype(jnp.float32), axis=0))

    def pre_norm(slot_index):
        window = padded_block(slot_index)
        start = (jnp.maximum(2 * global_x[slot_index], 0).astype(jnp.int32), jnp.maximum(2 * global_y[slot_index], 0).astype(jnp.int32), jnp.maximum(2 * global_z[slot_index], 0).astype(jnp.int32), jnp.int32(0))
        coarse_part = lax.dynamic_slice(coarse_out, start, (2, 2, 2, C))
        upsampled = jnp.broadcast_to(coarse_part[:, None, :, None, :, None, :], (2, half_edge, 2, half_edge, 2, half_edge, C))
        upsampled = upsampled.reshape(volume, C).astype(jnp.float32)
        return conv_taps(window, conv_weight) + time_bias + upsampled
    weight_live = occupied.astype(jnp.float32)
    activations = lax.map(pre_norm, slot_ids) * weight_live[:, None, None]
    grouped = activations.reshape(SLOTS, volume, G, per_group)
    sums = lax.optimization_barrier(jnp.sum(grouped, axis=(0, 1, 3)))
    squares = lax.optimization_barrier(jnp.sum(grouped * grouped, axis=(0, 1, 3)))
    voxels = jnp.sum(weight_live) * volume
    count = voxels * per_group
    mean_group = sums / count
    var_group = squares / count - mean_group * mean_group
    rstd_group = 1.0 / jnp.sqrt(var_group + EPS)
    mean_chan = jnp.repeat(mean_group, per_group)
    rstd_chan = jnp.repeat(rstd_group, per_group)
    scale = 1.0 / (voxels * C)

    def head(slot_index):
        normalized = (activations[slot_index] - mean_chan) * rstd_chan
        shifted = normalized * norm_gain + norm_bias
        hidden = jax.nn.silu(shifted).astype(jnp.bfloat16)
        output = jnp.dot(hidden, out_weight, preferred_element_type=jnp.float32)
        residue = (output - target[slot_index].reshape(volume, C).astype(jnp.float32)) * weight_live[slot_index]
        upstream = (2.0 * scale * residue).astype(jnp.bfloat16)
        back = lax.dot_general(upstream, out_weight, (((1,), (1,)), ((), ())), preferred_element_type=jnp.float32)
        sigma = jax.nn.sigmoid(shifted)
        dshift = back * sigma * (1.0 + shifted * (1.0 - sigma))
        return (normalized, hidden, output, residue, upstream, dshift)

    def second_pass(carry, slot_index):
        grad_out, grad_gain, grad_bias, loss_sum = carry
        normalized, hidden, output, residue, upstream, dshift = head(slot_index)
        grad_out = grad_out + lax.dot_general(hidden, upstream, (((0,), (0,)), ((), ())), preferred_element_type=jnp.float32)
        grad_gain = grad_gain + lax.optimization_barrier(jnp.sum(dshift * normalized, axis=0))
        grad_bias = grad_bias + lax.optimization_barrier(jnp.sum(dshift, axis=0))
        loss_sum = loss_sum + jnp.sum(residue * residue)
        shown = (output * weight_live[slot_index]).astype(jnp.bfloat16)
        return ((grad_out, grad_gain, grad_bias, loss_sum), shown)
    start_carry = (jnp.zeros((C, C), jnp.float32), jnp.zeros((C,), jnp.float32), jnp.zeros((C,), jnp.float32), jnp.zeros((), jnp.float32))
    (grad_out, grad_gain, grad_bias, loss_sum), predicted = lax.scan(second_pass, start_carry, slot_ids)
    mean_loss = (loss_sum * scale).reshape(1)
    first_mean = jnp.repeat(lax.optimization_barrier(jnp.sum((norm_gain * grad_bias).reshape(G, per_group), axis=1)) / count, per_group)
    second_mean = jnp.repeat(lax.optimization_barrier(jnp.sum((norm_gain * grad_gain).reshape(G, per_group), axis=1)) / count, per_group)

    def third_pass(carry, slot_index):
        grad_conv, act_sum = carry
        normalized, hidden, output, residue, upstream, dshift = head(slot_index)
        dact = ((dshift * norm_gain - first_mean - normalized * second_mean) * rstd_chan * weight_live[slot_index]).astype(jnp.bfloat16)
        grad_conv = grad_conv + conv_grad(padded_block(slot_index), dact)
        act_sum = act_sum + lax.optimization_barrier(jnp.sum(dact, axis=0, dtype=jnp.float32))
        cell_grads = lax.optimization_barrier(jnp.sum(dact.reshape(2, half_edge, 2, half_edge, 2, half_edge, C), axis=(1, 3, 5), dtype=jnp.float32)).astype(jnp.bfloat16)
        return ((grad_conv, act_sum), cell_grads)
    (grad_conv, act_sum), cell_grads = lax.scan(third_pass, (jnp.zeros((27, C, C), jnp.float32), jnp.zeros((C,), jnp.float32)), slot_ids)
    dcoarse = jnp.zeros((2 * grid_x, 2 * grid_y, 2 * grid_z, C), jnp.bfloat16).at[coarse_x, coarse_y, coarse_z].set(cell_grads, mode='drop')
    grad_coarse = conv_grad(coarse_pad, dcoarse.reshape(-1, C))
    grad_time = temb[:, None] * act_sum[None, :]
    return (predicted.reshape(SLOTS, BS, BS, BS, C), mean_loss, grad_conv, grad_coarse, grad_out, grad_time, grad_gain, grad_bias)
```

```python
import math

import jax
import jax.numpy as jnp
from jax import lax
from jax.sharding import PartitionSpec as P

G = 32
RX = 2
RY = 2
GZH = 2


EPS = 1e-05


def with_halo(cells, sides, width):
    for axis, dim in sides:
        count = lax.axis_size(axis)
        ends = count - 1
        head = lax.slice_in_dim(cells, 0, width, axis=dim)
        tail = lax.slice_in_dim(cells, cells.shape[dim] - width, cells.shape[dim], axis=dim)
        cells = jnp.concatenate(
            [
                lax.ppermute(tail, axis, [(i, (i + 1) % count) for i in range(ends)]),
                cells,
                lax.ppermute(head, axis, [((i + 1) % count, i) for i in range(ends)]),
            ],
            axis=dim,
        )
    return cells


def time_embedding(timestep, width):
    halfway = width // 2
    indices = jnp.arange(halfway).astype(jnp.float32)
    freqs = jnp.exp(indices * (-math.log(10000.0) / halfway))
    angles = timestep[0].astype(jnp.float32) * freqs
    return jnp.concatenate([jnp.sin(angles), jnp.cos(angles)])


def conv_taps(padded, weight):
    extent_x, extent_y, extent_z = (padded.shape[0] - 2, padded.shape[1] - 2, padded.shape[2] - 2)
    cells_all = extent_x * extent_y * extent_z
    running = jnp.zeros((cells_all, weight.shape[2]), jnp.float32)
    for tap_index in range(27):
        off_x, off_y, off_z = (tap_index // 9, tap_index // 3 % 3, tap_index % 3)
        shifted = padded[
            off_x : off_x + extent_x, off_y : off_y + extent_y, off_z : off_z + extent_z
        ]
        shifted = shifted.reshape(cells_all, padded.shape[3])
        running = running + jnp.dot(shifted, weight[tap_index], preferred_element_type=jnp.float32)
    return running


def conv_grad(padded, upstream):
    extent_x, extent_y, extent_z = (padded.shape[0] - 2, padded.shape[1] - 2, padded.shape[2] - 2)
    cells_all = extent_x * extent_y * extent_z
    results = []
    for tap_index in range(27):
        off_x, off_y, off_z = (tap_index // 9, tap_index // 3 % 3, tap_index % 3)
        shifted = padded[
            off_x : off_x + extent_x, off_y : off_y + extent_y, off_z : off_z + extent_z
        ]
        shifted = shifted.reshape(cells_all, padded.shape[3])
        results.append(
            lax.dot_general(
                shifted, upstream, (((0,), (0,)), ((), ())), preferred_element_type=jnp.float32
            )
        )
    return jnp.stack(results)


def slab_planes(edge_len):
    planes = min(edge_len, max(1, 1024 // (edge_len * edge_len)))
    while edge_len % planes != 0:
        planes = planes - 1
    return planes


def slab_patch(window, first, planes):
    edge_len = window.shape[1] - 2
    columns = []
    for tap_index in range(27):
        off_x, off_y, off_z = (tap_index // 9, tap_index // 3 % 3, tap_index % 3)
        shifted = window[
            first + off_x : first + off_x + planes,
            off_y : off_y + edge_len,
            off_z : off_z + edge_len,
        ]
        columns.append(shifted.reshape(planes * edge_len * edge_len, window.shape[3]))
    return jnp.concatenate(columns, axis=1)


def block_conv(window, weight_flat):
    edge_len = window.shape[0] - 2
    planes = slab_planes(edge_len)
    results = []
    for first in range(0, edge_len, planes):
        results.append(
            jnp.dot(
                slab_patch(window, first, planes), weight_flat, preferred_element_type=jnp.float32
            )
        )
    return jnp.concatenate(results, axis=0)


def block_conv_grad(window, upstream):
    edge_len = window.shape[0] - 2
    planes = slab_planes(edge_len)
    rows = planes * edge_len * edge_len
    total = jnp.zeros((27 * window.shape[3], upstream.shape[1]), jnp.float32)
    for first in range(0, edge_len, planes):
        part = upstream[first * edge_len * edge_len : first * edge_len * edge_len + rows]
        total = total + lax.dot_general(
            slab_patch(window, first, planes),
            part,
            (((0,), (0,)), ((), ())),
            preferred_element_type=jnp.float32,
        )
    return total.reshape(27, window.shape[3], upstream.shape[1])


def place_blocks(pieces, block_coords):
    edge_len = pieces.shape[1]
    channels = pieces.shape[4]
    positions = RX * RY * GZH
    occupied = block_coords[:, 0] >= 0
    flat_index = jnp.where(
        occupied,
        (block_coords[:, 0] * RY + block_coords[:, 1]) * GZH + block_coords[:, 2],
        positions,
    )
    dense = (
        jnp.zeros((positions, edge_len, edge_len, edge_len, channels), pieces.dtype)
        .at[flat_index]
        .set(pieces, mode="drop")
    )
    dense = dense.reshape(RX, RY, GZH, edge_len, edge_len, edge_len, channels).transpose(
        0, 3, 1, 4, 2, 5, 6
    )
    return dense.reshape(RX * edge_len, RY * edge_len, GZH * edge_len, channels)


ALL = ("bx", "by", "cz")
CHIPS = ("bx", "by")


def gather_rows(rows, axes):
    count = 1
    for axis in axes:
        count = count * lax.axis_size(axis)
    copies = jnp.broadcast_to(rows[None], (count,) + rows.shape)
    return lax.all_to_all(copies, axes, 0, 0, tiled=True)


def sum_small(values):
    rows = jnp.pad(values, (0, -values.shape[0] % 128)).reshape(-1, 128)
    return jnp.sum(gather_rows(rows, ALL), axis=0).reshape(-1)[: values.shape[0]]


def sum_large(values):
    chips = lax.axis_size("bx") * lax.axis_size("by")
    half = chips * 8 * 128
    rows = jnp.pad(values, (0, 2 * half - values.shape[0])).reshape(2, chips * 8, 128)
    core = lax.axis_index("cz")
    swap = [(0, 1), (1, 0)]
    mine = jnp.where(core == 0, rows[0], rows[1])
    other = jnp.where(core == 0, rows[1], rows[0])
    mine = mine + lax.ppermute(other, "cz", swap)
    pieces = mine.astype(jnp.bfloat16).reshape(chips, 8, 128)
    pieces = lax.all_to_all(pieces, CHIPS, 0, 0, tiled=True)
    piece = jnp.sum(pieces.astype(jnp.float32), axis=0).astype(jnp.bfloat16)
    whole = gather_rows(piece, CHIPS)
    away = lax.ppermute(whole, "cz", swap)
    both = jnp.stack([jnp.where(core == 0, whole, away), jnp.where(core == 0, away, whole)])
    return both.reshape(-1)[: values.shape[0]].astype(jnp.float32)


def shards(
    latents,
    target,
    block_coords,
    timestep,
    conv_weight,
    coarse_weight,
    out_weight,
    time_weight,
    norm_gain,
    norm_bias,
):
    slot_count = latents.shape[0]
    edge_len = latents.shape[1]
    channels = latents.shape[4]
    volume = edge_len**3
    half_edge = edge_len // 2
    per_group = channels // G
    occupied = block_coords[:, 0] >= 0
    live_count = jnp.sum(occupied.astype(jnp.int32))
    weight_live = occupied.astype(jnp.float32)
    corners = jnp.maximum(block_coords, 0)
    weight_flat = conv_weight.reshape(27 * channels, channels)
    region = place_blocks(latents, block_coords)
    padded = with_halo(region, (("bx", 0), ("by", 1), ("cz", 2)), 1)
    pooled = jnp.sum(
        latents.reshape(slot_count, 2, half_edge, 2, half_edge, 2, half_edge, channels),
        axis=(2, 4, 6),
        dtype=jnp.float32,
    )
    pooled = (pooled * (1.0 / math.sqrt(half_edge**3))).astype(jnp.bfloat16)
    coarse_in = place_blocks(pooled, block_coords)
    coarse_pad = with_halo(coarse_in, (("bx", 0), ("by", 1), ("cz", 2)), 1)
    coarse_out = conv_taps(coarse_pad, coarse_weight).reshape(coarse_in.shape).astype(jnp.bfloat16)
    temb = time_embedding(timestep, time_weight.shape[0])
    time_bias = jnp.sum(temb[:, None] * time_weight.astype(jnp.float32), axis=0)

    def block_window(slot_index):
        corner = corners[slot_index]
        return lax.dynamic_slice(
            padded,
            (corner[0] * edge_len, corner[1] * edge_len, corner[2] * edge_len, 0),
            (edge_len + 2, edge_len + 2, edge_len + 2, channels),
        )

    def forward_slot(slot_index, activations):
        corner = corners[slot_index]
        coarse_part = lax.dynamic_slice(
            coarse_out, (corner[0] * 2, corner[1] * 2, corner[2] * 2, 0), (2, 2, 2, channels)
        )
        upsampled = jnp.broadcast_to(
            coarse_part[:, None, :, None, :, None, :],
            (2, half_edge, 2, half_edge, 2, half_edge, channels),
        )
        upsampled = upsampled.reshape(volume, channels).astype(jnp.float32)
        preact = block_conv(block_window(slot_index), weight_flat) + time_bias + upsampled
        return lax.dynamic_update_slice(activations, preact[None], (slot_index, 0, 0))

    activations = lax.fori_loop(
        0, live_count, forward_slot, jnp.zeros((slot_count, volume, channels), jnp.float32)
    )
    grouped = activations.reshape(slot_count, volume, G, per_group)
    sums = jnp.sum(grouped, axis=(0, 1, 3))
    squares = jnp.sum(grouped * grouped, axis=(0, 1, 3))
    voxels = live_count.astype(jnp.float32) * volume
    totals = sum_small(jnp.concatenate([sums, squares, voxels[None]]))
    sums, squares, voxels = totals[:G], totals[G : 2 * G], totals[2 * G]
    count = voxels * per_group
    mean_group = sums / count
    var_group = squares / count - mean_group * mean_group
    rstd_group = 1.0 / jnp.sqrt(var_group + EPS)
    mean_chan = jnp.repeat(mean_group, per_group)
    rstd_chan = jnp.repeat(rstd_group, per_group)
    scale = 1.0 / (voxels * channels)
    mask_rows = jnp.repeat(weight_live, volume)[:, None]
    normalized = (activations.reshape(slot_count * volume, channels) - mean_chan) * rstd_chan
    shifted = normalized * norm_gain + norm_bias
    hidden = jax.nn.silu(shifted).astype(jnp.bfloat16)
    output = jnp.dot(hidden, out_weight, preferred_element_type=jnp.float32)
    residue = (
        output - target.reshape(slot_count * volume, channels).astype(jnp.float32)
    ) * mask_rows
    predicted = (output * mask_rows).astype(jnp.bfloat16).reshape(latents.shape)
    upstream = (2.0 * scale * residue).astype(jnp.bfloat16)
    back = lax.dot_general(
        upstream, out_weight, (((1,), (1,)), ((), ())), preferred_element_type=jnp.float32
    )
    sigma = jax.nn.sigmoid(shifted)
    dshift = back * sigma * (1.0 + shifted * (1.0 - sigma))
    gain_part = jnp.sum(dshift * normalized, axis=0)
    bias_part = jnp.sum(dshift, axis=0)
    out_part = lax.dot_general(
        hidden, upstream, (((0,), (0,)), ((), ())), preferred_element_type=jnp.float32
    )
    loss_part = jnp.sum(residue * residue)
    totals = sum_small(jnp.concatenate([gain_part, bias_part, loss_part[None]]))
    grad_gain, grad_bias = totals[:channels], totals[channels : 2 * channels]
    loss_sum = totals[2 * channels]
    mean_loss = (loss_sum * scale).reshape(1)
    first_mean = jnp.repeat(
        jnp.sum((norm_gain * grad_bias).reshape(G, per_group), axis=1) / count, per_group
    )
    second_mean = jnp.repeat(
        jnp.sum((norm_gain * grad_gain).reshape(G, per_group), axis=1) / count, per_group
    )
    dact = (
        (dshift * norm_gain - first_mean - normalized * second_mean) * rstd_chan * mask_rows
    ).astype(jnp.bfloat16)
    dact = dact.reshape(slot_count, volume, channels)

    def grad_slot(slot_index, running):
        return running + block_conv_grad(block_window(slot_index), dact[slot_index])

    conv_part = lax.fori_loop(
        0, live_count, grad_slot, jnp.zeros((27, channels, channels), jnp.float32)
    )
    act_part = jnp.sum(dact, axis=(0, 1), dtype=jnp.float32)
    cell_grads = jnp.sum(
        dact.reshape(slot_count, 2, half_edge, 2, half_edge, 2, half_edge, channels),
        axis=(2, 4, 6),
        dtype=jnp.float32,
    ).astype(jnp.bfloat16)
    dcoarse = place_blocks(cell_grads, block_coords)
    coarse_part = conv_grad(coarse_pad, dcoarse.reshape(-1, channels))
    act_high = act_part.astype(jnp.bfloat16).astype(jnp.float32)
    act_low = act_part - act_high
    taps = 27 * channels * channels
    totals = sum_large(
        jnp.concatenate(
            [conv_part.reshape(-1), coarse_part.reshape(-1), out_part.reshape(-1), act_high, act_low]
        )
    )
    grad_conv = totals[:taps].reshape(27, channels, channels)
    grad_coarse = totals[taps : 2 * taps].reshape(27, channels, channels)
    rest = totals[2 * taps :]
    grad_out = rest[: channels * channels].reshape(channels, channels)
    act_sum = rest[channels * channels :].reshape(2, channels).sum(axis=0)
    grad_time = temb[:, None] * act_sum[None, :]
    return (predicted, mean_loss, grad_conv, grad_coarse, grad_out, grad_time, grad_gain, grad_bias)


def solution(mesh):
    placed = (
        P(("bx", "by", "cz"), None, None, None, None),
        P(("bx", "by", "cz"), None, None, None, None),
        P(("bx", "by", "cz"), None),
        P(),
        P(),
        P(),
        P(),
        P(),
        P(),
        P(),
    )
    return jax.shard_map(
        shards,
        mesh=mesh,
        in_specs=placed,
        out_specs=(
            P(("bx", "by", "cz"), None, None, None, None),
            P(),
            P(),
            P(),
            P(),
            P(),
            P(),
            P(),
        ),
        check_vma=False,
    )
```

```python
import math

import jax
import jax.numpy as jnp
import numpy as np
from jax import lax
from jax.experimental import pallas as pl
from jax.experimental.pallas import tpu as pltpu
from jax.sharding import PartitionSpec as P

ALL = ("bx", "by", "cz")
CHIPS = ("bx", "by")
BF = jnp.bfloat16
F32 = jnp.float32
EPS = 1e-05
GROUP = 2
VMEM_LIMIT = 56 * 1024 * 1024
LOSS_ROW = 768


def face_spec(dim, index):
    shape = tuple(1 if d == dim else 16 for d in range(3)) + (64,)
    where = tuple(index if d == dim else 0 for d in range(4))
    return pl.BlockSpec(shape, lambda i: where)


def call(kernel, outs, args, scratch=(), faces=()):
    vmem = pl.BlockSpec(memory_space=pltpu.VMEM)
    specs = list(faces) + [vmem] * (len(args) - 1 - len(faces))
    return pl.pallas_call(
        kernel,
        grid=(1,),
        out_shape=outs,
        in_specs=[pl.BlockSpec(memory_space=pltpu.SMEM)] + specs,
        out_specs=[vmem] * len(outs),
        scratch_shapes=list(scratch),
        compiler_params=pltpu.CompilerParams(vmem_limit_bytes=VMEM_LIMIT),
    )(*args)


def like(shape, dtype):
    return jax.ShapeDtypeStruct(shape, dtype)


def keep(cond, value):
    return jnp.where(cond, value, jnp.zeros_like(value))


def bits(info):
    return info[0, 0], info[0, 1], info[0, 2], lax.axis_index("cz")


def start16(bit):
    return pl.multiple_of(bit * 16, 16)


def cell_rows(first, second, face, on):
    rows = []
    for r in range(4):
        for s in range(4):
            here = on & (first == r // 2) & (second == s // 2)
            rows.append(keep(here, face[r % 2][s % 2]))
    return jnp.concatenate(rows, axis=0)


def row_of(cells, p):
    return cells[p : p + 1]


def z_message(info, lat, out, pooled):
    px, py, pz, kz = bits(info)
    on = pz == 1 - kz
    zsel = 15 * (1 - kz)
    out[...] = jnp.zeros(out.shape, BF)
    pick = lax.broadcasted_iota(jnp.int32, (16, 16, 64), 1) == zsel
    sums = [[None, None], [None, None]]
    for y in range(16):
        slab = lat[:, y].astype(F32)
        face = jnp.sum(jnp.where(pick, slab, 0.0), axis=1)
        out[py * 16 + y, pl.ds(start16(px), 16), :] = keep(on, face).astype(BF)
        for a in range(2):
            part = jnp.sum(slab[8 * a : 8 * a + 8], axis=0)
            old = sums[a][y // 8]
            sums[a][y // 8] = part if old is None else old + part
    cells = []
    for a in range(2):
        for b in range(2):
            for c in range(2):
                cells.append(jnp.sum(sums[a][b][8 * c : 8 * c + 8], axis=0, keepdims=True))
    cells = jnp.concatenate(cells, axis=0) * (1.0 / math.sqrt(512.0))
    cells = cells.astype(BF).astype(F32)
    pooled[...] = jnp.concatenate([cells, jnp.zeros((8, 64), F32)], axis=0).astype(BF)
    face = [
        [jnp.where(kz == 0, row_of(cells, 4 * a + 2 * b + 1), row_of(cells, 4 * a + 2 * b)) for a in range(2)]
        for b in range(2)
    ]
    rows = cell_rows(py, px, face, on)
    out[32] = jnp.concatenate([rows, jnp.zeros((16, 64), F32)], axis=0).astype(BF)


def y_messages(info, low, high, rz, pooled, down, up):
    px, py, pz, kz = bits(info)
    cells = pooled[...].astype(F32)
    halo = rz[32].astype(F32)
    for out, face, bit, line, q in ((down, low, 0, 0, 0), (up, high, 1, 31, 1)):
        on = py == bit
        out[...] = jnp.zeros(out.shape, BF)
        out[pl.ds(start16(px), 16), pl.ds(start16(pz), 16), :] = keep(on, face[:, 0])
        out[32] = rz[line]
        picked = [[row_of(cells, 4 * a + 2 * q + c) for c in range(2)] for a in range(2)]
        rows = cell_rows(px, pz, picked, on)
        tail = halo[12:16] if q else halo[0:4]
        out[33] = jnp.concatenate([rows, tail, jnp.zeros((12, 64), F32)], axis=0).astype(BF)


def x_messages(info, low, high, rz, rym, ryp, pooled, down, up):
    px, py, pz, kz = bits(info)
    cells = pooled[...].astype(F32)
    halo = rz[32].astype(F32)
    halo_m = rym[33].astype(F32)
    halo_p = ryp[33].astype(F32)
    line_m = rym[32].astype(F32)
    line_p = ryp[32].astype(F32)
    where16 = lax.broadcasted_iota(jnp.int32, (32, 16, 64), 1)
    for out, face, bit, line, q in ((down, low, 0, 0, 0), (up, high, 1, 31, 1)):
        on = px == bit
        out[...] = jnp.zeros(out.shape, BF)
        out[pl.ds(start16(py), 16), pl.ds(start16(pz), 16), :] = keep(on, face[0])
        slab = rz[0:32, 16 * q : 16 * q + 16, :].astype(F32)
        out[32] = jnp.sum(jnp.where(where16 == 15 * q, slab, 0.0), axis=1).astype(BF)
        out[33] = rym[line]
        out[34] = ryp[line]
        picked = [[row_of(cells, 4 * q + 2 * b + c) for c in range(2)] for b in range(2)]
        rows = cell_rows(py, pz, picked, on)
        corners = [line_m[line : line + 1], line_p[line : line + 1], jnp.zeros((14, 64), F32)]
        out[35] = jnp.concatenate(corners + [rows], axis=0).astype(BF)
        c0 = 3 * q
        parts = [row_of(halo, 4 * cy + c0) for cy in range(4)]
        parts += [halo_m[4 * c0 : 4 * c0 + 4], halo_p[4 * c0 : 4 * c0 + 4]]
        parts += [row_of(halo_m, 16 + c0), row_of(halo_p, 16 + c0), jnp.zeros((18, 64), F32)]
        out[36] = jnp.concatenate(parts, axis=0).astype(BF)


def coarse_table():
    pooled, rz, rym, ryp, rxm, rxp = 0, 16, 32, 64, 96, 128
    table = np.zeros((16, 224, 160), np.float32)
    for combo in range(16):
        bit = ((combo >> 3) & 1, (combo >> 2) & 1, (combo >> 1) & 1)
        core = combo & 1
        for tap in range(27):
            off = (tap // 9, tap // 3 % 3, tap % 3)
            for p in range(8):
                at = (p // 4, p // 2 % 2, p % 2)
                pos = [2 * bit[d] - 1 + off[d] + at[d] for d in range(3)]
                x, y, z = pos
                out_z = z < 0 or z > 3
                if out_z and (z < 0) != (core == 1):
                    continue
                if x < 0 or x > 3:
                    base = rxm if x < 0 else rxp
                    if y < 0 or y > 3:
                        side = 0 if y < 0 else 1
                        row = 16 + (12 + side if out_z else 4 + 4 * side + z)
                    else:
                        row = 16 + y if out_z else 4 * y + z
                    row = base + row
                elif y < 0 or y > 3:
                    row = (rym if y < 0 else ryp) + (16 + x if out_z else 4 * x + z)
                elif out_z:
                    row = rz + 4 * y + x
                else:
                    own = [pos[d] - 2 * bit[d] for d in range(3)]
                    if min(own) < 0 or max(own) > 1:
                        continue
                    row = pooled + 4 * own[0] + 2 * own[1] + own[2]
                table[combo, 8 * tap + p, row] = 1.0
    return table


def forward(info, lat, rz, rym, ryp, rxm, rxp, pooled, table, weight, coarse_weight, time_bias, act, scene, patch_out, stats):
    px, py, pz, kz = bits(info)
    z0 = pl.ds(start16(pz), 16)
    z1 = pl.ds(start16(1 - pz), 16)
    xs = pl.ds(start16(px), 16)
    ys = pl.ds(start16(py), 16)
    xlo, xhi, ylo, yhi = px == 0, px == 1, py == 0, py == 1
    row16 = lax.broadcasted_iota(jnp.int32, (16, 16, 64), 1)

    def edge(block):
        n = block.shape[0]
        return jnp.sum(jnp.where(row16[:n] == 15 * pz, block.astype(F32), 0.0), axis=1)

    def edge1(ref, i):
        return edge(ref[i : i + 1, z1, :])

    def one(ref, i, j):
        return ref[i].astype(F32)[j : j + 1]

    y_low = keep(ylo, rym[xs, z0, :])
    y_high = keep(yhi, ryp[xs, z0, :])
    nought = jnp.zeros((16, 64), BF)

    def sides(rx, out, inner):
        first = jnp.where(
            out,
            jnp.where(ylo, rx[33, z0, :], rx[15, z0, :]),
            jnp.where(ylo, rym[inner, z0, :], nought),
        )
        last = jnp.where(
            out,
            jnp.where(yhi, rx[34, z0, :], rx[16, z0, :]),
            jnp.where(yhi, ryp[inner, z0, :], nought),
        )
        return first, last

    e_low = keep(ylo, edge(rym[xs, z1, :]))
    e_high = keep(yhi, edge(ryp[xs, z1, :]))
    h_low = jnp.where(ylo, rym[32, xs, :], rz[15, xs, :]).astype(F32)
    h_high = jnp.where(yhi, ryp[32, xs, :], rz[16, xs, :]).astype(F32)
    h_mid = rz[ys, xs, :].astype(F32)
    on_low = (pz == 0) & (kz == 1)
    on_high = (pz == 1) & (kz == 0)

    def low_of(e, h):
        return keep(pz == 1, e) + keep(on_low, h)

    def high_of(e, h):
        return keep(pz == 0, e) + keep(on_high, h)

    def packed(of):
        rows = [of(e_low, h_low)] + [of(jnp.zeros((16, 64), F32), h_mid[y]) for y in range(16)]
        rows.append(of(e_high, h_high))
        return [jnp.concatenate([rows[2 * k], rows[2 * k + 1]], axis=1) for k in range(9)]

    below, above = packed(low_of), packed(high_of)

    def side_columns(rx, out, inner, of):
        half = rz[ys, 0:16, :] if inner < 16 else rz[ys, 16:32, :]
        inner_h = jnp.sum(jnp.where(row16 == inner % 16, half.astype(F32), 0.0), axis=1)
        e_mid = keep(out, edge(rx[ys, z1, :]))
        hh = jnp.where(out, rx[32, ys, :].astype(F32), inner_h)
        e_first = jnp.where(
            out,
            jnp.where(ylo, edge1(rx, 33), edge1(rx, 15)),
            keep(ylo, edge1(rym, inner)),
        )
        h_first = jnp.where(
            out,
            jnp.where(ylo, one(rx, 35, 0), one(rx, 32, 15)),
            jnp.where(ylo, one(rym, 32, inner), one(rz, 15, inner)),
        )
        e_last = jnp.where(
            out,
            jnp.where(yhi, edge1(rx, 34), edge1(rx, 16)),
            keep(yhi, edge1(ryp, inner)),
        )
        h_last = jnp.where(
            out,
            jnp.where(yhi, one(rx, 35, 1), one(rx, 32, 16)),
            jnp.where(yhi, one(ryp, 32, inner), one(rz, 16, inner)),
        )
        mid = of(e_mid, hh)
        rows = [of(e_first, h_first)] + [mid[y : y + 1] for y in range(16)] + [of(e_last, h_last)]
        return [jnp.concatenate([rows[2 * k], rows[2 * k + 1]], axis=1)[None] for k in range(9)]

    z_row = lax.broadcasted_iota(jnp.int32, (9, 16, 128), 1)

    def put(xp, evens, odds, first, last, zl, zh):
        left = jnp.concatenate([first[None], odds], axis=0)
        right = jnp.concatenate([evens, last[None]], axis=0)
        tile = jnp.concatenate([left, right], axis=2)
        wide = tile.astype(F32)
        scene[1, xp] = tile
        scene[0, xp] = jnp.where(z_row == 0, zl, pltpu.roll(wide, 1, 1)).astype(BF)
        scene[2, xp] = jnp.where(z_row == 15, zh, pltpu.roll(wide, 15, 1)).astype(BF)

    for xp, rx, out, inner in ((0, rxm, xlo, 15), (17, rxp, xhi, 16)):
        zl = jnp.concatenate(side_columns(rx, out, inner, low_of), axis=0)
        zh = jnp.concatenate(side_columns(rx, out, inner, high_of), axis=0)
        first, last = sides(rx, out, inner)
        plane = keep(out, rx[ys, z0, :]).reshape(8, 2, 16, 64)
        put(xp, plane[:, 0], plane[:, 1], first, last, zl, zh)
    for x in range(16):
        zl = jnp.concatenate([below[k][x : x + 1][None] for k in range(9)], axis=0)
        zh = jnp.concatenate([above[k][x : x + 1][None] for k in range(9)], axis=0)
        put(x + 1, lat[x, :, 0], lat[x, :, 1], y_low[x], y_high[x], zl, zh)

    source = jnp.concatenate(
        [pooled[...], rz[32, 0:16, :], rym[33], ryp[33], rxm[35, 16:32, :], rxm[36, 0:16, :], rxp[35, 16:32, :], rxp[36, 0:16, :]],
        axis=0,
    )
    taps = jnp.dot(table[...], source, preferred_element_type=F32)
    patch = jnp.concatenate([taps[8 * t : 8 * t + 8] for t in range(27)], axis=1)
    patch_out[...] = jnp.concatenate([patch, jnp.zeros((8, 1728), F32)], axis=0).astype(BF)
    coarse = jnp.dot(patch_out[...], coarse_weight[...], preferred_element_type=F32)
    coarse = coarse.astype(BF).astype(F32)
    coarse = jnp.concatenate([coarse, coarse], axis=1)
    z_half = lax.broadcasted_iota(jnp.int32, (16, 128), 0) < 8
    added = []
    for q in range(4):
        added.append(jnp.where(z_half, coarse[2 * q : 2 * q + 1], coarse[2 * q + 1 : 2 * q + 2]) + time_bias[...])

    total = jnp.zeros((1, 128), F32)
    squares = jnp.zeros((1, 128), F32)
    for first in range(0, 16, 4):
        pieces = []
        for tap in range(9):
            ox, oz = tap // 3, tap % 3
            for dk in range(2):
                pieces.append(scene[oz, first + ox : first + ox + 4, dk : dk + 8].reshape(512, 128))
        value = jnp.dot(jnp.concatenate(pieces, axis=1), weight[...], preferred_element_type=F32)
        value = value.reshape(4, 2, 4, 16, 128)
        a = first // 8
        value = jnp.concatenate(
            [(value[:, b] + added[2 * a + b][None, None])[:, None] for b in range(2)], axis=1
        ).reshape(512, 128)
        act[first * 128 : first * 128 + 512] = value
        total = total + jnp.sum(value, axis=0, keepdims=True)
        squares = squares + jnp.sum(value * value, axis=0, keepdims=True)
    lane = lax.broadcasted_iota(jnp.int32, (1, 128), 1)
    row = jnp.where(lane < 64, total + pltpu.roll(total, 64, 1), squares + pltpu.roll(squares, 64, 1))
    stats[...] = jnp.broadcast_to(row, stats.shape)


def pair_sum(row):
    lane = lax.broadcasted_iota(jnp.int32, row.shape, 1)
    return row + jnp.where(lane % 2 == 0, pltpu.roll(row, 127, 1), pltpu.roll(row, 1, 1))


def halves(row):
    lane = lax.broadcasted_iota(jnp.int32, row.shape, 1)
    other = pltpu.roll(row, 64, 1)
    return jnp.where(lane < 64, row, other), jnp.where(lane < 64, other, row)


def moments(gathered, count):
    sums, squares = halves(jnp.sum(gathered[...], axis=0, keepdims=True))
    mean = pair_sum(sums) / count
    var = pair_sum(squares) / count - mean * mean
    return sums, mean, 1.0 / jnp.sqrt(var + EPS)


def head(voxels):
    count = float(voxels * GROUP)
    scale = 1.0 / (voxels * 64)

    def kernel(info, act, gathered, target, gain, bias, weight, weight_t, predicted, dshift, piece, grad_out, loss):
        _, mean, rstd = moments(gathered, count)
        gains = jnp.zeros((1, 128), F32)
        biases = jnp.zeros((1, 128), F32)
        lost = jnp.zeros((1, 128), F32)
        outer = jnp.zeros((128, 128), F32)
        for x in range(0, 16, 2):
            rows = slice(x * 128, x * 128 + 256)
            normalized = (act[rows] - mean) * rstd
            shifted = normalized * gain[...] + bias[...]
            sigma = jax.nn.sigmoid(shifted)
            hidden = (shifted * sigma).astype(BF)
            output = jnp.dot(hidden, weight[...], preferred_element_type=F32)
            goal = jnp.concatenate([target[x : x + 2, :, 0], target[x : x + 2, :, 1]], axis=3)
            residue = output - goal.reshape(256, 128).astype(F32)
            shown = output.astype(BF).reshape(2, 8, 16, 128)
            predicted[x : x + 2, :, 0] = shown[..., :64]
            predicted[x : x + 2, :, 1] = shown[..., 64:]
            upstream = (2.0 * scale * residue).astype(BF)
            back = jnp.dot(upstream, weight_t[...], preferred_element_type=F32)
            value = back * sigma * (1.0 + shifted * (1.0 - sigma))
            dshift[rows] = value
            gains = gains + jnp.sum(value * normalized, axis=0, keepdims=True)
            biases = biases + jnp.sum(value, axis=0, keepdims=True)
            lost = lost + jnp.sum(residue * residue, axis=0, keepdims=True)
            outer = outer + lax.dot_general(hidden, upstream, (((0,), (0,)), ((), ())), preferred_element_type=F32)
        lane = lax.broadcasted_iota(jnp.int32, (1, 128), 1)
        row = jnp.where(lane < 64, gains + pltpu.roll(gains, 64, 1), biases + pltpu.roll(biases, 64, 1))
        piece[...] = jnp.broadcast_to(row, piece.shape)
        grad_out[...] = outer[:64, :64] + outer[64:, 64:]
        loss[...] = jnp.broadcast_to(jnp.sum(lost, axis=1, keepdims=True), (1, 128))

    return kernel


def gradients(voxels):
    count = float(voxels * GROUP)

    def kernel(info, act, dshift, first, second, gain, scene, patch, grad_out, loss, mine, other, act_sum, grads, cotangent):
        kz = lax.axis_index("cz")

        def store(half, row, value):
            @pl.when(kz == half)
            def _():
                mine[row : row + value.shape[0]] = value

            @pl.when(kz != half)
            def _():
                other[row : row + value.shape[0]] = value

        sums, mean, rstd = moments(first, count)
        totals = jnp.sum(second[...], axis=0, keepdims=True)
        grad_gain, grad_bias = halves(totals)
        m1 = pair_sum(gain[...] * grad_bias) / count
        m2 = pair_sum(gain[...] * grad_gain) / count
        grads[...] = totals
        centred = (sums - voxels * mean) * rstd
        act_sum[...] = rstd * (gain[...] * grad_bias - voxels * m1 - m2 * centred)
        cells = [None] * 4
        for x in range(16):
            rows = slice(x * 128, x * 128 + 128)
            normalized = (act[rows] - mean) * rstd
            value = ((dshift[rows] * gain[...] - m1 - normalized * m2) * rstd).astype(BF)
            wide = value.astype(F32)
            cotangent[:, rows] = wide.T.astype(BF)
            parts = wide.reshape(2, 4, 16, 128)
            for b in range(2):
                q = 2 * (x // 8) + b
                part = jnp.sum(parts[b], axis=0)
                cells[q] = part if cells[q] is None else cells[q] + part
        rows = []
        for q in range(4):
            for c in range(2):
                row = jnp.sum(cells[q][8 * c : 8 * c + 8], axis=0, keepdims=True)
                rows.append(row[:, :64] + row[:, 64:])
        dcoarse = jnp.concatenate(rows + [jnp.zeros((8, 64), F32)], axis=0).astype(BF)
        coarse = lax.dot_general(patch[...], dcoarse, (((0,), (0,)), ((), ())), preferred_element_type=F32)
        for ox in range(3):
            for oz in range(3):
                window = jnp.concatenate(
                    [scene[oz, ox : ox + 16, dk : dk + 8].reshape(2048, 128) for dk in range(2)], axis=1
                )
                product = jnp.dot(cotangent[...], window, preferred_element_type=F32).T
                for oy in range(3):
                    tap = 9 * ox + 3 * oy + oz
                    conv = product[64 * oy : 64 * oy + 64, :64] + product[64 * oy + 64 : 64 * oy + 128, 64:]
                    both = jnp.concatenate([conv, coarse[tap * 64 : tap * 64 + 64]], axis=1)
                    store(tap // 16, (tap % 16) * 64, both)
        store(1, LOSS_ROW - 64, jnp.concatenate([grad_out[...], jnp.zeros((64, 64), F32)], axis=1))
        high = jnp.broadcast_to(loss[...].astype(BF).astype(F32), (4, 128))
        low = jnp.broadcast_to(loss[...], (4, 128)) - high
        part = lax.broadcasted_iota(jnp.int32, (4, 128), 0)
        split = jnp.where(part // 2 == kz, jnp.where(part % 2 == 0, high, low), 0.0)
        store(1, LOSS_ROW, jnp.concatenate([split, jnp.zeros((1024 - LOSS_ROW - 4, 128), F32)], axis=0))

    return kernel


def exchange(rows):
    out = lax.all_to_all(rows.reshape(rows.shape[0], 1, 128), ALL, 0, 0, tiled=True)
    return out.reshape(rows.shape)


def neighbours(down, up, axis):
    ends = lax.axis_size(axis) - 1
    before = lax.ppermute(up, axis, [(i, i + 1) for i in range(ends)])
    after = lax.ppermute(down, axis, [(i + 1, i) for i in range(ends)])
    return before, after


def pair_add(info, mine, other, out):
    out[...] = (mine[...] + other[...]).astype(BF).reshape(out.shape)


def piece_sum(info, pieces, out):
    total = jnp.sum(pieces[...].astype(F32), axis=0)
    chip = lax.axis_index("bx") * lax.axis_size("by") + lax.axis_index("by")
    owner = (chip == LOSS_ROW // 8) & (lax.axis_index("cz") == 1)
    lost = (total - total.astype(BF).astype(F32))[:4]
    split = jnp.concatenate([total[:4], lost], axis=0)
    total = jnp.where(owner, split, total).astype(BF)
    out[...] = jnp.broadcast_to(total[None], out.shape)


def sum_payload(info, mine, other):
    chips = lax.axis_size("bx") * lax.axis_size("by")
    core = lax.axis_index("cz")
    swap = [(0, 1), (1, 0)]
    shape = like((chips, 8, 128), BF)
    (pieces,) = call(pair_add, [shape], [info, mine, lax.ppermute(other, "cz", swap)])
    pieces = lax.all_to_all(pieces, CHIPS, 0, 0, tiled=True)
    (copies,) = call(piece_sum, [shape], [info, pieces])
    whole = lax.all_to_all(copies, CHIPS, 0, 0, tiled=True)
    away = lax.ppermute(whole, "cz", swap)
    both = jnp.stack([jnp.where(core == 0, whole, away), jnp.where(core == 0, away, whole)])
    return both.reshape(-1, 128).astype(F32)


def time_embedding(timestep, width):
    halfway = width // 2
    indices = jnp.arange(halfway).astype(F32)
    freqs = jnp.exp(indices * (-math.log(10000.0) / halfway))
    angles = timestep[0].astype(F32) * freqs
    return jnp.concatenate([jnp.sin(angles), jnp.cos(angles)])


def twice(row):
    return jnp.concatenate([row, row]).reshape(1, 128)


def diagonal(square):
    nought = jnp.zeros_like(square)
    return jnp.block([[square, nought], [nought, square]])


def shards(latents, target, block_coords, timestep, conv_weight, coarse_weight, out_weight, time_weight, norm_gain, norm_bias):
    devices = lax.axis_size("bx") * lax.axis_size("by") * lax.axis_size("cz")
    voxels = devices * 4096
    core = lax.axis_index("cz").astype(jnp.int32)
    at = block_coords[0]
    info = block_coords
    lat = latents[0]
    lat_pairs = lat.reshape(16, 8, 2, 16, 64)

    mz, pooled = call(z_message, [like((33, 32, 64), BF), like((16, 64), BF)], [info, lat])
    rz = lax.ppermute(mz, "cz", [(0, 1), (1, 0)])
    plane = like((34, 32, 64), BF)
    down, up = call(y_messages, [plane, plane], [info, lat, lat, rz, pooled], (), [face_spec(1, 0), face_spec(1, 15)])
    rym, ryp = neighbours(down, up, "by")
    plane = like((37, 32, 64), BF)
    down, up = call(x_messages, [plane, plane], [info, lat, lat, rz, rym, ryp, pooled], (), [face_spec(0, 0), face_spec(0, 15)])
    rxm, rxp = neighbours(down, up, "bx")

    temb = time_embedding(timestep, time_weight.shape[0])
    time_bias = jnp.sum(temb[:, None] * time_weight.astype(F32), axis=0)
    taps = conv_weight.reshape(3, 3, 3, 64, 64).transpose(0, 2, 1, 3, 4)
    taps = jnp.stack(
        [jnp.pad(taps, ((0, 0), (0, 0), (b, 1 - b), (0, 0), (0, 0))) for b in range(2)], axis=4
    ).reshape(9 * 256, 128)
    combo = 8 * at[0] + 4 * at[1] + 2 * at[2] + core
    table = lax.dynamic_index_in_dim(jnp.asarray(coarse_table(), BF), combo, keepdims=False)

    act, scene, patch, stats = call(
        forward,
        [like((2048, 128), F32), like((3, 18, 9, 16, 128), BF), like((16, 1728), BF), like((devices, 128), F32)],
        [info, lat_pairs, rz, rym, ryp, rxm, rxp, pooled, table, taps, coarse_weight.reshape(1728, 64), twice(time_bias)],
    )
    first = exchange(stats)
    gain, bias = twice(norm_gain), twice(norm_bias)
    predicted, dshift, piece, grad_out, loss = call(
        head(voxels),
        [
            like((16, 8, 2, 16, 64), BF),
            like((2048, 128), F32),
            like((devices, 128), F32),
            like((64, 64), F32),
            like((1, 128), F32),
        ],
        [
            info,
            act,
            first,
            target.reshape(16, 8, 2, 16, 64),
            gain,
            bias,
            diagonal(out_weight),
            diagonal(out_weight.T),
        ],
    )
    second = exchange(piece)
    mine, other, act_sum, grads = call(
        gradients(voxels),
        [like((1024, 128), F32), like((1024, 128), F32), like((1, 128), F32), like((1, 128), F32)],
        [info, act, dshift, first, second, gain, scene, patch, grad_out, loss],
        [pltpu.VMEM((128, 2048), BF)],
    )
    totals = sum_payload(info, mine, other)
    grad_conv = totals[:1728, :64].reshape(27, 64, 64)
    grad_coarse = totals[:1728, 64:].reshape(27, 64, 64)
    mean_loss = jnp.sum(totals[1024 + LOSS_ROW : 1032 + LOSS_ROW, 0]).reshape(1) * (1.0 / (voxels * 64))
    grad_time = temb[:, None] * act_sum[:, :64]
    return (
        predicted.reshape(latents.shape),
        mean_loss,
        grad_conv,
        grad_coarse,
        totals[1728:1792, :64],
        grad_time,
        grads[0, :64],
        grads[0, 64:],
    )


def solution(mesh):
    blocks = P(ALL, None, None, None, None)
    return jax.shard_map(
        shards,
        mesh=mesh,
        in_specs=(blocks, blocks, P(ALL, None)) + (P(),) * 7,
        out_specs=(blocks,) + (P(),) * 7,
        check_vma=False,
    )
```

```python
import math

import jax
import jax.numpy as jnp
import numpy as np
from jax import lax
from jax.experimental import pallas as pl
from jax.experimental.pallas import tpu as pltpu
from jax.sharding import PartitionSpec as P

ALL = ("bx", "by", "cz")
CHIPS = ("bx", "by")
BF = jnp.bfloat16
F32 = jnp.float32
EPS = 1e-05
GROUP = 2
VMEM_LIMIT = 56 * 1024 * 1024
SHIFT_LANE = 65


def face_spec(dim, index):
    shape = tuple(1 if d == dim else 16 for d in range(3)) + (64,)
    where = tuple(index if d == dim else 0 for d in range(4))
    return pl.BlockSpec(shape, lambda i: where)


def call(kernel, outs, args, scratch=(), faces=()):
    vmem = pl.BlockSpec(memory_space=pltpu.VMEM)
    specs = list(faces) + [vmem] * (len(args) - 1 - len(faces))
    return pl.pallas_call(
        kernel,
        grid=(1,),
        out_shape=outs,
        in_specs=[pl.BlockSpec(memory_space=pltpu.SMEM)] + specs,
        out_specs=[vmem] * len(outs),
        scratch_shapes=list(scratch),
        compiler_params=pltpu.CompilerParams(vmem_limit_bytes=VMEM_LIMIT),
    )(*args)


def like(shape, dtype):
    return jax.ShapeDtypeStruct(shape, dtype)


def keep(cond, value):
    return jnp.where(cond, value, jnp.zeros_like(value))


def bits(info):
    return info[0, 0], info[0, 1], info[0, 2], lax.axis_index("cz")


def start16(bit):
    return pl.multiple_of(bit * 16, 16)


def cell_rows(first, second, face, on):
    rows = []
    for r in range(4):
        for s in range(4):
            here = on & (first == r // 2) & (second == s // 2)
            rows.append(keep(here, face[r % 2][s % 2]))
    return jnp.concatenate(rows, axis=0)


def row_of(cells, p):
    return cells[p : p + 1]


def z_message(info, lat, out, pooled):
    px, py, pz, kz = bits(info)
    on = pz == 1 - kz
    zsel = 15 * (1 - kz)
    out[...] = jnp.zeros(out.shape, BF)
    pick = lax.broadcasted_iota(jnp.int32, (16, 16, 64), 1) == zsel
    sums = [[None, None], [None, None]]
    for y in range(16):
        slab = lat[:, y].astype(F32)
        face = jnp.sum(jnp.where(pick, slab, 0.0), axis=1)
        out[py * 16 + y, pl.ds(start16(px), 16), :] = keep(on, face).astype(BF)
        for a in range(2):
            part = jnp.sum(slab[8 * a : 8 * a + 8], axis=0)
            old = sums[a][y // 8]
            sums[a][y // 8] = part if old is None else old + part
    cells = []
    for a in range(2):
        for b in range(2):
            for c in range(2):
                cells.append(jnp.sum(sums[a][b][8 * c : 8 * c + 8], axis=0, keepdims=True))
    cells = jnp.concatenate(cells, axis=0) * (1.0 / math.sqrt(512.0))
    cells = cells.astype(BF).astype(F32)
    pooled[...] = jnp.concatenate([cells, jnp.zeros((8, 64), F32)], axis=0).astype(BF)
    face = [
        [jnp.where(kz == 0, row_of(cells, 4 * a + 2 * b + 1), row_of(cells, 4 * a + 2 * b)) for a in range(2)]
        for b in range(2)
    ]
    rows = cell_rows(py, px, face, on)
    out[32] = jnp.concatenate([rows, jnp.zeros((16, 64), F32)], axis=0).astype(BF)


def y_messages(info, low, high, rz, pooled, down, up):
    px, py, pz, kz = bits(info)
    cells = pooled[...].astype(F32)
    halo = rz[32].astype(F32)
    for out, face, bit, line, q in ((down, low, 0, 0, 0), (up, high, 1, 31, 1)):
        on = py == bit
        out[...] = jnp.zeros(out.shape, BF)
        out[pl.ds(start16(px), 16), pl.ds(start16(pz), 16), :] = keep(on, face[:, 0])
        out[32] = rz[line]
        picked = [[row_of(cells, 4 * a + 2 * q + c) for c in range(2)] for a in range(2)]
        rows = cell_rows(px, pz, picked, on)
        tail = halo[12:16] if q else halo[0:4]
        out[33] = jnp.concatenate([rows, tail, jnp.zeros((12, 64), F32)], axis=0).astype(BF)


def x_messages(info, low, high, rz, rym, ryp, pooled, down, up):
    px, py, pz, kz = bits(info)
    cells = pooled[...].astype(F32)
    halo = rz[32].astype(F32)
    halo_m = rym[33].astype(F32)
    halo_p = ryp[33].astype(F32)
    line_m = rym[32].astype(F32)
    line_p = ryp[32].astype(F32)
    where16 = lax.broadcasted_iota(jnp.int32, (32, 16, 64), 1)
    for out, face, bit, line, q in ((down, low, 0, 0, 0), (up, high, 1, 31, 1)):
        on = px == bit
        out[...] = jnp.zeros(out.shape, BF)
        out[pl.ds(start16(py), 16), pl.ds(start16(pz), 16), :] = keep(on, face[0])
        slab = rz[0:32, 16 * q : 16 * q + 16, :].astype(F32)
        out[32] = jnp.sum(jnp.where(where16 == 15 * q, slab, 0.0), axis=1).astype(BF)
        out[33] = rym[line]
        out[34] = ryp[line]
        picked = [[row_of(cells, 4 * q + 2 * b + c) for c in range(2)] for b in range(2)]
        rows = cell_rows(py, pz, picked, on)
        corners = [line_m[line : line + 1], line_p[line : line + 1], jnp.zeros((14, 64), F32)]
        out[35] = jnp.concatenate(corners + [rows], axis=0).astype(BF)
        c0 = 3 * q
        parts = [row_of(halo, 4 * cy + c0) for cy in range(4)]
        parts += [halo_m[4 * c0 : 4 * c0 + 4], halo_p[4 * c0 : 4 * c0 + 4]]
        parts += [row_of(halo_m, 16 + c0), row_of(halo_p, 16 + c0), jnp.zeros((18, 64), F32)]
        out[36] = jnp.concatenate(parts, axis=0).astype(BF)


def coarse_table():
    pooled, rz, rym, ryp, rxm, rxp = 0, 16, 32, 64, 96, 128
    table = np.zeros((16, 224, 160), np.float32)
    for combo in range(16):
        bit = ((combo >> 3) & 1, (combo >> 2) & 1, (combo >> 1) & 1)
        core = combo & 1
        for tap in range(27):
            off = (tap // 9, tap // 3 % 3, tap % 3)
            for p in range(8):
                at = (p // 4, p // 2 % 2, p % 2)
                pos = [2 * bit[d] - 1 + off[d] + at[d] for d in range(3)]
                x, y, z = pos
                out_z = z < 0 or z > 3
                if out_z and (z < 0) != (core == 1):
                    continue
                if x < 0 or x > 3:
                    base = rxm if x < 0 else rxp
                    if y < 0 or y > 3:
                        side = 0 if y < 0 else 1
                        row = 16 + (12 + side if out_z else 4 + 4 * side + z)
                    else:
                        row = 16 + y if out_z else 4 * y + z
                    row = base + row
                elif y < 0 or y > 3:
                    row = (rym if y < 0 else ryp) + (16 + x if out_z else 4 * x + z)
                elif out_z:
                    row = rz + 4 * y + x
                else:
                    own = [pos[d] - 2 * bit[d] for d in range(3)]
                    if min(own) < 0 or max(own) > 1:
                        continue
                    row = pooled + 4 * own[0] + 2 * own[1] + own[2]
                table[combo, 8 * tap + p, row] = 1.0
    return table


class Window:
    def __init__(self, info, rz, rym, ryp):
        px, py, pz, kz = bits(info)
        self.pz, self.rz, self.rym, self.ryp = pz, rz, rym, ryp
        self.z0 = pl.ds(start16(pz), 16)
        self.z1 = pl.ds(start16(1 - pz), 16)
        self.xs = pl.ds(start16(px), 16)
        self.ys = pl.ds(start16(py), 16)
        self.xlo, self.xhi, self.ylo, self.yhi = px == 0, px == 1, py == 0, py == 1
        self.on_low = (pz == 0) & (kz == 1)
        self.on_high = (pz == 1) & (kz == 0)
        self.row16 = lax.broadcasted_iota(jnp.int32, (16, 16, 64), 1)
        self.z_row = lax.broadcasted_iota(jnp.int32, (9, 16, 128), 1)

    def edge(self, block):
        return jnp.sum(jnp.where(self.row16[: block.shape[0]] == 15 * self.pz, block.astype(F32), 0.0), axis=1)

    def edge1(self, ref, i):
        return self.edge(ref[i : i + 1, self.z1, :])

    def low_of(self, e, h):
        return keep(self.pz == 1, e) + keep(self.on_low, h)

    def high_of(self, e, h):
        return keep(self.pz == 0, e) + keep(self.on_high, h)

    def offsets(self, evens, odds, first, last, zl, zh):
        left = jnp.concatenate([first[None], odds], axis=0)
        right = jnp.concatenate([evens, last[None]], axis=0)
        tile = jnp.concatenate([left, right], axis=2)
        wide = tile.astype(F32)
        down = jnp.where(self.z_row == 0, zl, pltpu.roll(wide, 1, 1)).astype(BF)
        up = jnp.where(self.z_row == 15, zh, pltpu.roll(wide, 15, 1)).astype(BF)
        return down, tile, up


def one(ref, i, j):
    return ref[i].astype(F32)[j : j + 1]


def interior(info, lat, rz, rym, ryp, weight, raw, scene, columns):
    w = Window(info, rz, rym, ryp)
    y_low = keep(w.ylo, rym[w.xs, w.z0, :])
    y_high = keep(w.yhi, ryp[w.xs, w.z0, :])
    e_low = keep(w.ylo, w.edge(rym[w.xs, w.z1, :]))
    e_high = keep(w.yhi, w.edge(ryp[w.xs, w.z1, :]))
    h_low = jnp.where(w.ylo, rym[32, w.xs, :], rz[15, w.xs, :]).astype(F32)
    h_high = jnp.where(w.yhi, ryp[32, w.xs, :], rz[16, w.xs, :]).astype(F32)
    h_mid = rz[w.ys, w.xs, :].astype(F32)

    def packed(of):
        rows = [of(e_low, h_low)] + [of(jnp.zeros((16, 64), F32), h_mid[y]) for y in range(16)]
        rows.append(of(e_high, h_high))
        return [jnp.concatenate([rows[2 * k], rows[2 * k + 1]], axis=1) for k in range(9)]

    below, above = packed(w.low_of), packed(w.high_of)
    inner = [None] * 3
    for x in range(16):
        zl = jnp.concatenate([below[k][x : x + 1][None] for k in range(9)], axis=0)
        zh = jnp.concatenate([above[k][x : x + 1][None] for k in range(9)], axis=0)
        planes = w.offsets(lat[x, :, 0], lat[x, :, 1], y_low[x], y_high[x], zl, zh)
        for oz, plane in enumerate(planes):
            scene[oz, x] = plane
            wide = plane.astype(F32)
            inner[oz] = wide if x == 0 else inner[oz] + wide
    for oz in range(3):
        columns[oz] = jnp.sum(inner[oz], axis=1)
    for first, count in ((1, 4), (5, 4), (9, 4), (13, 2)):
        pieces = []
        for tap in range(9):
            ox, oz = tap // 3, tap % 3
            for dk in range(2):
                at = first + ox - 1
                pieces.append(scene[oz, at : at + count, dk : dk + 8].reshape(128 * count, 128))
        value = jnp.dot(jnp.concatenate(pieces, axis=1), weight[...], preferred_element_type=F32)
        raw[(first - 1) * 128 : (first - 1 + count) * 128] = value


def forward(info, near_low, near_high, raw, columns, rz, rym, ryp, rxm, rxp, pooled, table, weight, coarse_weight, time_bias, act, ends, patch_out, stats, shift):
    w = Window(info, rz, rym, ryp)
    nought = jnp.zeros((16, 64), BF)

    def sides(rx, out, inner):
        first = jnp.where(
            out,
            jnp.where(w.ylo, rx[33, w.z0, :], rx[15, w.z0, :]),
            jnp.where(w.ylo, rym[inner, w.z0, :], nought),
        )
        last = jnp.where(
            out,
            jnp.where(w.yhi, rx[34, w.z0, :], rx[16, w.z0, :]),
            jnp.where(w.yhi, ryp[inner, w.z0, :], nought),
        )
        return first, last

    def side_columns(rx, out, inner, of):
        half = rz[w.ys, 0:16, :] if inner < 16 else rz[w.ys, 16:32, :]
        inner_h = jnp.sum(jnp.where(w.row16 == inner % 16, half.astype(F32), 0.0), axis=1)
        e_mid = keep(out, w.edge(rx[w.ys, w.z1, :]))
        hh = jnp.where(out, rx[32, w.ys, :].astype(F32), inner_h)
        e_first = jnp.where(
            out,
            jnp.where(w.ylo, w.edge1(rx, 33), w.edge1(rx, 15)),
            keep(w.ylo, w.edge1(rym, inner)),
        )
        h_first = jnp.where(
            out,
            jnp.where(w.ylo, one(rx, 35, 0), one(rx, 32, 15)),
            jnp.where(w.ylo, one(rym, 32, inner), one(rz, 15, inner)),
        )
        e_last = jnp.where(
            out,
            jnp.where(w.yhi, w.edge1(rx, 34), w.edge1(rx, 16)),
            keep(w.yhi, w.edge1(ryp, inner)),
        )
        h_last = jnp.where(
            out,
            jnp.where(w.yhi, one(rx, 35, 1), one(rx, 32, 16)),
            jnp.where(w.yhi, one(ryp, 32, inner), one(rz, 16, inner)),
        )
        mid = of(e_mid, hh)
        rows = [of(e_first, h_first)] + [mid[y : y + 1] for y in range(16)] + [of(e_last, h_last)]
        return [jnp.concatenate([rows[2 * k], rows[2 * k + 1]], axis=1)[None] for k in range(9)]

    for e, rx, out, inner in ((0, rxm, w.xlo, 15), (1, rxp, w.xhi, 16)):
        zl = jnp.concatenate(side_columns(rx, out, inner, w.low_of), axis=0)
        zh = jnp.concatenate(side_columns(rx, out, inner, w.high_of), axis=0)
        first, last = sides(rx, out, inner)
        plane = keep(out, rx[w.ys, w.z0, :]).reshape(8, 2, 16, 64)
        for oz, tile in enumerate(w.offsets(plane[:, 0], plane[:, 1], first, last, zl, zh)):
            ends[e, oz] = tile

    source = jnp.concatenate(
        [pooled[...], rz[32, 0:16, :], rym[33], ryp[33], rxm[35, 16:32, :], rxm[36, 0:16, :], rxp[35, 16:32, :], rxp[36, 0:16, :]],
        axis=0,
    )
    taps = jnp.dot(table[...], source, preferred_element_type=F32)
    patch = jnp.concatenate([taps[8 * t : 8 * t + 8] for t in range(27)], axis=1)
    patch_out[...] = jnp.concatenate([patch, patch], axis=0).astype(BF)
    coarse = jnp.dot(patch_out[...], coarse_weight[...], preferred_element_type=F32)
    coarse = coarse.astype(BF).astype(F32)
    coarse = jnp.concatenate([coarse, coarse], axis=1)
    z_half = lax.broadcasted_iota(jnp.int32, (16, 128), 0) < 8
    added = []
    for q in range(4):
        added.append(jnp.where(z_half, coarse[2 * q : 2 * q + 1], coarse[2 * q + 1 : 2 * q + 2]) + time_bias[...])

    pieces = []
    for tap in range(9):
        ox, oz = tap // 3, tap % 3
        low = ends[0, oz] if ox == 0 else near_low[oz, ox - 1]
        high = ends[1, oz] if ox == 2 else near_high[oz, ox]
        for dk in range(2):
            pieces.append(jnp.concatenate([low[dk : dk + 8], high[dk : dk + 8]], axis=0).reshape(256, 128))
    edges = jnp.dot(jnp.concatenate(pieces, axis=1), weight[...], preferred_element_type=F32)

    total = jnp.zeros((1, 128), F32)
    squares = jnp.zeros((1, 128), F32)
    for x in range(16):
        if x == 0:
            value = edges[:128]
        elif x == 15:
            value = edges[128:]
        else:
            value = raw[(x - 1) * 128 : x * 128]
        value = value.reshape(2, 4, 16, 128)
        a = x // 8
        value = jnp.concatenate([(value[b] + added[2 * a + b][None])[None] for b in range(2)], axis=0).reshape(128, 128)
        act[x * 128 : x * 128 + 128] = value
        total = total + jnp.sum(value, axis=0, keepdims=True)
        squares = squares + jnp.sum(value * value, axis=0, keepdims=True)
    shift[...] = jnp.zeros(shift.shape, F32)

    def place(tap, slot, value):
        row = SHIFT_LANE + 2 * (tap // 4 + slot)
        u = tap % 4
        shift[u // 2, row : row + 1, 64 * (u % 2) : 64 * (u % 2) + 64] = value

    for oz in range(3):
        inner = columns[oz]
        planes = (ends[0, oz], near_low[oz, 0], near_high[oz, 1], ends[1, oz])
        outer = [jnp.sum(plane.astype(F32), axis=1) for plane in planes]
        for ox, part in enumerate((inner + outer[0] - outer[2], inner, inner - outer[1] + outer[3])):
            all_columns = jnp.sum(part, axis=0, keepdims=True)
            whole = all_columns[:, :64] + all_columns[:, 64:]
            y0, y1 = part[0:1, :64], part[0:1, 64:]
            y16, y17 = part[8:9, :64], part[8:9, 64:]
            for oy, window in enumerate((whole - y16 - y17, whole - y0 - y17, whole - y0 - y1)):
                place(9 * ox + 3 * oy + oz, 0, window)
    for t in range(27):
        place(t, 7, 512.0 * jnp.sum(taps[8 * t : 8 * t + 8], axis=0, keepdims=True))

    lane = lax.broadcasted_iota(jnp.int32, (1, 128), 1)
    pairs = pair_sum(squares + pltpu.roll(squares, 64, 1))
    row = jnp.where(lane < 64, total + pltpu.roll(total, 64, 1), jnp.where(lane % 2 == 0, pairs, 0.0))
    for u in range(2):
        stats[128 * u : 128 * u + 128] = shift[u].T + row


def pair_sum(row):
    lane = lax.broadcasted_iota(jnp.int32, row.shape, 1)
    return row + jnp.where(lane % 2 == 0, pltpu.roll(row, 127, 1), pltpu.roll(row, 1, 1))


def halves(row):
    lane = lax.broadcasted_iota(jnp.int32, row.shape, 1)
    other = pltpu.roll(row, 64, 1)
    return jnp.where(lane < 64, row, other), jnp.where(lane < 64, other, row)


def moments(gathered, count):
    row = jnp.sum(gathered[...], axis=0, keepdims=True)
    sums, upper = halves(row)
    lane = lax.broadcasted_iota(jnp.int32, row.shape, 1)
    squares = jnp.where(lane % 2 == 0, upper, pltpu.roll(upper, 1, 1))
    mean = pair_sum(sums) / count
    var = squares / count - mean * mean
    return row, sums, mean, 1.0 / jnp.sqrt(var + EPS)


def backward(voxels):
    count = float(voxels * GROUP)
    scale = 1.0 / (voxels * 64)

    def kernel(info, act, gathered, target, gain, bias, weight, weight_t, scene, ends, patch, stats, predicted, payload, cotangent):
        kz = lax.axis_index("cz")
        _, _, mean, rstd = moments(gathered, count)
        gains = jnp.zeros((1, 128), F32)
        biases = jnp.zeros((1, 128), F32)
        lost = jnp.zeros((1, 128), F32)
        outer = jnp.zeros((128, 128), F32)
        cells = [[None] * 4, [None] * 4]
        for x in range(0, 16, 2):
            rows = slice(x * 128, x * 128 + 256)
            normalized = (act[rows] - mean) * rstd
            shifted = normalized * gain[...] + bias[...]
            sigma = jax.nn.sigmoid(shifted)
            hidden = (shifted * sigma).astype(BF)
            output = jnp.dot(hidden, weight[...], preferred_element_type=F32)
            goal = jnp.concatenate([target[x : x + 2, :, 0], target[x : x + 2, :, 1]], axis=3)
            residue = output - goal.reshape(256, 128).astype(F32)
            shown = output.astype(BF).reshape(2, 8, 16, 128)
            predicted[x : x + 2, :, 0] = shown[..., :64]
            predicted[x : x + 2, :, 1] = shown[..., 64:]
            upstream = (2.0 * scale * residue).astype(BF)
            back = jnp.dot(upstream, weight_t[...], preferred_element_type=F32)
            value = back * sigma * (1.0 + shifted * (1.0 - sigma))
            gains = gains + jnp.sum(value * normalized, axis=0, keepdims=True)
            biases = biases + jnp.sum(value, axis=0, keepdims=True)
            lost = lost + jnp.sum(residue * residue, axis=0, keepdims=True)
            outer = outer + lax.dot_general(hidden, upstream, (((0,), (0,)), ((), ())), preferred_element_type=F32)
            value = value * (gain[...] * rstd)
            for part, wide in enumerate((value, normalized)):
                flipped = wide.T.astype(BF)
                cotangent[64 * part : 64 * part + 64, rows] = flipped[:64]
                cotangent[128 + 64 * part : 192 + 64 * part, rows] = flipped[64:]
                planes = wide.reshape(2, 2, 4, 16, 128)
                for b in range(2):
                    q = 2 * (x // 8) + b
                    cell = jnp.sum(planes[:, b], axis=(0, 1))
                    old = cells[part][q]
                    cells[part][q] = cell if old is None else old + cell

        def store(tap, slot, value):
            u = tap % 4
            half = jnp.where(kz == u // 2, 0, 1)
            payload.at[half][pl.ds(1024 * (u % 2) + slot + tap // 4, 64, stride=16), :] = value

        rows = []
        for q in range(4):
            for c in range(2):
                sums = [jnp.sum(cells[p][q][8 * c : 8 * c + 8], axis=0, keepdims=True) for p in range(2)]
                rows.append(jnp.concatenate([r[:, :64] + r[:, 64:] for r in sums], axis=1))
        rows = jnp.concatenate(rows, axis=0)
        high = rows.astype(BF)
        split = jnp.concatenate([high.astype(F32), rows - high.astype(F32)], axis=0).astype(BF)
        coarse = lax.dot_general(patch[...], split, (((0,), (0,)), ((), ())), preferred_element_type=F32)
        for t in range(27):
            store(t, 7, coarse[64 * t : 64 * t + 64])
        for ox in range(3):
            for oz in range(3):
                parts = []
                for dk in range(2):
                    planes = [scene[oz, max(ox - 1, 0) : min(ox + 15, 16), dk : dk + 8]]
                    if ox == 0:
                        planes = [ends[0, oz, dk : dk + 8][None]] + planes
                    if ox == 2:
                        planes = planes + [ends[1, oz, dk : dk + 8][None]]
                    parts.append(jnp.concatenate(planes, axis=0).reshape(2048, 128))
                window = jnp.concatenate(parts, axis=1)
                product = jnp.dot(cotangent[...], window, preferred_element_type=F32).T
                for oy in range(3):
                    value = product[64 * oy : 64 * oy + 64, :128] + product[64 * oy + 64 : 64 * oy + 128, 128:]
                    store(9 * ox + 3 * oy + oz, 0, value)
        nought = jnp.zeros((64, 64), F32)
        store(27, 0, jnp.concatenate([outer[:64, :64] + outer[64:, 64:], nought], axis=1))
        loss = jnp.broadcast_to(jnp.sum(lost, axis=1, keepdims=True), (64, 128))
        high = loss.astype(BF).astype(F32)
        lane = lax.broadcasted_iota(jnp.int32, (64, 128), 1)
        mine = jnp.where(lane == 2 * kz, high, jnp.where(lane == 2 * kz + 1, loss - high, 0.0))
        store(27, 7, mine)
        lane = lax.broadcasted_iota(jnp.int32, (1, 128), 1)
        row = jnp.where(lane < 64, gains + pltpu.roll(gains, 64, 1), biases + pltpu.roll(biases, 64, 1))
        wide = jnp.broadcast_to(row, (128, 128))
        for half in range(2):
            payload.at[half][pl.ds(14, 128, stride=16), :] = wide
            slot = jnp.where(kz == half, 0, 1)
            payload.at[slot][pl.ds(15, 128, stride=16), :] = stats[128 * half : 128 * half + 128]

    return kernel


def slopes(norms, gain, count):
    grad_gain, grad_bias = halves(norms)
    return pair_sum(gain * grad_bias) / count, pair_sum(gain * grad_gain) / count


def pair_add(voxels):
    total_count = float(voxels * GROUP)
    count = float(2 * 4096 * GROUP)

    def kernel(info, mine, other, gathered, gain, out):
        _, _, _, rstd = moments(gathered, total_count)
        total = (mine[...] + other[...]).reshape(-1, 16, 128)
        m1, m2 = slopes(total[0, 14:15], gain[...], count)
        row = lax.broadcasted_iota(jnp.int32, total.shape, 1)
        lane = lax.broadcasted_iota(jnp.int32, total.shape, 2)
        picked = (lane == SHIFT_LANE + 2 * row) & (row < 14)
        ones = jnp.sum(jnp.where(picked, total[:, 15:16], 0.0), axis=2, keepdims=True)
        centred = total - (m1 * rstd)[None] * ones - (m2 * rstd)[None] * pltpu.roll(total, 64, 2)
        total = jnp.where((lane < 64) & (row < 14), centred, total)
        lost = pltpu.roll(total - total.astype(BF).astype(F32), 1, 1)
        out[...] = jnp.where(row == 15, lost, total).astype(BF)

    return kernel


def combine(voxels):
    count = float(voxels * GROUP)
    pair_count = float(2 * 4096 * GROUP)

    def kernel(info, pieces, gathered, gain, copies, act_sum, grads):
        _, sums, mean, rstd = moments(gathered, count)
        value = pieces[...].astype(F32)
        chips = value.shape[0]
        seen = value[:, 14] + value[:, 15]
        norms = jnp.sum(seen, axis=0, keepdims=True)
        grads[...] = norms
        grad_gain, grad_bias = halves(norms)
        m1, m2 = slopes(norms, gain[...], count)
        centred = (sums - voxels * mean) * rstd
        act_sum[...] = rstd * (gain[...] * grad_bias - voxels * m1 - m2 * centred)
        own1, own2 = slopes(seen, gain[...], pair_count)
        delta1, delta2 = (own1 - m1) * rstd, (own2 - m2) * rstd
        ones = gathered[0:chips] + gathered[chips : 2 * chips]
        back = lax.dot_general(
            ones, delta1, (((0,), (0,)), ((), ())), preferred_element_type=F32, precision=lax.Precision.HIGHEST
        )
        back = [back[SHIFT_LANE + 2 * r : SHIFT_LANE + 2 * r + 1] for r in range(14)]
        back = jnp.concatenate(back + [jnp.zeros((2, 128), F32)], axis=0)
        total = jnp.sum(value + delta2[:, None] * pltpu.roll(value, 64, 2), axis=0) + back
        lane = lax.broadcasted_iota(jnp.int32, (7, 128), 1)
        both = jnp.where(lane < 64, total[:7], pltpu.roll(total[7:14], 64, 1))
        lost = both[6:7] - both[6:7].astype(BF).astype(F32)
        piece = jnp.concatenate([both, lost], axis=0).astype(BF)
        copies[...] = jnp.broadcast_to(piece[None], copies.shape)

    return kernel


def spread(info, near, far, conv, coarse, out, loss, rows):
    kz = lax.axis_index("cz")
    rows[pl.ds(pl.multiple_of(1024 * kz, 1024), 1024), :] = near[...].astype(F32).reshape(1024, 128)
    rows[pl.ds(pl.multiple_of(1024 * (1 - kz), 1024), 1024), :] = far[...].astype(F32).reshape(1024, 128)
    for tap in range(28):
        tile = rows[pl.ds(512 * (tap % 4) + tap // 4, 64, stride=8), :]
        if tap < 27:
            conv[tap] = tile[:, :64]
            coarse[tap] = tile[:, 64:]
        else:
            out[...] = tile[:, :64]
            parts = tile[0:1] + rows[2048 - 512 + 7 : 2048 - 512 + 8, :]
            lane = lax.broadcasted_iota(jnp.int32, (1, 128), 1)
            whole = jnp.sum(jnp.where((lane >= 64) & (lane < 68), parts, 0.0), axis=1, keepdims=True)
            loss[...] = jnp.broadcast_to(whole, (1, 128))


def exchange(rows):
    out = lax.all_to_all(rows.reshape(rows.shape[0], 1, 128), ("cz",) + CHIPS, 0, 0, tiled=True)
    return out.reshape(rows.shape)


def neighbours(down, up, axis):
    ends = lax.axis_size(axis) - 1
    before = lax.ppermute(up, axis, [(i, i + 1) for i in range(ends)])
    after = lax.ppermute(down, axis, [(i + 1, i) for i in range(ends)])
    return before, after


def time_embedding(timestep, width):
    halfway = width // 2
    indices = jnp.arange(halfway).astype(F32)
    freqs = jnp.exp(indices * (-math.log(10000.0) / halfway))
    angles = timestep[0].astype(F32) * freqs
    return jnp.concatenate([jnp.sin(angles), jnp.cos(angles)])


def twice(row):
    return jnp.concatenate([row, row]).reshape(1, 128)


def diagonal(square):
    nought = jnp.zeros_like(square)
    return jnp.block([[square, nought], [nought, square]])


def shards(latents, target, block_coords, timestep, conv_weight, coarse_weight, out_weight, time_weight, norm_gain, norm_bias):
    devices = lax.axis_size("bx") * lax.axis_size("by") * lax.axis_size("cz")
    voxels = devices * 4096
    core = lax.axis_index("cz").astype(jnp.int32)
    at = block_coords[0]
    info = block_coords
    lat = latents[0]
    lat_pairs = lat.reshape(16, 8, 2, 16, 64)

    mz, pooled = call(z_message, [like((33, 32, 64), BF), like((16, 64), BF)], [info, lat])
    rz = lax.ppermute(mz, "cz", [(0, 1), (1, 0)])
    plane = like((34, 32, 64), BF)
    down, up = call(y_messages, [plane, plane], [info, lat, lat, rz, pooled], (), [face_spec(1, 0), face_spec(1, 15)])
    rym, ryp = neighbours(down, up, "by")
    plane = like((37, 32, 64), BF)
    down, up = call(x_messages, [plane, plane], [info, lat, lat, rz, rym, ryp, pooled], (), [face_spec(0, 0), face_spec(0, 15)])
    rxm, rxp = neighbours(down, up, "bx")

    temb = time_embedding(timestep, time_weight.shape[0])
    time_bias = jnp.sum(temb[:, None] * time_weight.astype(F32), axis=0)
    taps = conv_weight.reshape(3, 3, 3, 64, 64).transpose(0, 2, 1, 3, 4)
    taps = jnp.stack(
        [jnp.pad(taps, ((0, 0), (0, 0), (b, 1 - b), (0, 0), (0, 0))) for b in range(2)], axis=4
    ).reshape(9 * 256, 128)
    combo = 8 * at[0] + 4 * at[1] + 2 * at[2] + core
    table = lax.dynamic_index_in_dim(jnp.asarray(coarse_table(), BF), combo, keepdims=False)

    raw, scene, columns = call(
        interior,
        [like((1792, 128), F32), like((3, 16, 9, 16, 128), BF), like((3, 9, 128), F32)],
        [info, lat_pairs, rz, rym, ryp, taps],
    )
    pair = (3, 2, 9, 16, 128)
    act, ends, patch, stats = call(
        forward,
        [like((2048, 128), F32), like((2, 3, 9, 16, 128), BF), like((16, 1728), BF), like((devices, 128), F32)],
        [info, scene, scene, raw, columns, rz, rym, ryp, rxm, rxp, pooled, table, taps]
        + [coarse_weight.reshape(1728, 64), twice(time_bias)],
        [pltpu.VMEM((2, 128, 128), F32)],
        [pl.BlockSpec(pair, lambda i: (0, 0, 0, 0, 0)), pl.BlockSpec(pair, lambda i: (0, 7, 0, 0, 0))],
    )
    first = exchange(stats)
    gain, bias = twice(norm_gain), twice(norm_bias)
    weights = [diagonal(out_weight), diagonal(out_weight.T)]
    predicted, payload = call(
        backward(voxels),
        [like((16, 8, 2, 16, 64), BF), like((2, 2048, 128), F32)],
        [info, act, first, target.reshape(16, 8, 2, 16, 64), gain, bias] + weights + [scene, ends, patch, stats],
        [pltpu.VMEM((256, 2048), BF)],
    )
    swap = [(0, 1), (1, 0)]
    chips = devices // 2
    other = lax.ppermute(payload[1], "cz", swap)
    (pieces,) = call(pair_add(voxels), [like((chips, 16, 128), BF)], [info, payload[0], other, first, gain])
    pieces = lax.all_to_all(pieces, CHIPS, 0, 0, tiled=True)
    copies, act_sum, grads = call(
        combine(voxels),
        [like((chips, 8, 128), BF), like((1, 128), F32), like((1, 128), F32)],
        [info, pieces, first, gain],
    )
    near = lax.all_to_all(copies, CHIPS, 0, 0, tiled=True)
    far = lax.ppermute(near, "cz", swap)
    grad_conv, grad_coarse, grad_out, loss = call(
        spread,
        [like((27, 64, 64), F32), like((27, 64, 64), F32), like((64, 64), F32), like((1, 128), F32)],
        [info, near, far],
        [pltpu.VMEM((2048, 128), F32)],
    )
    return (
        predicted.reshape(latents.shape),
        loss[0, :1] * (1.0 / (voxels * 64)),
        grad_conv,
        grad_coarse,
        grad_out,
        temb[:, None] * act_sum[:, :64],
        grads[0, :64],
        grads[0, 64:],
    )


def solution(mesh):
    blocks = P(ALL, None, None, None, None)
    return jax.shard_map(
        shards,
        mesh=mesh,
        in_specs=(blocks, blocks, P(ALL, None)) + (P(),) * 7,
        out_specs=(blocks,) + (P(),) * 7,
        check_vma=False,
    )
```

```python
import functools
import math

import jax
import jax.numpy as jnp
import numpy as np
from jax import lax
from jax.experimental import pallas as pl
from jax.experimental.pallas import tpu as pltpu
from jax.sharding import PartitionSpec as P

ALL = ("bx", "by", "cz")
CHIPS = ("bx", "by")
BF = jnp.bfloat16
F32 = jnp.float32
EPS = 1e-05
GROUP = 2
VMEM_LIMIT = 56 * 1024 * 1024
SHIFT_LANE = 65


def face_spec(dim, index):
    shape = tuple(1 if d == dim else 16 for d in range(3)) + (64,)
    where = tuple(index if d == dim else 0 for d in range(4))
    return pl.BlockSpec(shape, lambda i: where)


def call(kernel, outs, args, scratch=(), faces=(), far_args=0, far_outs=0):
    vmem = pl.BlockSpec(memory_space=pltpu.VMEM)
    far = pl.BlockSpec(memory_space=pl.ANY)
    specs = list(faces) + [vmem] * (len(args) - 1 - len(faces) - far_args) + [far] * far_args
    return pl.pallas_call(
        kernel,
        grid=(1,),
        out_shape=outs,
        in_specs=[pl.BlockSpec(memory_space=pltpu.SMEM)] + specs,
        out_specs=[vmem] * (len(outs) - far_outs) + [far] * far_outs,
        scratch_shapes=list(scratch),
        compiler_params=pltpu.CompilerParams(vmem_limit_bytes=VMEM_LIMIT),
    )(*args)


def like(shape, dtype):
    return jax.ShapeDtypeStruct(shape, dtype)


def keep(cond, value):
    return jnp.where(cond, value, jnp.zeros_like(value))


def bits(info):
    return info[0, 0], info[0, 1], info[0, 2], lax.axis_index("cz")


def start16(bit):
    return pl.multiple_of(bit * 16, 16)


def cell_rows(first, second, face, on):
    rows = []
    for r in range(4):
        for s in range(4):
            here = on & (first == r // 2) & (second == s // 2)
            rows.append(keep(here, face[r % 2][s % 2]))
    return jnp.concatenate(rows, axis=0)


def row_of(cells, p):
    return cells[p : p + 1]


Z_TILES, Y_TILES, X_TILES = 1, 2, 5


def message(tiles):
    return like((9 + tiles, 16, 128), BF)


def plane(tiles):
    return pltpu.VMEM((32 + tiles, 32, 64), BF)


def side_by_side(rows):
    half = rows.shape[0] // 2
    return jnp.concatenate([rows[:half], rows[half:]], axis=rows.ndim - 1)


def write_message(out, face, tiles, first, second, on):
    out[0:8] = side_by_side(face)
    for t, rows in enumerate(tiles):
        out[8 + t] = side_by_side(rows).astype(BF)
    row = lax.broadcasted_iota(jnp.int32, (16, 128), 0)
    here = jnp.where(on, 2 * first + second, 99)
    out[8 + len(tiles)] = jnp.where(row == here, 1.0, 0.0).astype(BF)


def open_message(ref, out):
    tiles = ref.shape[0] - 9
    face = jnp.concatenate([ref[0:8, :, :64], ref[0:8, :, 64:]], axis=0)
    flags = ref[8 + tiles].astype(F32)
    for q in range(4):
        here = jnp.broadcast_to(flags[q : q + 1, :64], (16, 64))[None]
        out[16 * (q // 2) : 16 * (q // 2) + 16, 16 * (q % 2) : 16 * (q % 2) + 16, :] = jnp.where(
            here > 0.5, face.astype(F32), 0.0
        ).astype(BF)
    for t in range(tiles):
        out[32 + t] = jnp.concatenate([ref[8 + t, :, :64], ref[8 + t, :, 64:]], axis=0)


def z_message(info, lat, out, pooled):
    px, py, pz, kz = bits(info)
    zsel = 15 * (1 - kz)
    pick = lax.broadcasted_iota(jnp.int32, (16, 16, 64), 1) == zsel
    sums = [[None, None], [None, None]]
    faces = []
    for y in range(16):
        slab = lat[:, y].astype(F32)
        faces.append(jnp.sum(jnp.where(pick, slab, 0.0), axis=1)[None])
        for a in range(2):
            part = jnp.sum(slab[8 * a : 8 * a + 8], axis=0)
            old = sums[a][y // 8]
            sums[a][y // 8] = part if old is None else old + part
    cells = []
    for a in range(2):
        for b in range(2):
            for c in range(2):
                cells.append(jnp.sum(sums[a][b][8 * c : 8 * c + 8], axis=0, keepdims=True))
    cells = jnp.concatenate(cells, axis=0) * (1.0 / math.sqrt(512.0))
    cells = cells.astype(BF).astype(F32)
    pooled[...] = jnp.concatenate([cells, jnp.zeros((8, 64), F32)], axis=0).astype(BF)
    on = pz == 1 - kz
    face = [
        [jnp.where(kz == 0, row_of(cells, 4 * a + 2 * b + 1), row_of(cells, 4 * a + 2 * b)) for a in range(2)]
        for b in range(2)
    ]
    rows = jnp.concatenate([cell_rows(py, px, face, on), jnp.zeros((16, 64), F32)], axis=0)
    write_message(out, jnp.concatenate(faces, axis=0).astype(BF), [rows], py, px, on)


def y_messages(info, low, high, rz_in, pooled, down, up, rz):
    px, py, pz, kz = bits(info)
    open_message(rz_in, rz)
    cells = pooled[...].astype(F32)
    halo = rz[32].astype(F32)
    for out, face, bit, line, q in ((down, low, 0, 0, 0), (up, high, 1, 31, 1)):
        on = py == bit
        picked = [[row_of(cells, 4 * a + 2 * q + c) for c in range(2)] for a in range(2)]
        tail = halo[12:16] if q else halo[0:4]
        rows = jnp.concatenate([cell_rows(px, pz, picked, on), tail, jnp.zeros((12, 64), F32)], axis=0)
        write_message(out, face[:, 0], [rz[line], rows], px, pz, on)


def x_messages(info, low, high, rz_in, rym_in, ryp_in, pooled, down, up, rz, rym, ryp):
    px, py, pz, kz = bits(info)
    for ref, out in ((rz_in, rz), (rym_in, rym), (ryp_in, ryp)):
        open_message(ref, out)
    cells = pooled[...].astype(F32)
    halo = rz[32].astype(F32)
    halo_m = rym[33].astype(F32)
    halo_p = ryp[33].astype(F32)
    line_m = rym[32].astype(F32)
    line_p = ryp[32].astype(F32)
    where16 = lax.broadcasted_iota(jnp.int32, (32, 16, 64), 1)
    for out, face, bit, line, q in ((down, low, 0, 0, 0), (up, high, 1, 31, 1)):
        on = px == bit
        slab = rz[0:32, 16 * q : 16 * q + 16, :].astype(F32)
        z_line = jnp.sum(jnp.where(where16 == 15 * q, slab, 0.0), axis=1).astype(BF)
        picked = [[row_of(cells, 4 * q + 2 * b + c) for c in range(2)] for b in range(2)]
        corners = [line_m[line : line + 1], line_p[line : line + 1], jnp.zeros((14, 64), F32)]
        corners = jnp.concatenate(corners + [cell_rows(py, pz, picked, on)], axis=0)
        c0 = 3 * q
        parts = [row_of(halo, 4 * cy + c0) for cy in range(4)]
        parts += [halo_m[4 * c0 : 4 * c0 + 4], halo_p[4 * c0 : 4 * c0 + 4]]
        parts += [row_of(halo_m, 16 + c0), row_of(halo_p, 16 + c0), jnp.zeros((18, 64), F32)]
        tiles = [z_line, rym[line], ryp[line], corners, jnp.concatenate(parts, axis=0)]
        write_message(out, face[0], tiles, py, pz, on)


def coarse_table():
    pooled, rz, rym, ryp, rxm, rxp = 0, 16, 32, 64, 96, 128
    table = np.zeros((16, 224, 160), np.float32)
    for combo in range(16):
        bit = ((combo >> 3) & 1, (combo >> 2) & 1, (combo >> 1) & 1)
        core = combo & 1
        for tap in range(27):
            off = (tap // 9, tap // 3 % 3, tap % 3)
            for p in range(8):
                at = (p // 4, p // 2 % 2, p % 2)
                pos = [2 * bit[d] - 1 + off[d] + at[d] for d in range(3)]
                x, y, z = pos
                out_z = z < 0 or z > 3
                if out_z and (z < 0) != (core == 1):
                    continue
                if x < 0 or x > 3:
                    base = rxm if x < 0 else rxp
                    if y < 0 or y > 3:
                        side = 0 if y < 0 else 1
                        row = 16 + (12 + side if out_z else 4 + 4 * side + z)
                    else:
                        row = 16 + y if out_z else 4 * y + z
                    row = base + row
                elif y < 0 or y > 3:
                    row = (rym if y < 0 else ryp) + (16 + x if out_z else 4 * x + z)
                elif out_z:
                    row = rz + 4 * y + x
                else:
                    own = [pos[d] - 2 * bit[d] for d in range(3)]
                    if min(own) < 0 or max(own) > 1:
                        continue
                    row = pooled + 4 * own[0] + 2 * own[1] + own[2]
                table[combo, 8 * tap + p, row] = 1.0
    return table


class Window:
    def __init__(self, info, rz, rym, ryp):
        px, py, pz, kz = bits(info)
        self.pz, self.rz, self.rym, self.ryp = pz, rz, rym, ryp
        self.z0 = pl.ds(start16(pz), 16)
        self.z1 = pl.ds(start16(1 - pz), 16)
        self.xs = pl.ds(start16(px), 16)
        self.ys = pl.ds(start16(py), 16)
        self.xlo, self.xhi, self.ylo, self.yhi = px == 0, px == 1, py == 0, py == 1
        self.on_low = (pz == 0) & (kz == 1)
        self.on_high = (pz == 1) & (kz == 0)
        self.row16 = lax.broadcasted_iota(jnp.int32, (16, 16, 64), 1)
        self.z_row = lax.broadcasted_iota(jnp.int32, (9, 16, 128), 1)

    def edge(self, block):
        return jnp.sum(jnp.where(self.row16[: block.shape[0]] == 15 * self.pz, block.astype(F32), 0.0), axis=1)

    def edge1(self, ref, i):
        return self.edge(ref[i : i + 1, self.z1, :])

    def low_of(self, e, h):
        return keep(self.pz == 1, e) + keep(self.on_low, h)

    def high_of(self, e, h):
        return keep(self.pz == 0, e) + keep(self.on_high, h)

    def offsets(self, evens, odds, first, last, zl, zh):
        left = jnp.concatenate([first[None], odds], axis=0)
        right = jnp.concatenate([evens, last[None]], axis=0)
        tile = jnp.concatenate([left, right], axis=2)
        wide = tile.astype(F32)
        down = jnp.where(self.z_row == 0, zl, pltpu.roll(wide, 1, 1)).astype(BF)
        up = jnp.where(self.z_row == 15, zh, pltpu.roll(wide, 15, 1)).astype(BF)
        return down, tile, up


def one(ref, i, j):
    return ref[i].astype(F32)[j : j + 1]


def interior(info, lat, rz_in, rym_in, ryp_in, taps, raw, scene, columns, weight, rz, rym, ryp):
    for ref, out in ((rz_in, rz), (rym_in, rym), (ryp_in, ryp)):
        open_message(ref, out)
    nought = jnp.zeros((64, 64), BF)
    for tap in range(9):
        ox, oz = tap // 3, tap % 3
        for a in range(4):
            left = nought if a == 3 else taps[9 * ox + 3 * a + oz]
            right = nought if a == 0 else taps[9 * ox + 3 * a - 3 + oz]
            weight[256 * tap + 64 * a : 256 * tap + 64 * a + 64] = jnp.concatenate([left, right], axis=1)
    w = Window(info, rz, rym, ryp)
    y_low = keep(w.ylo, rym[w.xs, w.z0, :])
    y_high = keep(w.yhi, ryp[w.xs, w.z0, :])
    e_low = keep(w.ylo, w.edge(rym[w.xs, w.z1, :]))
    e_high = keep(w.yhi, w.edge(ryp[w.xs, w.z1, :]))
    h_low = jnp.where(w.ylo, rym[32, w.xs, :], rz[15, w.xs, :]).astype(F32)
    h_high = jnp.where(w.yhi, ryp[32, w.xs, :], rz[16, w.xs, :]).astype(F32)
    h_mid = rz[w.ys, w.xs, :].astype(F32)

    def packed(of):
        rows = [of(e_low, h_low)] + [of(jnp.zeros((16, 64), F32), h_mid[y]) for y in range(16)]
        rows.append(of(e_high, h_high))
        return [jnp.concatenate([rows[2 * k], rows[2 * k + 1]], axis=1) for k in range(9)]

    below, above = packed(w.low_of), packed(w.high_of)
    inner = [None] * 3
    for x in range(16):
        zl = jnp.concatenate([below[k][x : x + 1][None] for k in range(9)], axis=0)
        zh = jnp.concatenate([above[k][x : x + 1][None] for k in range(9)], axis=0)
        planes = w.offsets(lat[x, :, 0], lat[x, :, 1], y_low[x], y_high[x], zl, zh)
        for oz, plane in enumerate(planes):
            scene[oz, x] = plane
            wide = plane.astype(F32)
            inner[oz] = wide if x == 0 else inner[oz] + wide
    for oz in range(3):
        columns[oz] = jnp.sum(inner[oz], axis=1)
    for first, count in ((1, 4), (5, 4), (9, 4), (13, 2)):
        pieces = []
        for tap in range(9):
            ox, oz = tap // 3, tap % 3
            for dk in range(2):
                at = first + ox - 1
                pieces.append(scene[oz, at : at + count, dk : dk + 8].reshape(128 * count, 128))
        value = jnp.dot(jnp.concatenate(pieces, axis=1), weight[...], preferred_element_type=F32)
        raw[(first - 1) * 128 : (first - 1 + count) * 128] = value


def forward(
    info, near_low, near_high, raw, columns, rz_in, rym_in, ryp_in, rxm_in, rxp_in, pooled, weight,
    coarse_weight, temb, time_weight, tables, act, ends, patch_out, stats,
    shift, table, arrived, rz, rym, ryp, rxm, rxp
):
    px, py, pz, kz = bits(info)
    fetch = pltpu.make_async_copy(tables.at[8 * px + 4 * py + 2 * pz + kz], table, arrived)
    fetch.start()
    for ref, out in ((rz_in, rz), (rym_in, rym), (ryp_in, ryp), (rxm_in, rxm), (rxp_in, rxp)):
        open_message(ref, out)
    w = Window(info, rz, rym, ryp)
    nought = jnp.zeros((16, 64), BF)

    def sides(rx, out, inner):
        first = jnp.where(
            out,
            jnp.where(w.ylo, rx[33, w.z0, :], rx[15, w.z0, :]),
            jnp.where(w.ylo, rym[inner, w.z0, :], nought),
        )
        last = jnp.where(
            out,
            jnp.where(w.yhi, rx[34, w.z0, :], rx[16, w.z0, :]),
            jnp.where(w.yhi, ryp[inner, w.z0, :], nought),
        )
        return first, last

    def side_columns(rx, out, inner, of):
        half = rz[w.ys, 0:16, :] if inner < 16 else rz[w.ys, 16:32, :]
        inner_h = jnp.sum(jnp.where(w.row16 == inner % 16, half.astype(F32), 0.0), axis=1)
        e_mid = keep(out, w.edge(rx[w.ys, w.z1, :]))
        hh = jnp.where(out, rx[32, w.ys, :].astype(F32), inner_h)
        e_first = jnp.where(
            out,
            jnp.where(w.ylo, w.edge1(rx, 33), w.edge1(rx, 15)),
            keep(w.ylo, w.edge1(rym, inner)),
        )
        h_first = jnp.where(
            out,
            jnp.where(w.ylo, one(rx, 35, 0), one(rx, 32, 15)),
            jnp.where(w.ylo, one(rym, 32, inner), one(rz, 15, inner)),
        )
        e_last = jnp.where(
            out,
            jnp.where(w.yhi, w.edge1(rx, 34), w.edge1(rx, 16)),
            keep(w.yhi, w.edge1(ryp, inner)),
        )
        h_last = jnp.where(
            out,
            jnp.where(w.yhi, one(rx, 35, 1), one(rx, 32, 16)),
            jnp.where(w.yhi, one(ryp, 32, inner), one(rz, 16, inner)),
        )
        mid = of(e_mid, hh)
        rows = [of(e_first, h_first)] + [mid[y : y + 1] for y in range(16)] + [of(e_last, h_last)]
        return [jnp.concatenate([rows[2 * k], rows[2 * k + 1]], axis=1)[None] for k in range(9)]

    for e, rx, out, inner in ((0, rxm, w.xlo, 15), (1, rxp, w.xhi, 16)):
        zl = jnp.concatenate(side_columns(rx, out, inner, w.low_of), axis=0)
        zh = jnp.concatenate(side_columns(rx, out, inner, w.high_of), axis=0)
        first, last = sides(rx, out, inner)
        plane = keep(out, rx[w.ys, w.z0, :]).reshape(8, 2, 16, 64)
        for oz, tile in enumerate(w.offsets(plane[:, 0], plane[:, 1], first, last, zl, zh)):
            ends[e, oz] = tile

    source = jnp.concatenate(
        [pooled[...], rz[32, 0:16, :], rym[33], ryp[33], rxm[35, 16:32, :], rxm[36, 0:16, :], rxp[35, 16:32, :], rxp[36, 0:16, :]],
        axis=0,
    )
    fetch.wait()
    taps = jnp.dot(table[...], source, preferred_element_type=F32)
    patch = jnp.concatenate([taps[8 * t : 8 * t + 8] for t in range(27)], axis=1)
    patch_out[...] = jnp.concatenate([patch, patch], axis=0).astype(BF)
    coarse = jnp.dot(patch_out[...], coarse_weight[...], preferred_element_type=F32)
    coarse = coarse.astype(BF).astype(F32)
    coarse = jnp.concatenate([coarse, coarse], axis=1)
    time_bias = lax.dot_general(
        jnp.broadcast_to(temb[...], (8, 256)),
        time_weight[...].astype(F32),
        (((1,), (1,)), ((), ())),
        preferred_element_type=F32,
        precision=lax.Precision.HIGHEST,
    )[:1]
    time_bias = jnp.concatenate([time_bias, time_bias], axis=1)
    z_half = lax.broadcasted_iota(jnp.int32, (16, 128), 0) < 8
    added = []
    for q in range(4):
        added.append(jnp.where(z_half, coarse[2 * q : 2 * q + 1], coarse[2 * q + 1 : 2 * q + 2]) + time_bias)

    pieces = []
    for tap in range(9):
        ox, oz = tap // 3, tap % 3
        low = ends[0, oz] if ox == 0 else near_low[oz, ox - 1]
        high = ends[1, oz] if ox == 2 else near_high[oz, ox]
        for dk in range(2):
            pieces.append(jnp.concatenate([low[dk : dk + 8], high[dk : dk + 8]], axis=0).reshape(256, 128))
    edges = jnp.dot(jnp.concatenate(pieces, axis=1), weight[...], preferred_element_type=F32)

    total = jnp.zeros((1, 128), F32)
    squares = jnp.zeros((1, 128), F32)
    for x in range(16):
        if x == 0:
            value = edges[:128]
        elif x == 15:
            value = edges[128:]
        else:
            value = raw[(x - 1) * 128 : x * 128]
        value = value.reshape(2, 4, 16, 128)
        a = x // 8
        value = jnp.concatenate([(value[b] + added[2 * a + b][None])[None] for b in range(2)], axis=0).reshape(128, 128)
        act[x * 128 : x * 128 + 128] = value
        total = total + jnp.sum(value, axis=0, keepdims=True)
        squares = squares + jnp.sum(value * value, axis=0, keepdims=True)
    shift[...] = jnp.zeros(shift.shape, F32)

    def place(tap, slot, value):
        row = SHIFT_LANE + 2 * (tap // 4 + slot)
        u = tap % 4
        shift[u // 2, row : row + 1, 64 * (u % 2) : 64 * (u % 2) + 64] = value

    for oz in range(3):
        inner = columns[oz]
        planes = (ends[0, oz], near_low[oz, 0], near_high[oz, 1], ends[1, oz])
        outer = [jnp.sum(plane.astype(F32), axis=1) for plane in planes]
        for ox, part in enumerate((inner + outer[0] - outer[2], inner, inner - outer[1] + outer[3])):
            all_columns = jnp.sum(part, axis=0, keepdims=True)
            whole = all_columns[:, :64] + all_columns[:, 64:]
            y0, y1 = part[0:1, :64], part[0:1, 64:]
            y16, y17 = part[8:9, :64], part[8:9, 64:]
            for oy, window in enumerate((whole - y16 - y17, whole - y0 - y17, whole - y0 - y1)):
                place(9 * ox + 3 * oy + oz, 0, window)
    for t in range(27):
        place(t, 7, 512.0 * jnp.sum(taps[8 * t : 8 * t + 8], axis=0, keepdims=True))

    lane = lax.broadcasted_iota(jnp.int32, (1, 128), 1)
    pairs = pair_sum(squares + pltpu.roll(squares, 64, 1))
    row = jnp.where(lane < 64, total + pltpu.roll(total, 64, 1), jnp.where(lane % 2 == 0, pairs, 0.0))
    for u in range(2):
        stats[128 * u : 128 * u + 128] = shift[u].T + row


def pair_sum(row):
    lane = lax.broadcasted_iota(jnp.int32, row.shape, 1)
    return row + jnp.where(lane % 2 == 0, pltpu.roll(row, 127, 1), pltpu.roll(row, 1, 1))


def halves(row):
    lane = lax.broadcasted_iota(jnp.int32, row.shape, 1)
    other = pltpu.roll(row, 64, 1)
    return jnp.where(lane < 64, row, other), jnp.where(lane < 64, other, row)


def moments(gathered, count):
    row = jnp.sum(gathered[...], axis=0, keepdims=True)
    sums, upper = halves(row)
    lane = lax.broadcasted_iota(jnp.int32, row.shape, 1)
    squares = jnp.where(lane % 2 == 0, upper, pltpu.roll(upper, 1, 1))
    mean = pair_sum(sums) / count
    var = squares / count - mean * mean
    return row, sums, mean, 1.0 / jnp.sqrt(var + EPS)


def backward(voxels):
    count = float(voxels * GROUP)
    scale = 1.0 / (voxels * 64)

    def kernel(info, act, gathered, target, gain, bias, weight, weight_t, scene, ends, patch, stats, predicted, mine, other, cotangent, payload, sent):
        kz = lax.axis_index("cz")
        _, _, mean, rstd = moments(gathered, count)
        gains = jnp.zeros((1, 128), F32)
        biases = jnp.zeros((1, 128), F32)
        lost = jnp.zeros((1, 128), F32)
        outer = jnp.zeros((128, 128), F32)
        cells = [[None] * 4, [None] * 4]
        for x in range(0, 16, 2):
            rows = slice(x * 128, x * 128 + 256)
            normalized = (act[rows] - mean) * rstd
            shifted = normalized * gain[...] + bias[...]
            sigma = jax.nn.sigmoid(shifted)
            hidden = (shifted * sigma).astype(BF)
            output = jnp.dot(hidden, weight[...], preferred_element_type=F32)
            goal = jnp.concatenate([target[x : x + 2, :, 0], target[x : x + 2, :, 1]], axis=3)
            residue = output - goal.reshape(256, 128).astype(F32)
            shown = output.astype(BF).reshape(2, 8, 16, 128)
            predicted[x : x + 2, :, 0] = shown[..., :64]
            predicted[x : x + 2, :, 1] = shown[..., 64:]
            upstream = (2.0 * scale * residue).astype(BF)
            back = jnp.dot(upstream, weight_t[...], preferred_element_type=F32)
            value = back * sigma * (1.0 + shifted * (1.0 - sigma))
            gains = gains + jnp.sum(value * normalized, axis=0, keepdims=True)
            biases = biases + jnp.sum(value, axis=0, keepdims=True)
            lost = lost + jnp.sum(residue * residue, axis=0, keepdims=True)
            outer = outer + lax.dot_general(hidden, upstream, (((0,), (0,)), ((), ())), preferred_element_type=F32)
            value = value * (gain[...] * rstd)
            for part, wide in enumerate((value, normalized)):
                flipped = wide.T.astype(BF)
                cotangent[64 * part : 64 * part + 64, rows] = flipped[:64]
                cotangent[128 + 64 * part : 192 + 64 * part, rows] = flipped[64:]
                planes = wide.reshape(2, 2, 4, 16, 128)
                for b in range(2):
                    q = 2 * (x // 8) + b
                    cell = jnp.sum(planes[:, b], axis=(0, 1))
                    old = cells[part][q]
                    cells[part][q] = cell if old is None else old + cell

        def store(tap, slot, value):
            u = tap % 4
            half = jnp.where(kz == u // 2, 0, 1)
            payload.at[half][pl.ds(1024 * (u % 2) + slot + tap // 4, 64, stride=16), :] = value

        rows = []
        for q in range(4):
            for c in range(2):
                sums = [jnp.sum(cells[p][q][8 * c : 8 * c + 8], axis=0, keepdims=True) for p in range(2)]
                rows.append(jnp.concatenate([r[:, :64] + r[:, 64:] for r in sums], axis=1))
        rows = jnp.concatenate(rows, axis=0)
        high = rows.astype(BF)
        split = jnp.concatenate([high.astype(F32), rows - high.astype(F32)], axis=0).astype(BF)
        coarse = lax.dot_general(patch[...], split, (((0,), (0,)), ((), ())), preferred_element_type=F32)
        for t in range(27):
            store(t, 7, coarse[64 * t : 64 * t + 64])
        for ox in range(3):
            for oz in range(3):
                parts = []
                for dk in range(2):
                    planes = [scene[oz, max(ox - 1, 0) : min(ox + 15, 16), dk : dk + 8]]
                    if ox == 0:
                        planes = [ends[0, oz, dk : dk + 8][None]] + planes
                    if ox == 2:
                        planes = planes + [ends[1, oz, dk : dk + 8][None]]
                    parts.append(jnp.concatenate(planes, axis=0).reshape(2048, 128))
                window = jnp.concatenate(parts, axis=1)
                product = jnp.dot(cotangent[...], window, preferred_element_type=F32).T
                for oy in range(3):
                    value = product[64 * oy : 64 * oy + 64, :128] + product[64 * oy + 64 : 64 * oy + 128, 128:]
                    store(9 * ox + 3 * oy + oz, 0, value)
        nought = jnp.zeros((64, 64), F32)
        store(27, 0, jnp.concatenate([outer[:64, :64] + outer[64:, 64:], nought], axis=1))
        loss = jnp.broadcast_to(jnp.sum(lost, axis=1, keepdims=True), (64, 128))
        high = loss.astype(BF).astype(F32)
        lane = lax.broadcasted_iota(jnp.int32, (64, 128), 1)
        split = jnp.where(lane == 2 * kz, high, jnp.where(lane == 2 * kz + 1, loss - high, 0.0))
        store(27, 7, split)
        lane = lax.broadcasted_iota(jnp.int32, (1, 128), 1)
        row = jnp.where(lane < 64, gains + pltpu.roll(gains, 64, 1), biases + pltpu.roll(biases, 64, 1))
        wide = jnp.broadcast_to(row, (128, 128))
        for half in range(2):
            payload.at[half][pl.ds(14, 128, stride=16), :] = wide
            slot = jnp.where(kz == half, 0, 1)
            payload.at[slot][pl.ds(15, 128, stride=16), :] = stats[128 * half : 128 * half + 128]
        copies = [pltpu.make_async_copy(payload.at[n], ref, sent.at[n]) for n, ref in ((0, mine), (1, other))]
        for copy in copies:
            copy.start()
        for copy in copies:
            copy.wait()

    return kernel


def slopes(norms, gain, count):
    grad_gain, grad_bias = halves(norms)
    return pair_sum(gain * grad_bias) / count, pair_sum(gain * grad_gain) / count


def pair_add(voxels):
    total_count = float(voxels * GROUP)
    count = float(2 * 4096 * GROUP)

    def kernel(info, mine, other, gathered, gain, out):
        _, _, _, rstd = moments(gathered, total_count)
        total = (mine[...] + other[...]).reshape(-1, 16, 128)
        m1, m2 = slopes(total[0, 14:15], gain[...], count)
        row = lax.broadcasted_iota(jnp.int32, total.shape, 1)
        lane = lax.broadcasted_iota(jnp.int32, total.shape, 2)
        picked = (lane == SHIFT_LANE + 2 * row) & (row < 14)
        ones = jnp.sum(jnp.where(picked, total[:, 15:16], 0.0), axis=2, keepdims=True)
        centred = total - (m1 * rstd)[None] * ones - (m2 * rstd)[None] * pltpu.roll(total, 64, 2)
        total = jnp.where((lane < 64) & (row < 14), centred, total)
        lost = pltpu.roll(total - total.astype(BF).astype(F32), 1, 1)
        out[...] = jnp.where(row == 15, lost, total).astype(BF)

    return kernel


def combine(voxels):
    count = float(voxels * GROUP)
    pair_count = float(2 * 4096 * GROUP)

    def kernel(info, pieces, gathered, gain, temb, copies, grad_time, gain_out, bias_out):
        _, sums, mean, rstd = moments(gathered, count)
        value = pieces[...].astype(F32)
        chips = value.shape[0]
        seen = value[:, 14] + value[:, 15]
        norms = jnp.sum(seen, axis=0, keepdims=True)
        grad_gain, grad_bias = halves(norms)
        gain_out[...] = grad_gain[:, :64]
        bias_out[...] = grad_bias[:, :64]
        m1, m2 = slopes(norms, gain[...], count)
        centred = (sums - voxels * mean) * rstd
        act_sum = rstd * (gain[...] * grad_bias - voxels * m1 - m2 * centred)
        column = jnp.broadcast_to(act_sum, (128, 128)).T[:64]
        grad_time[...] = jnp.concatenate([column, column], axis=1) * temb[...]
        own1, own2 = slopes(seen, gain[...], pair_count)
        delta1, delta2 = (own1 - m1) * rstd, (own2 - m2) * rstd
        ones = gathered[0:chips] + gathered[chips : 2 * chips]
        back = lax.dot_general(
            ones, delta1, (((0,), (0,)), ((), ())), preferred_element_type=F32, precision=lax.Precision.HIGHEST
        )
        back = [back[SHIFT_LANE + 2 * r : SHIFT_LANE + 2 * r + 1] for r in range(14)]
        back = jnp.concatenate(back + [jnp.zeros((2, 128), F32)], axis=0)
        total = jnp.sum(value + delta2[:, None] * pltpu.roll(value, 64, 2), axis=0) + back
        lane = lax.broadcasted_iota(jnp.int32, (7, 128), 1)
        both = jnp.where(lane < 64, total[:7], pltpu.roll(total[7:14], 64, 1))
        lost = both[6:7] - both[6:7].astype(BF).astype(F32)
        piece = jnp.concatenate([both, lost], axis=0).astype(BF)
        copies[...] = jnp.broadcast_to(piece[None], copies.shape)

    return kernel


def spread(scale, info, near, far, conv, coarse, out, loss, rows):
    kz = lax.axis_index("cz")
    rows[pl.ds(pl.multiple_of(1024 * kz, 1024), 1024), :] = near[...].astype(F32).reshape(1024, 128)
    rows[pl.ds(pl.multiple_of(1024 * (1 - kz), 1024), 1024), :] = far[...].astype(F32).reshape(1024, 128)
    for tap in range(28):
        tile = rows[pl.ds(512 * (tap % 4) + tap // 4, 64, stride=8), :]
        if tap < 27:
            conv[tap] = tile[:, :64]
            coarse[tap] = tile[:, 64:]
        else:
            out[...] = tile[:, :64]
            parts = tile[0:1] + rows[2048 - 512 + 7 : 2048 - 512 + 8, :]
            lane = lax.broadcasted_iota(jnp.int32, (1, 128), 1)
            whole = jnp.sum(jnp.where((lane >= 64) & (lane < 68), parts, 0.0), axis=1, keepdims=True)
            loss[...] = whole * scale


def exchange(rows):
    out = lax.all_to_all(rows.reshape(rows.shape[0], 1, 128), ("cz",) + CHIPS, 0, 0, tiled=True)
    return out.reshape(rows.shape)


def neighbours(down, up, axis):
    ends = lax.axis_size(axis) - 1
    before = lax.ppermute(up, axis, [(i, i + 1) for i in range(ends)])
    after = lax.ppermute(down, axis, [(i + 1, i) for i in range(ends)])
    return before, after


def time_embedding(timestep, width):
    halfway = width // 2
    indices = jnp.arange(halfway).astype(F32)
    freqs = jnp.exp(indices * (-math.log(10000.0) / halfway))
    angles = timestep[0].astype(F32) * freqs
    return jnp.concatenate([jnp.sin(angles), jnp.cos(angles)])


def twice(row):
    return jnp.concatenate([row, row]).reshape(1, 128)


def diagonal(square):
    nought = jnp.zeros_like(square)
    return jnp.block([[square, nought], [nought, square]])


def shards(latents, target, block_coords, timestep, conv_weight, coarse_weight, out_weight, time_weight, norm_gain, norm_bias):
    devices = lax.axis_size("bx") * lax.axis_size("by") * lax.axis_size("cz")
    voxels = devices * 4096
    info = block_coords
    lat = latents[0]
    lat_pairs = lat.reshape(16, 8, 2, 16, 64)

    mz, pooled = call(z_message, [message(Z_TILES), like((16, 64), BF)], [info, lat])
    rz = lax.ppermute(mz, "cz", [(0, 1), (1, 0)])
    out = message(Y_TILES)
    down, up = call(
        y_messages, [out, out], [info, lat, lat, rz, pooled], [plane(Z_TILES)], [face_spec(1, 0), face_spec(1, 15)]
    )
    rym, ryp = neighbours(down, up, "by")
    out = message(X_TILES)
    planes = [plane(Z_TILES), plane(Y_TILES), plane(Y_TILES)]
    down, up = call(
        x_messages,
        [out, out],
        [info, lat, lat, rz, rym, ryp, pooled],
        planes,
        [face_spec(0, 0), face_spec(0, 15)],
    )
    rxm, rxp = neighbours(down, up, "bx")

    temb = time_embedding(timestep, time_weight.shape[0]).reshape(1, -1)
    raw, scene, columns, taps = call(
        interior,
        [like((1792, 128), F32), like((3, 16, 9, 16, 128), BF), like((3, 9, 128), F32), like((2304, 128), BF)],
        [info, lat_pairs, rz, rym, ryp, conv_weight],
        planes,
    )
    pair = (3, 2, 9, 16, 128)
    tables = jnp.asarray(coarse_table(), BF)
    act, ends, patch, stats = call(
        forward,
        [like((2048, 128), F32), like((2, 3, 9, 16, 128), BF), like((16, 1728), BF), like((devices, 128), F32)],
        [info, scene, scene, raw, columns, rz, rym, ryp, rxm, rxp, pooled, taps]
        + [coarse_weight.reshape(1728, 64), temb, time_weight.T, tables],
        [pltpu.VMEM((2, 128, 128), F32), pltpu.VMEM((224, 160), BF), pltpu.SemaphoreType.DMA]
        + planes
        + [plane(X_TILES), plane(X_TILES)],
        [pl.BlockSpec(pair, lambda i: (0, 0, 0, 0, 0)), pl.BlockSpec(pair, lambda i: (0, 7, 0, 0, 0))],
        far_args=1,
    )
    first = exchange(stats)
    gain, bias = twice(norm_gain), twice(norm_bias)
    weights = [diagonal(out_weight), diagonal(out_weight.T)]
    predicted, mine, other = call(
        backward(voxels),
        [like((16, 8, 2, 16, 64), BF), like((2048, 128), F32), like((2048, 128), F32)],
        [info, act, first, target.reshape(16, 8, 2, 16, 64), gain, bias] + weights + [scene, ends, patch, stats],
        [pltpu.VMEM((256, 2048), BF), pltpu.VMEM((2, 2048, 128), F32), pltpu.SemaphoreType.DMA((2,))],
        far_outs=2,
    )
    swap = [(0, 1), (1, 0)]
    chips = devices // 2
    other = lax.ppermute(other, "cz", swap)
    (pieces,) = call(pair_add(voxels), [like((chips, 16, 128), BF)], [info, mine, other, first, gain])
    pieces = lax.all_to_all(pieces, CHIPS, 0, 0, tiled=True)
    copies, grad_time, grad_gain, grad_bias = call(
        combine(voxels),
        [like((chips, 8, 128), BF), like((64, 256), F32), like((1, 64), F32), like((1, 64), F32)],
        [info, pieces, first, gain, temb],
    )
    near = lax.all_to_all(copies, CHIPS, 0, 0, tiled=True)
    far = lax.ppermute(near, "cz", swap)
    grad_conv, grad_coarse, grad_out, loss = call(
        functools.partial(spread, 1.0 / (voxels * 64)),
        [like((27, 64, 64), F32), like((27, 64, 64), F32), like((64, 64), F32), like((1, 1), F32)],
        [info, near, far],
        [pltpu.VMEM((2048, 128), F32)],
    )
    return (
        predicted.reshape(latents.shape),
        loss.reshape(1),
        grad_conv,
        grad_coarse,
        grad_out,
        grad_time.T,
        grad_gain.reshape(64),
        grad_bias.reshape(64),
    )


def solution(mesh):
    blocks = P(ALL, None, None, None, None)
    return jax.shard_map(
        shards,
        mesh=mesh,
        in_specs=(blocks, blocks, P(ALL, None)) + (P(),) * 7,
        out_specs=(blocks,) + (P(),) * 7,
        check_vma=False,
    )
```

```python
import functools
import math

import jax
import jax.numpy as jnp
import numpy as np
from jax import lax
from jax.experimental import pallas as pl
from jax.experimental.pallas import tpu as pltpu
from jax.sharding import PartitionSpec as P

ALL = ("bx", "by", "cz")
CHIPS = ("bx", "by")
BF = jnp.bfloat16
F32 = jnp.float32
EPS = 1e-05
GROUP = 2
VMEM_LIMIT = 40 * 1024 * 1024
SHIFT_LANE = 65


def face_spec(dim, index):
    shape = tuple(1 if d == dim else 16 for d in range(3)) + (64,)
    where = tuple(index if d == dim else 0 for d in range(4))
    return pl.BlockSpec(shape, lambda i: where)


def call(kernel, outs, args, scratch=(), faces=(), far_args=0, far_outs=0):
    vmem = pl.BlockSpec(memory_space=pltpu.VMEM)
    far = pl.BlockSpec(memory_space=pl.ANY)
    specs = list(faces) + [vmem] * (len(args) - 1 - len(faces) - far_args) + [far] * far_args
    args = [
        pltpu.with_memory_space_constraint(arg, pltpu.VMEM) if spec is vmem else arg
        for arg, spec in zip(args, [None] + specs)
    ]
    return pl.pallas_call(
        kernel,
        grid=(1,),
        out_shape=outs,
        in_specs=[pl.BlockSpec(memory_space=pltpu.SMEM)] + specs,
        out_specs=[vmem] * (len(outs) - far_outs) + [far] * far_outs,
        scratch_shapes=list(scratch),
        compiler_params=pltpu.CompilerParams(vmem_limit_bytes=VMEM_LIMIT),
    )(*args)


def like(shape, dtype):
    return jax.ShapeDtypeStruct(shape, dtype)


def keep(cond, value):
    return jnp.where(cond, value, jnp.zeros_like(value))


def bits(info):
    return info[0, 0], info[0, 1], info[0, 2], lax.axis_index("cz")


def start16(bit):
    return pl.multiple_of(bit * 16, 16)


def cell_rows(first, second, face, on):
    rows = []
    for r in range(4):
        for s in range(4):
            here = on & (first == r // 2) & (second == s // 2)
            rows.append(keep(here, face[r % 2][s % 2]))
    return jnp.concatenate(rows, axis=0)


def row_of(cells, p):
    return cells[p : p + 1]


Z_TILES, Y_TILES, X_TILES = 1, 2, 5


def message(tiles):
    return like((9 + tiles, 16, 128), BF)


def plane(tiles):
    return pltpu.VMEM((32 + tiles, 32, 64), BF)


def side_by_side(rows):
    half = rows.shape[0] // 2
    return jnp.concatenate([rows[:half], rows[half:]], axis=rows.ndim - 1)


def write_message(out, face, tiles, first, second, on):
    out[0:8] = side_by_side(face)
    for t, rows in enumerate(tiles):
        out[8 + t] = side_by_side(rows).astype(BF)
    row = lax.broadcasted_iota(jnp.int32, (16, 128), 0)
    here = jnp.where(on, 2 * first + second, 99)
    out[8 + len(tiles)] = jnp.where(row == here, 1.0, 0.0).astype(BF)


def open_message(ref, out):
    tiles = ref.shape[0] - 9
    face = jnp.concatenate([ref[0:8, :, :64], ref[0:8, :, 64:]], axis=0)
    flags = ref[8 + tiles].astype(F32)
    for q in range(4):
        here = jnp.broadcast_to(flags[q : q + 1, :64], (16, 64))[None]
        out[16 * (q // 2) : 16 * (q // 2) + 16, 16 * (q % 2) : 16 * (q % 2) + 16, :] = jnp.where(
            here > 0.5, face.astype(F32), 0.0
        ).astype(BF)
    for t in range(tiles):
        out[32 + t] = jnp.concatenate([ref[8 + t, :, :64], ref[8 + t, :, 64:]], axis=0)


def z_message(info, lat, out, pooled):
    px, py, pz, kz = bits(info)
    zsel = 15 * (1 - kz)
    pick = lax.broadcasted_iota(jnp.int32, (16, 16, 64), 1) == zsel
    sums = [[None, None], [None, None]]
    faces = []
    for y in range(16):
        slab = lat[:, y].astype(F32)
        faces.append(jnp.sum(jnp.where(pick, slab, 0.0), axis=1)[None])
        for a in range(2):
            part = jnp.sum(slab[8 * a : 8 * a + 8], axis=0)
            old = sums[a][y // 8]
            sums[a][y // 8] = part if old is None else old + part
    cells = []
    for a in range(2):
        for b in range(2):
            for c in range(2):
                cells.append(jnp.sum(sums[a][b][8 * c : 8 * c + 8], axis=0, keepdims=True))
    cells = jnp.concatenate(cells, axis=0) * (1.0 / math.sqrt(512.0))
    cells = cells.astype(BF).astype(F32)
    pooled[...] = jnp.concatenate([cells, jnp.zeros((8, 64), F32)], axis=0).astype(BF)
    on = pz == 1 - kz
    face = [
        [jnp.where(kz == 0, row_of(cells, 4 * a + 2 * b + 1), row_of(cells, 4 * a + 2 * b)) for a in range(2)]
        for b in range(2)
    ]
    rows = jnp.concatenate([cell_rows(py, px, face, on), jnp.zeros((16, 64), F32)], axis=0)
    write_message(out, jnp.concatenate(faces, axis=0).astype(BF), [rows], py, px, on)


def y_messages(info, low, high, rz_in, pooled, down, up, rz):
    px, py, pz, kz = bits(info)
    open_message(rz_in, rz)
    cells = pooled[...].astype(F32)
    halo = rz[32].astype(F32)
    for out, face, bit, line, q in ((down, low, 0, 0, 0), (up, high, 1, 31, 1)):
        on = py == bit
        picked = [[row_of(cells, 4 * a + 2 * q + c) for c in range(2)] for a in range(2)]
        tail = halo[12:16] if q else halo[0:4]
        rows = jnp.concatenate([cell_rows(px, pz, picked, on), tail, jnp.zeros((12, 64), F32)], axis=0)
        write_message(out, face[:, 0], [rz[line], rows], px, pz, on)


def x_messages(info, low, high, rz_in, rym_in, ryp_in, pooled, down, up, rz, rym, ryp):
    px, py, pz, kz = bits(info)
    for ref, out in ((rz_in, rz), (rym_in, rym), (ryp_in, ryp)):
        open_message(ref, out)
    cells = pooled[...].astype(F32)
    halo = rz[32].astype(F32)
    halo_m = rym[33].astype(F32)
    halo_p = ryp[33].astype(F32)
    line_m = rym[32].astype(F32)
    line_p = ryp[32].astype(F32)
    where16 = lax.broadcasted_iota(jnp.int32, (32, 16, 64), 1)
    for out, face, bit, line, q in ((down, low, 0, 0, 0), (up, high, 1, 31, 1)):
        on = px == bit
        slab = rz[0:32, 16 * q : 16 * q + 16, :].astype(F32)
        z_line = jnp.sum(jnp.where(where16 == 15 * q, slab, 0.0), axis=1).astype(BF)
        picked = [[row_of(cells, 4 * q + 2 * b + c) for c in range(2)] for b in range(2)]
        corners = [line_m[line : line + 1], line_p[line : line + 1], jnp.zeros((14, 64), F32)]
        corners = jnp.concatenate(corners + [cell_rows(py, pz, picked, on)], axis=0)
        c0 = 3 * q
        parts = [row_of(halo, 4 * cy + c0) for cy in range(4)]
        parts += [halo_m[4 * c0 : 4 * c0 + 4], halo_p[4 * c0 : 4 * c0 + 4]]
        parts += [row_of(halo_m, 16 + c0), row_of(halo_p, 16 + c0), jnp.zeros((18, 64), F32)]
        tiles = [z_line, rym[line], ryp[line], corners, jnp.concatenate(parts, axis=0)]
        write_message(out, face[0], tiles, py, pz, on)


def coarse_table():
    pooled, rz, rym, ryp, rxm, rxp = 0, 16, 32, 64, 96, 128
    table = np.zeros((16, 224, 160), np.float32)
    for combo in range(16):
        bit = ((combo >> 3) & 1, (combo >> 2) & 1, (combo >> 1) & 1)
        core = combo & 1
        for tap in range(27):
            off = (tap // 9, tap // 3 % 3, tap % 3)
            for p in range(8):
                at = (p // 4, p // 2 % 2, p % 2)
                pos = [2 * bit[d] - 1 + off[d] + at[d] for d in range(3)]
                x, y, z = pos
                out_z = z < 0 or z > 3
                if out_z and (z < 0) != (core == 1):
                    continue
                if x < 0 or x > 3:
                    base = rxm if x < 0 else rxp
                    if y < 0 or y > 3:
                        side = 0 if y < 0 else 1
                        row = 16 + (12 + side if out_z else 4 + 4 * side + z)
                    else:
                        row = 16 + y if out_z else 4 * y + z
                    row = base + row
                elif y < 0 or y > 3:
                    row = (rym if y < 0 else ryp) + (16 + x if out_z else 4 * x + z)
                elif out_z:
                    row = rz + 4 * y + x
                else:
                    own = [pos[d] - 2 * bit[d] for d in range(3)]
                    if min(own) < 0 or max(own) > 1:
                        continue
                    row = pooled + 4 * own[0] + 2 * own[1] + own[2]
                table[combo, 8 * tap + p, row] = 1.0
    return table


class Window:
    def __init__(self, info, rz, rym, ryp):
        px, py, pz, kz = bits(info)
        self.pz, self.rz, self.rym, self.ryp = pz, rz, rym, ryp
        self.z0 = pl.ds(start16(pz), 16)
        self.z1 = pl.ds(start16(1 - pz), 16)
        self.xs = pl.ds(start16(px), 16)
        self.ys = pl.ds(start16(py), 16)
        self.xlo, self.xhi, self.ylo, self.yhi = px == 0, px == 1, py == 0, py == 1
        self.on_low = (pz == 0) & (kz == 1)
        self.on_high = (pz == 1) & (kz == 0)
        self.row16 = lax.broadcasted_iota(jnp.int32, (16, 16, 64), 1)
        self.z_row = lax.broadcasted_iota(jnp.int32, (9, 16, 128), 1)

    def edge(self, block):
        return jnp.sum(jnp.where(self.row16[: block.shape[0]] == 15 * self.pz, block.astype(F32), 0.0), axis=1)

    def edge1(self, ref, i):
        return self.edge(ref[i : i + 1, self.z1, :])

    def low_of(self, e, h):
        return keep(self.pz == 1, e) + keep(self.on_low, h)

    def high_of(self, e, h):
        return keep(self.pz == 0, e) + keep(self.on_high, h)

    def offsets(self, evens, odds, first, last, zl, zh):
        left = jnp.concatenate([first[None], odds], axis=0)
        right = jnp.concatenate([evens, last[None]], axis=0)
        tile = jnp.concatenate([left, right], axis=2)
        wide = tile.astype(F32)
        down = jnp.where(self.z_row == 0, zl, pltpu.roll(wide, 1, 1)).astype(BF)
        up = jnp.where(self.z_row == 15, zh, pltpu.roll(wide, 15, 1)).astype(BF)
        return down, tile, up


def one(ref, i, j):
    return ref[i].astype(F32)[j : j + 1]


def interior(info, lat, rz_in, rym_in, ryp_in, taps, raw, scene, columns, weight, rz, rym, ryp):
    for ref, out in ((rz_in, rz), (rym_in, rym), (ryp_in, ryp)):
        open_message(ref, out)
    nought = jnp.zeros((64, 64), BF)
    for tap in range(9):
        ox, oz = tap // 3, tap % 3
        for a in range(4):
            left = nought if a == 3 else taps[9 * ox + 3 * a + oz]
            right = nought if a == 0 else taps[9 * ox + 3 * a - 3 + oz]
            weight[256 * tap + 64 * a : 256 * tap + 64 * a + 64] = jnp.concatenate([left, right], axis=1)
    w = Window(info, rz, rym, ryp)
    y_low = keep(w.ylo, rym[w.xs, w.z0, :])
    y_high = keep(w.yhi, ryp[w.xs, w.z0, :])
    e_low = keep(w.ylo, w.edge(rym[w.xs, w.z1, :]))
    e_high = keep(w.yhi, w.edge(ryp[w.xs, w.z1, :]))
    h_low = jnp.where(w.ylo, rym[32, w.xs, :], rz[15, w.xs, :]).astype(F32)
    h_high = jnp.where(w.yhi, ryp[32, w.xs, :], rz[16, w.xs, :]).astype(F32)
    h_mid = rz[w.ys, w.xs, :].astype(F32)

    def packed(of):
        rows = [of(e_low, h_low)] + [of(jnp.zeros((16, 64), F32), h_mid[y]) for y in range(16)]
        rows.append(of(e_high, h_high))
        return [jnp.concatenate([rows[2 * k], rows[2 * k + 1]], axis=1) for k in range(9)]

    below, above = packed(w.low_of), packed(w.high_of)
    inner = [None] * 3
    for x in range(16):
        zl = jnp.concatenate([below[k][x : x + 1][None] for k in range(9)], axis=0)
        zh = jnp.concatenate([above[k][x : x + 1][None] for k in range(9)], axis=0)
        planes = w.offsets(lat[x, :, 0], lat[x, :, 1], y_low[x], y_high[x], zl, zh)
        for oz, plane in enumerate(planes):
            scene[oz, x] = plane
            wide = plane.astype(F32)
            inner[oz] = wide if x == 0 else inner[oz] + wide
    for oz in range(3):
        columns[oz] = jnp.sum(inner[oz], axis=1)
    for first, count in ((1, 4), (5, 4), (9, 4), (13, 2)):
        pieces = []
        for tap in range(9):
            ox, oz = tap // 3, tap % 3
            for dk in range(2):
                at = first + ox - 1
                pieces.append(scene[oz, at : at + count, dk : dk + 8].reshape(128 * count, 128))
        value = jnp.dot(jnp.concatenate(pieces, axis=1), weight[...], preferred_element_type=F32)
        raw[(first - 1) * 128 : (first - 1 + count) * 128] = value


def forward(
    info, near_low, near_high, raw, columns, rz_in, rym_in, ryp_in, rxm_in, rxp_in, pooled, weight,
    coarse_weight, temb, time_weight, tables, act, ends, patch_out, stats,
    shift, table, arrived, rz, rym, ryp, rxm, rxp
):
    px, py, pz, kz = bits(info)
    fetch = pltpu.make_async_copy(tables.at[8 * px + 4 * py + 2 * pz + kz], table, arrived)
    fetch.start()
    for ref, out in ((rz_in, rz), (rym_in, rym), (ryp_in, ryp), (rxm_in, rxm), (rxp_in, rxp)):
        open_message(ref, out)
    w = Window(info, rz, rym, ryp)
    nought = jnp.zeros((16, 64), BF)

    def sides(rx, out, inner):
        first = jnp.where(
            out,
            jnp.where(w.ylo, rx[33, w.z0, :], rx[15, w.z0, :]),
            jnp.where(w.ylo, rym[inner, w.z0, :], nought),
        )
        last = jnp.where(
            out,
            jnp.where(w.yhi, rx[34, w.z0, :], rx[16, w.z0, :]),
            jnp.where(w.yhi, ryp[inner, w.z0, :], nought),
        )
        return first, last

    def side_columns(rx, out, inner, of):
        half = rz[w.ys, 0:16, :] if inner < 16 else rz[w.ys, 16:32, :]
        inner_h = jnp.sum(jnp.where(w.row16 == inner % 16, half.astype(F32), 0.0), axis=1)
        e_mid = keep(out, w.edge(rx[w.ys, w.z1, :]))
        hh = jnp.where(out, rx[32, w.ys, :].astype(F32), inner_h)
        e_first = jnp.where(
            out,
            jnp.where(w.ylo, w.edge1(rx, 33), w.edge1(rx, 15)),
            keep(w.ylo, w.edge1(rym, inner)),
        )
        h_first = jnp.where(
            out,
            jnp.where(w.ylo, one(rx, 35, 0), one(rx, 32, 15)),
            jnp.where(w.ylo, one(rym, 32, inner), one(rz, 15, inner)),
        )
        e_last = jnp.where(
            out,
            jnp.where(w.yhi, w.edge1(rx, 34), w.edge1(rx, 16)),
            keep(w.yhi, w.edge1(ryp, inner)),
        )
        h_last = jnp.where(
            out,
            jnp.where(w.yhi, one(rx, 35, 1), one(rx, 32, 16)),
            jnp.where(w.yhi, one(ryp, 32, inner), one(rz, 16, inner)),
        )
        mid = of(e_mid, hh)
        rows = [of(e_first, h_first)] + [mid[y : y + 1] for y in range(16)] + [of(e_last, h_last)]
        return [jnp.concatenate([rows[2 * k], rows[2 * k + 1]], axis=1)[None] for k in range(9)]

    for e, rx, out, inner in ((0, rxm, w.xlo, 15), (1, rxp, w.xhi, 16)):
        zl = jnp.concatenate(side_columns(rx, out, inner, w.low_of), axis=0)
        zh = jnp.concatenate(side_columns(rx, out, inner, w.high_of), axis=0)
        first, last = sides(rx, out, inner)
        plane = keep(out, rx[w.ys, w.z0, :]).reshape(8, 2, 16, 64)
        for oz, tile in enumerate(w.offsets(plane[:, 0], plane[:, 1], first, last, zl, zh)):
            ends[e, oz] = tile

    source = jnp.concatenate(
        [pooled[...], rz[32, 0:16, :], rym[33], ryp[33], rxm[35, 16:32, :], rxm[36, 0:16, :], rxp[35, 16:32, :], rxp[36, 0:16, :]],
        axis=0,
    )
    fetch.wait()
    taps = jnp.dot(table[...], source, preferred_element_type=F32)
    patch = jnp.concatenate([taps[8 * t : 8 * t + 8] for t in range(27)], axis=1)
    patch_out[...] = jnp.concatenate([patch, patch], axis=0).astype(BF)
    coarse = jnp.dot(patch_out[...], coarse_weight[...], preferred_element_type=F32)
    coarse = coarse.astype(BF).astype(F32)
    coarse = jnp.concatenate([coarse, coarse], axis=1)
    time_bias = lax.dot_general(
        jnp.broadcast_to(temb[...], (8, 256)),
        time_weight[...].astype(F32),
        (((1,), (1,)), ((), ())),
        preferred_element_type=F32,
        precision=lax.Precision.HIGHEST,
    )[:1]
    time_bias = jnp.concatenate([time_bias, time_bias], axis=1)
    z_half = lax.broadcasted_iota(jnp.int32, (16, 128), 0) < 8
    added = []
    for q in range(4):
        added.append(jnp.where(z_half, coarse[2 * q : 2 * q + 1], coarse[2 * q + 1 : 2 * q + 2]) + time_bias)

    pieces = []
    for tap in range(9):
        ox, oz = tap // 3, tap % 3
        low = ends[0, oz] if ox == 0 else near_low[oz, ox - 1]
        high = ends[1, oz] if ox == 2 else near_high[oz, ox]
        for dk in range(2):
            pieces.append(jnp.concatenate([low[dk : dk + 8], high[dk : dk + 8]], axis=0).reshape(256, 128))
    edges = jnp.dot(jnp.concatenate(pieces, axis=1), weight[...], preferred_element_type=F32)

    total = jnp.zeros((1, 128), F32)
    squares = jnp.zeros((1, 128), F32)
    for x in range(16):
        if x == 0:
            value = edges[:128]
        elif x == 15:
            value = edges[128:]
        else:
            value = raw[(x - 1) * 128 : x * 128]
        value = value.reshape(2, 4, 16, 128)
        a = x // 8
        value = jnp.concatenate([(value[b] + added[2 * a + b][None])[None] for b in range(2)], axis=0).reshape(128, 128)
        act[x * 128 : x * 128 + 128] = value
        total = total + jnp.sum(value, axis=0, keepdims=True)
        squares = squares + jnp.sum(value * value, axis=0, keepdims=True)
    shift[...] = jnp.zeros(shift.shape, F32)

    def place(tap, slot, value):
        row = SHIFT_LANE + 2 * (tap // 4 + slot)
        u = tap % 4
        shift[u // 2, row : row + 1, 64 * (u % 2) : 64 * (u % 2) + 64] = value

    for oz in range(3):
        inner = columns[oz]
        planes = (ends[0, oz], near_low[oz, 0], near_high[oz, 1], ends[1, oz])
        outer = [jnp.sum(plane.astype(F32), axis=1) for plane in planes]
        for ox, part in enumerate((inner + outer[0] - outer[2], inner, inner - outer[1] + outer[3])):
            all_columns = jnp.sum(part, axis=0, keepdims=True)
            whole = all_columns[:, :64] + all_columns[:, 64:]
            y0, y1 = part[0:1, :64], part[0:1, 64:]
            y16, y17 = part[8:9, :64], part[8:9, 64:]
            for oy, window in enumerate((whole - y16 - y17, whole - y0 - y17, whole - y0 - y1)):
                place(9 * ox + 3 * oy + oz, 0, window)
    for t in range(27):
        place(t, 7, 512.0 * jnp.sum(taps[8 * t : 8 * t + 8], axis=0, keepdims=True))

    lane = lax.broadcasted_iota(jnp.int32, (1, 128), 1)
    pairs = pair_sum(squares + pltpu.roll(squares, 64, 1))
    row = jnp.where(lane < 64, total + pltpu.roll(total, 64, 1), jnp.where(lane % 2 == 0, pairs, 0.0))
    for u in range(2):
        stats[128 * u : 128 * u + 128] = shift[u].T + row


def turn(info, scene, ends, turned):
    for oz in range(3):
        for xp in range(18):
            for dk in range(2):
                tile = scene[oz, xp - 1, dk : dk + 8] if 1 <= xp <= 16 else ends[xp // 17, oz, dk : dk + 8]
                turned[oz, 128 * dk : 128 * dk + 128, 128 * xp : 128 * xp + 128] = tile.reshape(128, 128).T


def pair_sum(row):
    lane = lax.broadcasted_iota(jnp.int32, row.shape, 1)
    return row + jnp.where(lane % 2 == 0, pltpu.roll(row, 127, 1), pltpu.roll(row, 1, 1))


def halves(row):
    lane = lax.broadcasted_iota(jnp.int32, row.shape, 1)
    other = pltpu.roll(row, 64, 1)
    return jnp.where(lane < 64, row, other), jnp.where(lane < 64, other, row)


def moments(gathered, count):
    row = jnp.sum(gathered[...], axis=0, keepdims=True)
    sums, upper = halves(row)
    lane = lax.broadcasted_iota(jnp.int32, row.shape, 1)
    squares = jnp.where(lane % 2 == 0, upper, pltpu.roll(upper, 1, 1))
    mean = pair_sum(sums) / count
    var = squares / count - mean * mean
    return row, sums, mean, 1.0 / jnp.sqrt(var + EPS)


def backward(voxels):
    count = float(voxels * GROUP)
    scale = 1.0 / (voxels * 64)

    def kernel(info, act, gathered, target, gain, bias, weight, weight_t, turned, patch, stats, predicted, mine, other, cotangent, payload, sent):
        kz = lax.axis_index("cz")
        _, _, mean, rstd = moments(gathered, count)
        gains = jnp.zeros((1, 128), F32)
        biases = jnp.zeros((1, 128), F32)
        lost = jnp.zeros((1, 128), F32)
        outer = jnp.zeros((128, 128), F32)
        cells = [[None] * 4, [None] * 4]
        for x in range(0, 16, 2):
            rows = slice(x * 128, x * 128 + 256)
            normalized = (act[rows] - mean) * rstd
            shifted = normalized * gain[...] + bias[...]
            sigma = jax.nn.sigmoid(shifted)
            hidden = (shifted * sigma).astype(BF)
            output = jnp.dot(hidden, weight[...], preferred_element_type=F32)
            goal = jnp.concatenate([target[x : x + 2, :, 0], target[x : x + 2, :, 1]], axis=3)
            residue = output - goal.reshape(256, 128).astype(F32)
            shown = output.astype(BF).reshape(2, 8, 16, 128)
            predicted[x : x + 2, :, 0] = shown[..., :64]
            predicted[x : x + 2, :, 1] = shown[..., 64:]
            upstream = (2.0 * scale * residue).astype(BF)
            back = jnp.dot(upstream, weight_t[...], preferred_element_type=F32)
            value = back * sigma * (1.0 + shifted * (1.0 - sigma))
            gains = gains + jnp.sum(value * normalized, axis=0, keepdims=True)
            biases = biases + jnp.sum(value, axis=0, keepdims=True)
            lost = lost + jnp.sum(residue * residue, axis=0, keepdims=True)
            outer = outer + lax.dot_general(hidden, upstream, (((0,), (0,)), ((), ())), preferred_element_type=F32)
            value = value * (gain[...] * rstd)
            narrow = [value.astype(BF), normalized.astype(BF)]
            cotangent[rows, :128] = jnp.concatenate([part[:, :64] for part in narrow], axis=1)
            cotangent[rows, 128:] = jnp.concatenate([part[:, 64:] for part in narrow], axis=1)
            for part, wide in enumerate((value, normalized)):
                planes = wide.reshape(2, 2, 4, 16, 128)
                for b in range(2):
                    q = 2 * (x // 8) + b
                    cell = jnp.sum(planes[:, b], axis=(0, 1))
                    old = cells[part][q]
                    cells[part][q] = cell if old is None else old + cell

        def store(tap, slot, value):
            u = tap % 4
            half = jnp.where(kz == u // 2, 0, 1)
            payload.at[half][pl.ds(1024 * (u % 2) + slot + tap // 4, 64, stride=16), :] = value

        rows = []
        for q in range(4):
            for c in range(2):
                sums = [jnp.sum(cells[p][q][8 * c : 8 * c + 8], axis=0, keepdims=True) for p in range(2)]
                rows.append(jnp.concatenate([r[:, :64] + r[:, 64:] for r in sums], axis=1))
        rows = jnp.concatenate(rows, axis=0)
        high = rows.astype(BF)
        split = jnp.concatenate([high.astype(F32), rows - high.astype(F32)], axis=0).astype(BF)
        coarse = lax.dot_general(patch[...], split, (((0,), (0,)), ((), ())), preferred_element_type=F32)
        for t in range(27):
            store(t, 7, coarse[64 * t : 64 * t + 64])
        for ox in range(3):
            windows = turned[:, :, 128 * ox : 128 * ox + 2048].reshape(768, 2048)
            products = jnp.dot(windows, cotangent[...], preferred_element_type=F32)
            for oz in range(3):
                product = products[256 * oz : 256 * oz + 256]
                for oy in range(3):
                    value = product[64 * oy : 64 * oy + 64, :128] + product[64 * oy + 64 : 64 * oy + 128, 128:]
                    store(9 * ox + 3 * oy + oz, 0, value)
        nought = jnp.zeros((64, 64), F32)
        store(27, 0, jnp.concatenate([outer[:64, :64] + outer[64:, 64:], nought], axis=1))
        loss = jnp.broadcast_to(jnp.sum(lost, axis=1, keepdims=True), (64, 128))
        high = loss.astype(BF).astype(F32)
        lane = lax.broadcasted_iota(jnp.int32, (64, 128), 1)
        split = jnp.where(lane == 2 * kz, high, jnp.where(lane == 2 * kz + 1, loss - high, 0.0))
        store(27, 7, split)
        lane = lax.broadcasted_iota(jnp.int32, (1, 128), 1)
        row = jnp.where(lane < 64, gains + pltpu.roll(gains, 64, 1), biases + pltpu.roll(biases, 64, 1))
        wide = jnp.broadcast_to(row, (128, 128))
        for half in range(2):
            payload.at[half][pl.ds(14, 128, stride=16), :] = wide
            slot = jnp.where(kz == half, 0, 1)
            payload.at[slot][pl.ds(15, 128, stride=16), :] = stats[128 * half : 128 * half + 128]
        copies = [pltpu.make_async_copy(payload.at[n], ref, sent.at[n]) for n, ref in ((0, mine), (1, other))]
        for copy in copies:
            copy.start()
        for copy in copies:
            copy.wait()

    return kernel


def slopes(norms, gain, count):
    grad_gain, grad_bias = halves(norms)
    return pair_sum(gain * grad_bias) / count, pair_sum(gain * grad_gain) / count


def pair_add(voxels):
    total_count = float(voxels * GROUP)
    count = float(2 * 4096 * GROUP)

    def kernel(info, mine, other, gathered, gain, out):
        _, _, _, rstd = moments(gathered, total_count)
        total = (mine[...] + other[...]).reshape(-1, 16, 128)
        m1, m2 = slopes(total[0, 14:15], gain[...], count)
        row = lax.broadcasted_iota(jnp.int32, total.shape, 1)
        lane = lax.broadcasted_iota(jnp.int32, total.shape, 2)
        picked = (lane == SHIFT_LANE + 2 * row) & (row < 14)
        ones = jnp.sum(jnp.where(picked, total[:, 15:16], 0.0), axis=2, keepdims=True)
        centred = total - (m1 * rstd)[None] * ones - (m2 * rstd)[None] * pltpu.roll(total, 64, 2)
        total = jnp.where((lane < 64) & (row < 14), centred, total)
        lost = pltpu.roll(total - total.astype(BF).astype(F32), 1, 1)
        out[...] = jnp.where(row == 15, lost, total).astype(BF)

    return kernel


def combine(voxels):
    count = float(voxels * GROUP)
    pair_count = float(2 * 4096 * GROUP)

    def kernel(info, pieces, gathered, gain, temb, copies, grad_time, gain_out, bias_out):
        _, sums, mean, rstd = moments(gathered, count)
        value = pieces[...].astype(F32)
        chips = value.shape[0]
        seen = value[:, 14] + value[:, 15]
        norms = jnp.sum(seen, axis=0, keepdims=True)
        grad_gain, grad_bias = halves(norms)
        gain_out[...] = grad_gain[:, :64]
        bias_out[...] = grad_bias[:, :64]
        m1, m2 = slopes(norms, gain[...], count)
        centred = (sums - voxels * mean) * rstd
        act_sum = rstd * (gain[...] * grad_bias - voxels * m1 - m2 * centred)
        column = jnp.broadcast_to(act_sum, (128, 128)).T[:64]
        grad_time[...] = jnp.concatenate([column, column], axis=1) * temb[...]
        own1, own2 = slopes(seen, gain[...], pair_count)
        delta1, delta2 = (own1 - m1) * rstd, (own2 - m2) * rstd
        ones = gathered[0:chips] + gathered[chips : 2 * chips]
        back = lax.dot_general(
            ones, delta1, (((0,), (0,)), ((), ())), preferred_element_type=F32, precision=lax.Precision.HIGHEST
        )
        back = [back[SHIFT_LANE + 2 * r : SHIFT_LANE + 2 * r + 1] for r in range(14)]
        back = jnp.concatenate(back + [jnp.zeros((2, 128), F32)], axis=0)
        total = jnp.sum(value + delta2[:, None] * pltpu.roll(value, 64, 2), axis=0) + back
        lane = lax.broadcasted_iota(jnp.int32, (7, 128), 1)
        both = jnp.where(lane < 64, total[:7], pltpu.roll(total[7:14], 64, 1))
        lost = both[6:7] - both[6:7].astype(BF).astype(F32)
        piece = jnp.concatenate([both, lost], axis=0).astype(BF)
        copies[...] = jnp.broadcast_to(piece[None], copies.shape)

    return kernel


def spread(scale, info, near, far, conv, coarse, out, loss, rows):
    kz = lax.axis_index("cz")
    rows[pl.ds(pl.multiple_of(1024 * kz, 1024), 1024), :] = near[...].astype(F32).reshape(1024, 128)
    rows[pl.ds(pl.multiple_of(1024 * (1 - kz), 1024), 1024), :] = far[...].astype(F32).reshape(1024, 128)
    for tap in range(28):
        tile = rows[pl.ds(512 * (tap % 4) + tap // 4, 64, stride=8), :]
        if tap < 27:
            conv[tap] = tile[:, :64]
            coarse[tap] = tile[:, 64:]
        else:
            out[...] = tile[:, :64]
            parts = tile[0:1] + rows[2048 - 512 + 7 : 2048 - 512 + 8, :]
            lane = lax.broadcasted_iota(jnp.int32, (1, 128), 1)
            whole = jnp.sum(jnp.where((lane >= 64) & (lane < 68), parts, 0.0), axis=1, keepdims=True)
            loss[...] = whole * scale


def exchange(rows):
    out = lax.all_to_all(rows.reshape(rows.shape[0], 1, 128), ("cz",) + CHIPS, 0, 0, tiled=True)
    return out.reshape(rows.shape)


def neighbours(down, up, axis):
    ends = lax.axis_size(axis) - 1
    before = lax.ppermute(up, axis, [(i, i + 1) for i in range(ends)])
    after = lax.ppermute(down, axis, [(i + 1, i) for i in range(ends)])
    return before, after


def time_embedding(timestep, width):
    halfway = width // 2
    indices = jnp.arange(halfway).astype(F32)
    freqs = jnp.exp(indices * (-math.log(10000.0) / halfway))
    angles = timestep[0].astype(F32) * freqs
    return jnp.concatenate([jnp.sin(angles), jnp.cos(angles)])


def twice(row):
    return jnp.concatenate([row, row]).reshape(1, 128)


def diagonal(square):
    nought = jnp.zeros_like(square)
    return jnp.block([[square, nought], [nought, square]])


def shards(latents, target, block_coords, timestep, conv_weight, coarse_weight, out_weight, time_weight, norm_gain, norm_bias):
    devices = lax.axis_size("bx") * lax.axis_size("by") * lax.axis_size("cz")
    voxels = devices * 4096
    info = block_coords
    lat = latents[0]
    lat_pairs = lat.reshape(16, 8, 2, 16, 64)

    mz, pooled = call(z_message, [message(Z_TILES), like((16, 64), BF)], [info, lat])
    rz = lax.ppermute(mz, "cz", [(0, 1), (1, 0)])
    out = message(Y_TILES)
    down, up = call(
        y_messages, [out, out], [info, lat, lat, rz, pooled], [plane(Z_TILES)], [face_spec(1, 0), face_spec(1, 15)]
    )
    rym, ryp = neighbours(down, up, "by")
    out = message(X_TILES)
    planes = [plane(Z_TILES), plane(Y_TILES), plane(Y_TILES)]
    down, up = call(
        x_messages,
        [out, out],
        [info, lat, lat, rz, rym, ryp, pooled],
        planes,
        [face_spec(0, 0), face_spec(0, 15)],
    )
    rxm, rxp = neighbours(down, up, "bx")

    temb = time_embedding(timestep, time_weight.shape[0]).reshape(1, -1)
    raw, scene, columns, taps = call(
        interior,
        [like((1792, 128), F32), like((3, 16, 9, 16, 128), BF), like((3, 9, 128), F32), like((2304, 128), BF)],
        [info, lat_pairs, rz, rym, ryp, conv_weight],
        planes,
    )
    pair = (3, 2, 9, 16, 128)
    tables = jnp.asarray(coarse_table(), BF)
    act, ends, patch, stats = call(
        forward,
        [like((2048, 128), F32), like((2, 3, 9, 16, 128), BF), like((16, 1728), BF), like((devices, 128), F32)],
        [info, scene, scene, raw, columns, rz, rym, ryp, rxm, rxp, pooled, taps]
        + [coarse_weight.reshape(1728, 64), temb, time_weight.T, tables],
        [pltpu.VMEM((2, 128, 128), F32), pltpu.VMEM((224, 160), BF), pltpu.SemaphoreType.DMA]
        + planes
        + [plane(X_TILES), plane(X_TILES)],
        [pl.BlockSpec(pair, lambda i: (0, 0, 0, 0, 0)), pl.BlockSpec(pair, lambda i: (0, 7, 0, 0, 0))],
        far_args=1,
    )
    first = exchange(stats)
    (turned,) = call(turn, [like((3, 256, 18 * 128), BF)], [info, scene, ends])
    gain, bias = twice(norm_gain), twice(norm_bias)
    weights = [diagonal(out_weight), diagonal(out_weight.T)]
    predicted, mine, other = call(
        backward(voxels),
        [like((16, 8, 2, 16, 64), BF), like((2048, 128), F32), like((2048, 128), F32)],
        [info, act, first, target.reshape(16, 8, 2, 16, 64), gain, bias] + weights + [turned, patch, stats],
        [pltpu.VMEM((2048, 256), BF), pltpu.VMEM((2, 2048, 128), F32), pltpu.SemaphoreType.DMA((2,))],
        far_outs=2,
    )
    swap = [(0, 1), (1, 0)]
    chips = devices // 2
    other = lax.ppermute(other, "cz", swap)
    (pieces,) = call(pair_add(voxels), [like((chips, 16, 128), BF)], [info, mine, other, first, gain])
    pieces = lax.all_to_all(pieces, CHIPS, 0, 0, tiled=True)
    copies, grad_time, grad_gain, grad_bias = call(
        combine(voxels),
        [like((chips, 8, 128), BF), like((64, 256), F32), like((1, 64), F32), like((1, 64), F32)],
        [info, pieces, first, gain, temb],
    )
    near = lax.all_to_all(copies, CHIPS, 0, 0, tiled=True)
    far = lax.ppermute(near, "cz", swap)
    grad_conv, grad_coarse, grad_out, loss = call(
        functools.partial(spread, 1.0 / (voxels * 64)),
        [like((27, 64, 64), F32), like((27, 64, 64), F32), like((64, 64), F32), like((1, 1), F32)],
        [info, near, far],
        [pltpu.VMEM((2048, 128), F32)],
    )
    return (
        predicted.reshape(latents.shape),
        loss.reshape(1),
        grad_conv,
        grad_coarse,
        grad_out,
        grad_time.T,
        grad_gain.reshape(64),
        grad_bias.reshape(64),
    )


def solution(mesh):
    blocks = P(ALL, None, None, None, None)
    return jax.shard_map(
        shards,
        mesh=mesh,
        in_specs=(blocks, blocks, P(ALL, None)) + (P(),) * 7,
        out_specs=(blocks,) + (P(),) * 7,
        check_vma=False,
    )
```

```python
import functools
import math

import jax
import jax.numpy as jnp
import numpy as np
from jax import lax
from jax.experimental import pallas as pl
from jax.experimental.pallas import tpu as pltpu
from jax.sharding import PartitionSpec as P

ALL = ("bx", "by", "cz")
CHIPS = ("bx", "by")
BF = jnp.bfloat16
F32 = jnp.float32
EPS = 1e-05
GROUP = 2
VMEM_LIMIT = 40 * 1024 * 1024
SHIFT_LANE = 65


def face_spec(dim, index):
    shape = tuple(1 if d == dim else 16 for d in range(3)) + (64,)
    where = tuple(index if d == dim else 0 for d in range(4))
    return pl.BlockSpec(shape, lambda i: where)


def call(kernel, outs, args, scratch=(), faces=(), far_args=0, far_outs=0):
    vmem = pl.BlockSpec(memory_space=pltpu.VMEM)
    far = pl.BlockSpec(memory_space=pl.ANY)
    specs = list(faces) + [vmem] * (len(args) - 1 - len(faces) - far_args) + [far] * far_args
    args = [
        pltpu.with_memory_space_constraint(arg, pltpu.VMEM) if spec is vmem else arg
        for arg, spec in zip(args, [None] + specs)
    ]
    return pl.pallas_call(
        kernel,
        grid=(1,),
        out_shape=outs,
        in_specs=[pl.BlockSpec(memory_space=pltpu.SMEM)] + specs,
        out_specs=[vmem] * (len(outs) - far_outs) + [far] * far_outs,
        scratch_shapes=list(scratch),
        compiler_params=pltpu.CompilerParams(vmem_limit_bytes=VMEM_LIMIT),
    )(*args)


def like(shape, dtype):
    return jax.ShapeDtypeStruct(shape, dtype)


def keep(cond, value):
    return jnp.where(cond, value, jnp.zeros_like(value))


def bits(info):
    return info[0, 0], info[0, 1], info[0, 2], lax.axis_index("cz")


def start16(bit):
    return pl.multiple_of(bit * 16, 16)


def cell_rows(first, second, face, on):
    rows = []
    for r in range(4):
        for s in range(4):
            here = on & (first == r // 2) & (second == s // 2)
            rows.append(keep(here, face[r % 2][s % 2]))
    return jnp.concatenate(rows, axis=0)


def row_of(cells, p):
    return cells[p : p + 1]


Z_TILES, Y_TILES, X_TILES = 1, 2, 5


def message(tiles):
    return like((9 + tiles, 16, 128), BF)


def plane(tiles):
    return pltpu.VMEM((32 + tiles, 32, 64), BF)


def side_by_side(rows):
    half = rows.shape[0] // 2
    return jnp.concatenate([rows[:half], rows[half:]], axis=rows.ndim - 1)


def write_message(out, face, tiles, first, second, on):
    out[0:8] = side_by_side(face)
    for t, rows in enumerate(tiles):
        out[8 + t] = side_by_side(rows).astype(BF)
    row = lax.broadcasted_iota(jnp.int32, (16, 128), 0)
    here = jnp.where(on, 2 * first + second, 99)
    out[8 + len(tiles)] = jnp.where(row == here, 1.0, 0.0).astype(BF)


def open_message(ref, out):
    tiles = ref.shape[0] - 9
    face = jnp.concatenate([ref[0:8, :, :64], ref[0:8, :, 64:]], axis=0)
    flags = ref[8 + tiles].astype(F32)
    for q in range(4):
        here = jnp.broadcast_to(flags[q : q + 1, :64], (16, 64))[None]
        out[16 * (q // 2) : 16 * (q // 2) + 16, 16 * (q % 2) : 16 * (q % 2) + 16, :] = jnp.where(
            here > 0.5, face.astype(F32), 0.0
        ).astype(BF)
    for t in range(tiles):
        out[32 + t] = jnp.concatenate([ref[8 + t, :, :64], ref[8 + t, :, 64:]], axis=0)


def z_message(info, lat_in, out, pooled, lat, fetched):
    px, py, pz, kz = bits(info)
    zsel = 15 * (1 - kz)

    def chunk(n):
        part = pl.ds(4 * n, 4)
        return pltpu.make_async_copy(lat_in.at[:, part], lat.at[:, part], fetched.at[n])

    for n in range(4):
        chunk(n).start()
    pick = lax.broadcasted_iota(jnp.int32, (16, 16, 64), 1) == zsel
    sums = [[None, None], [None, None]]
    faces = []
    for y in range(16):
        if y % 4 == 0:
            chunk(y // 4).wait()
        slab = lat[:, y].astype(F32)
        faces.append(jnp.sum(jnp.where(pick, slab, 0.0), axis=1)[None])
        for a in range(2):
            part = jnp.sum(slab[8 * a : 8 * a + 8], axis=0)
            old = sums[a][y // 8]
            sums[a][y // 8] = part if old is None else old + part
    cells = []
    for a in range(2):
        for b in range(2):
            for c in range(2):
                cells.append(jnp.sum(sums[a][b][8 * c : 8 * c + 8], axis=0, keepdims=True))
    cells = jnp.concatenate(cells, axis=0) * (1.0 / math.sqrt(512.0))
    cells = cells.astype(BF).astype(F32)
    pooled[...] = jnp.concatenate([cells, jnp.zeros((8, 64), F32)], axis=0).astype(BF)
    on = pz == 1 - kz
    face = [
        [jnp.where(kz == 0, row_of(cells, 4 * a + 2 * b + 1), row_of(cells, 4 * a + 2 * b)) for a in range(2)]
        for b in range(2)
    ]
    rows = jnp.concatenate([cell_rows(py, px, face, on), jnp.zeros((16, 64), F32)], axis=0)
    write_message(out, jnp.concatenate(faces, axis=0).astype(BF), [rows], py, px, on)


def y_messages(info, low, high, rz_in, pooled, down, up, rz):
    px, py, pz, kz = bits(info)
    open_message(rz_in, rz)
    cells = pooled[...].astype(F32)
    halo = rz[32].astype(F32)
    for out, face, bit, line, q in ((down, low, 0, 0, 0), (up, high, 1, 31, 1)):
        on = py == bit
        picked = [[row_of(cells, 4 * a + 2 * q + c) for c in range(2)] for a in range(2)]
        tail = halo[12:16] if q else halo[0:4]
        rows = jnp.concatenate([cell_rows(px, pz, picked, on), tail, jnp.zeros((12, 64), F32)], axis=0)
        write_message(out, face[:, 0], [rz[line], rows], px, pz, on)


def x_messages(info, low, high, rz_in, rym_in, ryp_in, pooled, down, up, rz, rym, ryp):
    px, py, pz, kz = bits(info)
    for ref, out in ((rz_in, rz), (rym_in, rym), (ryp_in, ryp)):
        open_message(ref, out)
    cells = pooled[...].astype(F32)
    halo = rz[32].astype(F32)
    halo_m = rym[33].astype(F32)
    halo_p = ryp[33].astype(F32)
    line_m = rym[32].astype(F32)
    line_p = ryp[32].astype(F32)
    where16 = lax.broadcasted_iota(jnp.int32, (32, 16, 64), 1)
    for out, face, bit, line, q in ((down, low, 0, 0, 0), (up, high, 1, 31, 1)):
        on = px == bit
        slab = rz[0:32, 16 * q : 16 * q + 16, :].astype(F32)
        z_line = jnp.sum(jnp.where(where16 == 15 * q, slab, 0.0), axis=1).astype(BF)
        picked = [[row_of(cells, 4 * q + 2 * b + c) for c in range(2)] for b in range(2)]
        corners = [line_m[line : line + 1], line_p[line : line + 1], jnp.zeros((14, 64), F32)]
        corners = jnp.concatenate(corners + [cell_rows(py, pz, picked, on)], axis=0)
        c0 = 3 * q
        parts = [row_of(halo, 4 * cy + c0) for cy in range(4)]
        parts += [halo_m[4 * c0 : 4 * c0 + 4], halo_p[4 * c0 : 4 * c0 + 4]]
        parts += [row_of(halo_m, 16 + c0), row_of(halo_p, 16 + c0), jnp.zeros((18, 64), F32)]
        tiles = [z_line, rym[line], ryp[line], corners, jnp.concatenate(parts, axis=0)]
        write_message(out, face[0], tiles, py, pz, on)


def coarse_table():
    pooled, rz, rym, ryp, rxm, rxp = 0, 16, 32, 64, 96, 128
    table = np.zeros((16, 224, 160), np.float32)
    for combo in range(16):
        bit = ((combo >> 3) & 1, (combo >> 2) & 1, (combo >> 1) & 1)
        core = combo & 1
        for tap in range(27):
            off = (tap // 9, tap // 3 % 3, tap % 3)
            for p in range(8):
                at = (p // 4, p // 2 % 2, p % 2)
                pos = [2 * bit[d] - 1 + off[d] + at[d] for d in range(3)]
                x, y, z = pos
                out_z = z < 0 or z > 3
                if out_z and (z < 0) != (core == 1):
                    continue
                if x < 0 or x > 3:
                    base = rxm if x < 0 else rxp
                    if y < 0 or y > 3:
                        side = 0 if y < 0 else 1
                        row = 16 + (12 + side if out_z else 4 + 4 * side + z)
                    else:
                        row = 16 + y if out_z else 4 * y + z
                    row = base + row
                elif y < 0 or y > 3:
                    row = (rym if y < 0 else ryp) + (16 + x if out_z else 4 * x + z)
                elif out_z:
                    row = rz + 4 * y + x
                else:
                    own = [pos[d] - 2 * bit[d] for d in range(3)]
                    if min(own) < 0 or max(own) > 1:
                        continue
                    row = pooled + 4 * own[0] + 2 * own[1] + own[2]
                table[combo, 8 * tap + p, row] = 1.0
    return table


class Window:
    def __init__(self, info, rz, rym, ryp):
        px, py, pz, kz = bits(info)
        self.pz, self.rz, self.rym, self.ryp = pz, rz, rym, ryp
        self.z0 = pl.ds(start16(pz), 16)
        self.z1 = pl.ds(start16(1 - pz), 16)
        self.xs = pl.ds(start16(px), 16)
        self.ys = pl.ds(start16(py), 16)
        self.xlo, self.xhi, self.ylo, self.yhi = px == 0, px == 1, py == 0, py == 1
        self.on_low = (pz == 0) & (kz == 1)
        self.on_high = (pz == 1) & (kz == 0)
        self.row16 = lax.broadcasted_iota(jnp.int32, (16, 16, 64), 1)
        self.z_row = lax.broadcasted_iota(jnp.int32, (9, 16, 128), 1)

    def edge(self, block):
        return jnp.sum(jnp.where(self.row16[: block.shape[0]] == 15 * self.pz, block.astype(F32), 0.0), axis=1)

    def edge1(self, ref, i):
        return self.edge(ref[i : i + 1, self.z1, :])

    def low_of(self, e, h):
        return keep(self.pz == 1, e) + keep(self.on_low, h)

    def high_of(self, e, h):
        return keep(self.pz == 0, e) + keep(self.on_high, h)

    def offsets(self, evens, odds, first, last, zl, zh):
        left = jnp.concatenate([first[None], odds], axis=0)
        right = jnp.concatenate([evens, last[None]], axis=0)
        tile = jnp.concatenate([left, right], axis=2)
        wide = tile.astype(F32)
        down = jnp.where(self.z_row == 0, zl, pltpu.roll(wide, 1, 1)).astype(BF)
        up = jnp.where(self.z_row == 15, zh, pltpu.roll(wide, 15, 1)).astype(BF)
        return down, tile, up


def one(ref, i, j):
    return ref[i].astype(F32)[j : j + 1]


def interior(info, lat, rz_in, rym_in, ryp_in, taps, raw, scene, columns, weight, rz, rym, ryp):
    for ref, out in ((rz_in, rz), (rym_in, rym), (ryp_in, ryp)):
        open_message(ref, out)
    nought = jnp.zeros((64, 64), BF)
    for tap in range(9):
        ox, oz = tap // 3, tap % 3
        for a in range(4):
            left = nought if a == 3 else taps[9 * ox + 3 * a + oz]
            right = nought if a == 0 else taps[9 * ox + 3 * a - 3 + oz]
            weight[256 * tap + 64 * a : 256 * tap + 64 * a + 64] = jnp.concatenate([left, right], axis=1)
    w = Window(info, rz, rym, ryp)
    y_low = keep(w.ylo, rym[w.xs, w.z0, :])
    y_high = keep(w.yhi, ryp[w.xs, w.z0, :])
    e_low = keep(w.ylo, w.edge(rym[w.xs, w.z1, :]))
    e_high = keep(w.yhi, w.edge(ryp[w.xs, w.z1, :]))
    h_low = jnp.where(w.ylo, rym[32, w.xs, :], rz[15, w.xs, :]).astype(F32)
    h_high = jnp.where(w.yhi, ryp[32, w.xs, :], rz[16, w.xs, :]).astype(F32)
    h_mid = rz[w.ys, w.xs, :].astype(F32)

    def packed(of):
        rows = [of(e_low, h_low)] + [of(jnp.zeros((16, 64), F32), h_mid[y]) for y in range(16)]
        rows.append(of(e_high, h_high))
        return [jnp.concatenate([rows[2 * k], rows[2 * k + 1]], axis=1) for k in range(9)]

    below, above = packed(w.low_of), packed(w.high_of)
    inner = [None] * 3
    for x in range(16):
        zl = jnp.concatenate([below[k][x : x + 1][None] for k in range(9)], axis=0)
        zh = jnp.concatenate([above[k][x : x + 1][None] for k in range(9)], axis=0)
        planes = w.offsets(lat[x, :, 0], lat[x, :, 1], y_low[x], y_high[x], zl, zh)
        for oz, plane in enumerate(planes):
            scene[oz, x] = plane
            wide = plane.astype(F32)
            inner[oz] = wide if x == 0 else inner[oz] + wide
    for oz in range(3):
        columns[oz] = jnp.sum(inner[oz], axis=1)
    for first, count in ((1, 4), (5, 4), (9, 4), (13, 2)):
        pieces = []
        for tap in range(9):
            ox, oz = tap // 3, tap % 3
            for dk in range(2):
                at = first + ox - 1
                pieces.append(scene[oz, at : at + count, dk : dk + 8].reshape(128 * count, 128))
        value = jnp.dot(jnp.concatenate(pieces, axis=1), weight[...], preferred_element_type=F32)
        raw[(first - 1) * 128 : (first - 1 + count) * 128] = value


def forward(
    info, near_low, near_high, raw, columns, rz_in, rym_in, ryp_in, rxm_in, rxp_in, pooled, weight,
    coarse_weight, temb, time_weight, tables, act, ends, patch_out, stats,
    shift, table, arrived, rz, rym, ryp, rxm, rxp
):
    px, py, pz, kz = bits(info)
    fetch = pltpu.make_async_copy(tables.at[8 * px + 4 * py + 2 * pz + kz], table, arrived)
    fetch.start()
    for ref, out in ((rz_in, rz), (rym_in, rym), (ryp_in, ryp), (rxm_in, rxm), (rxp_in, rxp)):
        open_message(ref, out)
    w = Window(info, rz, rym, ryp)
    nought = jnp.zeros((16, 64), BF)

    def sides(rx, out, inner):
        first = jnp.where(
            out,
            jnp.where(w.ylo, rx[33, w.z0, :], rx[15, w.z0, :]),
            jnp.where(w.ylo, rym[inner, w.z0, :], nought),
        )
        last = jnp.where(
            out,
            jnp.where(w.yhi, rx[34, w.z0, :], rx[16, w.z0, :]),
            jnp.where(w.yhi, ryp[inner, w.z0, :], nought),
        )
        return first, last

    def side_columns(rx, out, inner, of):
        half = rz[w.ys, 0:16, :] if inner < 16 else rz[w.ys, 16:32, :]
        inner_h = jnp.sum(jnp.where(w.row16 == inner % 16, half.astype(F32), 0.0), axis=1)
        e_mid = keep(out, w.edge(rx[w.ys, w.z1, :]))
        hh = jnp.where(out, rx[32, w.ys, :].astype(F32), inner_h)
        e_first = jnp.where(
            out,
            jnp.where(w.ylo, w.edge1(rx, 33), w.edge1(rx, 15)),
            keep(w.ylo, w.edge1(rym, inner)),
        )
        h_first = jnp.where(
            out,
            jnp.where(w.ylo, one(rx, 35, 0), one(rx, 32, 15)),
            jnp.where(w.ylo, one(rym, 32, inner), one(rz, 15, inner)),
        )
        e_last = jnp.where(
            out,
            jnp.where(w.yhi, w.edge1(rx, 34), w.edge1(rx, 16)),
            keep(w.yhi, w.edge1(ryp, inner)),
        )
        h_last = jnp.where(
            out,
            jnp.where(w.yhi, one(rx, 35, 1), one(rx, 32, 16)),
            jnp.where(w.yhi, one(ryp, 32, inner), one(rz, 16, inner)),
        )
        mid = of(e_mid, hh)
        rows = [of(e_first, h_first)] + [mid[y : y + 1] for y in range(16)] + [of(e_last, h_last)]
        return [jnp.concatenate([rows[2 * k], rows[2 * k + 1]], axis=1)[None] for k in range(9)]

    for e, rx, out, inner in ((0, rxm, w.xlo, 15), (1, rxp, w.xhi, 16)):
        zl = jnp.concatenate(side_columns(rx, out, inner, w.low_of), axis=0)
        zh = jnp.concatenate(side_columns(rx, out, inner, w.high_of), axis=0)
        first, last = sides(rx, out, inner)
        plane = keep(out, rx[w.ys, w.z0, :]).reshape(8, 2, 16, 64)
        for oz, tile in enumerate(w.offsets(plane[:, 0], plane[:, 1], first, last, zl, zh)):
            ends[e, oz] = tile

    source = jnp.concatenate(
        [pooled[...], rz[32, 0:16, :], rym[33], ryp[33], rxm[35, 16:32, :], rxm[36, 0:16, :], rxp[35, 16:32, :], rxp[36, 0:16, :]],
        axis=0,
    )
    fetch.wait()
    taps = jnp.dot(table[...], source, preferred_element_type=F32)
    patch = jnp.concatenate([taps[8 * t : 8 * t + 8] for t in range(27)], axis=1)
    patch_out[...] = jnp.concatenate([patch, patch], axis=0).astype(BF)
    coarse = jnp.dot(patch_out[...], coarse_weight[...], preferred_element_type=F32)
    coarse = coarse.astype(BF).astype(F32)
    coarse = jnp.concatenate([coarse, coarse], axis=1)
    time_bias = lax.dot_general(
        jnp.broadcast_to(temb[...], (8, 256)),
        time_weight[...].astype(F32),
        (((1,), (1,)), ((), ())),
        preferred_element_type=F32,
        precision=lax.Precision.HIGHEST,
    )[:1]
    time_bias = jnp.concatenate([time_bias, time_bias], axis=1)
    z_half = lax.broadcasted_iota(jnp.int32, (16, 128), 0) < 8
    added = []
    for q in range(4):
        added.append(jnp.where(z_half, coarse[2 * q : 2 * q + 1], coarse[2 * q + 1 : 2 * q + 2]) + time_bias)

    pieces = []
    for tap in range(9):
        ox, oz = tap // 3, tap % 3
        low = ends[0, oz] if ox == 0 else near_low[oz, ox - 1]
        high = ends[1, oz] if ox == 2 else near_high[oz, ox]
        for dk in range(2):
            pieces.append(jnp.concatenate([low[dk : dk + 8], high[dk : dk + 8]], axis=0).reshape(256, 128))
    edges = jnp.dot(jnp.concatenate(pieces, axis=1), weight[...], preferred_element_type=F32)

    total = jnp.zeros((1, 128), F32)
    squares = jnp.zeros((1, 128), F32)
    for x in range(16):
        if x == 0:
            value = edges[:128]
        elif x == 15:
            value = edges[128:]
        else:
            value = raw[(x - 1) * 128 : x * 128]
        value = value.reshape(2, 4, 16, 128)
        a = x // 8
        value = jnp.concatenate([(value[b] + added[2 * a + b][None])[None] for b in range(2)], axis=0).reshape(128, 128)
        act[x * 128 : x * 128 + 128] = value
        total = total + jnp.sum(value, axis=0, keepdims=True)
        squares = squares + jnp.sum(value * value, axis=0, keepdims=True)
    shift[...] = jnp.zeros(shift.shape, F32)

    def place(tap, slot, value):
        row = SHIFT_LANE + 2 * (tap // 4 + slot)
        u = tap % 4
        shift[u // 2, row : row + 1, 64 * (u % 2) : 64 * (u % 2) + 64] = value

    for oz in range(3):
        inner = columns[oz]
        planes = (ends[0, oz], near_low[oz, 0], near_high[oz, 1], ends[1, oz])
        outer = [jnp.sum(plane.astype(F32), axis=1) for plane in planes]
        for ox, part in enumerate((inner + outer[0] - outer[2], inner, inner - outer[1] + outer[3])):
            all_columns = jnp.sum(part, axis=0, keepdims=True)
            whole = all_columns[:, :64] + all_columns[:, 64:]
            y0, y1 = part[0:1, :64], part[0:1, 64:]
            y16, y17 = part[8:9, :64], part[8:9, 64:]
            for oy, window in enumerate((whole - y16 - y17, whole - y0 - y17, whole - y0 - y1)):
                place(9 * ox + 3 * oy + oz, 0, window)
    for t in range(27):
        place(t, 7, 512.0 * jnp.sum(taps[8 * t : 8 * t + 8], axis=0, keepdims=True))

    lane = lax.broadcasted_iota(jnp.int32, (1, 128), 1)
    pairs = pair_sum(squares + pltpu.roll(squares, 64, 1))
    row = jnp.where(lane < 64, total + pltpu.roll(total, 64, 1), jnp.where(lane % 2 == 0, pairs, 0.0))
    for u in range(2):
        stats[128 * u : 128 * u + 128] = shift[u].T + row


def turn(info, scene, ends, turned):
    for oz in range(3):
        for xp in range(18):
            for dk in range(2):
                tile = scene[oz, xp - 1, dk : dk + 8] if 1 <= xp <= 16 else ends[xp // 17, oz, dk : dk + 8]
                turned[oz, 128 * dk : 128 * dk + 128, 128 * xp : 128 * xp + 128] = tile.reshape(128, 128).T


def pair_sum(row):
    lane = lax.broadcasted_iota(jnp.int32, row.shape, 1)
    return row + jnp.where(lane % 2 == 0, pltpu.roll(row, 127, 1), pltpu.roll(row, 1, 1))


def halves(row):
    lane = lax.broadcasted_iota(jnp.int32, row.shape, 1)
    other = pltpu.roll(row, 64, 1)
    return jnp.where(lane < 64, row, other), jnp.where(lane < 64, other, row)


def moments(gathered, count):
    row = jnp.sum(gathered[...], axis=0, keepdims=True)
    sums, upper = halves(row)
    lane = lax.broadcasted_iota(jnp.int32, row.shape, 1)
    squares = jnp.where(lane % 2 == 0, upper, pltpu.roll(upper, 1, 1))
    mean = pair_sum(sums) / count
    var = squares / count - mean * mean
    return row, sums, mean, 1.0 / jnp.sqrt(var + EPS)


def backward(voxels):
    count = float(voxels * GROUP)
    scale = 1.0 / (voxels * 64)

    def kernel(
        info, gathered, target, gain, bias, weight, weight_t, patch, stats, act_in, turned_in,
        predicted, mine, other, cotangent, payload, act, turned, fetched, sent
    ):
        def chunk(n):
            rows = pl.ds(256 * n, 256)
            return pltpu.make_async_copy(act_in.at[rows], act.at[rows], fetched.at[n])

        whole = pltpu.make_async_copy(turned_in, turned, fetched.at[8])
        for n in range(8):
            chunk(n).start()
        whole.start()
        kz = lax.axis_index("cz")
        _, _, mean, rstd = moments(gathered, count)
        gains = jnp.zeros((1, 128), F32)
        biases = jnp.zeros((1, 128), F32)
        lost = jnp.zeros((1, 128), F32)
        outer = jnp.zeros((128, 128), F32)
        cells = [[None] * 4, [None] * 4]
        for x in range(0, 16, 2):
            rows = slice(x * 128, x * 128 + 256)
            chunk(x // 2).wait()
            normalized = (act[rows] - mean) * rstd
            shifted = normalized * gain[...] + bias[...]
            sigma = jax.nn.sigmoid(shifted)
            hidden = (shifted * sigma).astype(BF)
            output = jnp.dot(hidden, weight[...], preferred_element_type=F32)
            goal = jnp.concatenate([target[x : x + 2, :, 0], target[x : x + 2, :, 1]], axis=3)
            residue = output - goal.reshape(256, 128).astype(F32)
            shown = output.astype(BF).reshape(2, 8, 16, 128)
            predicted[x : x + 2, :, 0] = shown[..., :64]
            predicted[x : x + 2, :, 1] = shown[..., 64:]
            upstream = (2.0 * scale * residue).astype(BF)
            back = jnp.dot(upstream, weight_t[...], preferred_element_type=F32)
            value = back * sigma * (1.0 + shifted * (1.0 - sigma))
            gains = gains + jnp.sum(value * normalized, axis=0, keepdims=True)
            biases = biases + jnp.sum(value, axis=0, keepdims=True)
            lost = lost + jnp.sum(residue * residue, axis=0, keepdims=True)
            outer = outer + lax.dot_general(hidden, upstream, (((0,), (0,)), ((), ())), preferred_element_type=F32)
            value = value * (gain[...] * rstd)
            narrow = [value.astype(BF), normalized.astype(BF)]
            cotangent[rows, :128] = jnp.concatenate([part[:, :64] for part in narrow], axis=1)
            cotangent[rows, 128:] = jnp.concatenate([part[:, 64:] for part in narrow], axis=1)
            for part, wide in enumerate((value, normalized)):
                planes = wide.reshape(2, 2, 4, 16, 128)
                for b in range(2):
                    q = 2 * (x // 8) + b
                    cell = jnp.sum(planes[:, b], axis=(0, 1))
                    old = cells[part][q]
                    cells[part][q] = cell if old is None else old + cell

        def store(tap, slot, value):
            u = tap % 4
            half = jnp.where(kz == u // 2, 0, 1)
            payload.at[half][pl.ds(1024 * (u % 2) + slot + tap // 4, 64, stride=16), :] = value

        rows = []
        for q in range(4):
            for c in range(2):
                sums = [jnp.sum(cells[p][q][8 * c : 8 * c + 8], axis=0, keepdims=True) for p in range(2)]
                rows.append(jnp.concatenate([r[:, :64] + r[:, 64:] for r in sums], axis=1))
        rows = jnp.concatenate(rows, axis=0)
        high = rows.astype(BF)
        split = jnp.concatenate([high.astype(F32), rows - high.astype(F32)], axis=0).astype(BF)
        coarse = lax.dot_general(patch[...], split, (((0,), (0,)), ((), ())), preferred_element_type=F32)
        for t in range(27):
            store(t, 7, coarse[64 * t : 64 * t + 64])
        whole.wait()
        for ox in range(3):
            windows = turned[:, :, 128 * ox : 128 * ox + 2048].reshape(768, 2048)
            products = jnp.dot(windows, cotangent[...], preferred_element_type=F32)
            for oz in range(3):
                product = products[256 * oz : 256 * oz + 256]
                for oy in range(3):
                    value = product[64 * oy : 64 * oy + 64, :128] + product[64 * oy + 64 : 64 * oy + 128, 128:]
                    store(9 * ox + 3 * oy + oz, 0, value)
        nought = jnp.zeros((64, 64), F32)
        store(27, 0, jnp.concatenate([outer[:64, :64] + outer[64:, 64:], nought], axis=1))
        loss = jnp.broadcast_to(jnp.sum(lost, axis=1, keepdims=True), (64, 128))
        high = loss.astype(BF).astype(F32)
        lane = lax.broadcasted_iota(jnp.int32, (64, 128), 1)
        split = jnp.where(lane == 2 * kz, high, jnp.where(lane == 2 * kz + 1, loss - high, 0.0))
        store(27, 7, split)
        lane = lax.broadcasted_iota(jnp.int32, (1, 128), 1)
        row = jnp.where(lane < 64, gains + pltpu.roll(gains, 64, 1), biases + pltpu.roll(biases, 64, 1))
        wide = jnp.broadcast_to(row, (128, 128))
        for half in range(2):
            payload.at[half][pl.ds(14, 128, stride=16), :] = wide
            slot = jnp.where(kz == half, 0, 1)
            payload.at[slot][pl.ds(15, 128, stride=16), :] = stats[128 * half : 128 * half + 128]
        copies = [pltpu.make_async_copy(payload.at[n], ref, sent.at[n]) for n, ref in ((0, mine), (1, other))]
        for copy in copies:
            copy.start()
        for copy in copies:
            copy.wait()

    return kernel


def slopes(norms, gain, count):
    grad_gain, grad_bias = halves(norms)
    return pair_sum(gain * grad_bias) / count, pair_sum(gain * grad_gain) / count


def pair_add(voxels):
    total_count = float(voxels * GROUP)
    count = float(2 * 4096 * GROUP)

    def kernel(info, mine, other, gathered, gain, out):
        _, _, _, rstd = moments(gathered, total_count)
        total = (mine[...] + other[...]).reshape(-1, 16, 128)
        m1, m2 = slopes(total[0, 14:15], gain[...], count)
        row = lax.broadcasted_iota(jnp.int32, total.shape, 1)
        lane = lax.broadcasted_iota(jnp.int32, total.shape, 2)
        picked = (lane == SHIFT_LANE + 2 * row) & (row < 14)
        ones = jnp.sum(jnp.where(picked, total[:, 15:16], 0.0), axis=2, keepdims=True)
        centred = total - (m1 * rstd)[None] * ones - (m2 * rstd)[None] * pltpu.roll(total, 64, 2)
        total = jnp.where((lane < 64) & (row < 14), centred, total)
        lost = pltpu.roll(total - total.astype(BF).astype(F32), 1, 1)
        out[...] = jnp.where(row == 15, lost, total).astype(BF)

    return kernel


def combine(voxels):
    count = float(voxels * GROUP)
    pair_count = float(2 * 4096 * GROUP)

    def kernel(info, pieces, gathered, gain, temb, copies, grad_time, gain_out, bias_out):
        _, sums, mean, rstd = moments(gathered, count)
        value = pieces[...].astype(F32)
        chips = value.shape[0]
        seen = value[:, 14] + value[:, 15]
        norms = jnp.sum(seen, axis=0, keepdims=True)
        grad_gain, grad_bias = halves(norms)
        gain_out[...] = grad_gain[:, :64]
        bias_out[...] = grad_bias[:, :64]
        m1, m2 = slopes(norms, gain[...], count)
        centred = (sums - voxels * mean) * rstd
        act_sum = rstd * (gain[...] * grad_bias - voxels * m1 - m2 * centred)
        column = jnp.broadcast_to(act_sum, (128, 128)).T[:64]
        grad_time[...] = jnp.concatenate([column, column], axis=1) * temb[...]
        own1, own2 = slopes(seen, gain[...], pair_count)
        delta1, delta2 = (own1 - m1) * rstd, (own2 - m2) * rstd
        ones = gathered[0:chips] + gathered[chips : 2 * chips]
        back = lax.dot_general(
            ones, delta1, (((0,), (0,)), ((), ())), preferred_element_type=F32, precision=lax.Precision.HIGHEST
        )
        back = [back[SHIFT_LANE + 2 * r : SHIFT_LANE + 2 * r + 1] for r in range(14)]
        back = jnp.concatenate(back + [jnp.zeros((2, 128), F32)], axis=0)
        total = jnp.sum(value + delta2[:, None] * pltpu.roll(value, 64, 2), axis=0) + back
        lane = lax.broadcasted_iota(jnp.int32, (7, 128), 1)
        both = jnp.where(lane < 64, total[:7], pltpu.roll(total[7:14], 64, 1))
        lost = both[6:7] - both[6:7].astype(BF).astype(F32)
        piece = jnp.concatenate([both, lost], axis=0).astype(BF)
        copies[...] = jnp.broadcast_to(piece[None], copies.shape)

    return kernel


def spread(scale, info, near, far, conv, coarse, out, loss, rows):
    kz = lax.axis_index("cz")
    rows[pl.ds(pl.multiple_of(1024 * kz, 1024), 1024), :] = near[...].astype(F32).reshape(1024, 128)
    rows[pl.ds(pl.multiple_of(1024 * (1 - kz), 1024), 1024), :] = far[...].astype(F32).reshape(1024, 128)
    for tap in range(28):
        tile = rows[pl.ds(512 * (tap % 4) + tap // 4, 64, stride=8), :]
        if tap < 27:
            conv[tap] = tile[:, :64]
            coarse[tap] = tile[:, 64:]
        else:
            out[...] = tile[:, :64]
            parts = tile[0:1] + rows[2048 - 512 + 7 : 2048 - 512 + 8, :]
            lane = lax.broadcasted_iota(jnp.int32, (1, 128), 1)
            whole = jnp.sum(jnp.where((lane >= 64) & (lane < 68), parts, 0.0), axis=1, keepdims=True)
            loss[...] = whole * scale


def exchange(rows):
    out = lax.all_to_all(rows.reshape(rows.shape[0], 1, 128), ("cz",) + CHIPS, 0, 0, tiled=True)
    return out.reshape(rows.shape)


def neighbours(down, up, axis):
    ends = lax.axis_size(axis) - 1
    before = lax.ppermute(up, axis, [(i, i + 1) for i in range(ends)])
    after = lax.ppermute(down, axis, [(i + 1, i) for i in range(ends)])
    return before, after


def time_embedding(timestep, width):
    halfway = width // 2
    indices = jnp.arange(halfway).astype(F32)
    freqs = jnp.exp(indices * (-math.log(10000.0) / halfway))
    angles = timestep[0].astype(F32) * freqs
    return jnp.concatenate([jnp.sin(angles), jnp.cos(angles)])


def twice(row):
    return jnp.concatenate([row, row]).reshape(1, 128)


def diagonal(square):
    nought = jnp.zeros_like(square)
    return jnp.block([[square, nought], [nought, square]])


def shards(latents, target, block_coords, timestep, conv_weight, coarse_weight, out_weight, time_weight, norm_gain, norm_bias):
    devices = lax.axis_size("bx") * lax.axis_size("by") * lax.axis_size("cz")
    voxels = devices * 4096
    info = pltpu.with_memory_space_constraint(block_coords, pltpu.HBM)
    lat = latents[0]
    lat_far = pltpu.with_memory_space_constraint(lat, pltpu.HBM)
    lat_pairs = lat.reshape(16, 8, 2, 16, 64)

    scratch = [pltpu.VMEM((16, 16, 16, 64), BF), pltpu.SemaphoreType.DMA((4,))]
    mz, pooled = call(z_message, [message(Z_TILES), like((16, 64), BF)], [info, lat_far], scratch, far_args=1)
    rz = lax.ppermute(mz, "cz", [(0, 1), (1, 0)])
    out = message(Y_TILES)
    down, up = call(
        y_messages, [out, out], [info, lat, lat, rz, pooled], [plane(Z_TILES)], [face_spec(1, 0), face_spec(1, 15)]
    )
    rym, ryp = neighbours(down, up, "by")
    out = message(X_TILES)
    planes = [plane(Z_TILES), plane(Y_TILES), plane(Y_TILES)]
    down, up = call(
        x_messages,
        [out, out],
        [info, lat, lat, rz, rym, ryp, pooled],
        planes,
        [face_spec(0, 0), face_spec(0, 15)],
    )
    rxm, rxp = neighbours(down, up, "bx")

    temb = time_embedding(timestep, time_weight.shape[0]).reshape(1, -1)
    raw, scene, columns, taps = call(
        interior,
        [like((1792, 128), F32), like((3, 16, 9, 16, 128), BF), like((3, 9, 128), F32), like((2304, 128), BF)],
        [info, lat_pairs, rz, rym, ryp, conv_weight],
        planes,
    )
    pair = (3, 2, 9, 16, 128)
    tables = jnp.asarray(coarse_table(), BF)
    act, ends, patch, stats = call(
        forward,
        [like((2048, 128), F32), like((2, 3, 9, 16, 128), BF), like((16, 1728), BF), like((devices, 128), F32)],
        [info, scene, scene, raw, columns, rz, rym, ryp, rxm, rxp, pooled, taps]
        + [coarse_weight.reshape(1728, 64), temb, time_weight.T, tables],
        [pltpu.VMEM((2, 128, 128), F32), pltpu.VMEM((224, 160), BF), pltpu.SemaphoreType.DMA]
        + planes
        + [plane(X_TILES), plane(X_TILES)],
        [pl.BlockSpec(pair, lambda i: (0, 0, 0, 0, 0)), pl.BlockSpec(pair, lambda i: (0, 7, 0, 0, 0))],
        far_args=1,
    )
    first = exchange(stats)
    (turned,) = call(turn, [like((3, 256, 18 * 128), BF)], [info, scene, ends])
    gain, bias = twice(norm_gain), twice(norm_bias)
    weights = [diagonal(out_weight), diagonal(out_weight.T)]
    predicted, mine, other = call(
        backward(voxels),
        [like((16, 8, 2, 16, 64), BF), like((2048, 128), F32), like((2048, 128), F32)],
        [info, first, target.reshape(16, 8, 2, 16, 64), gain, bias] + weights + [patch, stats, act, turned],
        [
            pltpu.VMEM((2048, 256), BF),
            pltpu.VMEM((2, 2048, 128), F32),
            pltpu.VMEM((2048, 128), F32),
            pltpu.VMEM((3, 256, 18 * 128), BF),
            pltpu.SemaphoreType.DMA((9,)),
            pltpu.SemaphoreType.DMA((2,)),
        ],
        far_args=2,
        far_outs=2,
    )
    swap = [(0, 1), (1, 0)]
    chips = devices // 2
    other = lax.ppermute(other, "cz", swap)
    (pieces,) = call(pair_add(voxels), [like((chips, 16, 128), BF)], [info, mine, other, first, gain])
    pieces = lax.all_to_all(pieces, CHIPS, 0, 0, tiled=True)
    copies, grad_time, grad_gain, grad_bias = call(
        combine(voxels),
        [like((chips, 8, 128), BF), like((64, 256), F32), like((1, 64), F32), like((1, 64), F32)],
        [info, pieces, first, gain, temb],
    )
    near = lax.all_to_all(copies, CHIPS, 0, 0, tiled=True)
    far = lax.ppermute(near, "cz", swap)
    grad_conv, grad_coarse, grad_out, loss = call(
        functools.partial(spread, 1.0 / (voxels * 64)),
        [like((27, 64, 64), F32), like((27, 64, 64), F32), like((64, 64), F32), like((1, 1), F32)],
        [info, near, far],
        [pltpu.VMEM((2048, 128), F32)],
    )
    return (
        predicted.reshape(latents.shape),
        loss.reshape(1),
        grad_conv,
        grad_coarse,
        grad_out,
        grad_time.T,
        grad_gain.reshape(64),
        grad_bias.reshape(64),
    )


def solution(mesh):
    blocks = P(ALL, None, None, None, None)
    return jax.shard_map(
        shards,
        mesh=mesh,
        in_specs=(blocks, blocks, P(ALL, None)) + (P(),) * 7,
        out_specs=(blocks,) + (P(),) * 7,
        check_vma=False,
    )
```

```python
import functools
import math

import jax
import jax.numpy as jnp
import numpy as np
from jax import lax
from jax.experimental import pallas as pl
from jax.experimental.pallas import tpu as pltpu
from jax.sharding import PartitionSpec as P

ALL = ("bx", "by", "cz")
CHIPS = ("bx", "by")
BF = jnp.bfloat16
F32 = jnp.float32
EPS = 1e-05
GROUP = 2
VMEM_LIMIT = 40 * 1024 * 1024
SHIFT_LANE = 65


def face_spec(dim, index):
    shape = tuple(1 if d == dim else 16 for d in range(3)) + (64,)
    where = tuple(index if d == dim else 0 for d in range(4))
    return pl.BlockSpec(shape, lambda i: where)


def call(kernel, outs, args, scratch=(), faces=(), far_args=0, far_outs=0):
    vmem = pl.BlockSpec(memory_space=pltpu.VMEM)
    far = pl.BlockSpec(memory_space=pl.ANY)
    specs = list(faces) + [vmem] * (len(args) - 1 - len(faces) - far_args) + [far] * far_args
    args = [
        pltpu.with_memory_space_constraint(arg, pltpu.VMEM) if spec is vmem else arg
        for arg, spec in zip(args, [None] + specs)
    ]
    return pl.pallas_call(
        kernel,
        grid=(1,),
        out_shape=outs,
        in_specs=[pl.BlockSpec(memory_space=pltpu.SMEM)] + specs,
        out_specs=[vmem] * (len(outs) - far_outs) + [far] * far_outs,
        scratch_shapes=list(scratch),
        compiler_params=pltpu.CompilerParams(vmem_limit_bytes=VMEM_LIMIT),
    )(*args)


def in_hbm(array):
    return pltpu.with_memory_space_constraint(array, pltpu.HBM)


def like(shape, dtype):
    return jax.ShapeDtypeStruct(shape, dtype)


def keep(cond, value):
    return jnp.where(cond, value, jnp.zeros_like(value))


def bits(info):
    return info[0, 0], info[0, 1], info[0, 2], lax.axis_index("cz")


def start16(bit):
    return pl.multiple_of(bit * 16, 16)


def cell_rows(first, second, face, on):
    rows = []
    for r in range(4):
        for s in range(4):
            here = on & (first == r // 2) & (second == s // 2)
            rows.append(keep(here, face[r % 2][s % 2]))
    return jnp.concatenate(rows, axis=0)


def row_of(cells, p):
    return cells[p : p + 1]


Z_TILES, Y_TILES, X_TILES = 1, 2, 5


def message(tiles):
    return like((9 + tiles, 16, 128), BF)


def plane(tiles):
    return pltpu.VMEM((32 + tiles, 32, 64), BF)


def side_by_side(rows):
    half = rows.shape[0] // 2
    return jnp.concatenate([rows[:half], rows[half:]], axis=rows.ndim - 1)


def write_message(out, face, tiles, first, second, on):
    out[0:8] = side_by_side(face)
    for t, rows in enumerate(tiles):
        out[8 + t] = side_by_side(rows).astype(BF)
    row = lax.broadcasted_iota(jnp.int32, (16, 128), 0)
    here = jnp.where(on, 2 * first + second, 99)
    out[8 + len(tiles)] = jnp.where(row == here, 1.0, 0.0).astype(BF)


def open_message(ref, out):
    tiles = ref.shape[0] - 9
    face = jnp.concatenate([ref[0:8, :, :64], ref[0:8, :, 64:]], axis=0)
    flags = ref[8 + tiles].astype(F32)
    for q in range(4):
        here = jnp.broadcast_to(flags[q : q + 1, :64], (16, 64))[None]
        out[16 * (q // 2) : 16 * (q // 2) + 16, 16 * (q % 2) : 16 * (q % 2) + 16, :] = jnp.where(
            here > 0.5, face.astype(F32), 0.0
        ).astype(BF)
    for t in range(tiles):
        out[32 + t] = jnp.concatenate([ref[8 + t, :, :64], ref[8 + t, :, 64:]], axis=0)


def z_message(info, lat, out, pooled):
    px, py, pz, kz = bits(info)
    zsel = 15 * (1 - kz)
    pick = lax.broadcasted_iota(jnp.int32, (16, 16, 64), 1) == zsel
    sums = [[None, None], [None, None]]
    faces = []
    for y in range(16):
        slab = lat[:, y].astype(F32)
        faces.append(jnp.sum(jnp.where(pick, slab, 0.0), axis=1)[None])
        for a in range(2):
            part = jnp.sum(slab[8 * a : 8 * a + 8], axis=0)
            old = sums[a][y // 8]
            sums[a][y // 8] = part if old is None else old + part
    cells = []
    for a in range(2):
        for b in range(2):
            for c in range(2):
                cells.append(jnp.sum(sums[a][b][8 * c : 8 * c + 8], axis=0, keepdims=True))
    cells = jnp.concatenate(cells, axis=0) * (1.0 / math.sqrt(512.0))
    cells = cells.astype(BF).astype(F32)
    pooled[...] = jnp.concatenate([cells, jnp.zeros((8, 64), F32)], axis=0).astype(BF)
    on = pz == 1 - kz
    face = [
        [jnp.where(kz == 0, row_of(cells, 4 * a + 2 * b + 1), row_of(cells, 4 * a + 2 * b)) for a in range(2)]
        for b in range(2)
    ]
    rows = jnp.concatenate([cell_rows(py, px, face, on), jnp.zeros((16, 64), F32)], axis=0)
    write_message(out, jnp.concatenate(faces, axis=0).astype(BF), [rows], py, px, on)


def y_messages(info, low, high, rz_in, pooled, down, up, rz):
    px, py, pz, kz = bits(info)
    open_message(rz_in, rz)
    cells = pooled[...].astype(F32)
    halo = rz[32].astype(F32)
    for out, face, bit, line, q in ((down, low, 0, 0, 0), (up, high, 1, 31, 1)):
        on = py == bit
        picked = [[row_of(cells, 4 * a + 2 * q + c) for c in range(2)] for a in range(2)]
        tail = halo[12:16] if q else halo[0:4]
        rows = jnp.concatenate([cell_rows(px, pz, picked, on), tail, jnp.zeros((12, 64), F32)], axis=0)
        write_message(out, face[:, 0], [rz[line], rows], px, pz, on)


def x_messages(info, low, high, rz_in, rym_in, ryp_in, pooled, down, up, rz, rym, ryp):
    px, py, pz, kz = bits(info)
    for ref, out in ((rz_in, rz), (rym_in, rym), (ryp_in, ryp)):
        open_message(ref, out)
    cells = pooled[...].astype(F32)
    halo = rz[32].astype(F32)
    halo_m = rym[33].astype(F32)
    halo_p = ryp[33].astype(F32)
    line_m = rym[32].astype(F32)
    line_p = ryp[32].astype(F32)
    where16 = lax.broadcasted_iota(jnp.int32, (32, 16, 64), 1)
    for out, face, bit, line, q in ((down, low, 0, 0, 0), (up, high, 1, 31, 1)):
        on = px == bit
        slab = rz[0:32, 16 * q : 16 * q + 16, :].astype(F32)
        z_line = jnp.sum(jnp.where(where16 == 15 * q, slab, 0.0), axis=1).astype(BF)
        picked = [[row_of(cells, 4 * q + 2 * b + c) for c in range(2)] for b in range(2)]
        corners = [line_m[line : line + 1], line_p[line : line + 1], jnp.zeros((14, 64), F32)]
        corners = jnp.concatenate(corners + [cell_rows(py, pz, picked, on)], axis=0)
        c0 = 3 * q
        parts = [row_of(halo, 4 * cy + c0) for cy in range(4)]
        parts += [halo_m[4 * c0 : 4 * c0 + 4], halo_p[4 * c0 : 4 * c0 + 4]]
        parts += [row_of(halo_m, 16 + c0), row_of(halo_p, 16 + c0), jnp.zeros((18, 64), F32)]
        tiles = [z_line, rym[line], ryp[line], corners, jnp.concatenate(parts, axis=0)]
        write_message(out, face[0], tiles, py, pz, on)


def coarse_table():
    pooled, rz, rym, ryp, rxm, rxp = 0, 16, 32, 64, 96, 128
    table = np.zeros((16, 224, 160), np.float32)
    for combo in range(16):
        bit = ((combo >> 3) & 1, (combo >> 2) & 1, (combo >> 1) & 1)
        core = combo & 1
        for tap in range(27):
            off = (tap // 9, tap // 3 % 3, tap % 3)
            for p in range(8):
                at = (p // 4, p // 2 % 2, p % 2)
                pos = [2 * bit[d] - 1 + off[d] + at[d] for d in range(3)]
                x, y, z = pos
                out_z = z < 0 or z > 3
                if out_z and (z < 0) != (core == 1):
                    continue
                if x < 0 or x > 3:
                    base = rxm if x < 0 else rxp
                    if y < 0 or y > 3:
                        side = 0 if y < 0 else 1
                        row = 16 + (12 + side if out_z else 4 + 4 * side + z)
                    else:
                        row = 16 + y if out_z else 4 * y + z
                    row = base + row
                elif y < 0 or y > 3:
                    row = (rym if y < 0 else ryp) + (16 + x if out_z else 4 * x + z)
                elif out_z:
                    row = rz + 4 * y + x
                else:
                    own = [pos[d] - 2 * bit[d] for d in range(3)]
                    if min(own) < 0 or max(own) > 1:
                        continue
                    row = pooled + 4 * own[0] + 2 * own[1] + own[2]
                table[combo, 8 * tap + p, row] = 1.0
    return table


class Window:
    def __init__(self, info, rz, rym, ryp):
        px, py, pz, kz = bits(info)
        self.pz, self.rz, self.rym, self.ryp = pz, rz, rym, ryp
        self.z0 = pl.ds(start16(pz), 16)
        self.z1 = pl.ds(start16(1 - pz), 16)
        self.xs = pl.ds(start16(px), 16)
        self.ys = pl.ds(start16(py), 16)
        self.xlo, self.xhi, self.ylo, self.yhi = px == 0, px == 1, py == 0, py == 1
        self.on_low = (pz == 0) & (kz == 1)
        self.on_high = (pz == 1) & (kz == 0)
        self.row16 = lax.broadcasted_iota(jnp.int32, (16, 16, 64), 1)
        self.z_row = lax.broadcasted_iota(jnp.int32, (9, 16, 128), 1)

    def edge(self, block):
        return jnp.sum(jnp.where(self.row16[: block.shape[0]] == 15 * self.pz, block.astype(F32), 0.0), axis=1)

    def edge1(self, ref, i):
        return self.edge(ref[i : i + 1, self.z1, :])

    def low_of(self, e, h):
        return keep(self.pz == 1, e) + keep(self.on_low, h)

    def high_of(self, e, h):
        return keep(self.pz == 0, e) + keep(self.on_high, h)

    def offsets(self, evens, odds, first, last, zl, zh):
        left = jnp.concatenate([first[None], odds], axis=0)
        right = jnp.concatenate([evens, last[None]], axis=0)
        tile = jnp.concatenate([left, right], axis=2)
        wide = tile.astype(F32)
        down = jnp.where(self.z_row == 0, zl, pltpu.roll(wide, 1, 1)).astype(BF)
        up = jnp.where(self.z_row == 15, zh, pltpu.roll(wide, 15, 1)).astype(BF)
        return down, tile, up


def one(ref, i, j):
    return ref[i].astype(F32)[j : j + 1]


def interior(info, lat, rz_in, rym_in, ryp_in, taps, raw, scene, columns, weight, rz, rym, ryp):
    for ref, out in ((rz_in, rz), (rym_in, rym), (ryp_in, ryp)):
        open_message(ref, out)
    nought = jnp.zeros((64, 64), BF)
    for tap in range(9):
        ox, oz = tap // 3, tap % 3
        for a in range(4):
            left = nought if a == 3 else taps[9 * ox + 3 * a + oz]
            right = nought if a == 0 else taps[9 * ox + 3 * a - 3 + oz]
            weight[256 * tap + 64 * a : 256 * tap + 64 * a + 64] = jnp.concatenate([left, right], axis=1)
    w = Window(info, rz, rym, ryp)
    y_low = keep(w.ylo, rym[w.xs, w.z0, :])
    y_high = keep(w.yhi, ryp[w.xs, w.z0, :])
    e_low = keep(w.ylo, w.edge(rym[w.xs, w.z1, :]))
    e_high = keep(w.yhi, w.edge(ryp[w.xs, w.z1, :]))
    h_low = jnp.where(w.ylo, rym[32, w.xs, :], rz[15, w.xs, :]).astype(F32)
    h_high = jnp.where(w.yhi, ryp[32, w.xs, :], rz[16, w.xs, :]).astype(F32)
    h_mid = rz[w.ys, w.xs, :].astype(F32)

    def packed(of):
        rows = [of(e_low, h_low)] + [of(jnp.zeros((16, 64), F32), h_mid[y]) for y in range(16)]
        rows.append(of(e_high, h_high))
        return [jnp.concatenate([rows[2 * k], rows[2 * k + 1]], axis=1) for k in range(9)]

    below, above = packed(w.low_of), packed(w.high_of)
    inner = [None] * 3
    for x in range(16):
        zl = jnp.concatenate([below[k][x : x + 1][None] for k in range(9)], axis=0)
        zh = jnp.concatenate([above[k][x : x + 1][None] for k in range(9)], axis=0)
        planes = w.offsets(lat[x, :, 0], lat[x, :, 1], y_low[x], y_high[x], zl, zh)
        for oz, plane in enumerate(planes):
            scene[oz, x] = plane
            wide = plane.astype(F32)
            inner[oz] = wide if x == 0 else inner[oz] + wide
    for oz in range(3):
        columns[oz] = jnp.sum(inner[oz], axis=1)
    for first, count in ((1, 4), (5, 4), (9, 4), (13, 2)):
        pieces = []
        for tap in range(9):
            ox, oz = tap // 3, tap % 3
            for dk in range(2):
                at = first + ox - 1
                pieces.append(scene[oz, at : at + count, dk : dk + 8].reshape(128 * count, 128))
        value = jnp.dot(jnp.concatenate(pieces, axis=1), weight[...], preferred_element_type=F32)
        raw[(first - 1) * 128 : (first - 1 + count) * 128] = value


def forward(
    info, near_low, near_high, raw, columns, rz_in, rym_in, ryp_in, rxm_in, rxp_in, pooled, weight,
    coarse_weight, temb, time_weight, tables, act, ends, patch_out, stats,
    shift, table, arrived, rz, rym, ryp, rxm, rxp
):
    px, py, pz, kz = bits(info)
    fetch = pltpu.make_async_copy(tables.at[8 * px + 4 * py + 2 * pz + kz], table, arrived)
    fetch.start()
    for ref, out in ((rz_in, rz), (rym_in, rym), (ryp_in, ryp), (rxm_in, rxm), (rxp_in, rxp)):
        open_message(ref, out)
    w = Window(info, rz, rym, ryp)
    nought = jnp.zeros((16, 64), BF)

    def sides(rx, out, inner):
        first = jnp.where(
            out,
            jnp.where(w.ylo, rx[33, w.z0, :], rx[15, w.z0, :]),
            jnp.where(w.ylo, rym[inner, w.z0, :], nought),
        )
        last = jnp.where(
            out,
            jnp.where(w.yhi, rx[34, w.z0, :], rx[16, w.z0, :]),
            jnp.where(w.yhi, ryp[inner, w.z0, :], nought),
        )
        return first, last

    def side_columns(rx, out, inner, of):
        half = rz[w.ys, 0:16, :] if inner < 16 else rz[w.ys, 16:32, :]
        inner_h = jnp.sum(jnp.where(w.row16 == inner % 16, half.astype(F32), 0.0), axis=1)
        e_mid = keep(out, w.edge(rx[w.ys, w.z1, :]))
        hh = jnp.where(out, rx[32, w.ys, :].astype(F32), inner_h)
        e_first = jnp.where(
            out,
            jnp.where(w.ylo, w.edge1(rx, 33), w.edge1(rx, 15)),
            keep(w.ylo, w.edge1(rym, inner)),
        )
        h_first = jnp.where(
            out,
            jnp.where(w.ylo, one(rx, 35, 0), one(rx, 32, 15)),
            jnp.where(w.ylo, one(rym, 32, inner), one(rz, 15, inner)),
        )
        e_last = jnp.where(
            out,
            jnp.where(w.yhi, w.edge1(rx, 34), w.edge1(rx, 16)),
            keep(w.yhi, w.edge1(ryp, inner)),
        )
        h_last = jnp.where(
            out,
            jnp.where(w.yhi, one(rx, 35, 1), one(rx, 32, 16)),
            jnp.where(w.yhi, one(ryp, 32, inner), one(rz, 16, inner)),
        )
        mid = of(e_mid, hh)
        rows = [of(e_first, h_first)] + [mid[y : y + 1] for y in range(16)] + [of(e_last, h_last)]
        return [jnp.concatenate([rows[2 * k], rows[2 * k + 1]], axis=1)[None] for k in range(9)]

    for e, rx, out, inner in ((0, rxm, w.xlo, 15), (1, rxp, w.xhi, 16)):
        zl = jnp.concatenate(side_columns(rx, out, inner, w.low_of), axis=0)
        zh = jnp.concatenate(side_columns(rx, out, inner, w.high_of), axis=0)
        first, last = sides(rx, out, inner)
        plane = keep(out, rx[w.ys, w.z0, :]).reshape(8, 2, 16, 64)
        for oz, tile in enumerate(w.offsets(plane[:, 0], plane[:, 1], first, last, zl, zh)):
            ends[e, oz] = tile

    source = jnp.concatenate(
        [pooled[...], rz[32, 0:16, :], rym[33], ryp[33], rxm[35, 16:32, :], rxm[36, 0:16, :], rxp[35, 16:32, :], rxp[36, 0:16, :]],
        axis=0,
    )
    fetch.wait()
    taps = jnp.dot(table[...], source, preferred_element_type=F32)
    patch = jnp.concatenate([taps[8 * t : 8 * t + 8] for t in range(27)], axis=1)
    patch_out[...] = jnp.concatenate([patch, patch], axis=0).astype(BF)
    coarse = jnp.dot(patch_out[...], coarse_weight[...], preferred_element_type=F32)
    coarse = coarse.astype(BF).astype(F32)
    coarse = jnp.concatenate([coarse, coarse], axis=1)
    time_bias = lax.dot_general(
        jnp.broadcast_to(temb[...], (8, 256)),
        time_weight[...].astype(F32),
        (((1,), (1,)), ((), ())),
        preferred_element_type=F32,
        precision=lax.Precision.HIGHEST,
    )[:1]
    time_bias = jnp.concatenate([time_bias, time_bias], axis=1)
    z_half = lax.broadcasted_iota(jnp.int32, (16, 128), 0) < 8
    added = []
    for q in range(4):
        added.append(jnp.where(z_half, coarse[2 * q : 2 * q + 1], coarse[2 * q + 1 : 2 * q + 2]) + time_bias)

    pieces = []
    for tap in range(9):
        ox, oz = tap // 3, tap % 3
        low = ends[0, oz] if ox == 0 else near_low[oz, ox - 1]
        high = ends[1, oz] if ox == 2 else near_high[oz, ox]
        for dk in range(2):
            pieces.append(jnp.concatenate([low[dk : dk + 8], high[dk : dk + 8]], axis=0).reshape(256, 128))
    edges = jnp.dot(jnp.concatenate(pieces, axis=1), weight[...], preferred_element_type=F32)

    total = jnp.zeros((1, 128), F32)
    squares = jnp.zeros((1, 128), F32)
    for x in range(16):
        if x == 0:
            value = edges[:128]
        elif x == 15:
            value = edges[128:]
        else:
            value = raw[(x - 1) * 128 : x * 128]
        value = value.reshape(2, 4, 16, 128)
        a = x // 8
        value = jnp.concatenate([(value[b] + added[2 * a + b][None])[None] for b in range(2)], axis=0).reshape(128, 128)
        act[x * 128 : x * 128 + 128] = value
        total = total + jnp.sum(value, axis=0, keepdims=True)
        squares = squares + jnp.sum(value * value, axis=0, keepdims=True)
    shift[...] = jnp.zeros(shift.shape, F32)

    def place(tap, slot, value):
        row = SHIFT_LANE + 2 * (tap // 4 + slot)
        u = tap % 4
        shift[u // 2, row : row + 1, 64 * (u % 2) : 64 * (u % 2) + 64] = value

    for oz in range(3):
        inner = columns[oz]
        planes = (ends[0, oz], near_low[oz, 0], near_high[oz, 1], ends[1, oz])
        outer = [jnp.sum(plane.astype(F32), axis=1) for plane in planes]
        for ox, part in enumerate((inner + outer[0] - outer[2], inner, inner - outer[1] + outer[3])):
            all_columns = jnp.sum(part, axis=0, keepdims=True)
            whole = all_columns[:, :64] + all_columns[:, 64:]
            y0, y1 = part[0:1, :64], part[0:1, 64:]
            y16, y17 = part[8:9, :64], part[8:9, 64:]
            for oy, window in enumerate((whole - y16 - y17, whole - y0 - y17, whole - y0 - y1)):
                place(9 * ox + 3 * oy + oz, 0, window)
    for t in range(27):
        place(t, 7, 512.0 * jnp.sum(taps[8 * t : 8 * t + 8], axis=0, keepdims=True))

    lane = lax.broadcasted_iota(jnp.int32, (1, 128), 1)
    pairs = pair_sum(squares + pltpu.roll(squares, 64, 1))
    row = jnp.where(lane < 64, total + pltpu.roll(total, 64, 1), jnp.where(lane % 2 == 0, pairs, 0.0))
    for u in range(2):
        stats[128 * u : 128 * u + 128] = shift[u].T + row


def turn(info, scene, ends, turned):
    for oz in range(3):
        for xp in range(18):
            for dk in range(2):
                tile = scene[oz, xp - 1, dk : dk + 8] if 1 <= xp <= 16 else ends[xp // 17, oz, dk : dk + 8]
                turned[oz, 128 * dk : 128 * dk + 128, 128 * xp : 128 * xp + 128] = tile.reshape(128, 128).T


def pair_sum(row):
    lane = lax.broadcasted_iota(jnp.int32, row.shape, 1)
    return row + jnp.where(lane % 2 == 0, pltpu.roll(row, 127, 1), pltpu.roll(row, 1, 1))


def halves(row):
    lane = lax.broadcasted_iota(jnp.int32, row.shape, 1)
    other = pltpu.roll(row, 64, 1)
    return jnp.where(lane < 64, row, other), jnp.where(lane < 64, other, row)


def moments(gathered, count):
    row = jnp.sum(gathered[...], axis=0, keepdims=True)
    sums, upper = halves(row)
    lane = lax.broadcasted_iota(jnp.int32, row.shape, 1)
    squares = jnp.where(lane % 2 == 0, upper, pltpu.roll(upper, 1, 1))
    mean = pair_sum(sums) / count
    var = squares / count - mean * mean
    return row, sums, mean, 1.0 / jnp.sqrt(var + EPS)


def backward(voxels):
    count = float(voxels * GROUP)
    scale = 1.0 / (voxels * 64)

    def kernel(
        info, gathered, target, gain, bias, weight, weight_t, patch, stats, act_in, turned_in,
        predicted, payload, other, cotangent, act, turned, fetched, sent
    ):
        def chunk(n):
            rows = pl.ds(256 * n, 256)
            return pltpu.make_async_copy(act_in.at[rows], act.at[rows], fetched.at[n])

        whole = pltpu.make_async_copy(turned_in, turned, fetched.at[8])
        for n in range(8):
            chunk(n).start()
        whole.start()
        kz = lax.axis_index("cz")
        _, _, mean, rstd = moments(gathered, count)
        gains = jnp.zeros((1, 128), F32)
        biases = jnp.zeros((1, 128), F32)
        lost = jnp.zeros((1, 128), F32)
        outer = jnp.zeros((128, 128), F32)
        cells = [[None] * 4, [None] * 4]
        for x in range(0, 16, 2):
            rows = slice(x * 128, x * 128 + 256)
            chunk(x // 2).wait()
            normalized = (act[rows] - mean) * rstd
            shifted = normalized * gain[...] + bias[...]
            sigma = jax.nn.sigmoid(shifted)
            hidden = (shifted * sigma).astype(BF)
            output = jnp.dot(hidden, weight[...], preferred_element_type=F32)
            goal = jnp.concatenate([target[x : x + 2, :, 0], target[x : x + 2, :, 1]], axis=3)
            residue = output - goal.reshape(256, 128).astype(F32)
            shown = output.astype(BF).reshape(2, 8, 16, 128)
            predicted[x : x + 2, :, 0] = shown[..., :64]
            predicted[x : x + 2, :, 1] = shown[..., 64:]
            upstream = (2.0 * scale * residue).astype(BF)
            back = jnp.dot(upstream, weight_t[...], preferred_element_type=F32)
            value = back * sigma * (1.0 + shifted * (1.0 - sigma))
            gains = gains + jnp.sum(value * normalized, axis=0, keepdims=True)
            biases = biases + jnp.sum(value, axis=0, keepdims=True)
            lost = lost + jnp.sum(residue * residue, axis=0, keepdims=True)
            outer = outer + lax.dot_general(hidden, upstream, (((0,), (0,)), ((), ())), preferred_element_type=F32)
            value = value * (gain[...] * rstd)
            narrow = [value.astype(BF), normalized.astype(BF)]
            cotangent[rows, :128] = jnp.concatenate([part[:, :64] for part in narrow], axis=1)
            cotangent[rows, 128:] = jnp.concatenate([part[:, 64:] for part in narrow], axis=1)
            for part, wide in enumerate((value, normalized)):
                planes = wide.reshape(2, 2, 4, 16, 128)
                for b in range(2):
                    q = 2 * (x // 8) + b
                    cell = jnp.sum(planes[:, b], axis=(0, 1))
                    old = cells[part][q]
                    cells[part][q] = cell if old is None else old + cell

        def store(tap, slot, value):
            u = tap % 4
            half = jnp.where(kz == u // 2, 0, 1)
            payload.at[half][pl.ds(1024 * (u % 2) + slot + tap // 4, 64, stride=16), :] = value

        rows = []
        for q in range(4):
            for c in range(2):
                sums = [jnp.sum(cells[p][q][8 * c : 8 * c + 8], axis=0, keepdims=True) for p in range(2)]
                rows.append(jnp.concatenate([r[:, :64] + r[:, 64:] for r in sums], axis=1))
        rows = jnp.concatenate(rows, axis=0)
        high = rows.astype(BF)
        split = jnp.concatenate([high.astype(F32), rows - high.astype(F32)], axis=0).astype(BF)
        coarse = lax.dot_general(patch[...], split, (((0,), (0,)), ((), ())), preferred_element_type=F32)
        for t in range(27):
            store(t, 7, coarse[64 * t : 64 * t + 64])
        whole.wait()
        for ox in range(3):
            windows = turned[:, :, 128 * ox : 128 * ox + 2048].reshape(768, 2048)
            products = jnp.dot(windows, cotangent[...], preferred_element_type=F32)
            for oz in range(3):
                product = products[256 * oz : 256 * oz + 256]
                for oy in range(3):
                    value = product[64 * oy : 64 * oy + 64, :128] + product[64 * oy + 64 : 64 * oy + 128, 128:]
                    store(9 * ox + 3 * oy + oz, 0, value)
        nought = jnp.zeros((64, 64), F32)
        store(27, 0, jnp.concatenate([outer[:64, :64] + outer[64:, 64:], nought], axis=1))
        loss = jnp.broadcast_to(jnp.sum(lost, axis=1, keepdims=True), (64, 128))
        high = loss.astype(BF).astype(F32)
        lane = lax.broadcasted_iota(jnp.int32, (64, 128), 1)
        split = jnp.where(lane == 2 * kz, high, jnp.where(lane == 2 * kz + 1, loss - high, 0.0))
        store(27, 7, split)
        lane = lax.broadcasted_iota(jnp.int32, (1, 128), 1)
        row = jnp.where(lane < 64, gains + pltpu.roll(gains, 64, 1), biases + pltpu.roll(biases, 64, 1))
        wide = jnp.broadcast_to(row, (128, 128))
        for half in range(2):
            payload.at[half][pl.ds(14, 128, stride=16), :] = wide
            slot = jnp.where(kz == half, 0, 1)
            payload.at[slot][pl.ds(15, 128, stride=16), :] = stats[128 * half : 128 * half + 128]
        copy = pltpu.make_async_copy(payload.at[1], other, sent)
        copy.start()
        copy.wait()

    return kernel


def slopes(norms, gain, count):
    grad_gain, grad_bias = halves(norms)
    return pair_sum(gain * grad_bias) / count, pair_sum(gain * grad_gain) / count


def pair_add(voxels):
    total_count = float(voxels * GROUP)
    count = float(2 * 4096 * GROUP)

    def kernel(info, mine, other, gathered, gain, out):
        _, _, _, rstd = moments(gathered, total_count)
        total = (mine[0] + other[...]).reshape(-1, 16, 128)
        m1, m2 = slopes(total[0, 14:15], gain[...], count)
        row = lax.broadcasted_iota(jnp.int32, total.shape, 1)
        lane = lax.broadcasted_iota(jnp.int32, total.shape, 2)
        picked = (lane == SHIFT_LANE + 2 * row) & (row < 14)
        ones = jnp.sum(jnp.where(picked, total[:, 15:16], 0.0), axis=2, keepdims=True)
        centred = total - (m1 * rstd)[None] * ones - (m2 * rstd)[None] * pltpu.roll(total, 64, 2)
        total = jnp.where((lane < 64) & (row < 14), centred, total)
        lost = pltpu.roll(total - total.astype(BF).astype(F32), 1, 1)
        out[...] = jnp.where(row == 15, lost, total).astype(BF)

    return kernel


def combine(voxels):
    count = float(voxels * GROUP)
    pair_count = float(2 * 4096 * GROUP)

    def kernel(info, pieces, gathered, gain, temb, copies, grad_time, gain_out, bias_out):
        _, sums, mean, rstd = moments(gathered, count)
        value = pieces[...].astype(F32)
        chips = value.shape[0]
        seen = value[:, 14] + value[:, 15]
        norms = jnp.sum(seen, axis=0, keepdims=True)
        grad_gain, grad_bias = halves(norms)
        gain_out[...] = grad_gain[:, :64]
        bias_out[...] = grad_bias[:, :64]
        m1, m2 = slopes(norms, gain[...], count)
        centred = (sums - voxels * mean) * rstd
        act_sum = rstd * (gain[...] * grad_bias - voxels * m1 - m2 * centred)
        column = jnp.broadcast_to(act_sum, (128, 128)).T[:64]
        grad_time[...] = jnp.concatenate([column, column], axis=1) * temb[...]
        own1, own2 = slopes(seen, gain[...], pair_count)
        delta1, delta2 = (own1 - m1) * rstd, (own2 - m2) * rstd
        ones = gathered[0:chips] + gathered[chips : 2 * chips]
        back = lax.dot_general(
            ones, delta1, (((0,), (0,)), ((), ())), preferred_element_type=F32, precision=lax.Precision.HIGHEST
        )
        back = [back[SHIFT_LANE + 2 * r : SHIFT_LANE + 2 * r + 1] for r in range(14)]
        back = jnp.concatenate(back + [jnp.zeros((2, 128), F32)], axis=0)
        total = jnp.sum(value + delta2[:, None] * pltpu.roll(value, 64, 2), axis=0) + back
        lane = lax.broadcasted_iota(jnp.int32, (7, 128), 1)
        both = jnp.where(lane < 64, total[:7], pltpu.roll(total[7:14], 64, 1))
        lost = both[6:7] - both[6:7].astype(BF).astype(F32)
        piece = jnp.concatenate([both, lost], axis=0).astype(BF)
        copies[...] = jnp.broadcast_to(piece[None], copies.shape)

    return kernel


def spread(scale, info, near, far, conv, coarse, out, loss, rows):
    kz = lax.axis_index("cz")
    rows[pl.ds(pl.multiple_of(1024 * kz, 1024), 1024), :] = near[...].astype(F32).reshape(1024, 128)
    rows[pl.ds(pl.multiple_of(1024 * (1 - kz), 1024), 1024), :] = far[...].astype(F32).reshape(1024, 128)
    for tap in range(28):
        tile = rows[pl.ds(512 * (tap % 4) + tap // 4, 64, stride=8), :]
        if tap < 27:
            conv[tap] = tile[:, :64]
            coarse[tap] = tile[:, 64:]
        else:
            out[...] = tile[:, :64]
            parts = tile[0:1] + rows[2048 - 512 + 7 : 2048 - 512 + 8, :]
            lane = lax.broadcasted_iota(jnp.int32, (1, 128), 1)
            whole = jnp.sum(jnp.where((lane >= 64) & (lane < 68), parts, 0.0), axis=1, keepdims=True)
            loss[...] = whole * scale


def exchange(rows):
    out = lax.all_to_all(rows.reshape(rows.shape[0], 1, 128), ("cz",) + CHIPS, 0, 0, tiled=True)
    return out.reshape(rows.shape)


def neighbours(down, up, axis):
    ends = lax.axis_size(axis) - 1
    before = lax.ppermute(up, axis, [(i, i + 1) for i in range(ends)])
    after = lax.ppermute(down, axis, [(i + 1, i) for i in range(ends)])
    return before, after


def time_embedding(timestep, width):
    halfway = width // 2
    indices = jnp.arange(halfway).astype(F32)
    freqs = jnp.exp(indices * (-math.log(10000.0) / halfway))
    angles = timestep[0].astype(F32) * freqs
    return jnp.concatenate([jnp.sin(angles), jnp.cos(angles)])


def twice(row):
    return jnp.concatenate([row, row]).reshape(1, 128)


def diagonal(square):
    nought = jnp.zeros_like(square)
    return jnp.block([[square, nought], [nought, square]])


def shards(latents, target, block_coords, timestep, conv_weight, coarse_weight, out_weight, time_weight, norm_gain, norm_bias):
    devices = lax.axis_size("bx") * lax.axis_size("by") * lax.axis_size("cz")
    voxels = devices * 4096
    info = block_coords
    lat = latents[0]
    lat_pairs = lat.reshape(16, 8, 2, 16, 64)

    mz, pooled = call(z_message, [message(Z_TILES), like((16, 64), BF)], [in_hbm(info), lat])
    rz = lax.ppermute(mz, "cz", [(0, 1), (1, 0)])
    out = message(Y_TILES)
    down, up = call(
        y_messages, [out, out], [info, lat, lat, rz, pooled], [plane(Z_TILES)], [face_spec(1, 0), face_spec(1, 15)]
    )
    rym, ryp = neighbours(down, up, "by")
    out = message(X_TILES)
    planes = [plane(Z_TILES), plane(Y_TILES), plane(Y_TILES)]
    down, up = call(
        x_messages,
        [out, out],
        [info, lat, lat, rz, rym, ryp, pooled],
        planes,
        [face_spec(0, 0), face_spec(0, 15)],
    )
    rxm, rxp = neighbours(down, up, "bx")

    temb = time_embedding(timestep, time_weight.shape[0]).reshape(1, -1)
    raw, scene, columns, taps = call(
        interior,
        [like((1792, 128), F32), like((3, 16, 9, 16, 128), BF), like((3, 9, 128), F32), like((2304, 128), BF)],
        [info, lat_pairs, rz, rym, ryp, conv_weight],
        planes,
    )
    pair = (3, 2, 9, 16, 128)
    tables = jnp.asarray(coarse_table(), BF)
    act, ends, patch, stats = call(
        forward,
        [pltpu.HBM((2048, 128), F32), like((2, 3, 9, 16, 128), BF), like((16, 1728), BF), like((devices, 128), F32)],
        [info, scene, scene, raw, columns, rz, rym, ryp, rxm, rxp, pooled, taps]
        + [coarse_weight.reshape(1728, 64), temb, time_weight.T, tables],
        [pltpu.VMEM((2, 128, 128), F32), pltpu.VMEM((224, 160), BF), pltpu.SemaphoreType.DMA]
        + planes
        + [plane(X_TILES), plane(X_TILES)],
        [pl.BlockSpec(pair, lambda i: (0, 0, 0, 0, 0)), pl.BlockSpec(pair, lambda i: (0, 7, 0, 0, 0))],
        far_args=1,
    )
    first = exchange(stats)
    (turned,) = call(turn, [pltpu.HBM((3, 256, 18 * 128), BF)], [info, scene, ends])
    gain, bias = twice(norm_gain), twice(norm_bias)
    weights = [diagonal(out_weight), diagonal(out_weight.T)]
    predicted, payload, other = call(
        backward(voxels),
        [like((16, 8, 2, 16, 64), BF), like((2, 2048, 128), F32), like((2048, 128), F32)],
        [info, first, target.reshape(16, 8, 2, 16, 64), gain, bias] + weights + [patch, stats, in_hbm(act), in_hbm(turned)],
        [
            pltpu.VMEM((2048, 256), BF),
            pltpu.VMEM((2048, 128), F32),
            pltpu.VMEM((3, 256, 18 * 128), BF),
            pltpu.SemaphoreType.DMA((9,)),
            pltpu.SemaphoreType.DMA,
        ],
        far_args=2,
        far_outs=1,
    )
    swap = [(0, 1), (1, 0)]
    chips = devices // 2
    other = lax.ppermute(other, "cz", swap)
    (pieces,) = call(pair_add(voxels), [like((chips, 16, 128), BF)], [info, payload, other, first, gain])
    pieces = lax.all_to_all(pieces, CHIPS, 0, 0, tiled=True)
    copies, grad_time, grad_gain, grad_bias = call(
        combine(voxels),
        [like((chips, 8, 128), BF), like((64, 256), F32), like((1, 64), F32), like((1, 64), F32)],
        [info, pieces, first, gain, temb],
    )
    near = lax.all_to_all(copies, CHIPS, 0, 0, tiled=True)
    far = lax.ppermute(near, "cz", swap)
    grad_conv, grad_coarse, grad_out, loss = call(
        functools.partial(spread, 1.0 / (voxels * 64)),
        [like((27, 64, 64), F32), like((27, 64, 64), F32), like((64, 64), F32), like((1, 1), F32)],
        [info, near, far],
        [pltpu.VMEM((2048, 128), F32)],
    )
    return (
        predicted.reshape(latents.shape),
        loss.reshape(1),
        grad_conv,
        grad_coarse,
        grad_out,
        grad_time.T,
        grad_gain.reshape(64),
        grad_bias.reshape(64),
    )


def solution(mesh):
    blocks = P(ALL, None, None, None, None)
    return jax.shard_map(
        shards,
        mesh=mesh,
        in_specs=(blocks, blocks, P(ALL, None)) + (P(),) * 7,
        out_specs=(blocks,) + (P(),) * 7,
        check_vma=False,
    )
```

```python
import functools
import math

import jax
import jax.numpy as jnp
import numpy as np
from jax import lax
from jax.experimental import pallas as pl
from jax.experimental.pallas import tpu as pltpu
from jax.sharding import PartitionSpec as P

ALL = ("bx", "by", "cz")
CHIPS = ("bx", "by")
BF = jnp.bfloat16
F32 = jnp.float32
EPS = 1e-05
GROUP = 2
VMEM_LIMIT = 40 * 1024 * 1024
SHIFT_LANE = 65


def face_spec(dim, index):
    shape = tuple(1 if d == dim else 16 for d in range(3)) + (64,)
    where = tuple(index if d == dim else 0 for d in range(4))
    return pl.BlockSpec(shape, lambda i: where)


def call(kernel, outs, args, scratch=(), faces=(), far_args=0, far_outs=0):
    vmem = pl.BlockSpec(memory_space=pltpu.VMEM)
    far = pl.BlockSpec(memory_space=pl.ANY)
    specs = list(faces) + [vmem] * (len(args) - 1 - len(faces) - far_args) + [far] * far_args
    args = [
        pltpu.with_memory_space_constraint(arg, pltpu.VMEM) if spec is vmem else arg
        for arg, spec in zip(args, [None] + specs)
    ]
    return pl.pallas_call(
        kernel,
        grid=(1,),
        out_shape=outs,
        in_specs=[pl.BlockSpec(memory_space=pltpu.SMEM)] + specs,
        out_specs=[vmem] * (len(outs) - far_outs) + [far] * far_outs,
        scratch_shapes=list(scratch),
        compiler_params=pltpu.CompilerParams(vmem_limit_bytes=VMEM_LIMIT),
    )(*args)


def in_hbm(array):
    return pltpu.with_memory_space_constraint(array, pltpu.HBM)


def like(shape, dtype):
    return jax.ShapeDtypeStruct(shape, dtype)


def keep(cond, value):
    return jnp.where(cond, value, jnp.zeros_like(value))


def bits(info):
    return info[0, 0], info[0, 1], info[0, 2], lax.axis_index("cz")


def start16(bit):
    return pl.multiple_of(bit * 16, 16)


def cell_rows(first, second, face, on):
    rows = []
    for r in range(4):
        for s in range(4):
            here = on & (first == r // 2) & (second == s // 2)
            rows.append(keep(here, face[r % 2][s % 2]))
    return jnp.concatenate(rows, axis=0)


def row_of(cells, p):
    return cells[p : p + 1]


Z_TILES, Y_TILES, X_TILES = 1, 2, 5


def message(tiles):
    return like((9 + tiles, 16, 128), BF)


def plane(tiles):
    return pltpu.VMEM((32 + tiles, 32, 64), BF)


def side_by_side(rows):
    half = rows.shape[0] // 2
    return jnp.concatenate([rows[:half], rows[half:]], axis=rows.ndim - 1)


def write_message(out, face, tiles, first, second, on):
    out[0:8] = side_by_side(face)
    for t, rows in enumerate(tiles):
        out[8 + t] = side_by_side(rows).astype(BF)
    row = lax.broadcasted_iota(jnp.int32, (16, 128), 0)
    here = jnp.where(on, 2 * first + second, 99)
    out[8 + len(tiles)] = jnp.where(row == here, 1.0, 0.0).astype(BF)


def open_message(ref, out):
    tiles = ref.shape[0] - 9
    face = jnp.concatenate([ref[0:8, :, :64], ref[0:8, :, 64:]], axis=0)
    flags = ref[8 + tiles].astype(F32)
    for q in range(4):
        here = jnp.broadcast_to(flags[q : q + 1, :64], (16, 64))[None]
        out[16 * (q // 2) : 16 * (q // 2) + 16, 16 * (q % 2) : 16 * (q % 2) + 16, :] = jnp.where(
            here > 0.5, face.astype(F32), 0.0
        ).astype(BF)
    for t in range(tiles):
        out[32 + t] = jnp.concatenate([ref[8 + t, :, :64], ref[8 + t, :, 64:]], axis=0)


def z_message(info, lat, out, pooled):
    px, py, pz, kz = bits(info)
    zsel = 15 * (1 - kz)
    pick = lax.broadcasted_iota(jnp.int32, (16, 16, 64), 1) == zsel
    sums = [[None, None], [None, None]]
    faces = []
    for y in range(16):
        slab = lat[:, y].astype(F32)
        faces.append(jnp.sum(jnp.where(pick, slab, 0.0), axis=1)[None])
        for a in range(2):
            part = jnp.sum(slab[8 * a : 8 * a + 8], axis=0)
            old = sums[a][y // 8]
            sums[a][y // 8] = part if old is None else old + part
    cells = []
    for a in range(2):
        for b in range(2):
            for c in range(2):
                cells.append(jnp.sum(sums[a][b][8 * c : 8 * c + 8], axis=0, keepdims=True))
    cells = jnp.concatenate(cells, axis=0) * (1.0 / math.sqrt(512.0))
    cells = cells.astype(BF).astype(F32)
    pooled[...] = jnp.concatenate([cells, jnp.zeros((8, 64), F32)], axis=0).astype(BF)
    on = pz == 1 - kz
    face = [
        [jnp.where(kz == 0, row_of(cells, 4 * a + 2 * b + 1), row_of(cells, 4 * a + 2 * b)) for a in range(2)]
        for b in range(2)
    ]
    rows = jnp.concatenate([cell_rows(py, px, face, on), jnp.zeros((16, 64), F32)], axis=0)
    write_message(out, jnp.concatenate(faces, axis=0).astype(BF), [rows], py, px, on)


def y_messages(info, low, high, rz_in, pooled, down, up, rz):
    px, py, pz, kz = bits(info)
    open_message(rz_in, rz)
    cells = pooled[...].astype(F32)
    halo = rz[32].astype(F32)
    for out, face, bit, line, q in ((down, low, 0, 0, 0), (up, high, 1, 31, 1)):
        on = py == bit
        picked = [[row_of(cells, 4 * a + 2 * q + c) for c in range(2)] for a in range(2)]
        tail = halo[12:16] if q else halo[0:4]
        rows = jnp.concatenate([cell_rows(px, pz, picked, on), tail, jnp.zeros((12, 64), F32)], axis=0)
        write_message(out, face[:, 0], [rz[line], rows], px, pz, on)


def x_messages(info, low, high, rz_in, rym_in, ryp_in, pooled, down, up, rz, rym, ryp):
    px, py, pz, kz = bits(info)
    for ref, out in ((rz_in, rz), (rym_in, rym), (ryp_in, ryp)):
        open_message(ref, out)
    cells = pooled[...].astype(F32)
    halo = rz[32].astype(F32)
    halo_m = rym[33].astype(F32)
    halo_p = ryp[33].astype(F32)
    line_m = rym[32].astype(F32)
    line_p = ryp[32].astype(F32)
    where16 = lax.broadcasted_iota(jnp.int32, (32, 16, 64), 1)
    for out, face, bit, line, q in ((down, low, 0, 0, 0), (up, high, 1, 31, 1)):
        on = px == bit
        slab = rz[0:32, 16 * q : 16 * q + 16, :].astype(F32)
        z_line = jnp.sum(jnp.where(where16 == 15 * q, slab, 0.0), axis=1).astype(BF)
        picked = [[row_of(cells, 4 * q + 2 * b + c) for c in range(2)] for b in range(2)]
        corners = [line_m[line : line + 1], line_p[line : line + 1], jnp.zeros((14, 64), F32)]
        corners = jnp.concatenate(corners + [cell_rows(py, pz, picked, on)], axis=0)
        c0 = 3 * q
        parts = [row_of(halo, 4 * cy + c0) for cy in range(4)]
        parts += [halo_m[4 * c0 : 4 * c0 + 4], halo_p[4 * c0 : 4 * c0 + 4]]
        parts += [row_of(halo_m, 16 + c0), row_of(halo_p, 16 + c0), jnp.zeros((18, 64), F32)]
        tiles = [z_line, rym[line], ryp[line], corners, jnp.concatenate(parts, axis=0)]
        write_message(out, face[0], tiles, py, pz, on)


def coarse_table():
    pooled, rz, rym, ryp, rxm, rxp = 0, 16, 32, 64, 96, 128
    table = np.zeros((16, 224, 160), np.float32)
    for combo in range(16):
        bit = ((combo >> 3) & 1, (combo >> 2) & 1, (combo >> 1) & 1)
        core = combo & 1
        for tap in range(27):
            off = (tap // 9, tap // 3 % 3, tap % 3)
            for p in range(8):
                at = (p // 4, p // 2 % 2, p % 2)
                pos = [2 * bit[d] - 1 + off[d] + at[d] for d in range(3)]
                x, y, z = pos
                out_z = z < 0 or z > 3
                if out_z and (z < 0) != (core == 1):
                    continue
                if x < 0 or x > 3:
                    base = rxm if x < 0 else rxp
                    if y < 0 or y > 3:
                        side = 0 if y < 0 else 1
                        row = 16 + (12 + side if out_z else 4 + 4 * side + z)
                    else:
                        row = 16 + y if out_z else 4 * y + z
                    row = base + row
                elif y < 0 or y > 3:
                    row = (rym if y < 0 else ryp) + (16 + x if out_z else 4 * x + z)
                elif out_z:
                    row = rz + 4 * y + x
                else:
                    own = [pos[d] - 2 * bit[d] for d in range(3)]
                    if min(own) < 0 or max(own) > 1:
                        continue
                    row = pooled + 4 * own[0] + 2 * own[1] + own[2]
                table[combo, 8 * tap + p, row] = 1.0
    return table


class Window:
    def __init__(self, info, rz, rym, ryp):
        px, py, pz, kz = bits(info)
        self.pz, self.rz, self.rym, self.ryp = pz, rz, rym, ryp
        self.z0 = pl.ds(start16(pz), 16)
        self.z1 = pl.ds(start16(1 - pz), 16)
        self.xs = pl.ds(start16(px), 16)
        self.ys = pl.ds(start16(py), 16)
        self.xlo, self.xhi, self.ylo, self.yhi = px == 0, px == 1, py == 0, py == 1
        self.on_low = (pz == 0) & (kz == 1)
        self.on_high = (pz == 1) & (kz == 0)
        self.row16 = lax.broadcasted_iota(jnp.int32, (16, 16, 64), 1)
        self.z_row = lax.broadcasted_iota(jnp.int32, (9, 16, 128), 1)

    def edge(self, block):
        return jnp.sum(jnp.where(self.row16[: block.shape[0]] == 15 * self.pz, block.astype(F32), 0.0), axis=1)

    def edge1(self, ref, i):
        return self.edge(ref[i : i + 1, self.z1, :])

    def low_of(self, e, h):
        return keep(self.pz == 1, e) + keep(self.on_low, h)

    def high_of(self, e, h):
        return keep(self.pz == 0, e) + keep(self.on_high, h)

    def offsets(self, evens, odds, first, last, zl, zh):
        left = jnp.concatenate([first[None], odds], axis=0)
        right = jnp.concatenate([evens, last[None]], axis=0)
        tile = jnp.concatenate([left, right], axis=2)
        wide = tile.astype(F32)
        down = jnp.where(self.z_row == 0, zl, pltpu.roll(wide, 1, 1)).astype(BF)
        up = jnp.where(self.z_row == 15, zh, pltpu.roll(wide, 15, 1)).astype(BF)
        return down, tile, up


def one(ref, i, j):
    return ref[i].astype(F32)[j : j + 1]


def interior(info, lat, rz_in, rym_in, ryp_in, taps, raw, scene, columns, weight, rz, rym, ryp):
    for ref, out in ((rz_in, rz), (rym_in, rym), (ryp_in, ryp)):
        open_message(ref, out)
    nought = jnp.zeros((64, 64), BF)
    for tap in range(9):
        ox, oz = tap // 3, tap % 3
        for a in range(4):
            left = nought if a == 3 else taps[9 * ox + 3 * a + oz]
            right = nought if a == 0 else taps[9 * ox + 3 * a - 3 + oz]
            weight[256 * tap + 64 * a : 256 * tap + 64 * a + 64] = jnp.concatenate([left, right], axis=1)
    w = Window(info, rz, rym, ryp)
    y_low = keep(w.ylo, rym[w.xs, w.z0, :])
    y_high = keep(w.yhi, ryp[w.xs, w.z0, :])
    e_low = keep(w.ylo, w.edge(rym[w.xs, w.z1, :]))
    e_high = keep(w.yhi, w.edge(ryp[w.xs, w.z1, :]))
    h_low = jnp.where(w.ylo, rym[32, w.xs, :], rz[15, w.xs, :]).astype(F32)
    h_high = jnp.where(w.yhi, ryp[32, w.xs, :], rz[16, w.xs, :]).astype(F32)
    h_mid = rz[w.ys, w.xs, :].astype(F32)

    def packed(of):
        rows = [of(e_low, h_low)] + [of(jnp.zeros((16, 64), F32), h_mid[y]) for y in range(16)]
        rows.append(of(e_high, h_high))
        return [jnp.concatenate([rows[2 * k], rows[2 * k + 1]], axis=1) for k in range(9)]

    below, above = packed(w.low_of), packed(w.high_of)
    inner = [None] * 3
    for x in range(16):
        zl = jnp.concatenate([below[k][x : x + 1][None] for k in range(9)], axis=0)
        zh = jnp.concatenate([above[k][x : x + 1][None] for k in range(9)], axis=0)
        planes = w.offsets(lat[x, :, 0], lat[x, :, 1], y_low[x], y_high[x], zl, zh)
        for oz, plane in enumerate(planes):
            scene[oz, x] = plane
            wide = plane.astype(F32)
            inner[oz] = wide if x == 0 else inner[oz] + wide
    for oz in range(3):
        columns[oz] = jnp.sum(inner[oz], axis=1)
    for first, count in ((1, 4), (5, 4), (9, 4), (13, 2)):
        pieces = []
        for tap in range(9):
            ox, oz = tap // 3, tap % 3
            for dk in range(2):
                at = first + ox - 1
                pieces.append(scene[oz, at : at + count, dk : dk + 8].reshape(128 * count, 128))
        value = jnp.dot(jnp.concatenate(pieces, axis=1), weight[...], preferred_element_type=F32)
        raw[(first - 1) * 128 : (first - 1 + count) * 128] = value


def forward(
    info, near_low, near_high, raw, columns, rz_in, rym_in, ryp_in, rxm_in, rxp_in, pooled, weight,
    coarse_weight, temb, time_weight, tables, ends, patch_out, stats, act_out,
    act, sent, shift, table, arrived, rz, rym, ryp, rxm, rxp
):
    px, py, pz, kz = bits(info)
    fetch = pltpu.make_async_copy(tables.at[8 * px + 4 * py + 2 * pz + kz], table, arrived)
    fetch.start()
    for ref, out in ((rz_in, rz), (rym_in, rym), (ryp_in, ryp), (rxm_in, rxm), (rxp_in, rxp)):
        open_message(ref, out)
    w = Window(info, rz, rym, ryp)
    nought = jnp.zeros((16, 64), BF)

    def sides(rx, out, inner):
        first = jnp.where(
            out,
            jnp.where(w.ylo, rx[33, w.z0, :], rx[15, w.z0, :]),
            jnp.where(w.ylo, rym[inner, w.z0, :], nought),
        )
        last = jnp.where(
            out,
            jnp.where(w.yhi, rx[34, w.z0, :], rx[16, w.z0, :]),
            jnp.where(w.yhi, ryp[inner, w.z0, :], nought),
        )
        return first, last

    def side_columns(rx, out, inner, of):
        half = rz[w.ys, 0:16, :] if inner < 16 else rz[w.ys, 16:32, :]
        inner_h = jnp.sum(jnp.where(w.row16 == inner % 16, half.astype(F32), 0.0), axis=1)
        e_mid = keep(out, w.edge(rx[w.ys, w.z1, :]))
        hh = jnp.where(out, rx[32, w.ys, :].astype(F32), inner_h)
        e_first = jnp.where(
            out,
            jnp.where(w.ylo, w.edge1(rx, 33), w.edge1(rx, 15)),
            keep(w.ylo, w.edge1(rym, inner)),
        )
        h_first = jnp.where(
            out,
            jnp.where(w.ylo, one(rx, 35, 0), one(rx, 32, 15)),
            jnp.where(w.ylo, one(rym, 32, inner), one(rz, 15, inner)),
        )
        e_last = jnp.where(
            out,
            jnp.where(w.yhi, w.edge1(rx, 34), w.edge1(rx, 16)),
            keep(w.yhi, w.edge1(ryp, inner)),
        )
        h_last = jnp.where(
            out,
            jnp.where(w.yhi, one(rx, 35, 1), one(rx, 32, 16)),
            jnp.where(w.yhi, one(ryp, 32, inner), one(rz, 16, inner)),
        )
        mid = of(e_mid, hh)
        rows = [of(e_first, h_first)] + [mid[y : y + 1] for y in range(16)] + [of(e_last, h_last)]
        return [jnp.concatenate([rows[2 * k], rows[2 * k + 1]], axis=1)[None] for k in range(9)]

    for e, rx, out, inner in ((0, rxm, w.xlo, 15), (1, rxp, w.xhi, 16)):
        zl = jnp.concatenate(side_columns(rx, out, inner, w.low_of), axis=0)
        zh = jnp.concatenate(side_columns(rx, out, inner, w.high_of), axis=0)
        first, last = sides(rx, out, inner)
        plane = keep(out, rx[w.ys, w.z0, :]).reshape(8, 2, 16, 64)
        for oz, tile in enumerate(w.offsets(plane[:, 0], plane[:, 1], first, last, zl, zh)):
            ends[e, oz] = tile

    source = jnp.concatenate(
        [pooled[...], rz[32, 0:16, :], rym[33], ryp[33], rxm[35, 16:32, :], rxm[36, 0:16, :], rxp[35, 16:32, :], rxp[36, 0:16, :]],
        axis=0,
    )
    fetch.wait()
    taps = jnp.dot(table[...], source, preferred_element_type=F32)
    patch = jnp.concatenate([taps[8 * t : 8 * t + 8] for t in range(27)], axis=1)
    patch_out[...] = jnp.concatenate([patch, patch], axis=0).astype(BF)
    coarse = jnp.dot(patch_out[...], coarse_weight[...], preferred_element_type=F32)
    coarse = coarse.astype(BF).astype(F32)
    coarse = jnp.concatenate([coarse, coarse], axis=1)
    time_bias = lax.dot_general(
        jnp.broadcast_to(temb[...], (8, 256)),
        time_weight[...].astype(F32),
        (((1,), (1,)), ((), ())),
        preferred_element_type=F32,
        precision=lax.Precision.HIGHEST,
    )[:1]
    time_bias = jnp.concatenate([time_bias, time_bias], axis=1)
    z_half = lax.broadcasted_iota(jnp.int32, (16, 128), 0) < 8
    added = []
    for q in range(4):
        added.append(jnp.where(z_half, coarse[2 * q : 2 * q + 1], coarse[2 * q + 1 : 2 * q + 2]) + time_bias)

    pieces = []
    for tap in range(9):
        ox, oz = tap // 3, tap % 3
        low = ends[0, oz] if ox == 0 else near_low[oz, ox - 1]
        high = ends[1, oz] if ox == 2 else near_high[oz, ox]
        for dk in range(2):
            pieces.append(jnp.concatenate([low[dk : dk + 8], high[dk : dk + 8]], axis=0).reshape(256, 128))
    edges = jnp.dot(jnp.concatenate(pieces, axis=1), weight[...], preferred_element_type=F32)

    def leave(n):
        rows = pl.ds(512 * n, 512)
        return pltpu.make_async_copy(act.at[rows], act_out.at[rows], sent.at[n])

    total = jnp.zeros((1, 128), F32)
    squares = jnp.zeros((1, 128), F32)
    for x in range(16):
        if x == 0:
            value = edges[:128]
        elif x == 15:
            value = edges[128:]
        else:
            value = raw[(x - 1) * 128 : x * 128]
        value = value.reshape(2, 4, 16, 128)
        a = x // 8
        value = jnp.concatenate([(value[b] + added[2 * a + b][None])[None] for b in range(2)], axis=0).reshape(128, 128)
        act[x * 128 : x * 128 + 128] = value
        if x % 4 == 3:
            leave(x // 4).start()
        total = total + jnp.sum(value, axis=0, keepdims=True)
        squares = squares + jnp.sum(value * value, axis=0, keepdims=True)
    shift[...] = jnp.zeros(shift.shape, F32)

    def place(tap, slot, value):
        row = SHIFT_LANE + 2 * (tap // 4 + slot)
        u = tap % 4
        shift[u // 2, row : row + 1, 64 * (u % 2) : 64 * (u % 2) + 64] = value

    for oz in range(3):
        inner = columns[oz]
        planes = (ends[0, oz], near_low[oz, 0], near_high[oz, 1], ends[1, oz])
        outer = [jnp.sum(plane.astype(F32), axis=1) for plane in planes]
        for ox, part in enumerate((inner + outer[0] - outer[2], inner, inner - outer[1] + outer[3])):
            all_columns = jnp.sum(part, axis=0, keepdims=True)
            whole = all_columns[:, :64] + all_columns[:, 64:]
            y0, y1 = part[0:1, :64], part[0:1, 64:]
            y16, y17 = part[8:9, :64], part[8:9, 64:]
            for oy, window in enumerate((whole - y16 - y17, whole - y0 - y17, whole - y0 - y1)):
                place(9 * ox + 3 * oy + oz, 0, window)
    for t in range(27):
        place(t, 7, 512.0 * jnp.sum(taps[8 * t : 8 * t + 8], axis=0, keepdims=True))

    lane = lax.broadcasted_iota(jnp.int32, (1, 128), 1)
    pairs = pair_sum(squares + pltpu.roll(squares, 64, 1))
    row = jnp.where(lane < 64, total + pltpu.roll(total, 64, 1), jnp.where(lane % 2 == 0, pairs, 0.0))
    for u in range(2):
        stats[128 * u : 128 * u + 128] = shift[u].T + row
    for n in range(4):
        leave(n).wait()


def turn(info, scene, ends, turned_out, turned, sent):
    for oz in range(3):
        for xp in range(18):
            for dk in range(2):
                tile = scene[oz, xp - 1, dk : dk + 8] if 1 <= xp <= 16 else ends[xp // 17, oz, dk : dk + 8]
                turned[oz, 128 * dk : 128 * dk + 128, 128 * xp : 128 * xp + 128] = tile.reshape(128, 128).T
        pltpu.make_async_copy(turned.at[oz], turned_out.at[oz], sent.at[oz]).start()
    for oz in range(3):
        pltpu.make_async_copy(turned.at[oz], turned_out.at[oz], sent.at[oz]).wait()


def pair_sum(row):
    lane = lax.broadcasted_iota(jnp.int32, row.shape, 1)
    return row + jnp.where(lane % 2 == 0, pltpu.roll(row, 127, 1), pltpu.roll(row, 1, 1))


def halves(row):
    lane = lax.broadcasted_iota(jnp.int32, row.shape, 1)
    other = pltpu.roll(row, 64, 1)
    return jnp.where(lane < 64, row, other), jnp.where(lane < 64, other, row)


def moments(gathered, count):
    row = jnp.sum(gathered[...], axis=0, keepdims=True)
    sums, upper = halves(row)
    lane = lax.broadcasted_iota(jnp.int32, row.shape, 1)
    squares = jnp.where(lane % 2 == 0, upper, pltpu.roll(upper, 1, 1))
    mean = pair_sum(sums) / count
    var = squares / count - mean * mean
    return row, sums, mean, 1.0 / jnp.sqrt(var + EPS)


def backward(voxels):
    count = float(voxels * GROUP)
    scale = 1.0 / (voxels * 64)

    def kernel(
        info, gathered, target, gain, bias, weight, weight_t, patch, stats, act_in, turned_in,
        payload, other, predicted_out, cotangent, act, turned, predicted, fetched, sent, shown_sent
    ):
        def chunk(n):
            rows = pl.ds(256 * n, 256)
            return pltpu.make_async_copy(act_in.at[rows], act.at[rows], fetched.at[n])

        def show(x):
            part = pl.ds(x, 2)
            return pltpu.make_async_copy(predicted.at[part], predicted_out.at[part], shown_sent.at[x // 2])

        whole = pltpu.make_async_copy(turned_in, turned, fetched.at[8])
        for n in range(8):
            chunk(n).start()
        kz = lax.axis_index("cz")
        _, _, mean, rstd = moments(gathered, count)
        gains = jnp.zeros((1, 128), F32)
        biases = jnp.zeros((1, 128), F32)
        lost = jnp.zeros((1, 128), F32)
        outer = jnp.zeros((128, 128), F32)
        cells = [[None] * 4, [None] * 4]
        for x in range(0, 16, 2):
            rows = slice(x * 128, x * 128 + 256)
            chunk(x // 2).wait()
            if x == 4:
                whole.start()
            normalized = (act[rows] - mean) * rstd
            shifted = normalized * gain[...] + bias[...]
            sigma = jax.nn.sigmoid(shifted)
            hidden = (shifted * sigma).astype(BF)
            output = jnp.dot(hidden, weight[...], preferred_element_type=F32)
            goal = jnp.concatenate([target[x : x + 2, :, 0], target[x : x + 2, :, 1]], axis=3)
            residue = output - goal.reshape(256, 128).astype(F32)
            shown = output.astype(BF).reshape(2, 8, 16, 128)
            predicted[x : x + 2, :, 0] = shown[..., :64]
            predicted[x : x + 2, :, 1] = shown[..., 64:]
            show(x).start()
            upstream = (2.0 * scale * residue).astype(BF)
            back = jnp.dot(upstream, weight_t[...], preferred_element_type=F32)
            value = back * sigma * (1.0 + shifted * (1.0 - sigma))
            gains = gains + jnp.sum(value * normalized, axis=0, keepdims=True)
            biases = biases + jnp.sum(value, axis=0, keepdims=True)
            lost = lost + jnp.sum(residue * residue, axis=0, keepdims=True)
            outer = outer + lax.dot_general(hidden, upstream, (((0,), (0,)), ((), ())), preferred_element_type=F32)
            value = value * (gain[...] * rstd)
            narrow = [value.astype(BF), normalized.astype(BF)]
            cotangent[rows, :128] = jnp.concatenate([part[:, :64] for part in narrow], axis=1)
            cotangent[rows, 128:] = jnp.concatenate([part[:, 64:] for part in narrow], axis=1)
            for part, wide in enumerate((value, normalized)):
                planes = wide.reshape(2, 2, 4, 16, 128)
                for b in range(2):
                    q = 2 * (x // 8) + b
                    cell = jnp.sum(planes[:, b], axis=(0, 1))
                    old = cells[part][q]
                    cells[part][q] = cell if old is None else old + cell

        def store(tap, slot, value):
            u = tap % 4
            half = jnp.where(kz == u // 2, 0, 1)
            payload.at[half][pl.ds(1024 * (u % 2) + slot + tap // 4, 64, stride=16), :] = value

        rows = []
        for q in range(4):
            for c in range(2):
                sums = [jnp.sum(cells[p][q][8 * c : 8 * c + 8], axis=0, keepdims=True) for p in range(2)]
                rows.append(jnp.concatenate([r[:, :64] + r[:, 64:] for r in sums], axis=1))
        rows = jnp.concatenate(rows, axis=0)
        high = rows.astype(BF)
        split = jnp.concatenate([high.astype(F32), rows - high.astype(F32)], axis=0).astype(BF)
        coarse = lax.dot_general(patch[...], split, (((0,), (0,)), ((), ())), preferred_element_type=F32)
        for t in range(27):
            store(t, 7, coarse[64 * t : 64 * t + 64])
        whole.wait()
        for ox in range(3):
            windows = turned[:, :, 128 * ox : 128 * ox + 2048].reshape(768, 2048)
            products = jnp.dot(windows, cotangent[...], preferred_element_type=F32)
            for oz in range(3):
                product = products[256 * oz : 256 * oz + 256]
                for oy in range(3):
                    value = product[64 * oy : 64 * oy + 64, :128] + product[64 * oy + 64 : 64 * oy + 128, 128:]
                    store(9 * ox + 3 * oy + oz, 0, value)
        nought = jnp.zeros((64, 64), F32)
        store(27, 0, jnp.concatenate([outer[:64, :64] + outer[64:, 64:], nought], axis=1))
        loss = jnp.broadcast_to(jnp.sum(lost, axis=1, keepdims=True), (64, 128))
        high = loss.astype(BF).astype(F32)
        lane = lax.broadcasted_iota(jnp.int32, (64, 128), 1)
        split = jnp.where(lane == 2 * kz, high, jnp.where(lane == 2 * kz + 1, loss - high, 0.0))
        store(27, 7, split)
        lane = lax.broadcasted_iota(jnp.int32, (1, 128), 1)
        row = jnp.where(lane < 64, gains + pltpu.roll(gains, 64, 1), biases + pltpu.roll(biases, 64, 1))
        wide = jnp.broadcast_to(row, (128, 128))
        for half in range(2):
            payload.at[half][pl.ds(14, 128, stride=16), :] = wide
            slot = jnp.where(kz == half, 0, 1)
            payload.at[slot][pl.ds(15, 128, stride=16), :] = stats[128 * half : 128 * half + 128]
        copy = pltpu.make_async_copy(payload.at[1], other, sent)
        copy.start()
        for x in range(0, 16, 2):
            show(x).wait()
        copy.wait()

    return kernel


def slopes(norms, gain, count):
    grad_gain, grad_bias = halves(norms)
    return pair_sum(gain * grad_bias) / count, pair_sum(gain * grad_gain) / count


def pair_add(voxels):
    total_count = float(voxels * GROUP)
    count = float(2 * 4096 * GROUP)

    def kernel(info, mine, other, gathered, gain, out):
        _, _, _, rstd = moments(gathered, total_count)
        total = (mine[0] + other[...]).reshape(-1, 16, 128)
        m1, m2 = slopes(total[0, 14:15], gain[...], count)
        row = lax.broadcasted_iota(jnp.int32, total.shape, 1)
        lane = lax.broadcasted_iota(jnp.int32, total.shape, 2)
        picked = (lane == SHIFT_LANE + 2 * row) & (row < 14)
        ones = jnp.sum(jnp.where(picked, total[:, 15:16], 0.0), axis=2, keepdims=True)
        centred = total - (m1 * rstd)[None] * ones - (m2 * rstd)[None] * pltpu.roll(total, 64, 2)
        total = jnp.where((lane < 64) & (row < 14), centred, total)
        lost = pltpu.roll(total - total.astype(BF).astype(F32), 1, 1)
        out[...] = jnp.where(row == 15, lost, total).astype(BF)

    return kernel


def combine(voxels):
    count = float(voxels * GROUP)
    pair_count = float(2 * 4096 * GROUP)

    def kernel(info, pieces, gathered, gain, temb, copies, grad_time, gain_out, bias_out):
        _, sums, mean, rstd = moments(gathered, count)
        value = pieces[...].astype(F32)
        chips = value.shape[0]
        seen = value[:, 14] + value[:, 15]
        norms = jnp.sum(seen, axis=0, keepdims=True)
        grad_gain, grad_bias = halves(norms)
        gain_out[...] = grad_gain[:, :64]
        bias_out[...] = grad_bias[:, :64]
        m1, m2 = slopes(norms, gain[...], count)
        centred = (sums - voxels * mean) * rstd
        act_sum = rstd * (gain[...] * grad_bias - voxels * m1 - m2 * centred)
        column = jnp.broadcast_to(act_sum, (128, 128)).T[:64]
        grad_time[...] = jnp.concatenate([column, column], axis=1) * temb[...]
        own1, own2 = slopes(seen, gain[...], pair_count)
        delta1, delta2 = (own1 - m1) * rstd, (own2 - m2) * rstd
        ones = gathered[0:chips] + gathered[chips : 2 * chips]
        back = lax.dot_general(
            ones, delta1, (((0,), (0,)), ((), ())), preferred_element_type=F32, precision=lax.Precision.HIGHEST
        )
        back = [back[SHIFT_LANE + 2 * r : SHIFT_LANE + 2 * r + 1] for r in range(14)]
        back = jnp.concatenate(back + [jnp.zeros((2, 128), F32)], axis=0)
        total = jnp.sum(value + delta2[:, None] * pltpu.roll(value, 64, 2), axis=0) + back
        lane = lax.broadcasted_iota(jnp.int32, (7, 128), 1)
        both = jnp.where(lane < 64, total[:7], pltpu.roll(total[7:14], 64, 1))
        lost = both[6:7] - both[6:7].astype(BF).astype(F32)
        piece = jnp.concatenate([both, lost], axis=0).astype(BF)
        copies[...] = jnp.broadcast_to(piece[None], copies.shape)

    return kernel


def spread(scale, info, near, far, conv, coarse, out, loss, rows):
    kz = lax.axis_index("cz")
    rows[pl.ds(pl.multiple_of(1024 * kz, 1024), 1024), :] = near[...].astype(F32).reshape(1024, 128)
    rows[pl.ds(pl.multiple_of(1024 * (1 - kz), 1024), 1024), :] = far[...].astype(F32).reshape(1024, 128)
    for tap in range(28):
        tile = rows[pl.ds(512 * (tap % 4) + tap // 4, 64, stride=8), :]
        if tap < 27:
            conv[tap] = tile[:, :64]
            coarse[tap] = tile[:, 64:]
        else:
            out[...] = tile[:, :64]
            parts = tile[0:1] + rows[2048 - 512 + 7 : 2048 - 512 + 8, :]
            lane = lax.broadcasted_iota(jnp.int32, (1, 128), 1)
            whole = jnp.sum(jnp.where((lane >= 64) & (lane < 68), parts, 0.0), axis=1, keepdims=True)
            loss[...] = whole * scale


def exchange(rows):
    out = lax.all_to_all(rows.reshape(rows.shape[0], 1, 128), ("cz",) + CHIPS, 0, 0, tiled=True)
    return out.reshape(rows.shape)


def neighbours(down, up, axis):
    ends = lax.axis_size(axis) - 1
    before = lax.ppermute(up, axis, [(i, i + 1) for i in range(ends)])
    after = lax.ppermute(down, axis, [(i + 1, i) for i in range(ends)])
    return before, after


def time_embedding(timestep, width):
    halfway = width // 2
    indices = jnp.arange(halfway).astype(F32)
    freqs = jnp.exp(indices * (-math.log(10000.0) / halfway))
    angles = timestep[0].astype(F32) * freqs
    return jnp.concatenate([jnp.sin(angles), jnp.cos(angles)])


def twice(row):
    return jnp.concatenate([row, row]).reshape(1, 128)


def diagonal(square):
    nought = jnp.zeros_like(square)
    return jnp.block([[square, nought], [nought, square]])


def shards(latents, target, block_coords, timestep, conv_weight, coarse_weight, out_weight, time_weight, norm_gain, norm_bias):
    devices = lax.axis_size("bx") * lax.axis_size("by") * lax.axis_size("cz")
    voxels = devices * 4096
    info = block_coords
    lat = latents[0]
    lat_pairs = lat.reshape(16, 8, 2, 16, 64)

    mz, pooled = call(z_message, [message(Z_TILES), like((16, 64), BF)], [info, lat])
    rz = lax.ppermute(mz, "cz", [(0, 1), (1, 0)])
    out = message(Y_TILES)
    down, up = call(
        y_messages, [out, out], [info, lat, lat, rz, pooled], [plane(Z_TILES)], [face_spec(1, 0), face_spec(1, 15)]
    )
    rym, ryp = neighbours(down, up, "by")
    out = message(X_TILES)
    planes = [plane(Z_TILES), plane(Y_TILES), plane(Y_TILES)]
    down, up = call(
        x_messages,
        [out, out],
        [info, lat, lat, rz, rym, ryp, pooled],
        planes,
        [face_spec(0, 0), face_spec(0, 15)],
    )
    rxm, rxp = neighbours(down, up, "bx")

    temb = time_embedding(timestep, time_weight.shape[0]).reshape(1, -1)
    raw, scene, columns, taps = call(
        interior,
        [like((1792, 128), F32), like((3, 16, 9, 16, 128), BF), like((3, 9, 128), F32), like((2304, 128), BF)],
        [info, lat_pairs, rz, rym, ryp, conv_weight],
        planes,
    )
    pair = (3, 2, 9, 16, 128)
    tables = jnp.asarray(coarse_table(), BF)
    ends, patch, stats, act = call(
        forward,
        [like((2, 3, 9, 16, 128), BF), like((16, 1728), BF), like((devices, 128), F32), pltpu.HBM((2048, 128), F32)],
        [info, scene, scene, raw, columns, rz, rym, ryp, rxm, rxp, pooled, taps]
        + [coarse_weight.reshape(1728, 64), temb, time_weight.T, tables],
        [pltpu.VMEM((2048, 128), F32), pltpu.SemaphoreType.DMA((4,))]
        + [pltpu.VMEM((2, 128, 128), F32), pltpu.VMEM((224, 160), BF), pltpu.SemaphoreType.DMA]
        + planes
        + [plane(X_TILES), plane(X_TILES)],
        [pl.BlockSpec(pair, lambda i: (0, 0, 0, 0, 0)), pl.BlockSpec(pair, lambda i: (0, 7, 0, 0, 0))],
        far_args=1,
        far_outs=1,
    )
    first = exchange(stats)
    (turned,) = call(
        turn,
        [pltpu.HBM((3, 256, 18 * 128), BF)],
        [info, scene, ends],
        [pltpu.VMEM((3, 256, 18 * 128), BF), pltpu.SemaphoreType.DMA((3,))],
        far_outs=1,
    )
    gain, bias = twice(norm_gain), twice(norm_bias)
    weights = [diagonal(out_weight), diagonal(out_weight.T)]
    payload, other, predicted = call(
        backward(voxels),
        [like((2, 2048, 128), F32), like((2048, 128), F32), pltpu.HBM((16, 8, 2, 16, 64), BF)],
        [info, first, target.reshape(16, 8, 2, 16, 64), gain, bias] + weights + [patch, stats, in_hbm(act), in_hbm(turned)],
        [
            pltpu.VMEM((2048, 256), BF),
            pltpu.VMEM((2048, 128), F32),
            pltpu.VMEM((3, 256, 18 * 128), BF),
            pltpu.VMEM((16, 8, 2, 16, 64), BF),
            pltpu.SemaphoreType.DMA((9,)),
            pltpu.SemaphoreType.DMA,
            pltpu.SemaphoreType.DMA((8,)),
        ],
        far_args=2,
        far_outs=2,
    )
    swap = [(0, 1), (1, 0)]
    chips = devices // 2
    other = lax.ppermute(other, "cz", swap)
    (pieces,) = call(pair_add(voxels), [like((chips, 16, 128), BF)], [info, payload, other, first, gain])
    pieces = lax.all_to_all(pieces, CHIPS, 0, 0, tiled=True)
    copies, grad_time, grad_gain, grad_bias = call(
        combine(voxels),
        [like((chips, 8, 128), BF), like((64, 256), F32), like((1, 64), F32), like((1, 64), F32)],
        [info, pieces, first, gain, temb],
    )
    near = lax.all_to_all(copies, CHIPS, 0, 0, tiled=True)
    far = lax.ppermute(near, "cz", swap)
    grad_conv, grad_coarse, grad_out, loss = call(
        functools.partial(spread, 1.0 / (voxels * 64)),
        [like((27, 64, 64), F32), like((27, 64, 64), F32), like((64, 64), F32), like((1, 1), F32)],
        [info, near, far],
        [pltpu.VMEM((2048, 128), F32)],
    )
    return (
        predicted.reshape(latents.shape),
        loss.reshape(1),
        grad_conv,
        grad_coarse,
        grad_out,
        grad_time.T,
        grad_gain.reshape(64),
        grad_bias.reshape(64),
    )


def solution(mesh):
    blocks = P(ALL, None, None, None, None)
    return jax.shard_map(
        shards,
        mesh=mesh,
        in_specs=(blocks, blocks, P(ALL, None)) + (P(),) * 7,
        out_specs=(blocks,) + (P(),) * 7,
        check_vma=False,
    )
```

```python
import functools
import math

import jax
import jax.numpy as jnp
import numpy as np
from jax import lax
from jax.experimental import pallas as pl
from jax.experimental.pallas import tpu as pltpu
from jax.sharding import PartitionSpec as P

ALL = ("bx", "by", "cz")
CHIPS = ("bx", "by")
BF = jnp.bfloat16
F32 = jnp.float32
EPS = 1e-05
GROUP = 2
VMEM_LIMIT = 40 * 1024 * 1024
SHIFT_LANE = 65


def face_spec(dim, index):
    shape = tuple(1 if d == dim else 16 for d in range(3)) + (64,)
    where = tuple(index if d == dim else 0 for d in range(4))
    return pl.BlockSpec(shape, lambda i: where)


def call(kernel, outs, args, scratch=(), faces=(), far_args=0, far_outs=0):
    vmem = pl.BlockSpec(memory_space=pltpu.VMEM)
    far = pl.BlockSpec(memory_space=pl.ANY)
    specs = list(faces) + [vmem] * (len(args) - 1 - len(faces) - far_args) + [far] * far_args
    args = [
        pltpu.with_memory_space_constraint(arg, pltpu.VMEM) if spec is vmem else arg
        for arg, spec in zip(args, [None] + specs)
    ]
    return pl.pallas_call(
        kernel,
        grid=(1,),
        out_shape=outs,
        in_specs=[pl.BlockSpec(memory_space=pltpu.SMEM)] + specs,
        out_specs=[vmem] * (len(outs) - far_outs) + [far] * far_outs,
        scratch_shapes=list(scratch),
        compiler_params=pltpu.CompilerParams(vmem_limit_bytes=VMEM_LIMIT),
    )(*args)


def in_hbm(array):
    return pltpu.with_memory_space_constraint(array, pltpu.HBM)


def like(shape, dtype):
    return jax.ShapeDtypeStruct(shape, dtype)


def keep(cond, value):
    return jnp.where(cond, value, jnp.zeros_like(value))


def bits(info):
    return info[0, 0], info[0, 1], info[0, 2], lax.axis_index("cz")


def start16(bit):
    return pl.multiple_of(bit * 16, 16)


def cell_rows(first, second, face, on):
    rows = []
    for r in range(4):
        for s in range(4):
            here = on & (first == r // 2) & (second == s // 2)
            rows.append(keep(here, face[r % 2][s % 2]))
    return jnp.concatenate(rows, axis=0)


def row_of(cells, p):
    return cells[p : p + 1]


Z_TILES, Y_TILES, X_TILES = 1, 2, 5


def message(tiles):
    return like((9 + tiles, 16, 128), BF)


def plane(tiles):
    return pltpu.VMEM((32 + tiles, 32, 64), BF)


def side_by_side(rows):
    half = rows.shape[0] // 2
    return jnp.concatenate([rows[:half], rows[half:]], axis=rows.ndim - 1)


def write_message(out, face, tiles, first, second, on):
    out[0:8] = side_by_side(face)
    for t, rows in enumerate(tiles):
        out[8 + t] = side_by_side(rows).astype(BF)
    row = lax.broadcasted_iota(jnp.int32, (16, 128), 0)
    here = jnp.where(on, 2 * first + second, 99)
    out[8 + len(tiles)] = jnp.where(row == here, 1.0, 0.0).astype(BF)


def open_message(ref, out):
    tiles = ref.shape[0] - 9
    face = jnp.concatenate([ref[0:8, :, :64], ref[0:8, :, 64:]], axis=0)
    flags = ref[8 + tiles].astype(F32)
    for q in range(4):
        here = jnp.broadcast_to(flags[q : q + 1, :64], (16, 64))[None]
        out[16 * (q // 2) : 16 * (q // 2) + 16, 16 * (q % 2) : 16 * (q % 2) + 16, :] = jnp.where(
            here > 0.5, face.astype(F32), 0.0
        ).astype(BF)
    for t in range(tiles):
        out[32 + t] = jnp.concatenate([ref[8 + t, :, :64], ref[8 + t, :, 64:]], axis=0)


def z_message(info, lat, out, pooled):
    px, py, pz, kz = bits(info)
    zsel = 15 * (1 - kz)
    pick = lax.broadcasted_iota(jnp.int32, (16, 16, 64), 1) == zsel
    sums = [[None, None], [None, None]]
    faces = []
    for y in range(16):
        slab = lat[:, y].astype(F32)
        faces.append(jnp.sum(jnp.where(pick, slab, 0.0), axis=1)[None])
        for a in range(2):
            part = jnp.sum(slab[8 * a : 8 * a + 8], axis=0)
            old = sums[a][y // 8]
            sums[a][y // 8] = part if old is None else old + part
    cells = []
    for a in range(2):
        for b in range(2):
            for c in range(2):
                cells.append(jnp.sum(sums[a][b][8 * c : 8 * c + 8], axis=0, keepdims=True))
    cells = jnp.concatenate(cells, axis=0) * (1.0 / math.sqrt(512.0))
    cells = cells.astype(BF).astype(F32)
    pooled[...] = jnp.concatenate([cells, jnp.zeros((8, 64), F32)], axis=0).astype(BF)
    on = pz == 1 - kz
    face = [
        [jnp.where(kz == 0, row_of(cells, 4 * a + 2 * b + 1), row_of(cells, 4 * a + 2 * b)) for a in range(2)]
        for b in range(2)
    ]
    rows = jnp.concatenate([cell_rows(py, px, face, on), jnp.zeros((16, 64), F32)], axis=0)
    write_message(out, jnp.concatenate(faces, axis=0).astype(BF), [rows], py, px, on)


def y_messages(info, low, high, rz_in, pooled, down, up, rz):
    px, py, pz, kz = bits(info)
    open_message(rz_in, rz)
    cells = pooled[...].astype(F32)
    halo = rz[32].astype(F32)
    for out, face, bit, line, q in ((down, low, 0, 0, 0), (up, high, 1, 31, 1)):
        on = py == bit
        picked = [[row_of(cells, 4 * a + 2 * q + c) for c in range(2)] for a in range(2)]
        tail = halo[12:16] if q else halo[0:4]
        rows = jnp.concatenate([cell_rows(px, pz, picked, on), tail, jnp.zeros((12, 64), F32)], axis=0)
        write_message(out, face[:, 0], [rz[line], rows], px, pz, on)


def x_messages(info, low, high, rz_in, rym_in, ryp_in, pooled, down, up, rz, rym, ryp):
    px, py, pz, kz = bits(info)
    for ref, out in ((rz_in, rz), (rym_in, rym), (ryp_in, ryp)):
        open_message(ref, out)
    cells = pooled[...].astype(F32)
    halo = rz[32].astype(F32)
    halo_m = rym[33].astype(F32)
    halo_p = ryp[33].astype(F32)
    line_m = rym[32].astype(F32)
    line_p = ryp[32].astype(F32)
    where16 = lax.broadcasted_iota(jnp.int32, (32, 16, 64), 1)
    for out, face, bit, line, q in ((down, low, 0, 0, 0), (up, high, 1, 31, 1)):
        on = px == bit
        slab = rz[0:32, 16 * q : 16 * q + 16, :].astype(F32)
        z_line = jnp.sum(jnp.where(where16 == 15 * q, slab, 0.0), axis=1).astype(BF)
        picked = [[row_of(cells, 4 * q + 2 * b + c) for c in range(2)] for b in range(2)]
        corners = [line_m[line : line + 1], line_p[line : line + 1], jnp.zeros((14, 64), F32)]
        corners = jnp.concatenate(corners + [cell_rows(py, pz, picked, on)], axis=0)
        c0 = 3 * q
        parts = [row_of(halo, 4 * cy + c0) for cy in range(4)]
        parts += [halo_m[4 * c0 : 4 * c0 + 4], halo_p[4 * c0 : 4 * c0 + 4]]
        parts += [row_of(halo_m, 16 + c0), row_of(halo_p, 16 + c0), jnp.zeros((18, 64), F32)]
        tiles = [z_line, rym[line], ryp[line], corners, jnp.concatenate(parts, axis=0)]
        write_message(out, face[0], tiles, py, pz, on)


def coarse_table():
    pooled, rz, rym, ryp, rxm, rxp = 0, 16, 32, 64, 96, 128
    table = np.zeros((16, 224, 160), np.float32)
    for combo in range(16):
        bit = ((combo >> 3) & 1, (combo >> 2) & 1, (combo >> 1) & 1)
        core = combo & 1
        for tap in range(27):
            off = (tap // 9, tap // 3 % 3, tap % 3)
            for p in range(8):
                at = (p // 4, p // 2 % 2, p % 2)
                pos = [2 * bit[d] - 1 + off[d] + at[d] for d in range(3)]
                x, y, z = pos
                out_z = z < 0 or z > 3
                if out_z and (z < 0) != (core == 1):
                    continue
                if x < 0 or x > 3:
                    base = rxm if x < 0 else rxp
                    if y < 0 or y > 3:
                        side = 0 if y < 0 else 1
                        row = 16 + (12 + side if out_z else 4 + 4 * side + z)
                    else:
                        row = 16 + y if out_z else 4 * y + z
                    row = base + row
                elif y < 0 or y > 3:
                    row = (rym if y < 0 else ryp) + (16 + x if out_z else 4 * x + z)
                elif out_z:
                    row = rz + 4 * y + x
                else:
                    own = [pos[d] - 2 * bit[d] for d in range(3)]
                    if min(own) < 0 or max(own) > 1:
                        continue
                    row = pooled + 4 * own[0] + 2 * own[1] + own[2]
                table[combo, 8 * tap + p, row] = 1.0
    return table


class Window:
    def __init__(self, info, rz, rym, ryp):
        px, py, pz, kz = bits(info)
        self.pz, self.rz, self.rym, self.ryp = pz, rz, rym, ryp
        self.z0 = pl.ds(start16(pz), 16)
        self.z1 = pl.ds(start16(1 - pz), 16)
        self.xs = pl.ds(start16(px), 16)
        self.ys = pl.ds(start16(py), 16)
        self.xlo, self.xhi, self.ylo, self.yhi = px == 0, px == 1, py == 0, py == 1
        self.on_low = (pz == 0) & (kz == 1)
        self.on_high = (pz == 1) & (kz == 0)
        self.row16 = lax.broadcasted_iota(jnp.int32, (16, 16, 64), 1)
        self.z_row = lax.broadcasted_iota(jnp.int32, (9, 16, 128), 1)

    def edge(self, block):
        return jnp.sum(jnp.where(self.row16[: block.shape[0]] == 15 * self.pz, block.astype(F32), 0.0), axis=1)

    def edge1(self, ref, i):
        return self.edge(ref[i : i + 1, self.z1, :])

    def low_of(self, e, h):
        return keep(self.pz == 1, e) + keep(self.on_low, h)

    def high_of(self, e, h):
        return keep(self.pz == 0, e) + keep(self.on_high, h)

    def offsets(self, evens, odds, first, last, zl, zh):
        left = jnp.concatenate([first[None], odds], axis=0)
        right = jnp.concatenate([evens, last[None]], axis=0)
        tile = jnp.concatenate([left, right], axis=2)
        wide = tile.astype(F32)
        down = jnp.where(self.z_row == 0, zl, pltpu.roll(wide, 1, 1)).astype(BF)
        up = jnp.where(self.z_row == 15, zh, pltpu.roll(wide, 15, 1)).astype(BF)
        return down, tile, up


def one(ref, i, j):
    return ref[i].astype(F32)[j : j + 1]


def interior(info, lat, rz_in, rym_in, ryp_in, taps, raw, scene, columns, weight, rz, rym, ryp):
    for ref, out in ((rz_in, rz), (rym_in, rym), (ryp_in, ryp)):
        open_message(ref, out)
    nought = jnp.zeros((64, 64), BF)
    for tap in range(9):
        ox, oz = tap // 3, tap % 3
        for a in range(4):
            left = nought if a == 3 else taps[9 * ox + 3 * a + oz]
            right = nought if a == 0 else taps[9 * ox + 3 * a - 3 + oz]
            weight[256 * tap + 64 * a : 256 * tap + 64 * a + 64] = jnp.concatenate([left, right], axis=1)
    w = Window(info, rz, rym, ryp)
    y_low = keep(w.ylo, rym[w.xs, w.z0, :])
    y_high = keep(w.yhi, ryp[w.xs, w.z0, :])
    e_low = keep(w.ylo, w.edge(rym[w.xs, w.z1, :]))
    e_high = keep(w.yhi, w.edge(ryp[w.xs, w.z1, :]))
    h_low = jnp.where(w.ylo, rym[32, w.xs, :], rz[15, w.xs, :]).astype(F32)
    h_high = jnp.where(w.yhi, ryp[32, w.xs, :], rz[16, w.xs, :]).astype(F32)
    h_mid = rz[w.ys, w.xs, :].astype(F32)

    def packed(of):
        rows = [of(e_low, h_low)] + [of(jnp.zeros((16, 64), F32), h_mid[y]) for y in range(16)]
        rows.append(of(e_high, h_high))
        return [jnp.concatenate([rows[2 * k], rows[2 * k + 1]], axis=1) for k in range(9)]

    below, above = packed(w.low_of), packed(w.high_of)
    inner = [None] * 3
    for x in range(16):
        zl = jnp.concatenate([below[k][x : x + 1][None] for k in range(9)], axis=0)
        zh = jnp.concatenate([above[k][x : x + 1][None] for k in range(9)], axis=0)
        planes = w.offsets(lat[x, :, 0], lat[x, :, 1], y_low[x], y_high[x], zl, zh)
        for oz, plane in enumerate(planes):
            scene[oz, x] = plane
            wide = plane.astype(F32)
            inner[oz] = wide if x == 0 else inner[oz] + wide
    for oz in range(3):
        columns[oz] = jnp.sum(inner[oz], axis=1)
    for first, count in ((1, 4), (5, 4), (9, 4), (13, 2)):
        pieces = []
        for tap in range(9):
            ox, oz = tap // 3, tap % 3
            for dk in range(2):
                at = first + ox - 1
                pieces.append(scene[oz, at : at + count, dk : dk + 8].reshape(128 * count, 128))
        value = jnp.dot(jnp.concatenate(pieces, axis=1), weight[...], preferred_element_type=F32)
        raw[(first - 1) * 128 : (first - 1 + count) * 128] = value


def forward(
    info, near_low, near_high, raw, columns, rz_in, rym_in, ryp_in, rxm_in, rxp_in, pooled, weight,
    coarse_weight, temb, time_weight, tables, act, ends, patch_out, stats,
    shift, table, arrived, rz, rym, ryp, rxm, rxp
):
    px, py, pz, kz = bits(info)
    fetch = pltpu.make_async_copy(tables.at[8 * px + 4 * py + 2 * pz + kz], table, arrived)
    fetch.start()
    for ref, out in ((rz_in, rz), (rym_in, rym), (ryp_in, ryp), (rxm_in, rxm), (rxp_in, rxp)):
        open_message(ref, out)
    w = Window(info, rz, rym, ryp)
    nought = jnp.zeros((16, 64), BF)

    def sides(rx, out, inner):
        first = jnp.where(
            out,
            jnp.where(w.ylo, rx[33, w.z0, :], rx[15, w.z0, :]),
            jnp.where(w.ylo, rym[inner, w.z0, :], nought),
        )
        last = jnp.where(
            out,
            jnp.where(w.yhi, rx[34, w.z0, :], rx[16, w.z0, :]),
            jnp.where(w.yhi, ryp[inner, w.z0, :], nought),
        )
        return first, last

    def side_columns(rx, out, inner, of):
        half = rz[w.ys, 0:16, :] if inner < 16 else rz[w.ys, 16:32, :]
        inner_h = jnp.sum(jnp.where(w.row16 == inner % 16, half.astype(F32), 0.0), axis=1)
        e_mid = keep(out, w.edge(rx[w.ys, w.z1, :]))
        hh = jnp.where(out, rx[32, w.ys, :].astype(F32), inner_h)
        e_first = jnp.where(
            out,
            jnp.where(w.ylo, w.edge1(rx, 33), w.edge1(rx, 15)),
            keep(w.ylo, w.edge1(rym, inner)),
        )
        h_first = jnp.where(
            out,
            jnp.where(w.ylo, one(rx, 35, 0), one(rx, 32, 15)),
            jnp.where(w.ylo, one(rym, 32, inner), one(rz, 15, inner)),
        )
        e_last = jnp.where(
            out,
            jnp.where(w.yhi, w.edge1(rx, 34), w.edge1(rx, 16)),
            keep(w.yhi, w.edge1(ryp, inner)),
        )
        h_last = jnp.where(
            out,
            jnp.where(w.yhi, one(rx, 35, 1), one(rx, 32, 16)),
            jnp.where(w.yhi, one(ryp, 32, inner), one(rz, 16, inner)),
        )
        mid = of(e_mid, hh)
        rows = [of(e_first, h_first)] + [mid[y : y + 1] for y in range(16)] + [of(e_last, h_last)]
        return [jnp.concatenate([rows[2 * k], rows[2 * k + 1]], axis=1)[None] for k in range(9)]

    for e, rx, out, inner in ((0, rxm, w.xlo, 15), (1, rxp, w.xhi, 16)):
        zl = jnp.concatenate(side_columns(rx, out, inner, w.low_of), axis=0)
        zh = jnp.concatenate(side_columns(rx, out, inner, w.high_of), axis=0)
        first, last = sides(rx, out, inner)
        plane = keep(out, rx[w.ys, w.z0, :]).reshape(8, 2, 16, 64)
        for oz, tile in enumerate(w.offsets(plane[:, 0], plane[:, 1], first, last, zl, zh)):
            ends[e, oz] = tile

    source = jnp.concatenate(
        [pooled[...], rz[32, 0:16, :], rym[33], ryp[33], rxm[35, 16:32, :], rxm[36, 0:16, :], rxp[35, 16:32, :], rxp[36, 0:16, :]],
        axis=0,
    )
    fetch.wait()
    taps = jnp.dot(table[...], source, preferred_element_type=F32)
    patch = jnp.concatenate([taps[8 * t : 8 * t + 8] for t in range(27)], axis=1)
    patch_out[...] = jnp.concatenate([patch, patch], axis=0).astype(BF)
    coarse = jnp.dot(patch_out[...], coarse_weight[...], preferred_element_type=F32)
    coarse = coarse.astype(BF).astype(F32)
    coarse = jnp.concatenate([coarse, coarse], axis=1)
    time_bias = lax.dot_general(
        jnp.broadcast_to(temb[...], (8, 256)),
        time_weight[...].astype(F32),
        (((1,), (1,)), ((), ())),
        preferred_element_type=F32,
        precision=lax.Precision.HIGHEST,
    )[:1]
    time_bias = jnp.concatenate([time_bias, time_bias], axis=1)
    z_half = lax.broadcasted_iota(jnp.int32, (16, 128), 0) < 8
    added = []
    for q in range(4):
        added.append(jnp.where(z_half, coarse[2 * q : 2 * q + 1], coarse[2 * q + 1 : 2 * q + 2]) + time_bias)

    pieces = []
    for tap in range(9):
        ox, oz = tap // 3, tap % 3
        low = ends[0, oz] if ox == 0 else near_low[oz, ox - 1]
        high = ends[1, oz] if ox == 2 else near_high[oz, ox]
        for dk in range(2):
            pieces.append(jnp.concatenate([low[dk : dk + 8], high[dk : dk + 8]], axis=0).reshape(256, 128))
    edges = jnp.dot(jnp.concatenate(pieces, axis=1), weight[...], preferred_element_type=F32)

    total = jnp.zeros((1, 128), F32)
    squares = jnp.zeros((1, 128), F32)
    for x in range(16):
        if x == 0:
            value = edges[:128]
        elif x == 15:
            value = edges[128:]
        else:
            value = raw[(x - 1) * 128 : x * 128]
        value = value.reshape(2, 4, 16, 128)
        a = x // 8
        value = jnp.concatenate([(value[b] + added[2 * a + b][None])[None] for b in range(2)], axis=0).reshape(128, 128)
        act[x * 128 : x * 128 + 128] = value
        total = total + jnp.sum(value, axis=0, keepdims=True)
        squares = squares + jnp.sum(value * value, axis=0, keepdims=True)
    shift[...] = jnp.zeros(shift.shape, F32)

    def place(tap, slot, value):
        row = SHIFT_LANE + 2 * (tap // 4 + slot)
        u = tap % 4
        shift[u // 2, row : row + 1, 64 * (u % 2) : 64 * (u % 2) + 64] = value

    for oz in range(3):
        inner = columns[oz]
        planes = (ends[0, oz], near_low[oz, 0], near_high[oz, 1], ends[1, oz])
        outer = [jnp.sum(plane.astype(F32), axis=1) for plane in planes]
        for ox, part in enumerate((inner + outer[0] - outer[2], inner, inner - outer[1] + outer[3])):
            all_columns = jnp.sum(part, axis=0, keepdims=True)
            whole = all_columns[:, :64] + all_columns[:, 64:]
            y0, y1 = part[0:1, :64], part[0:1, 64:]
            y16, y17 = part[8:9, :64], part[8:9, 64:]
            for oy, window in enumerate((whole - y16 - y17, whole - y0 - y17, whole - y0 - y1)):
                place(9 * ox + 3 * oy + oz, 0, window)
    for t in range(27):
        place(t, 7, 512.0 * jnp.sum(taps[8 * t : 8 * t + 8], axis=0, keepdims=True))

    lane = lax.broadcasted_iota(jnp.int32, (1, 128), 1)
    pairs = pair_sum(squares + pltpu.roll(squares, 64, 1))
    row = jnp.where(lane < 64, total + pltpu.roll(total, 64, 1), jnp.where(lane % 2 == 0, pairs, 0.0))
    for u in range(2):
        stats[128 * u : 128 * u + 128] = shift[u].T + row


def turn(info, scene, ends, turned_out, turned, sent):
    for oz in range(3):
        for xp in range(18):
            for dk in range(2):
                tile = scene[oz, xp - 1, dk : dk + 8] if 1 <= xp <= 16 else ends[xp // 17, oz, dk : dk + 8]
                turned[oz, 128 * dk : 128 * dk + 128, 128 * xp : 128 * xp + 128] = tile.reshape(128, 128).T
        pltpu.make_async_copy(turned.at[oz], turned_out.at[oz], sent.at[oz]).start()
    for oz in range(3):
        pltpu.make_async_copy(turned.at[oz], turned_out.at[oz], sent.at[oz]).wait()


def pair_sum(row):
    lane = lax.broadcasted_iota(jnp.int32, row.shape, 1)
    return row + jnp.where(lane % 2 == 0, pltpu.roll(row, 127, 1), pltpu.roll(row, 1, 1))


def halves(row):
    lane = lax.broadcasted_iota(jnp.int32, row.shape, 1)
    other = pltpu.roll(row, 64, 1)
    return jnp.where(lane < 64, row, other), jnp.where(lane < 64, other, row)


def moments(gathered, count):
    row = jnp.sum(gathered[...], axis=0, keepdims=True)
    sums, upper = halves(row)
    lane = lax.broadcasted_iota(jnp.int32, row.shape, 1)
    squares = jnp.where(lane % 2 == 0, upper, pltpu.roll(upper, 1, 1))
    mean = pair_sum(sums) / count
    var = squares / count - mean * mean
    return row, sums, mean, 1.0 / jnp.sqrt(var + EPS)


def backward(voxels):
    count = float(voxels * GROUP)
    scale = 1.0 / (voxels * 64)

    def kernel(
        info, gathered, target, gain, bias, weight, weight_t, patch, stats, act_in, turned_in,
        payload, other, predicted_out, cotangent, act, turned, predicted, fetched, sent, shown_sent
    ):
        def chunk(n):
            rows = (pl.ds(0, 512), pl.ds(512, 1536))[n]
            return pltpu.make_async_copy(act_in.at[rows], act.at[rows], fetched.at[n])

        def show(n):
            part = (pl.ds(0, 4), pl.ds(4, 12))[n]
            return pltpu.make_async_copy(predicted.at[part], predicted_out.at[part], shown_sent.at[n])

        whole = pltpu.make_async_copy(turned_in, turned, fetched.at[2])
        for n in range(2):
            chunk(n).start()
        kz = lax.axis_index("cz")
        _, _, mean, rstd = moments(gathered, count)
        gains = jnp.zeros((1, 128), F32)
        biases = jnp.zeros((1, 128), F32)
        lost = jnp.zeros((1, 128), F32)
        outer = jnp.zeros((128, 128), F32)
        cells = [[None] * 4, [None] * 4]
        for x in range(0, 16, 2):
            rows = slice(x * 128, x * 128 + 256)
            if x == 0:
                chunk(0).wait()
                whole.start()
            if x == 4:
                show(0).start()
                chunk(1).wait()
            normalized = (act[rows] - mean) * rstd
            shifted = normalized * gain[...] + bias[...]
            sigma = jax.nn.sigmoid(shifted)
            hidden = (shifted * sigma).astype(BF)
            output = jnp.dot(hidden, weight[...], preferred_element_type=F32)
            goal = jnp.concatenate([target[x : x + 2, :, 0], target[x : x + 2, :, 1]], axis=3)
            residue = output - goal.reshape(256, 128).astype(F32)
            shown = output.astype(BF).reshape(2, 8, 16, 128)
            predicted[x : x + 2, :, 0] = shown[..., :64]
            predicted[x : x + 2, :, 1] = shown[..., 64:]
            upstream = (2.0 * scale * residue).astype(BF)
            back = jnp.dot(upstream, weight_t[...], preferred_element_type=F32)
            value = back * sigma * (1.0 + shifted * (1.0 - sigma))
            gains = gains + jnp.sum(value * normalized, axis=0, keepdims=True)
            biases = biases + jnp.sum(value, axis=0, keepdims=True)
            lost = lost + jnp.sum(residue * residue, axis=0, keepdims=True)
            outer = outer + lax.dot_general(hidden, upstream, (((0,), (0,)), ((), ())), preferred_element_type=F32)
            value = value * (gain[...] * rstd)
            narrow = [value.astype(BF), normalized.astype(BF)]
            cotangent[rows, :128] = jnp.concatenate([part[:, :64] for part in narrow], axis=1)
            cotangent[rows, 128:] = jnp.concatenate([part[:, 64:] for part in narrow], axis=1)
            for part, wide in enumerate((value, normalized)):
                planes = wide.reshape(2, 2, 4, 16, 128)
                for b in range(2):
                    q = 2 * (x // 8) + b
                    cell = jnp.sum(planes[:, b], axis=(0, 1))
                    old = cells[part][q]
                    cells[part][q] = cell if old is None else old + cell

        def store(tap, slot, value):
            u = tap % 4
            half = jnp.where(kz == u // 2, 0, 1)
            payload.at[half][pl.ds(1024 * (u % 2) + slot + tap // 4, 64, stride=16), :] = value

        rows = []
        for q in range(4):
            for c in range(2):
                sums = [jnp.sum(cells[p][q][8 * c : 8 * c + 8], axis=0, keepdims=True) for p in range(2)]
                rows.append(jnp.concatenate([r[:, :64] + r[:, 64:] for r in sums], axis=1))
        rows = jnp.concatenate(rows, axis=0)
        high = rows.astype(BF)
        split = jnp.concatenate([high.astype(F32), rows - high.astype(F32)], axis=0).astype(BF)
        coarse = lax.dot_general(patch[...], split, (((0,), (0,)), ((), ())), preferred_element_type=F32)
        for t in range(27):
            store(t, 7, coarse[64 * t : 64 * t + 64])
        show(1).start()
        whole.wait()
        for ox in range(3):
            windows = turned[:, :, 128 * ox : 128 * ox + 2048].reshape(768, 2048)
            products = jnp.dot(windows, cotangent[...], preferred_element_type=F32)
            for oz in range(3):
                product = products[256 * oz : 256 * oz + 256]
                for oy in range(3):
                    value = product[64 * oy : 64 * oy + 64, :128] + product[64 * oy + 64 : 64 * oy + 128, 128:]
                    store(9 * ox + 3 * oy + oz, 0, value)
        nought = jnp.zeros((64, 64), F32)
        store(27, 0, jnp.concatenate([outer[:64, :64] + outer[64:, 64:], nought], axis=1))
        loss = jnp.broadcast_to(jnp.sum(lost, axis=1, keepdims=True), (64, 128))
        high = loss.astype(BF).astype(F32)
        lane = lax.broadcasted_iota(jnp.int32, (64, 128), 1)
        split = jnp.where(lane == 2 * kz, high, jnp.where(lane == 2 * kz + 1, loss - high, 0.0))
        store(27, 7, split)
        lane = lax.broadcasted_iota(jnp.int32, (1, 128), 1)
        row = jnp.where(lane < 64, gains + pltpu.roll(gains, 64, 1), biases + pltpu.roll(biases, 64, 1))
        wide = jnp.broadcast_to(row, (128, 128))
        for half in range(2):
            payload.at[half][pl.ds(14, 128, stride=16), :] = wide
            slot = jnp.where(kz == half, 0, 1)
            payload.at[slot][pl.ds(15, 128, stride=16), :] = stats[128 * half : 128 * half + 128]
        copy = pltpu.make_async_copy(payload.at[1], other, sent)
        copy.start()
        for n in range(2):
            show(n).wait()
        copy.wait()

    return kernel


def slopes(norms, gain, count):
    grad_gain, grad_bias = halves(norms)
    return pair_sum(gain * grad_bias) / count, pair_sum(gain * grad_gain) / count


def pair_add(voxels):
    total_count = float(voxels * GROUP)
    count = float(2 * 4096 * GROUP)

    def kernel(info, mine, other, gathered, gain, out):
        _, _, _, rstd = moments(gathered, total_count)
        total = (mine[0] + other[...]).reshape(-1, 16, 128)
        m1, m2 = slopes(total[0, 14:15], gain[...], count)
        row = lax.broadcasted_iota(jnp.int32, total.shape, 1)
        lane = lax.broadcasted_iota(jnp.int32, total.shape, 2)
        picked = (lane == SHIFT_LANE + 2 * row) & (row < 14)
        ones = jnp.sum(jnp.where(picked, total[:, 15:16], 0.0), axis=2, keepdims=True)
        centred = total - (m1 * rstd)[None] * ones - (m2 * rstd)[None] * pltpu.roll(total, 64, 2)
        total = jnp.where((lane < 64) & (row < 14), centred, total)
        lost = pltpu.roll(total - total.astype(BF).astype(F32), 1, 1)
        out[...] = jnp.where(row == 15, lost, total).astype(BF)

    return kernel


def combine(voxels):
    count = float(voxels * GROUP)
    pair_count = float(2 * 4096 * GROUP)

    def kernel(info, pieces, gathered, gain, temb, copies, grad_time, gain_out, bias_out):
        _, sums, mean, rstd = moments(gathered, count)
        value = pieces[...].astype(F32)
        chips = value.shape[0]
        seen = value[:, 14] + value[:, 15]
        norms = jnp.sum(seen, axis=0, keepdims=True)
        grad_gain, grad_bias = halves(norms)
        gain_out[...] = grad_gain[:, :64]
        bias_out[...] = grad_bias[:, :64]
        m1, m2 = slopes(norms, gain[...], count)
        centred = (sums - voxels * mean) * rstd
        act_sum = rstd * (gain[...] * grad_bias - voxels * m1 - m2 * centred)
        column = jnp.broadcast_to(act_sum, (128, 128)).T[:64]
        grad_time[...] = jnp.concatenate([column, column], axis=1) * temb[...]
        own1, own2 = slopes(seen, gain[...], pair_count)
        delta1, delta2 = (own1 - m1) * rstd, (own2 - m2) * rstd
        ones = gathered[0:chips] + gathered[chips : 2 * chips]
        back = lax.dot_general(
            ones, delta1, (((0,), (0,)), ((), ())), preferred_element_type=F32, precision=lax.Precision.HIGHEST
        )
        back = [back[SHIFT_LANE + 2 * r : SHIFT_LANE + 2 * r + 1] for r in range(14)]
        back = jnp.concatenate(back + [jnp.zeros((2, 128), F32)], axis=0)
        total = jnp.sum(value + delta2[:, None] * pltpu.roll(value, 64, 2), axis=0) + back
        lane = lax.broadcasted_iota(jnp.int32, (7, 128), 1)
        both = jnp.where(lane < 64, total[:7], pltpu.roll(total[7:14], 64, 1))
        lost = both[6:7] - both[6:7].astype(BF).astype(F32)
        piece = jnp.concatenate([both, lost], axis=0).astype(BF)
        copies[...] = jnp.broadcast_to(piece[None], copies.shape)

    return kernel


def spread(scale, info, near, far, conv, coarse, out, loss, rows):
    kz = lax.axis_index("cz")
    rows[pl.ds(pl.multiple_of(1024 * kz, 1024), 1024), :] = near[...].astype(F32).reshape(1024, 128)
    rows[pl.ds(pl.multiple_of(1024 * (1 - kz), 1024), 1024), :] = far[...].astype(F32).reshape(1024, 128)
    for tap in range(28):
        tile = rows[pl.ds(512 * (tap % 4) + tap // 4, 64, stride=8), :]
        if tap < 27:
            conv[tap] = tile[:, :64]
            coarse[tap] = tile[:, 64:]
        else:
            out[...] = tile[:, :64]
            parts = tile[0:1] + rows[2048 - 512 + 7 : 2048 - 512 + 8, :]
            lane = lax.broadcasted_iota(jnp.int32, (1, 128), 1)
            whole = jnp.sum(jnp.where((lane >= 64) & (lane < 68), parts, 0.0), axis=1, keepdims=True)
            loss[...] = whole * scale


def exchange(rows):
    out = lax.all_to_all(rows.reshape(rows.shape[0], 1, 128), ("cz",) + CHIPS, 0, 0, tiled=True)
    return out.reshape(rows.shape)


def neighbours(down, up, axis):
    ends = lax.axis_size(axis) - 1
    before = lax.ppermute(up, axis, [(i, i + 1) for i in range(ends)])
    after = lax.ppermute(down, axis, [(i + 1, i) for i in range(ends)])
    return before, after


def time_embedding(timestep, width):
    halfway = width // 2
    indices = jnp.arange(halfway).astype(F32)
    freqs = jnp.exp(indices * (-math.log(10000.0) / halfway))
    angles = timestep[0].astype(F32) * freqs
    return jnp.concatenate([jnp.sin(angles), jnp.cos(angles)])


def twice(row):
    return jnp.concatenate([row, row]).reshape(1, 128)


def diagonal(square):
    nought = jnp.zeros_like(square)
    return jnp.block([[square, nought], [nought, square]])


def shards(latents, target, block_coords, timestep, conv_weight, coarse_weight, out_weight, time_weight, norm_gain, norm_bias):
    devices = lax.axis_size("bx") * lax.axis_size("by") * lax.axis_size("cz")
    voxels = devices * 4096
    info = block_coords
    lat = latents[0]
    lat_pairs = lat.reshape(16, 8, 2, 16, 64)

    mz, pooled = call(z_message, [message(Z_TILES), like((16, 64), BF)], [info, lat])
    rz = lax.ppermute(mz, "cz", [(0, 1), (1, 0)])
    out = message(Y_TILES)
    down, up = call(
        y_messages, [out, out], [info, lat, lat, rz, pooled], [plane(Z_TILES)], [face_spec(1, 0), face_spec(1, 15)]
    )
    rym, ryp = neighbours(down, up, "by")
    out = message(X_TILES)
    planes = [plane(Z_TILES), plane(Y_TILES), plane(Y_TILES)]
    down, up = call(
        x_messages,
        [out, out],
        [info, lat, lat, rz, rym, ryp, pooled],
        planes,
        [face_spec(0, 0), face_spec(0, 15)],
    )
    rxm, rxp = neighbours(down, up, "bx")

    temb = time_embedding(timestep, time_weight.shape[0]).reshape(1, -1)
    raw, scene, columns, taps = call(
        interior,
        [like((1792, 128), F32), like((3, 16, 9, 16, 128), BF), like((3, 9, 128), F32), like((2304, 128), BF)],
        [info, lat_pairs, rz, rym, ryp, conv_weight],
        planes,
    )
    pair = (3, 2, 9, 16, 128)
    tables = jnp.asarray(coarse_table(), BF)
    act, ends, patch, stats = call(
        forward,
        [pltpu.HBM((2048, 128), F32), like((2, 3, 9, 16, 128), BF), like((16, 1728), BF), like((devices, 128), F32)],
        [info, scene, scene, raw, columns, rz, rym, ryp, rxm, rxp, pooled, taps]
        + [coarse_weight.reshape(1728, 64), temb, time_weight.T, tables],
        [pltpu.VMEM((2, 128, 128), F32), pltpu.VMEM((224, 160), BF), pltpu.SemaphoreType.DMA]
        + planes
        + [plane(X_TILES), plane(X_TILES)],
        [pl.BlockSpec(pair, lambda i: (0, 0, 0, 0, 0)), pl.BlockSpec(pair, lambda i: (0, 7, 0, 0, 0))],
        far_args=1,
    )
    first = exchange(stats)
    (turned,) = call(
        turn,
        [pltpu.HBM((3, 256, 18 * 128), BF)],
        [info, scene, ends],
        [pltpu.VMEM((3, 256, 18 * 128), BF), pltpu.SemaphoreType.DMA((3,))],
        far_outs=1,
    )
    gain, bias = twice(norm_gain), twice(norm_bias)
    weights = [diagonal(out_weight), diagonal(out_weight.T)]
    payload, other, predicted = call(
        backward(voxels),
        [like((2, 2048, 128), F32), like((2048, 128), F32), pltpu.HBM((16, 8, 2, 16, 64), BF)],
        [info, first, target.reshape(16, 8, 2, 16, 64), gain, bias] + weights + [patch, stats, in_hbm(act), in_hbm(turned)],
        [
            pltpu.VMEM((2048, 256), BF),
            pltpu.VMEM((2048, 128), F32),
            pltpu.VMEM((3, 256, 18 * 128), BF),
            pltpu.VMEM((16, 8, 2, 16, 64), BF),
            pltpu.SemaphoreType.DMA((3,)),
            pltpu.SemaphoreType.DMA,
            pltpu.SemaphoreType.DMA((2,)),
        ],
        far_args=2,
        far_outs=2,
    )
    swap = [(0, 1), (1, 0)]
    chips = devices // 2
    other = lax.ppermute(other, "cz", swap)
    (pieces,) = call(pair_add(voxels), [like((chips, 16, 128), BF)], [info, payload, other, first, gain])
    pieces = lax.all_to_all(pieces, CHIPS, 0, 0, tiled=True)
    copies, grad_time, grad_gain, grad_bias = call(
        combine(voxels),
        [like((chips, 8, 128), BF), like((64, 256), F32), like((1, 64), F32), like((1, 64), F32)],
        [info, pieces, first, gain, temb],
    )
    near = lax.all_to_all(copies, CHIPS, 0, 0, tiled=True)
    far = lax.ppermute(near, "cz", swap)
    grad_conv, grad_coarse, grad_out, loss = call(
        functools.partial(spread, 1.0 / (voxels * 64)),
        [like((27, 64, 64), F32), like((27, 64, 64), F32), like((64, 64), F32), like((1, 1), F32)],
        [info, near, far],
        [pltpu.VMEM((2048, 128), F32)],
    )
    return (
        predicted.reshape(latents.shape),
        loss.reshape(1),
        grad_conv,
        grad_coarse,
        grad_out,
        grad_time.T,
        grad_gain.reshape(64),
        grad_bias.reshape(64),
    )


def solution(mesh):
    blocks = P(ALL, None, None, None, None)
    return jax.shard_map(
        shards,
        mesh=mesh,
        in_specs=(blocks, blocks, P(ALL, None)) + (P(),) * 7,
        out_specs=(blocks,) + (P(),) * 7,
        check_vma=False,
    )
```

```python
import functools
import math

import jax
import jax.numpy as jnp
import numpy as np
from jax import lax
from jax.experimental import pallas as pl
from jax.experimental.pallas import tpu as pltpu
from jax.sharding import PartitionSpec as P

ALL = ("bx", "by", "cz")
CHIPS = ("bx", "by")
BF = jnp.bfloat16
F32 = jnp.float32
EPS = 1e-05
GROUP = 2
VMEM_LIMIT = 40 * 1024 * 1024
SHIFT_LANE = 65


def face_spec(dim, index):
    shape = tuple(1 if d == dim else 16 for d in range(3)) + (64,)
    where = tuple(index if d == dim else 0 for d in range(4))
    return pl.BlockSpec(shape, lambda i: where)


def call(kernel, outs, args, scratch=(), faces=(), far_args=0, far_outs=0):
    vmem = pl.BlockSpec(memory_space=pltpu.VMEM)
    far = pl.BlockSpec(memory_space=pl.ANY)
    specs = list(faces) + [vmem] * (len(args) - 1 - len(faces) - far_args) + [far] * far_args
    args = [
        pltpu.with_memory_space_constraint(arg, pltpu.VMEM) if spec is vmem else arg
        for arg, spec in zip(args, [None] + specs)
    ]
    return pl.pallas_call(
        kernel,
        grid=(1,),
        out_shape=outs,
        in_specs=[pl.BlockSpec(memory_space=pltpu.SMEM)] + specs,
        out_specs=[vmem] * (len(outs) - far_outs) + [far] * far_outs,
        scratch_shapes=list(scratch),
        compiler_params=pltpu.CompilerParams(vmem_limit_bytes=VMEM_LIMIT),
    )(*args)


def in_hbm(array):
    return pltpu.with_memory_space_constraint(array, pltpu.HBM)


def like(shape, dtype):
    return jax.ShapeDtypeStruct(shape, dtype)


def keep(cond, value):
    return jnp.where(cond, value, jnp.zeros_like(value))


def bits(info):
    return info[0, 0], info[0, 1], info[0, 2], lax.axis_index("cz")


def start16(bit):
    return pl.multiple_of(bit * 16, 16)


def cell_rows(first, second, face, on):
    rows = []
    for r in range(4):
        for s in range(4):
            here = on & (first == r // 2) & (second == s // 2)
            rows.append(keep(here, face[r % 2][s % 2]))
    return jnp.concatenate(rows, axis=0)


def row_of(cells, p):
    return cells[p : p + 1]


Z_TILES, Y_TILES, X_TILES = 1, 2, 5


def message(tiles):
    return like((9 + tiles, 16, 128), BF)


def plane(tiles):
    return pltpu.VMEM((32 + tiles, 32, 64), BF)


def side_by_side(rows):
    half = rows.shape[0] // 2
    return jnp.concatenate([rows[:half], rows[half:]], axis=rows.ndim - 1)


def write_message(out, face, tiles, first, second, on):
    out[0:8] = side_by_side(face)
    for t, rows in enumerate(tiles):
        out[8 + t] = side_by_side(rows).astype(BF)
    row = lax.broadcasted_iota(jnp.int32, (16, 128), 0)
    here = jnp.where(on, 2 * first + second, 99)
    out[8 + len(tiles)] = jnp.where(row == here, 1.0, 0.0).astype(BF)


def open_message(ref, out):
    tiles = ref.shape[0] - 9
    face = jnp.concatenate([ref[0:8, :, :64], ref[0:8, :, 64:]], axis=0)
    flags = ref[8 + tiles].astype(F32)
    for q in range(4):
        here = jnp.broadcast_to(flags[q : q + 1, :64], (16, 64))[None]
        out[16 * (q // 2) : 16 * (q // 2) + 16, 16 * (q % 2) : 16 * (q % 2) + 16, :] = jnp.where(
            here > 0.5, face.astype(F32), 0.0
        ).astype(BF)
    for t in range(tiles):
        out[32 + t] = jnp.concatenate([ref[8 + t, :, :64], ref[8 + t, :, 64:]], axis=0)


def z_message(info, lat, out, pooled):
    px, py, pz, kz = bits(info)
    zsel = 15 * (1 - kz)
    pick = lax.broadcasted_iota(jnp.int32, (16, 16, 64), 1) == zsel
    sums = [[None, None], [None, None]]
    faces = []
    for y in range(16):
        slab = lat[:, y].astype(F32)
        faces.append(jnp.sum(jnp.where(pick, slab, 0.0), axis=1)[None])
        for a in range(2):
            part = jnp.sum(slab[8 * a : 8 * a + 8], axis=0)
            old = sums[a][y // 8]
            sums[a][y // 8] = part if old is None else old + part
    cells = []
    for a in range(2):
        for b in range(2):
            for c in range(2):
                cells.append(jnp.sum(sums[a][b][8 * c : 8 * c + 8], axis=0, keepdims=True))
    cells = jnp.concatenate(cells, axis=0) * (1.0 / math.sqrt(512.0))
    cells = cells.astype(BF).astype(F32)
    pooled[...] = jnp.concatenate([cells, jnp.zeros((8, 64), F32)], axis=0).astype(BF)
    on = pz == 1 - kz
    face = [
        [jnp.where(kz == 0, row_of(cells, 4 * a + 2 * b + 1), row_of(cells, 4 * a + 2 * b)) for a in range(2)]
        for b in range(2)
    ]
    rows = jnp.concatenate([cell_rows(py, px, face, on), jnp.zeros((16, 64), F32)], axis=0)
    write_message(out, jnp.concatenate(faces, axis=0).astype(BF), [rows], py, px, on)


def y_messages(info, low, high, rz_in, pooled, down, up, rz):
    px, py, pz, kz = bits(info)
    open_message(rz_in, rz)
    cells = pooled[...].astype(F32)
    halo = rz[32].astype(F32)
    for out, face, bit, line, q in ((down, low, 0, 0, 0), (up, high, 1, 31, 1)):
        on = py == bit
        picked = [[row_of(cells, 4 * a + 2 * q + c) for c in range(2)] for a in range(2)]
        tail = halo[12:16] if q else halo[0:4]
        rows = jnp.concatenate([cell_rows(px, pz, picked, on), tail, jnp.zeros((12, 64), F32)], axis=0)
        write_message(out, face[:, 0], [rz[line], rows], px, pz, on)


def x_messages(info, low, high, rz_in, rym_in, ryp_in, pooled, down, up, rz, rym, ryp):
    px, py, pz, kz = bits(info)
    for ref, out in ((rz_in, rz), (rym_in, rym), (ryp_in, ryp)):
        open_message(ref, out)
    cells = pooled[...].astype(F32)
    halo = rz[32].astype(F32)
    halo_m = rym[33].astype(F32)
    halo_p = ryp[33].astype(F32)
    line_m = rym[32].astype(F32)
    line_p = ryp[32].astype(F32)
    where16 = lax.broadcasted_iota(jnp.int32, (32, 16, 64), 1)
    for out, face, bit, line, q in ((down, low, 0, 0, 0), (up, high, 1, 31, 1)):
        on = px == bit
        slab = rz[0:32, 16 * q : 16 * q + 16, :].astype(F32)
        z_line = jnp.sum(jnp.where(where16 == 15 * q, slab, 0.0), axis=1).astype(BF)
        picked = [[row_of(cells, 4 * q + 2 * b + c) for c in range(2)] for b in range(2)]
        corners = [line_m[line : line + 1], line_p[line : line + 1], jnp.zeros((14, 64), F32)]
        corners = jnp.concatenate(corners + [cell_rows(py, pz, picked, on)], axis=0)
        c0 = 3 * q
        parts = [row_of(halo, 4 * cy + c0) for cy in range(4)]
        parts += [halo_m[4 * c0 : 4 * c0 + 4], halo_p[4 * c0 : 4 * c0 + 4]]
        parts += [row_of(halo_m, 16 + c0), row_of(halo_p, 16 + c0), jnp.zeros((18, 64), F32)]
        tiles = [z_line, rym[line], ryp[line], corners, jnp.concatenate(parts, axis=0)]
        write_message(out, face[0], tiles, py, pz, on)


def coarse_table():
    pooled, rz, rym, ryp, rxm, rxp = 0, 16, 32, 64, 96, 128
    table = np.zeros((16, 224, 160), np.float32)
    for combo in range(16):
        bit = ((combo >> 3) & 1, (combo >> 2) & 1, (combo >> 1) & 1)
        core = combo & 1
        for tap in range(27):
            off = (tap // 9, tap // 3 % 3, tap % 3)
            for p in range(8):
                at = (p // 4, p // 2 % 2, p % 2)
                pos = [2 * bit[d] - 1 + off[d] + at[d] for d in range(3)]
                x, y, z = pos
                out_z = z < 0 or z > 3
                if out_z and (z < 0) != (core == 1):
                    continue
                if x < 0 or x > 3:
                    base = rxm if x < 0 else rxp
                    if y < 0 or y > 3:
                        side = 0 if y < 0 else 1
                        row = 16 + (12 + side if out_z else 4 + 4 * side + z)
                    else:
                        row = 16 + y if out_z else 4 * y + z
                    row = base + row
                elif y < 0 or y > 3:
                    row = (rym if y < 0 else ryp) + (16 + x if out_z else 4 * x + z)
                elif out_z:
                    row = rz + 4 * y + x
                else:
                    own = [pos[d] - 2 * bit[d] for d in range(3)]
                    if min(own) < 0 or max(own) > 1:
                        continue
                    row = pooled + 4 * own[0] + 2 * own[1] + own[2]
                table[combo, 8 * tap + p, row] = 1.0
    return table


class Window:
    def __init__(self, info, rz, rym, ryp):
        px, py, pz, kz = bits(info)
        self.pz, self.rz, self.rym, self.ryp = pz, rz, rym, ryp
        self.z0 = pl.ds(start16(pz), 16)
        self.z1 = pl.ds(start16(1 - pz), 16)
        self.xs = pl.ds(start16(px), 16)
        self.ys = pl.ds(start16(py), 16)
        self.xlo, self.xhi, self.ylo, self.yhi = px == 0, px == 1, py == 0, py == 1
        self.on_low = (pz == 0) & (kz == 1)
        self.on_high = (pz == 1) & (kz == 0)
        self.row16 = lax.broadcasted_iota(jnp.int32, (16, 16, 64), 1)
        self.z_row = lax.broadcasted_iota(jnp.int32, (9, 16, 128), 1)

    def edge(self, block):
        return jnp.sum(jnp.where(self.row16[: block.shape[0]] == 15 * self.pz, block.astype(F32), 0.0), axis=1)

    def edge1(self, ref, i):
        return self.edge(ref[i : i + 1, self.z1, :])

    def low_of(self, e, h):
        return keep(self.pz == 1, e) + keep(self.on_low, h)

    def high_of(self, e, h):
        return keep(self.pz == 0, e) + keep(self.on_high, h)

    def offsets(self, evens, odds, first, last, zl, zh):
        left = jnp.concatenate([first[None], odds], axis=0)
        right = jnp.concatenate([evens, last[None]], axis=0)
        tile = jnp.concatenate([left, right], axis=2)
        wide = tile.astype(F32)
        down = jnp.where(self.z_row == 0, zl, pltpu.roll(wide, 1, 1)).astype(BF)
        up = jnp.where(self.z_row == 15, zh, pltpu.roll(wide, 15, 1)).astype(BF)
        return down, tile, up


def one(ref, i, j):
    return ref[i].astype(F32)[j : j + 1]


def interior(info, lat, rz_in, rym_in, ryp_in, taps, raw, scene, columns, weight, rz, rym, ryp):
    for ref, out in ((rz_in, rz), (rym_in, rym), (ryp_in, ryp)):
        open_message(ref, out)
    nought = jnp.zeros((64, 64), BF)
    for tap in range(9):
        ox, oz = tap // 3, tap % 3
        for a in range(4):
            left = nought if a == 3 else taps[9 * ox + 3 * a + oz]
            right = nought if a == 0 else taps[9 * ox + 3 * a - 3 + oz]
            weight[256 * tap + 64 * a : 256 * tap + 64 * a + 64] = jnp.concatenate([left, right], axis=1)
    w = Window(info, rz, rym, ryp)
    y_low = keep(w.ylo, rym[w.xs, w.z0, :])
    y_high = keep(w.yhi, ryp[w.xs, w.z0, :])
    e_low = keep(w.ylo, w.edge(rym[w.xs, w.z1, :]))
    e_high = keep(w.yhi, w.edge(ryp[w.xs, w.z1, :]))
    h_low = jnp.where(w.ylo, rym[32, w.xs, :], rz[15, w.xs, :]).astype(F32)
    h_high = jnp.where(w.yhi, ryp[32, w.xs, :], rz[16, w.xs, :]).astype(F32)
    h_mid = rz[w.ys, w.xs, :].astype(F32)

    def packed(of):
        rows = [of(e_low, h_low)] + [of(jnp.zeros((16, 64), F32), h_mid[y]) for y in range(16)]
        rows.append(of(e_high, h_high))
        return [jnp.concatenate([rows[2 * k], rows[2 * k + 1]], axis=1) for k in range(9)]

    below, above = packed(w.low_of), packed(w.high_of)
    inner = [None] * 3
    for x in range(16):
        zl = jnp.concatenate([below[k][x : x + 1][None] for k in range(9)], axis=0)
        zh = jnp.concatenate([above[k][x : x + 1][None] for k in range(9)], axis=0)
        planes = w.offsets(lat[x, :, 0], lat[x, :, 1], y_low[x], y_high[x], zl, zh)
        for oz, plane in enumerate(planes):
            scene[oz, x] = plane
            wide = plane.astype(F32)
            inner[oz] = wide if x == 0 else inner[oz] + wide
    for oz in range(3):
        columns[oz] = jnp.sum(inner[oz], axis=1)
    for first, count in ((1, 4), (5, 4), (9, 4), (13, 2)):
        pieces = []
        for tap in range(9):
            ox, oz = tap // 3, tap % 3
            for dk in range(2):
                at = first + ox - 1
                pieces.append(scene[oz, at : at + count, dk : dk + 8].reshape(128 * count, 128))
        value = jnp.dot(jnp.concatenate(pieces, axis=1), weight[...], preferred_element_type=F32)
        raw[(first - 1) * 128 : (first - 1 + count) * 128] = value


def forward(
    info, near_low, near_high, raw, columns, rz_in, rym_in, ryp_in, rxm_in, rxp_in, pooled, weight,
    coarse_weight, temb, time_weight, tables, act, ends, patch_out, stats,
    shift, table, arrived, rz, rym, ryp, rxm, rxp
):
    px, py, pz, kz = bits(info)
    fetch = pltpu.make_async_copy(tables.at[8 * px + 4 * py + 2 * pz + kz], table, arrived)
    fetch.start()
    for ref, out in ((rz_in, rz), (rym_in, rym), (ryp_in, ryp), (rxm_in, rxm), (rxp_in, rxp)):
        open_message(ref, out)
    w = Window(info, rz, rym, ryp)
    nought = jnp.zeros((16, 64), BF)

    def sides(rx, out, inner):
        first = jnp.where(
            out,
            jnp.where(w.ylo, rx[33, w.z0, :], rx[15, w.z0, :]),
            jnp.where(w.ylo, rym[inner, w.z0, :], nought),
        )
        last = jnp.where(
            out,
            jnp.where(w.yhi, rx[34, w.z0, :], rx[16, w.z0, :]),
            jnp.where(w.yhi, ryp[inner, w.z0, :], nought),
        )
        return first, last

    def side_columns(rx, out, inner, of):
        half = rz[w.ys, 0:16, :] if inner < 16 else rz[w.ys, 16:32, :]
        inner_h = jnp.sum(jnp.where(w.row16 == inner % 16, half.astype(F32), 0.0), axis=1)
        e_mid = keep(out, w.edge(rx[w.ys, w.z1, :]))
        hh = jnp.where(out, rx[32, w.ys, :].astype(F32), inner_h)
        e_first = jnp.where(
            out,
            jnp.where(w.ylo, w.edge1(rx, 33), w.edge1(rx, 15)),
            keep(w.ylo, w.edge1(rym, inner)),
        )
        h_first = jnp.where(
            out,
            jnp.where(w.ylo, one(rx, 35, 0), one(rx, 32, 15)),
            jnp.where(w.ylo, one(rym, 32, inner), one(rz, 15, inner)),
        )
        e_last = jnp.where(
            out,
            jnp.where(w.yhi, w.edge1(rx, 34), w.edge1(rx, 16)),
            keep(w.yhi, w.edge1(ryp, inner)),
        )
        h_last = jnp.where(
            out,
            jnp.where(w.yhi, one(rx, 35, 1), one(rx, 32, 16)),
            jnp.where(w.yhi, one(ryp, 32, inner), one(rz, 16, inner)),
        )
        mid = of(e_mid, hh)
        rows = [of(e_first, h_first)] + [mid[y : y + 1] for y in range(16)] + [of(e_last, h_last)]
        return [jnp.concatenate([rows[2 * k], rows[2 * k + 1]], axis=1)[None] for k in range(9)]

    for e, rx, out, inner in ((0, rxm, w.xlo, 15), (1, rxp, w.xhi, 16)):
        zl = jnp.concatenate(side_columns(rx, out, inner, w.low_of), axis=0)
        zh = jnp.concatenate(side_columns(rx, out, inner, w.high_of), axis=0)
        first, last = sides(rx, out, inner)
        plane = keep(out, rx[w.ys, w.z0, :]).reshape(8, 2, 16, 64)
        for oz, tile in enumerate(w.offsets(plane[:, 0], plane[:, 1], first, last, zl, zh)):
            ends[e, oz] = tile

    source = jnp.concatenate(
        [pooled[...], rz[32, 0:16, :], rym[33], ryp[33], rxm[35, 16:32, :], rxm[36, 0:16, :], rxp[35, 16:32, :], rxp[36, 0:16, :]],
        axis=0,
    )
    fetch.wait()
    taps = jnp.dot(table[...], source, preferred_element_type=F32)
    patch = jnp.concatenate([taps[8 * t : 8 * t + 8] for t in range(27)], axis=1)
    patch_out[...] = jnp.concatenate([patch, patch], axis=0).astype(BF)
    coarse = jnp.dot(patch_out[...], coarse_weight[...], preferred_element_type=F32)
    coarse = coarse.astype(BF).astype(F32)
    coarse = jnp.concatenate([coarse, coarse], axis=1)
    time_bias = lax.dot_general(
        jnp.broadcast_to(temb[...], (8, 256)),
        time_weight[...].astype(F32),
        (((1,), (1,)), ((), ())),
        preferred_element_type=F32,
        precision=lax.Precision.HIGHEST,
    )[:1]
    time_bias = jnp.concatenate([time_bias, time_bias], axis=1)
    z_half = lax.broadcasted_iota(jnp.int32, (16, 128), 0) < 8
    added = []
    for q in range(4):
        added.append(jnp.where(z_half, coarse[2 * q : 2 * q + 1], coarse[2 * q + 1 : 2 * q + 2]) + time_bias)

    pieces = []
    for tap in range(9):
        ox, oz = tap // 3, tap % 3
        low = ends[0, oz] if ox == 0 else near_low[oz, ox - 1]
        high = ends[1, oz] if ox == 2 else near_high[oz, ox]
        for dk in range(2):
            pieces.append(jnp.concatenate([low[dk : dk + 8], high[dk : dk + 8]], axis=0).reshape(256, 128))
    edges = jnp.dot(jnp.concatenate(pieces, axis=1), weight[...], preferred_element_type=F32)

    total = jnp.zeros((1, 128), F32)
    squares = jnp.zeros((1, 128), F32)
    for x in range(16):
        if x == 0:
            value = edges[:128]
        elif x == 15:
            value = edges[128:]
        else:
            value = raw[(x - 1) * 128 : x * 128]
        value = value.reshape(2, 4, 16, 128)
        a = x // 8
        value = jnp.concatenate([(value[b] + added[2 * a + b][None])[None] for b in range(2)], axis=0).reshape(128, 128)
        act[x * 128 : x * 128 + 128] = value
        total = total + jnp.sum(value, axis=0, keepdims=True)
        squares = squares + jnp.sum(value * value, axis=0, keepdims=True)
    shift[...] = jnp.zeros(shift.shape, F32)

    def place(tap, slot, value):
        row = SHIFT_LANE + 2 * (tap // 4 + slot)
        u = tap % 4
        shift[u // 2, row : row + 1, 64 * (u % 2) : 64 * (u % 2) + 64] = value

    for oz in range(3):
        inner = columns[oz]
        planes = (ends[0, oz], near_low[oz, 0], near_high[oz, 1], ends[1, oz])
        outer = [jnp.sum(plane.astype(F32), axis=1) for plane in planes]
        for ox, part in enumerate((inner + outer[0] - outer[2], inner, inner - outer[1] + outer[3])):
            all_columns = jnp.sum(part, axis=0, keepdims=True)
            whole = all_columns[:, :64] + all_columns[:, 64:]
            y0, y1 = part[0:1, :64], part[0:1, 64:]
            y16, y17 = part[8:9, :64], part[8:9, 64:]
            for oy, window in enumerate((whole - y16 - y17, whole - y0 - y17, whole - y0 - y1)):
                place(9 * ox + 3 * oy + oz, 0, window)
    for t in range(27):
        place(t, 7, 512.0 * jnp.sum(taps[8 * t : 8 * t + 8], axis=0, keepdims=True))

    lane = lax.broadcasted_iota(jnp.int32, (1, 128), 1)
    pairs = pair_sum(squares + pltpu.roll(squares, 64, 1))
    row = jnp.where(lane < 64, total + pltpu.roll(total, 64, 1), jnp.where(lane % 2 == 0, pairs, 0.0))
    for u in range(2):
        stats[128 * u : 128 * u + 128] = shift[u].T + row


def turn(info, scene, ends, turned_out, turned, sent):
    for oz in range(3):
        for xp in range(18):
            for dk in range(2):
                tile = scene[oz, xp - 1, dk : dk + 8] if 1 <= xp <= 16 else ends[xp // 17, oz, dk : dk + 8]
                turned[oz, 128 * dk : 128 * dk + 128, 128 * xp : 128 * xp + 128] = tile.reshape(128, 128).T
        pltpu.make_async_copy(turned.at[oz], turned_out.at[oz], sent.at[oz]).start()
    for oz in range(3):
        pltpu.make_async_copy(turned.at[oz], turned_out.at[oz], sent.at[oz]).wait()


def pair_sum(row):
    lane = lax.broadcasted_iota(jnp.int32, row.shape, 1)
    return row + jnp.where(lane % 2 == 0, pltpu.roll(row, 127, 1), pltpu.roll(row, 1, 1))


def halves(row):
    lane = lax.broadcasted_iota(jnp.int32, row.shape, 1)
    other = pltpu.roll(row, 64, 1)
    return jnp.where(lane < 64, row, other), jnp.where(lane < 64, other, row)


def moments(gathered, count):
    row = jnp.sum(gathered[...], axis=0, keepdims=True)
    sums, upper = halves(row)
    lane = lax.broadcasted_iota(jnp.int32, row.shape, 1)
    squares = jnp.where(lane % 2 == 0, upper, pltpu.roll(upper, 1, 1))
    mean = pair_sum(sums) / count
    var = squares / count - mean * mean
    return row, sums, mean, 1.0 / jnp.sqrt(var + EPS)


def backward(voxels):
    count = float(voxels * GROUP)
    scale = 1.0 / (voxels * 64)

    def kernel(
        info, gathered, target, gain, bias, weight, weight_t, patch, stats, act_in, turned_in,
        payload, other, predicted_out, cotangent, act, turned, predicted, fetched, sent, shown_sent
    ):
        def chunk(n):
            rows = (pl.ds(0, 512), pl.ds(512, 1536))[n]
            return pltpu.make_async_copy(act_in.at[rows], act.at[rows], fetched.at[n])

        def show(n):
            part = (pl.ds(0, 4), pl.ds(4, 12))[n]
            return pltpu.make_async_copy(predicted.at[part], predicted_out.at[part], shown_sent.at[n])

        whole = pltpu.make_async_copy(turned_in, turned, fetched.at[2])
        for n in range(2):
            chunk(n).start()
        kz = lax.axis_index("cz")
        _, _, mean, rstd = moments(gathered, count)
        gains = jnp.zeros((1, 128), F32)
        biases = jnp.zeros((1, 128), F32)
        lost = jnp.zeros((1, 128), F32)
        outer = jnp.zeros((128, 128), F32)
        cells = [[None] * 4, [None] * 4]
        for x in range(0, 16, 2):
            rows = slice(x * 128, x * 128 + 256)
            if x == 0:
                chunk(0).wait()
                whole.start()
            if x == 4:
                show(0).start()
                chunk(1).wait()
            normalized = (act[rows] - mean) * rstd
            shifted = normalized * gain[...] + bias[...]
            sigma = jax.nn.sigmoid(shifted)
            hidden = (shifted * sigma).astype(BF)
            output = jnp.dot(hidden, weight[...], preferred_element_type=F32)
            goal = jnp.concatenate([target[x : x + 2, :, 0], target[x : x + 2, :, 1]], axis=3)
            residue = output - goal.reshape(256, 128).astype(F32)
            shown = output.astype(BF).reshape(2, 8, 16, 128)
            predicted[x : x + 2, :, 0] = shown[..., :64]
            predicted[x : x + 2, :, 1] = shown[..., 64:]
            upstream = (2.0 * scale * residue).astype(BF)
            back = jnp.dot(upstream, weight_t[...], preferred_element_type=F32)
            value = back * sigma * (1.0 + shifted * (1.0 - sigma))
            gains = gains + jnp.sum(value * normalized, axis=0, keepdims=True)
            biases = biases + jnp.sum(value, axis=0, keepdims=True)
            lost = lost + jnp.sum(residue * residue, axis=0, keepdims=True)
            outer = outer + lax.dot_general(hidden, upstream, (((0,), (0,)), ((), ())), preferred_element_type=F32)
            value = value * (gain[...] * rstd)
            narrow = [value.astype(BF), normalized.astype(BF)]
            cotangent[rows, :128] = jnp.concatenate([part[:, :64] for part in narrow], axis=1)
            cotangent[rows, 128:] = jnp.concatenate([part[:, 64:] for part in narrow], axis=1)
            for part, wide in enumerate((value, normalized)):
                planes = wide.reshape(2, 2, 4, 16, 128)
                for b in range(2):
                    q = 2 * (x // 8) + b
                    cell = jnp.sum(planes[:, b], axis=(0, 1))
                    old = cells[part][q]
                    cells[part][q] = cell if old is None else old + cell

        def store(tap, slot, value):
            u = tap % 4
            half = jnp.where(kz == u // 2, 0, 1)
            payload.at[half][pl.ds(1024 * (u % 2) + slot + tap // 4, 64, stride=16), :] = value

        rows = []
        for q in range(4):
            for c in range(2):
                sums = [jnp.sum(cells[p][q][8 * c : 8 * c + 8], axis=0, keepdims=True) for p in range(2)]
                rows.append(jnp.concatenate([r[:, :64] + r[:, 64:] for r in sums], axis=1))
        rows = jnp.concatenate(rows, axis=0)
        high = rows.astype(BF)
        split = jnp.concatenate([high.astype(F32), rows - high.astype(F32)], axis=0).astype(BF)
        coarse = lax.dot_general(patch[...], split, (((0,), (0,)), ((), ())), preferred_element_type=F32)
        for t in range(27):
            store(t, 7, coarse[64 * t : 64 * t + 64])
        show(1).start()
        whole.wait()
        for ox in range(3):
            windows = turned[:, :, 128 * ox : 128 * ox + 2048].reshape(768, 2048)
            products = jnp.dot(windows, cotangent[...], preferred_element_type=F32)
            for oz in range(3):
                product = products[256 * oz : 256 * oz + 256]
                for oy in range(3):
                    value = product[64 * oy : 64 * oy + 64, :128] + product[64 * oy + 64 : 64 * oy + 128, 128:]
                    store(9 * ox + 3 * oy + oz, 0, value)
        nought = jnp.zeros((64, 64), F32)
        store(27, 0, jnp.concatenate([outer[:64, :64] + outer[64:, 64:], nought], axis=1))
        loss = jnp.broadcast_to(jnp.sum(lost, axis=1, keepdims=True), (64, 128))
        high = loss.astype(BF).astype(F32)
        lane = lax.broadcasted_iota(jnp.int32, (64, 128), 1)
        split = jnp.where(lane == 2 * kz, high, jnp.where(lane == 2 * kz + 1, loss - high, 0.0))
        store(27, 7, split)
        lane = lax.broadcasted_iota(jnp.int32, (1, 128), 1)
        row = jnp.where(lane < 64, gains + pltpu.roll(gains, 64, 1), biases + pltpu.roll(biases, 64, 1))
        wide = jnp.broadcast_to(row, (128, 128))
        for half in range(2):
            payload.at[half][pl.ds(14, 128, stride=16), :] = wide
            slot = jnp.where(kz == half, 0, 1)
            payload.at[slot][pl.ds(15, 128, stride=16), :] = stats[128 * half : 128 * half + 128]
        copy = pltpu.make_async_copy(payload.at[1, pl.ds(0, 2048)], other, sent)
        copy.start()
        for n in range(2):
            show(n).wait()
        copy.wait()

    return kernel


def slopes(norms, gain, count):
    grad_gain, grad_bias = halves(norms)
    return pair_sum(gain * grad_bias) / count, pair_sum(gain * grad_gain) / count


def pair_add(voxels):
    total_count = float(voxels * GROUP)
    count = float(2 * 4096 * GROUP)

    def kernel(info, mine, other, gathered, gain, out):
        _, _, _, rstd = moments(gathered, total_count)
        total = (mine[0, 0:2048] + other[...]).reshape(-1, 16, 128)
        m1, m2 = slopes(total[0, 14:15], gain[...], count)
        row = lax.broadcasted_iota(jnp.int32, total.shape, 1)
        lane = lax.broadcasted_iota(jnp.int32, total.shape, 2)
        picked = (lane == SHIFT_LANE + 2 * row) & (row < 14)
        ones = jnp.sum(jnp.where(picked, total[:, 15:16], 0.0), axis=2, keepdims=True)
        centred = total - (m1 * rstd)[None] * ones - (m2 * rstd)[None] * pltpu.roll(total, 64, 2)
        total = jnp.where((lane < 64) & (row < 14), centred, total)
        lost = pltpu.roll(total - total.astype(BF).astype(F32), 1, 1)
        out[...] = jnp.where(row == 15, lost, total).astype(BF)

    return kernel


def combine(voxels):
    count = float(voxels * GROUP)
    pair_count = float(2 * 4096 * GROUP)

    def kernel(info, pieces, gathered, gain, temb, copies, grad_time, gain_out, bias_out):
        _, sums, mean, rstd = moments(gathered, count)
        value = pieces[...].astype(F32)
        chips = value.shape[0]
        seen = value[:, 14] + value[:, 15]
        norms = jnp.sum(seen, axis=0, keepdims=True)
        grad_gain, grad_bias = halves(norms)
        gain_out[...] = grad_gain[:, :64]
        bias_out[...] = grad_bias[:, :64]
        m1, m2 = slopes(norms, gain[...], count)
        centred = (sums - voxels * mean) * rstd
        act_sum = rstd * (gain[...] * grad_bias - voxels * m1 - m2 * centred)
        column = jnp.broadcast_to(act_sum, (128, 128)).T[:64]
        grad_time[...] = jnp.concatenate([column, column], axis=1) * temb[...]
        own1, own2 = slopes(seen, gain[...], pair_count)
        delta1, delta2 = (own1 - m1) * rstd, (own2 - m2) * rstd
        ones = gathered[0:chips] + gathered[chips : 2 * chips]
        back = lax.dot_general(
            ones, delta1, (((0,), (0,)), ((), ())), preferred_element_type=F32, precision=lax.Precision.HIGHEST
        )
        back = [back[SHIFT_LANE + 2 * r : SHIFT_LANE + 2 * r + 1] for r in range(14)]
        back = jnp.concatenate(back + [jnp.zeros((2, 128), F32)], axis=0)
        total = jnp.sum(value + delta2[:, None] * pltpu.roll(value, 64, 2), axis=0) + back
        lane = lax.broadcasted_iota(jnp.int32, (7, 128), 1)
        both = jnp.where(lane < 64, total[:7], pltpu.roll(total[7:14], 64, 1))
        lost = both[6:7] - both[6:7].astype(BF).astype(F32)
        piece = jnp.concatenate([both, lost], axis=0).astype(BF)
        copies[...] = jnp.broadcast_to(piece[None], copies.shape)

    return kernel


def spread(scale, info, near, far, conv, coarse, out, loss, rows):
    kz = lax.axis_index("cz")
    rows[pl.ds(pl.multiple_of(1024 * kz, 1024), 1024), :] = near[...].astype(F32).reshape(1024, 128)
    rows[pl.ds(pl.multiple_of(1024 * (1 - kz), 1024), 1024), :] = far[...].astype(F32).reshape(1024, 128)
    for tap in range(28):
        tile = rows[pl.ds(512 * (tap % 4) + tap // 4, 64, stride=8), :]
        if tap < 27:
            conv[tap] = tile[:, :64]
            coarse[tap] = tile[:, 64:]
        else:
            out[...] = tile[:, :64]
            parts = tile[0:1] + rows[2048 - 512 + 7 : 2048 - 512 + 8, :]
            lane = lax.broadcasted_iota(jnp.int32, (1, 128), 1)
            whole = jnp.sum(jnp.where((lane >= 64) & (lane < 68), parts, 0.0), axis=1, keepdims=True)
            loss[...] = whole * scale


def exchange(rows):
    out = lax.all_to_all(rows.reshape(rows.shape[0], 1, 128), ("cz",) + CHIPS, 0, 0, tiled=True)
    return out.reshape(rows.shape)


def neighbours(down, up, axis):
    ends = lax.axis_size(axis) - 1
    before = lax.ppermute(up, axis, [(i, i + 1) for i in range(ends)])
    after = lax.ppermute(down, axis, [(i + 1, i) for i in range(ends)])
    return before, after


def time_embedding(timestep, width):
    halfway = width // 2
    indices = jnp.arange(halfway).astype(F32)
    freqs = jnp.exp(indices * (-math.log(10000.0) / halfway))
    angles = timestep[0].astype(F32) * freqs
    return jnp.concatenate([jnp.sin(angles), jnp.cos(angles)])


def twice(row):
    return jnp.concatenate([row, row]).reshape(1, 128)


def diagonal(square):
    nought = jnp.zeros_like(square)
    return jnp.block([[square, nought], [nought, square]])


def shards(latents, target, block_coords, timestep, conv_weight, coarse_weight, out_weight, time_weight, norm_gain, norm_bias):
    devices = lax.axis_size("bx") * lax.axis_size("by") * lax.axis_size("cz")
    voxels = devices * 4096
    info = block_coords
    lat = latents[0]
    lat_pairs = lat.reshape(16, 8, 2, 16, 64)

    mz, pooled = call(z_message, [message(Z_TILES), like((16, 64), BF)], [info, lat])
    rz = lax.ppermute(mz, "cz", [(0, 1), (1, 0)])
    out = message(Y_TILES)
    down, up = call(
        y_messages, [out, out], [info, lat, lat, rz, pooled], [plane(Z_TILES)], [face_spec(1, 0), face_spec(1, 15)]
    )
    rym, ryp = neighbours(down, up, "by")
    out = message(X_TILES)
    planes = [plane(Z_TILES), plane(Y_TILES), plane(Y_TILES)]
    down, up = call(
        x_messages,
        [out, out],
        [info, lat, lat, rz, rym, ryp, pooled],
        planes,
        [face_spec(0, 0), face_spec(0, 15)],
    )
    rxm, rxp = neighbours(down, up, "bx")

    temb = time_embedding(timestep, time_weight.shape[0]).reshape(1, -1)
    raw, scene, columns, taps = call(
        interior,
        [like((1792, 128), F32), like((3, 16, 9, 16, 128), BF), like((3, 9, 128), F32), like((2304, 128), BF)],
        [info, lat_pairs, rz, rym, ryp, conv_weight],
        planes,
    )
    pair = (3, 2, 9, 16, 128)
    tables = jnp.asarray(coarse_table(), BF)
    act, ends, patch, stats = call(
        forward,
        [pltpu.HBM((2048, 128), F32), like((2, 3, 9, 16, 128), BF), like((16, 1728), BF), like((devices, 128), F32)],
        [info, scene, scene, raw, columns, rz, rym, ryp, rxm, rxp, pooled, taps]
        + [coarse_weight.reshape(1728, 64), temb, time_weight.T, tables],
        [pltpu.VMEM((2, 128, 128), F32), pltpu.VMEM((224, 160), BF), pltpu.SemaphoreType.DMA]
        + planes
        + [plane(X_TILES), plane(X_TILES)],
        [pl.BlockSpec(pair, lambda i: (0, 0, 0, 0, 0)), pl.BlockSpec(pair, lambda i: (0, 7, 0, 0, 0))],
        far_args=1,
    )
    first = exchange(stats)
    (turned,) = call(
        turn,
        [pltpu.HBM((3, 256, 18 * 128), BF)],
        [info, scene, ends],
        [pltpu.VMEM((3, 256, 18 * 128), BF), pltpu.SemaphoreType.DMA((3,))],
        far_outs=1,
    )
    gain, bias = twice(norm_gain), twice(norm_bias)
    weights = [diagonal(out_weight), diagonal(out_weight.T)]
    payload, other, predicted = call(
        backward(voxels),
        [like((2, 2064, 128), F32), like((2048, 128), F32), pltpu.HBM((16, 8, 2, 16, 64), BF)],
        [info, first, target.reshape(16, 8, 2, 16, 64), gain, bias] + weights + [patch, stats, in_hbm(act), in_hbm(turned)],
        [
            pltpu.VMEM((2048, 256), BF),
            pltpu.VMEM((2048, 128), F32),
            pltpu.VMEM((3, 256, 18 * 128), BF),
            pltpu.VMEM((16, 8, 2, 16, 64), BF),
            pltpu.SemaphoreType.DMA((3,)),
            pltpu.SemaphoreType.DMA,
            pltpu.SemaphoreType.DMA((2,)),
        ],
        far_args=2,
        far_outs=2,
    )
    swap = [(0, 1), (1, 0)]
    chips = devices // 2
    other = lax.ppermute(other, "cz", swap)
    (pieces,) = call(pair_add(voxels), [like((chips, 16, 128), BF)], [info, payload, other, first, gain])
    pieces = lax.all_to_all(pieces, CHIPS, 0, 0, tiled=True)
    copies, grad_time, grad_gain, grad_bias = call(
        combine(voxels),
        [like((chips, 8, 128), BF), like((64, 256), F32), like((1, 64), F32), like((1, 64), F32)],
        [info, pieces, first, gain, temb],
    )
    near = lax.all_to_all(copies, CHIPS, 0, 0, tiled=True)
    far = lax.ppermute(near, "cz", swap)
    grad_conv, grad_coarse, grad_out, loss = call(
        functools.partial(spread, 1.0 / (voxels * 64)),
        [like((27, 64, 64), F32), like((27, 64, 64), F32), like((64, 64), F32), like((1, 1), F32)],
        [info, near, far],
        [pltpu.VMEM((2056, 128), F32)],
    )
    return (
        predicted.reshape(latents.shape),
        loss.reshape(1),
        grad_conv,
        grad_coarse,
        grad_out,
        grad_time.T,
        grad_gain.reshape(64),
        grad_bias.reshape(64),
    )


def solution(mesh):
    blocks = P(ALL, None, None, None, None)
    return jax.shard_map(
        shards,
        mesh=mesh,
        in_specs=(blocks, blocks, P(ALL, None)) + (P(),) * 7,
        out_specs=(blocks,) + (P(),) * 7,
        check_vma=False,
    )
```

```python
import functools
import math

import jax
import jax.numpy as jnp
import numpy as np
from jax import lax
from jax.experimental import pallas as pl
from jax.experimental.pallas import tpu as pltpu
from jax.sharding import PartitionSpec as P

ALL = ("bx", "by", "cz")
CHIPS = ("bx", "by")
BF = jnp.bfloat16
F32 = jnp.float32
EPS = 1e-05
GROUP = 2
VMEM_LIMIT = 40 * 1024 * 1024
SHIFT_LANE = 65


def call(kernel, outs, args, scratch=(), far_args=0, far_outs=0, smem_outs=0):
    vmem = pl.BlockSpec(memory_space=pltpu.VMEM)
    far = pl.BlockSpec(memory_space=pl.ANY)
    smem = pl.BlockSpec(memory_space=pltpu.SMEM)
    specs = [vmem] * (len(args) - 1 - far_args) + [far] * far_args
    args = [
        pltpu.with_memory_space_constraint(arg, pltpu.VMEM) if spec is vmem else arg
        for arg, spec in zip(args, [None] + specs)
    ]
    return pl.pallas_call(
        kernel,
        grid=(1,),
        out_shape=outs,
        in_specs=[smem] + specs,
        out_specs=[vmem] * (len(outs) - far_outs - smem_outs) + [far] * far_outs + [smem] * smem_outs,
        scratch_shapes=list(scratch),
        compiler_params=pltpu.CompilerParams(vmem_limit_bytes=VMEM_LIMIT),
    )(*args)


def in_hbm(array):
    return pltpu.with_memory_space_constraint(array, pltpu.HBM)


def like(shape, dtype):
    return jax.ShapeDtypeStruct(shape, dtype)


def keep(cond, value):
    return jnp.where(cond, value, jnp.zeros_like(value))


def bits(info):
    return info[0, 0], info[0, 1], info[0, 2], lax.axis_index("cz")


def start16(bit):
    return pl.multiple_of(bit * 16, 16)


def cell_rows(first, second, face, on):
    rows = []
    for r in range(4):
        for s in range(4):
            here = on & (first == r // 2) & (second == s // 2)
            rows.append(keep(here, face[r % 2][s % 2]))
    return jnp.concatenate(rows, axis=0)


def row_of(cells, p):
    return cells[p : p + 1]


Z_TILES, Y_TILES, X_TILES = 1, 2, 5


def message(tiles):
    return like((9 + tiles, 16, 128), BF)


def plane(tiles):
    return pltpu.VMEM((32 + tiles, 32, 64), BF)


def side_by_side(rows):
    half = rows.shape[0] // 2
    return jnp.concatenate([rows[:half], rows[half:]], axis=rows.ndim - 1)


def write_message(out, face, tiles, first, second, on):
    out[0:8] = side_by_side(face)
    for t, rows in enumerate(tiles):
        out[8 + t] = side_by_side(rows).astype(BF)
    row = lax.broadcasted_iota(jnp.int32, (16, 128), 0)
    here = jnp.where(on, 2 * first + second, 99)
    out[8 + len(tiles)] = jnp.where(row == here, 1.0, 0.0).astype(BF)


def open_message(ref, out):
    tiles = ref.shape[0] - 9
    face = jnp.concatenate([ref[0:8, :, :64], ref[0:8, :, 64:]], axis=0)
    flags = ref[8 + tiles].astype(F32)
    for q in range(4):
        here = jnp.broadcast_to(flags[q : q + 1, :64], (16, 64))[None]
        out[16 * (q // 2) : 16 * (q // 2) + 16, 16 * (q % 2) : 16 * (q % 2) + 16, :] = jnp.where(
            here > 0.5, face.astype(F32), 0.0
        ).astype(BF)
    for t in range(tiles):
        out[32 + t] = jnp.concatenate([ref[8 + t, :, :64], ref[8 + t, :, 64:]], axis=0)


def z_message(info, lat_in, out, pooled, y_low, y_high, x_low, x_high, info_out, lat, fetched):
    px, py, pz, kz = bits(info)
    zsel = 15 * (1 - kz)
    for d in range(3):
        info_out[0, d] = info[0, d]

    def chunk(n):
        part = pl.ds(4 * n, 4)
        return pltpu.make_async_copy(lat_in.at[:, part], lat.at[:, part], fetched.at[n])

    for n in range(4):
        chunk(n).start()
    pick = lax.broadcasted_iota(jnp.int32, (16, 16, 64), 1) == zsel
    sums = [[None, None], [None, None]]
    faces = []
    for y in range(16):
        if y % 4 == 0:
            chunk(y // 4).wait()
        slab = lat[:, y].astype(F32)
        faces.append(jnp.sum(jnp.where(pick, slab, 0.0), axis=1)[None])
        for a in range(2):
            part = jnp.sum(slab[8 * a : 8 * a + 8], axis=0)
            old = sums[a][y // 8]
            sums[a][y // 8] = part if old is None else old + part
    y_low[...], y_high[...] = lat[:, 0], lat[:, 15]
    x_low[...], x_high[...] = lat[0], lat[15]
    cells = []
    for a in range(2):
        for b in range(2):
            for c in range(2):
                cells.append(jnp.sum(sums[a][b][8 * c : 8 * c + 8], axis=0, keepdims=True))
    cells = jnp.concatenate(cells, axis=0) * (1.0 / math.sqrt(512.0))
    cells = cells.astype(BF).astype(F32)
    pooled[...] = jnp.concatenate([cells, jnp.zeros((8, 64), F32)], axis=0).astype(BF)
    on = pz == 1 - kz
    face = [
        [jnp.where(kz == 0, row_of(cells, 4 * a + 2 * b + 1), row_of(cells, 4 * a + 2 * b)) for a in range(2)]
        for b in range(2)
    ]
    rows = jnp.concatenate([cell_rows(py, px, face, on), jnp.zeros((16, 64), F32)], axis=0)
    write_message(out, jnp.concatenate(faces, axis=0).astype(BF), [rows], py, px, on)


def y_messages(info, low, high, rz_in, pooled, down, up, rz):
    px, py, pz, kz = bits(info)
    open_message(rz_in, rz)
    cells = pooled[...].astype(F32)
    halo = rz[32].astype(F32)
    for out, face, bit, line, q in ((down, low, 0, 0, 0), (up, high, 1, 31, 1)):
        on = py == bit
        picked = [[row_of(cells, 4 * a + 2 * q + c) for c in range(2)] for a in range(2)]
        tail = halo[12:16] if q else halo[0:4]
        rows = jnp.concatenate([cell_rows(px, pz, picked, on), tail, jnp.zeros((12, 64), F32)], axis=0)
        write_message(out, face[...], [rz[line], rows], px, pz, on)


def x_messages(info, low, high, rz_in, rym_in, ryp_in, pooled, down, up, rz, rym, ryp):
    px, py, pz, kz = bits(info)
    for ref, out in ((rz_in, rz), (rym_in, rym), (ryp_in, ryp)):
        open_message(ref, out)
    cells = pooled[...].astype(F32)
    halo = rz[32].astype(F32)
    halo_m = rym[33].astype(F32)
    halo_p = ryp[33].astype(F32)
    line_m = rym[32].astype(F32)
    line_p = ryp[32].astype(F32)
    where16 = lax.broadcasted_iota(jnp.int32, (32, 16, 64), 1)
    for out, face, bit, line, q in ((down, low, 0, 0, 0), (up, high, 1, 31, 1)):
        on = px == bit
        slab = rz[0:32, 16 * q : 16 * q + 16, :].astype(F32)
        z_line = jnp.sum(jnp.where(where16 == 15 * q, slab, 0.0), axis=1).astype(BF)
        picked = [[row_of(cells, 4 * q + 2 * b + c) for c in range(2)] for b in range(2)]
        corners = [line_m[line : line + 1], line_p[line : line + 1], jnp.zeros((14, 64), F32)]
        corners = jnp.concatenate(corners + [cell_rows(py, pz, picked, on)], axis=0)
        c0 = 3 * q
        parts = [row_of(halo, 4 * cy + c0) for cy in range(4)]
        parts += [halo_m[4 * c0 : 4 * c0 + 4], halo_p[4 * c0 : 4 * c0 + 4]]
        parts += [row_of(halo_m, 16 + c0), row_of(halo_p, 16 + c0), jnp.zeros((18, 64), F32)]
        tiles = [z_line, rym[line], ryp[line], corners, jnp.concatenate(parts, axis=0)]
        write_message(out, face[...], tiles, py, pz, on)


def coarse_table():
    pooled, rz, rym, ryp, rxm, rxp = 0, 16, 32, 64, 96, 128
    table = np.zeros((16, 224, 160), np.float32)
    for combo in range(16):
        bit = ((combo >> 3) & 1, (combo >> 2) & 1, (combo >> 1) & 1)
        core = combo & 1
        for tap in range(27):
            off = (tap // 9, tap // 3 % 3, tap % 3)
            for p in range(8):
                at = (p // 4, p // 2 % 2, p % 2)
                pos = [2 * bit[d] - 1 + off[d] + at[d] for d in range(3)]
                x, y, z = pos
                out_z = z < 0 or z > 3
                if out_z and (z < 0) != (core == 1):
                    continue
                if x < 0 or x > 3:
                    base = rxm if x < 0 else rxp
                    if y < 0 or y > 3:
                        side = 0 if y < 0 else 1
                        row = 16 + (12 + side if out_z else 4 + 4 * side + z)
                    else:
                        row = 16 + y if out_z else 4 * y + z
                    row = base + row
                elif y < 0 or y > 3:
                    row = (rym if y < 0 else ryp) + (16 + x if out_z else 4 * x + z)
                elif out_z:
                    row = rz + 4 * y + x
                else:
                    own = [pos[d] - 2 * bit[d] for d in range(3)]
                    if min(own) < 0 or max(own) > 1:
                        continue
                    row = pooled + 4 * own[0] + 2 * own[1] + own[2]
                table[combo, 8 * tap + p, row] = 1.0
    return table


class Window:
    def __init__(self, info, rz, rym, ryp):
        px, py, pz, kz = bits(info)
        self.pz, self.rz, self.rym, self.ryp = pz, rz, rym, ryp
        self.z0 = pl.ds(start16(pz), 16)
        self.z1 = pl.ds(start16(1 - pz), 16)
        self.xs = pl.ds(start16(px), 16)
        self.ys = pl.ds(start16(py), 16)
        self.xlo, self.xhi, self.ylo, self.yhi = px == 0, px == 1, py == 0, py == 1
        self.on_low = (pz == 0) & (kz == 1)
        self.on_high = (pz == 1) & (kz == 0)
        self.row16 = lax.broadcasted_iota(jnp.int32, (16, 16, 64), 1)
        self.z_row = lax.broadcasted_iota(jnp.int32, (9, 16, 128), 1)

    def edge(self, block):
        return jnp.sum(jnp.where(self.row16[: block.shape[0]] == 15 * self.pz, block.astype(F32), 0.0), axis=1)

    def edge1(self, ref, i):
        return self.edge(ref[i : i + 1, self.z1, :])

    def low_of(self, e, h):
        return keep(self.pz == 1, e) + keep(self.on_low, h)

    def high_of(self, e, h):
        return keep(self.pz == 0, e) + keep(self.on_high, h)

    def offsets(self, evens, odds, first, last, zl, zh):
        left = jnp.concatenate([first[None], odds], axis=0)
        right = jnp.concatenate([evens, last[None]], axis=0)
        tile = jnp.concatenate([left, right], axis=2)
        wide = tile.astype(F32)
        down = jnp.where(self.z_row == 0, zl, pltpu.roll(wide, 1, 1)).astype(BF)
        up = jnp.where(self.z_row == 15, zh, pltpu.roll(wide, 15, 1)).astype(BF)
        return down, tile, up


def one(ref, i, j):
    return ref[i].astype(F32)[j : j + 1]


def interior(info, lat, rz_in, rym_in, ryp_in, taps, raw, scene, columns, weight, near_low, near_high, rz, rym, ryp):
    for ref, out in ((rz_in, rz), (rym_in, rym), (ryp_in, ryp)):
        open_message(ref, out)
    nought = jnp.zeros((64, 64), BF)
    for tap in range(9):
        ox, oz = tap // 3, tap % 3
        for a in range(4):
            left = nought if a == 3 else taps[9 * ox + 3 * a + oz]
            right = nought if a == 0 else taps[9 * ox + 3 * a - 3 + oz]
            weight[256 * tap + 64 * a : 256 * tap + 64 * a + 64] = jnp.concatenate([left, right], axis=1)
    w = Window(info, rz, rym, ryp)
    y_low = keep(w.ylo, rym[w.xs, w.z0, :])
    y_high = keep(w.yhi, ryp[w.xs, w.z0, :])
    e_low = keep(w.ylo, w.edge(rym[w.xs, w.z1, :]))
    e_high = keep(w.yhi, w.edge(ryp[w.xs, w.z1, :]))
    h_low = jnp.where(w.ylo, rym[32, w.xs, :], rz[15, w.xs, :]).astype(F32)
    h_high = jnp.where(w.yhi, ryp[32, w.xs, :], rz[16, w.xs, :]).astype(F32)
    h_mid = rz[w.ys, w.xs, :].astype(F32)

    def packed(of):
        rows = [of(e_low, h_low)] + [of(jnp.zeros((16, 64), F32), h_mid[y]) for y in range(16)]
        rows.append(of(e_high, h_high))
        return [jnp.concatenate([rows[2 * k], rows[2 * k + 1]], axis=1) for k in range(9)]

    below, above = packed(w.low_of), packed(w.high_of)
    inner = [None] * 3
    for x in range(16):
        zl = jnp.concatenate([below[k][x : x + 1][None] for k in range(9)], axis=0)
        zh = jnp.concatenate([above[k][x : x + 1][None] for k in range(9)], axis=0)
        planes = w.offsets(lat[x, :, 0], lat[x, :, 1], y_low[x], y_high[x], zl, zh)
        for oz, plane in enumerate(planes):
            scene[oz, x] = plane
            if x < 2:
                near_low[oz, x] = plane
            if x > 13:
                near_high[oz, x - 14] = plane
            wide = plane.astype(F32)
            inner[oz] = wide if x == 0 else inner[oz] + wide
    for oz in range(3):
        columns[oz] = jnp.sum(inner[oz], axis=1)
    for first, count in ((1, 4), (5, 4), (9, 4), (13, 2)):
        pieces = []
        for tap in range(9):
            ox, oz = tap // 3, tap % 3
            for dk in range(2):
                at = first + ox - 1
                pieces.append(scene[oz, at : at + count, dk : dk + 8].reshape(128 * count, 128))
        value = jnp.dot(jnp.concatenate(pieces, axis=1), weight[...], preferred_element_type=F32)
        raw[(first - 1) * 128 : (first - 1 + count) * 128] = value


def forward(
    info, near_low, near_high, raw, columns, rz_in, rym_in, ryp_in, rxm_in, rxp_in, pooled, weight,
    coarse_weight, temb, time_weight, tables, act, ends, patch_out, stats,
    shift, table, arrived, rz, rym, ryp, rxm, rxp
):
    px, py, pz, kz = bits(info)
    fetch = pltpu.make_async_copy(tables.at[8 * px + 4 * py + 2 * pz + kz], table, arrived)
    fetch.start()
    for ref, out in ((rz_in, rz), (rym_in, rym), (ryp_in, ryp), (rxm_in, rxm), (rxp_in, rxp)):
        open_message(ref, out)
    w = Window(info, rz, rym, ryp)
    nought = jnp.zeros((16, 64), BF)

    def sides(rx, out, inner):
        first = jnp.where(
            out,
            jnp.where(w.ylo, rx[33, w.z0, :], rx[15, w.z0, :]),
            jnp.where(w.ylo, rym[inner, w.z0, :], nought),
        )
        last = jnp.where(
            out,
            jnp.where(w.yhi, rx[34, w.z0, :], rx[16, w.z0, :]),
            jnp.where(w.yhi, ryp[inner, w.z0, :], nought),
        )
        return first, last

    def side_columns(rx, out, inner, of):
        half = rz[w.ys, 0:16, :] if inner < 16 else rz[w.ys, 16:32, :]
        inner_h = jnp.sum(jnp.where(w.row16 == inner % 16, half.astype(F32), 0.0), axis=1)
        e_mid = keep(out, w.edge(rx[w.ys, w.z1, :]))
        hh = jnp.where(out, rx[32, w.ys, :].astype(F32), inner_h)
        e_first = jnp.where(
            out,
            jnp.where(w.ylo, w.edge1(rx, 33), w.edge1(rx, 15)),
            keep(w.ylo, w.edge1(rym, inner)),
        )
        h_first = jnp.where(
            out,
            jnp.where(w.ylo, one(rx, 35, 0), one(rx, 32, 15)),
            jnp.where(w.ylo, one(rym, 32, inner), one(rz, 15, inner)),
        )
        e_last = jnp.where(
            out,
            jnp.where(w.yhi, w.edge1(rx, 34), w.edge1(rx, 16)),
            keep(w.yhi, w.edge1(ryp, inner)),
        )
        h_last = jnp.where(
            out,
            jnp.where(w.yhi, one(rx, 35, 1), one(rx, 32, 16)),
            jnp.where(w.yhi, one(ryp, 32, inner), one(rz, 16, inner)),
        )
        mid = of(e_mid, hh)
        rows = [of(e_first, h_first)] + [mid[y : y + 1] for y in range(16)] + [of(e_last, h_last)]
        return [jnp.concatenate([rows[2 * k], rows[2 * k + 1]], axis=1)[None] for k in range(9)]

    for e, rx, out, inner in ((0, rxm, w.xlo, 15), (1, rxp, w.xhi, 16)):
        zl = jnp.concatenate(side_columns(rx, out, inner, w.low_of), axis=0)
        zh = jnp.concatenate(side_columns(rx, out, inner, w.high_of), axis=0)
        first, last = sides(rx, out, inner)
        plane = keep(out, rx[w.ys, w.z0, :]).reshape(8, 2, 16, 64)
        for oz, tile in enumerate(w.offsets(plane[:, 0], plane[:, 1], first, last, zl, zh)):
            ends[e, oz] = tile

    source = jnp.concatenate(
        [pooled[...], rz[32, 0:16, :], rym[33], ryp[33], rxm[35, 16:32, :], rxm[36, 0:16, :], rxp[35, 16:32, :], rxp[36, 0:16, :]],
        axis=0,
    )
    fetch.wait()
    taps = jnp.dot(table[...], source, preferred_element_type=F32)
    patch = jnp.concatenate([taps[8 * t : 8 * t + 8] for t in range(27)], axis=1)
    patch_out[...] = jnp.concatenate([patch, patch], axis=0).astype(BF)
    coarse = jnp.dot(patch_out[...], coarse_weight[...], preferred_element_type=F32)
    coarse = coarse.astype(BF).astype(F32)
    coarse = jnp.concatenate([coarse, coarse], axis=1)
    time_bias = lax.dot_general(
        jnp.broadcast_to(temb[...], (8, 256)),
        time_weight[...].astype(F32),
        (((1,), (1,)), ((), ())),
        preferred_element_type=F32,
        precision=lax.Precision.HIGHEST,
    )[:1]
    time_bias = jnp.concatenate([time_bias, time_bias], axis=1)
    z_half = lax.broadcasted_iota(jnp.int32, (16, 128), 0) < 8
    added = []
    for q in range(4):
        added.append(jnp.where(z_half, coarse[2 * q : 2 * q + 1], coarse[2 * q + 1 : 2 * q + 2]) + time_bias)

    pieces = []
    for tap in range(9):
        ox, oz = tap // 3, tap % 3
        low = ends[0, oz] if ox == 0 else near_low[oz, ox - 1]
        high = ends[1, oz] if ox == 2 else near_high[oz, ox]
        for dk in range(2):
            pieces.append(jnp.concatenate([low[dk : dk + 8], high[dk : dk + 8]], axis=0).reshape(256, 128))
    edges = jnp.dot(jnp.concatenate(pieces, axis=1), weight[...], preferred_element_type=F32)

    total = jnp.zeros((1, 128), F32)
    squares = jnp.zeros((1, 128), F32)
    for x in range(16):
        if x == 0:
            value = edges[:128]
        elif x == 15:
            value = edges[128:]
        else:
            value = raw[(x - 1) * 128 : x * 128]
        value = value.reshape(2, 4, 16, 128)
        a = x // 8
        value = jnp.concatenate([(value[b] + added[2 * a + b][None])[None] for b in range(2)], axis=0).reshape(128, 128)
        act[x * 128 : x * 128 + 128] = value
        total = total + jnp.sum(value, axis=0, keepdims=True)
        squares = squares + jnp.sum(value * value, axis=0, keepdims=True)
    shift[...] = jnp.zeros(shift.shape, F32)

    def place(tap, slot, value):
        row = SHIFT_LANE + 2 * (tap // 4 + slot)
        u = tap % 4
        shift[u // 2, row : row + 1, 64 * (u % 2) : 64 * (u % 2) + 64] = value

    for oz in range(3):
        inner = columns[oz]
        planes = (ends[0, oz], near_low[oz, 0], near_high[oz, 1], ends[1, oz])
        outer = [jnp.sum(plane.astype(F32), axis=1) for plane in planes]
        for ox, part in enumerate((inner + outer[0] - outer[2], inner, inner - outer[1] + outer[3])):
            all_columns = jnp.sum(part, axis=0, keepdims=True)
            whole = all_columns[:, :64] + all_columns[:, 64:]
            y0, y1 = part[0:1, :64], part[0:1, 64:]
            y16, y17 = part[8:9, :64], part[8:9, 64:]
            for oy, window in enumerate((whole - y16 - y17, whole - y0 - y17, whole - y0 - y1)):
                place(9 * ox + 3 * oy + oz, 0, window)
    for t in range(27):
        place(t, 7, 512.0 * jnp.sum(taps[8 * t : 8 * t + 8], axis=0, keepdims=True))

    lane = lax.broadcasted_iota(jnp.int32, (1, 128), 1)
    pairs = pair_sum(squares + pltpu.roll(squares, 64, 1))
    row = jnp.where(lane < 64, total + pltpu.roll(total, 64, 1), jnp.where(lane % 2 == 0, pairs, 0.0))
    for u in range(2):
        stats[128 * u : 128 * u + 128] = shift[u].T + row


def turn(info, scene, ends, turned_out, turned, sent):
    for oz in range(3):
        for xp in range(18):
            for dk in range(2):
                tile = scene[oz, xp - 1, dk : dk + 8] if 1 <= xp <= 16 else ends[xp // 17, oz, dk : dk + 8]
                turned[oz, 128 * dk : 128 * dk + 128, 128 * xp : 128 * xp + 128] = tile.reshape(128, 128).T
        pltpu.make_async_copy(turned.at[oz], turned_out.at[oz], sent.at[oz]).start()
    for oz in range(3):
        pltpu.make_async_copy(turned.at[oz], turned_out.at[oz], sent.at[oz]).wait()


def pair_sum(row):
    lane = lax.broadcasted_iota(jnp.int32, row.shape, 1)
    return row + jnp.where(lane % 2 == 0, pltpu.roll(row, 127, 1), pltpu.roll(row, 1, 1))


def halves(row):
    lane = lax.broadcasted_iota(jnp.int32, row.shape, 1)
    other = pltpu.roll(row, 64, 1)
    return jnp.where(lane < 64, row, other), jnp.where(lane < 64, other, row)


def moments(gathered, count):
    row = jnp.sum(gathered[...], axis=0, keepdims=True)
    sums, upper = halves(row)
    lane = lax.broadcasted_iota(jnp.int32, row.shape, 1)
    squares = jnp.where(lane % 2 == 0, upper, pltpu.roll(upper, 1, 1))
    mean = pair_sum(sums) / count
    var = squares / count - mean * mean
    return row, sums, mean, 1.0 / jnp.sqrt(var + EPS)


def backward(voxels):
    count = float(voxels * GROUP)
    scale = 1.0 / (voxels * 64)

    def kernel(
        info, gathered, target, gain, bias, weight, weight_t, patch, stats, act_in, turned_in,
        payload, other, predicted_out, cotangent, act, turned, predicted, fetched, sent, shown_sent
    ):
        def chunk(n):
            rows = (pl.ds(0, 512), pl.ds(512, 1536))[n]
            return pltpu.make_async_copy(act_in.at[rows], act.at[rows], fetched.at[n])

        def show(n):
            part = (pl.ds(0, 4), pl.ds(4, 12))[n]
            return pltpu.make_async_copy(predicted.at[part], predicted_out.at[part], shown_sent.at[n])

        whole = pltpu.make_async_copy(turned_in, turned, fetched.at[2])
        for n in range(2):
            chunk(n).start()
        kz = lax.axis_index("cz")
        _, _, mean, rstd = moments(gathered, count)
        gains = jnp.zeros((1, 128), F32)
        biases = jnp.zeros((1, 128), F32)
        lost = jnp.zeros((1, 128), F32)
        outer = jnp.zeros((128, 128), F32)
        cells = [[None] * 4, [None] * 4]
        for x in range(0, 16, 2):
            rows = slice(x * 128, x * 128 + 256)
            if x == 0:
                chunk(0).wait()
                whole.start()
            if x == 4:
                show(0).start()
                chunk(1).wait()
            normalized = (act[rows] - mean) * rstd
            shifted = normalized * gain[...] + bias[...]
            sigma = jax.nn.sigmoid(shifted)
            hidden = (shifted * sigma).astype(BF)
            output = jnp.dot(hidden, weight[...], preferred_element_type=F32)
            goal = jnp.concatenate([target[x : x + 2, :, 0], target[x : x + 2, :, 1]], axis=3)
            residue = output - goal.reshape(256, 128).astype(F32)
            shown = output.astype(BF).reshape(2, 8, 16, 128)
            predicted[x : x + 2, :, 0] = shown[..., :64]
            predicted[x : x + 2, :, 1] = shown[..., 64:]
            upstream = (2.0 * scale * residue).astype(BF)
            back = jnp.dot(upstream, weight_t[...], preferred_element_type=F32)
            value = back * sigma * (1.0 + shifted * (1.0 - sigma))
            gains = gains + jnp.sum(value * normalized, axis=0, keepdims=True)
            biases = biases + jnp.sum(value, axis=0, keepdims=True)
            lost = lost + jnp.sum(residue * residue, axis=0, keepdims=True)
            outer = outer + lax.dot_general(hidden, upstream, (((0,), (0,)), ((), ())), preferred_element_type=F32)
            value = value * (gain[...] * rstd)
            narrow = [value.astype(BF), normalized.astype(BF)]
            cotangent[rows, :128] = jnp.concatenate([part[:, :64] for part in narrow], axis=1)
            cotangent[rows, 128:] = jnp.concatenate([part[:, 64:] for part in narrow], axis=1)
            for part, wide in enumerate((value, normalized)):
                planes = wide.reshape(2, 2, 4, 16, 128)
                for b in range(2):
                    q = 2 * (x // 8) + b
                    cell = jnp.sum(planes[:, b], axis=(0, 1))
                    old = cells[part][q]
                    cells[part][q] = cell if old is None else old + cell

        def store(tap, slot, value):
            u = tap % 4
            half = jnp.where(kz == u // 2, 0, 1)
            payload.at[half][pl.ds(1024 * (u % 2) + slot + tap // 4, 64, stride=16), :] = value

        rows = []
        for q in range(4):
            for c in range(2):
                sums = [jnp.sum(cells[p][q][8 * c : 8 * c + 8], axis=0, keepdims=True) for p in range(2)]
                rows.append(jnp.concatenate([r[:, :64] + r[:, 64:] for r in sums], axis=1))
        rows = jnp.concatenate(rows, axis=0)
        high = rows.astype(BF)
        split = jnp.concatenate([high.astype(F32), rows - high.astype(F32)], axis=0).astype(BF)
        coarse = lax.dot_general(patch[...], split, (((0,), (0,)), ((), ())), preferred_element_type=F32)
        for t in range(27):
            store(t, 7, coarse[64 * t : 64 * t + 64])
        show(1).start()
        whole.wait()
        for ox in range(3):
            windows = turned[:, :, 128 * ox : 128 * ox + 2048].reshape(768, 2048)
            products = jnp.dot(windows, cotangent[...], preferred_element_type=F32)
            for oz in range(3):
                product = products[256 * oz : 256 * oz + 256]
                for oy in range(3):
                    value = product[64 * oy : 64 * oy + 64, :128] + product[64 * oy + 64 : 64 * oy + 128, 128:]
                    store(9 * ox + 3 * oy + oz, 0, value)
        nought = jnp.zeros((64, 64), F32)
        store(27, 0, jnp.concatenate([outer[:64, :64] + outer[64:, 64:], nought], axis=1))
        loss = jnp.broadcast_to(jnp.sum(lost, axis=1, keepdims=True), (64, 128))
        high = loss.astype(BF).astype(F32)
        lane = lax.broadcasted_iota(jnp.int32, (64, 128), 1)
        split = jnp.where(lane == 2 * kz, high, jnp.where(lane == 2 * kz + 1, loss - high, 0.0))
        store(27, 7, split)
        lane = lax.broadcasted_iota(jnp.int32, (1, 128), 1)
        row = jnp.where(lane < 64, gains + pltpu.roll(gains, 64, 1), biases + pltpu.roll(biases, 64, 1))
        wide = jnp.broadcast_to(row, (128, 128))
        for half in range(2):
            payload.at[half][pl.ds(14, 128, stride=16), :] = wide
            slot = jnp.where(kz == half, 0, 1)
            payload.at[slot][pl.ds(15, 128, stride=16), :] = stats[128 * half : 128 * half + 128]
        copy = pltpu.make_async_copy(payload.at[1, pl.ds(0, 2048)], other, sent)
        copy.start()
        for n in range(2):
            show(n).wait()
        copy.wait()

    return kernel


def slopes(norms, gain, count):
    grad_gain, grad_bias = halves(norms)
    return pair_sum(gain * grad_bias) / count, pair_sum(gain * grad_gain) / count


def pair_add(voxels):
    total_count = float(voxels * GROUP)
    count = float(2 * 4096 * GROUP)

    def kernel(info, mine, other, gathered, gain, out):
        _, _, _, rstd = moments(gathered, total_count)
        total = (mine[0, 0:2048] + other[...]).reshape(-1, 16, 128)
        m1, m2 = slopes(total[0, 14:15], gain[...], count)
        row = lax.broadcasted_iota(jnp.int32, total.shape, 1)
        lane = lax.broadcasted_iota(jnp.int32, total.shape, 2)
        picked = (lane == SHIFT_LANE + 2 * row) & (row < 14)
        ones = jnp.sum(jnp.where(picked, total[:, 15:16], 0.0), axis=2, keepdims=True)
        centred = total - (m1 * rstd)[None] * ones - (m2 * rstd)[None] * pltpu.roll(total, 64, 2)
        total = jnp.where((lane < 64) & (row < 14), centred, total)
        lost = pltpu.roll(total - total.astype(BF).astype(F32), 1, 1)
        out[...] = jnp.where(row == 15, lost, total).astype(BF)

    return kernel


def combine(voxels):
    count = float(voxels * GROUP)
    pair_count = float(2 * 4096 * GROUP)

    def kernel(info, pieces, gathered, gain, temb, copies, grad_time, gain_out, bias_out):
        _, sums, mean, rstd = moments(gathered, count)
        value = pieces[...].astype(F32)
        chips = value.shape[0]
        seen = value[:, 14] + value[:, 15]
        norms = jnp.sum(seen, axis=0, keepdims=True)
        grad_gain, grad_bias = halves(norms)
        gain_out[...] = grad_gain[:, :64]
        bias_out[...] = grad_bias[:, :64]
        m1, m2 = slopes(norms, gain[...], count)
        centred = (sums - voxels * mean) * rstd
        act_sum = rstd * (gain[...] * grad_bias - voxels * m1 - m2 * centred)
        column = jnp.broadcast_to(act_sum, (128, 128)).T[:64]
        grad_time[...] = jnp.concatenate([column, column], axis=1) * temb[...]
        own1, own2 = slopes(seen, gain[...], pair_count)
        delta1, delta2 = (own1 - m1) * rstd, (own2 - m2) * rstd
        ones = gathered[0:chips] + gathered[chips : 2 * chips]
        back = lax.dot_general(
            ones, delta1, (((0,), (0,)), ((), ())), preferred_element_type=F32, precision=lax.Precision.HIGHEST
        )
        back = [back[SHIFT_LANE + 2 * r : SHIFT_LANE + 2 * r + 1] for r in range(14)]
        back = jnp.concatenate(back + [jnp.zeros((2, 128), F32)], axis=0)
        total = jnp.sum(value + delta2[:, None] * pltpu.roll(value, 64, 2), axis=0) + back
        lane = lax.broadcasted_iota(jnp.int32, (7, 128), 1)
        both = jnp.where(lane < 64, total[:7], pltpu.roll(total[7:14], 64, 1))
        lost = both[6:7] - both[6:7].astype(BF).astype(F32)
        piece = jnp.concatenate([both, lost], axis=0).astype(BF)
        copies[...] = jnp.broadcast_to(piece[None], copies.shape)

    return kernel


def spread(scale, info, near, far, conv, coarse, out, loss, rows):
    kz = lax.axis_index("cz")
    rows[pl.ds(pl.multiple_of(1024 * kz, 1024), 1024), :] = near[...].astype(F32).reshape(1024, 128)
    rows[pl.ds(pl.multiple_of(1024 * (1 - kz), 1024), 1024), :] = far[...].astype(F32).reshape(1024, 128)
    for tap in range(28):
        tile = rows[pl.ds(512 * (tap % 4) + tap // 4, 64, stride=8), :]
        if tap < 27:
            conv[tap] = tile[:, :64]
            coarse[tap] = tile[:, 64:]
        else:
            out[...] = tile[:, :64]
            parts = tile[0:1] + rows[2048 - 512 + 7 : 2048 - 512 + 8, :]
            lane = lax.broadcasted_iota(jnp.int32, (1, 128), 1)
            whole = jnp.sum(jnp.where((lane >= 64) & (lane < 68), parts, 0.0), axis=1, keepdims=True)
            loss[...] = whole * scale


def exchange(rows):
    out = lax.all_to_all(rows.reshape(rows.shape[0], 1, 128), ("cz",) + CHIPS, 0, 0, tiled=True)
    return out.reshape(rows.shape)


def neighbours(down, up, axis):
    ends = lax.axis_size(axis) - 1
    before = lax.ppermute(up, axis, [(i, i + 1) for i in range(ends)])
    after = lax.ppermute(down, axis, [(i + 1, i) for i in range(ends)])
    return before, after


def time_embedding(timestep, width):
    halfway = width // 2
    indices = jnp.arange(halfway).astype(F32)
    freqs = jnp.exp(indices * (-math.log(10000.0) / halfway))
    angles = timestep[0].astype(F32) * freqs
    return jnp.concatenate([jnp.sin(angles), jnp.cos(angles)])


def twice(row):
    return jnp.concatenate([row, row]).reshape(1, 128)


def diagonal(square):
    nought = jnp.zeros_like(square)
    return jnp.block([[square, nought], [nought, square]])


def shards(latents, target, block_coords, timestep, conv_weight, coarse_weight, out_weight, time_weight, norm_gain, norm_bias):
    devices = lax.axis_size("bx") * lax.axis_size("by") * lax.axis_size("cz")
    voxels = devices * 4096
    info = block_coords
    lat = latents[0]
    lat_pairs = lat.reshape(16, 8, 2, 16, 64)

    face = like((16, 16, 64), BF)
    mz, pooled, y_low, y_high, x_low, x_high, info = call(
        z_message,
        [message(Z_TILES), like((16, 64), BF), face, face, face, face, like((1, 3), jnp.int32)],
        [in_hbm(info), in_hbm(lat)],
        [pltpu.VMEM((16, 16, 16, 64), BF), pltpu.SemaphoreType.DMA((4,))],
        far_args=1,
        smem_outs=1,
    )
    rz = lax.ppermute(mz, "cz", [(0, 1), (1, 0)])
    out = message(Y_TILES)
    down, up = call(y_messages, [out, out], [info, y_low, y_high, rz, pooled], [plane(Z_TILES)])
    rym, ryp = neighbours(down, up, "by")
    out = message(X_TILES)
    planes = [plane(Z_TILES), plane(Y_TILES), plane(Y_TILES)]
    down, up = call(
        x_messages,
        [out, out],
        [info, x_low, x_high, rz, rym, ryp, pooled],
        planes,
    )
    rxm, rxp = neighbours(down, up, "bx")

    temb = time_embedding(timestep, time_weight.shape[0]).reshape(1, -1)
    pair = like((3, 2, 9, 16, 128), BF)
    raw, scene, columns, taps, near_low, near_high = call(
        interior,
        [like((1792, 128), F32), like((3, 16, 9, 16, 128), BF), like((3, 9, 128), F32), like((2304, 128), BF), pair, pair],
        [info, lat_pairs, rz, rym, ryp, conv_weight],
        planes,
    )
    tables = jnp.asarray(coarse_table(), BF)
    act, ends, patch, stats = call(
        forward,
        [pltpu.HBM((2048, 128), F32), like((2, 3, 9, 16, 128), BF), like((16, 1728), BF), like((devices, 128), F32)],
        [info, near_low, near_high, raw, columns, rz, rym, ryp, rxm, rxp, pooled, taps]
        + [coarse_weight.reshape(1728, 64), temb, time_weight.T, tables],
        [pltpu.VMEM((2, 128, 128), F32), pltpu.VMEM((224, 160), BF), pltpu.SemaphoreType.DMA]
        + planes
        + [plane(X_TILES), plane(X_TILES)],
        far_args=1,
    )
    first = exchange(stats)
    (turned,) = call(
        turn,
        [pltpu.HBM((3, 256, 18 * 128), BF)],
        [info, scene, ends],
        [pltpu.VMEM((3, 256, 18 * 128), BF), pltpu.SemaphoreType.DMA((3,))],
        far_outs=1,
    )
    gain, bias = twice(norm_gain), twice(norm_bias)
    weights = [diagonal(out_weight), diagonal(out_weight.T)]
    payload, other, predicted = call(
        backward(voxels),
        [like((2, 2064, 128), F32), like((2048, 128), F32), pltpu.HBM((16, 8, 2, 16, 64), BF)],
        [info, first, target.reshape(16, 8, 2, 16, 64), gain, bias] + weights + [patch, stats, in_hbm(act), in_hbm(turned)],
        [
            pltpu.VMEM((2048, 256), BF),
            pltpu.VMEM((2048, 128), F32),
            pltpu.VMEM((3, 256, 18 * 128), BF),
            pltpu.VMEM((16, 8, 2, 16, 64), BF),
            pltpu.SemaphoreType.DMA((3,)),
            pltpu.SemaphoreType.DMA,
            pltpu.SemaphoreType.DMA((2,)),
        ],
        far_args=2,
        far_outs=2,
    )
    swap = [(0, 1), (1, 0)]
    chips = devices // 2
    other = lax.ppermute(other, "cz", swap)
    (pieces,) = call(pair_add(voxels), [like((chips, 16, 128), BF)], [info, payload, other, first, gain])
    pieces = lax.all_to_all(pieces, CHIPS, 0, 0, tiled=True)
    copies, grad_time, grad_gain, grad_bias = call(
        combine(voxels),
        [like((chips, 8, 128), BF), like((64, 256), F32), like((1, 64), F32), like((1, 64), F32)],
        [info, pieces, first, gain, temb],
    )
    near = lax.all_to_all(copies, CHIPS, 0, 0, tiled=True)
    far = lax.ppermute(near, "cz", swap)
    grad_conv, grad_coarse, grad_out, loss = call(
        functools.partial(spread, 1.0 / (voxels * 64)),
        [like((27, 64, 64), F32), like((27, 64, 64), F32), like((64, 64), F32), like((1, 1), F32)],
        [info, near, far],
        [pltpu.VMEM((2056, 128), F32)],
    )
    return (
        predicted.reshape(latents.shape),
        loss.reshape(1),
        grad_conv,
        grad_coarse,
        grad_out,
        grad_time.T,
        grad_gain.reshape(64),
        grad_bias.reshape(64),
    )


def solution(mesh):
    blocks = P(ALL, None, None, None, None)
    return jax.shard_map(
        shards,
        mesh=mesh,
        in_specs=(blocks, blocks, P(ALL, None)) + (P(),) * 7,
        out_specs=(blocks,) + (P(),) * 7,
        check_vma=False,
    )
```

```python
import functools
import math

import jax
import jax.numpy as jnp
import numpy as np
from jax import lax
from jax.experimental import pallas as pl
from jax.experimental.pallas import tpu as pltpu
from jax.sharding import PartitionSpec as P

ALL = ("bx", "by", "cz")
CHIPS = ("bx", "by")
BF = jnp.bfloat16
F32 = jnp.float32
EPS = 1e-05
GROUP = 2
VMEM_LIMIT = 40 * 1024 * 1024
SHIFT_LANE = 65


def face_spec(dim, index):
    shape = tuple(1 if d == dim else 16 for d in range(3)) + (64,)
    where = tuple(index if d == dim else 0 for d in range(4))
    return pl.BlockSpec(shape, lambda i: where)


def call(kernel, outs, args, scratch=(), faces=(), far_args=0, far_outs=0):
    vmem = pl.BlockSpec(memory_space=pltpu.VMEM)
    far = pl.BlockSpec(memory_space=pl.ANY)
    specs = list(faces) + [vmem] * (len(args) - 1 - len(faces) - far_args) + [far] * far_args
    args = [
        pltpu.with_memory_space_constraint(arg, pltpu.VMEM) if spec is vmem else arg
        for arg, spec in zip(args, [None] + specs)
    ]
    return pl.pallas_call(
        kernel,
        grid=(1,),
        out_shape=outs,
        in_specs=[pl.BlockSpec(memory_space=pltpu.SMEM)] + specs,
        out_specs=[vmem] * (len(outs) - far_outs) + [far] * far_outs,
        scratch_shapes=list(scratch),
        compiler_params=pltpu.CompilerParams(vmem_limit_bytes=VMEM_LIMIT),
    )(*args)


def in_hbm(array):
    return pltpu.with_memory_space_constraint(array, pltpu.HBM)


def like(shape, dtype):
    return jax.ShapeDtypeStruct(shape, dtype)


def keep(cond, value):
    return jnp.where(cond, value, jnp.zeros_like(value))


def bits(info):
    return info[0, 0], info[0, 1], info[0, 2], lax.axis_index("cz")


def start16(bit):
    return pl.multiple_of(bit * 16, 16)


def cell_rows(first, second, face, on):
    rows = []
    for r in range(4):
        for s in range(4):
            here = on & (first == r // 2) & (second == s // 2)
            rows.append(keep(here, face[r % 2][s % 2]))
    return jnp.concatenate(rows, axis=0)


def row_of(cells, p):
    return cells[p : p + 1]


Z_TILES, Y_TILES, X_TILES = 1, 2, 5


def message(tiles):
    return like((9 + tiles, 16, 128), BF)


def plane(tiles):
    return pltpu.VMEM((32 + tiles, 32, 64), BF)


def side_by_side(rows):
    half = rows.shape[0] // 2
    return jnp.concatenate([rows[:half], rows[half:]], axis=rows.ndim - 1)


def write_message(out, face, tiles, first, second, on):
    out[0:8] = side_by_side(face)
    for t, rows in enumerate(tiles):
        out[8 + t] = side_by_side(rows).astype(BF)
    row = lax.broadcasted_iota(jnp.int32, (16, 128), 0)
    here = jnp.where(on, 2 * first + second, 99)
    out[8 + len(tiles)] = jnp.where(row == here, 1.0, 0.0).astype(BF)


def open_message(ref, out):
    tiles = ref.shape[0] - 9
    face = jnp.concatenate([ref[0:8, :, :64], ref[0:8, :, 64:]], axis=0)
    flags = ref[8 + tiles].astype(F32)
    for q in range(4):
        here = jnp.broadcast_to(flags[q : q + 1, :64], (16, 64))[None]
        out[16 * (q // 2) : 16 * (q // 2) + 16, 16 * (q % 2) : 16 * (q % 2) + 16, :] = jnp.where(
            here > 0.5, face.astype(F32), 0.0
        ).astype(BF)
    for t in range(tiles):
        out[32 + t] = jnp.concatenate([ref[8 + t, :, :64], ref[8 + t, :, 64:]], axis=0)


def z_message(info, lat, out, pooled):
    px, py, pz, kz = bits(info)
    zsel = 15 * (1 - kz)
    pick = lax.broadcasted_iota(jnp.int32, (16, 16, 64), 1) == zsel
    sums = [[None, None], [None, None]]
    faces = []
    for y in range(16):
        slab = lat[:, y].astype(F32)
        faces.append(jnp.sum(jnp.where(pick, slab, 0.0), axis=1)[None])
        for a in range(2):
            part = jnp.sum(slab[8 * a : 8 * a + 8], axis=0)
            old = sums[a][y // 8]
            sums[a][y // 8] = part if old is None else old + part
    cells = []
    for a in range(2):
        for b in range(2):
            for c in range(2):
                cells.append(jnp.sum(sums[a][b][8 * c : 8 * c + 8], axis=0, keepdims=True))
    cells = jnp.concatenate(cells, axis=0) * (1.0 / math.sqrt(512.0))
    cells = cells.astype(BF).astype(F32)
    pooled[...] = jnp.concatenate([cells, jnp.zeros((8, 64), F32)], axis=0).astype(BF)
    on = pz == 1 - kz
    face = [
        [jnp.where(kz == 0, row_of(cells, 4 * a + 2 * b + 1), row_of(cells, 4 * a + 2 * b)) for a in range(2)]
        for b in range(2)
    ]
    rows = jnp.concatenate([cell_rows(py, px, face, on), jnp.zeros((16, 64), F32)], axis=0)
    write_message(out, jnp.concatenate(faces, axis=0).astype(BF), [rows], py, px, on)


def y_messages(info, low, high, rz_in, pooled, down, up, rz):
    px, py, pz, kz = bits(info)
    open_message(rz_in, rz)
    cells = pooled[...].astype(F32)
    halo = rz[32].astype(F32)
    for out, face, bit, line, q in ((down, low, 0, 0, 0), (up, high, 1, 31, 1)):
        on = py == bit
        picked = [[row_of(cells, 4 * a + 2 * q + c) for c in range(2)] for a in range(2)]
        tail = halo[12:16] if q else halo[0:4]
        rows = jnp.concatenate([cell_rows(px, pz, picked, on), tail, jnp.zeros((12, 64), F32)], axis=0)
        write_message(out, face[:, 0], [rz[line], rows], px, pz, on)


def x_messages(info, low, high, rz_in, rym_in, ryp_in, pooled, down, up, rz, rym, ryp):
    px, py, pz, kz = bits(info)
    for ref, out in ((rz_in, rz), (rym_in, rym), (ryp_in, ryp)):
        open_message(ref, out)
    cells = pooled[...].astype(F32)
    halo = rz[32].astype(F32)
    halo_m = rym[33].astype(F32)
    halo_p = ryp[33].astype(F32)
    line_m = rym[32].astype(F32)
    line_p = ryp[32].astype(F32)
    where16 = lax.broadcasted_iota(jnp.int32, (32, 16, 64), 1)
    for out, face, bit, line, q in ((down, low, 0, 0, 0), (up, high, 1, 31, 1)):
        on = px == bit
        slab = rz[0:32, 16 * q : 16 * q + 16, :].astype(F32)
        z_line = jnp.sum(jnp.where(where16 == 15 * q, slab, 0.0), axis=1).astype(BF)
        picked = [[row_of(cells, 4 * q + 2 * b + c) for c in range(2)] for b in range(2)]
        corners = [line_m[line : line + 1], line_p[line : line + 1], jnp.zeros((14, 64), F32)]
        corners = jnp.concatenate(corners + [cell_rows(py, pz, picked, on)], axis=0)
        c0 = 3 * q
        parts = [row_of(halo, 4 * cy + c0) for cy in range(4)]
        parts += [halo_m[4 * c0 : 4 * c0 + 4], halo_p[4 * c0 : 4 * c0 + 4]]
        parts += [row_of(halo_m, 16 + c0), row_of(halo_p, 16 + c0), jnp.zeros((18, 64), F32)]
        tiles = [z_line, rym[line], ryp[line], corners, jnp.concatenate(parts, axis=0)]
        write_message(out, face[0], tiles, py, pz, on)


def coarse_table():
    pooled, rz, rym, ryp, rxm, rxp = 0, 16, 32, 64, 96, 128
    table = np.zeros((16, 224, 160), np.float32)
    for combo in range(16):
        bit = ((combo >> 3) & 1, (combo >> 2) & 1, (combo >> 1) & 1)
        core = combo & 1
        for tap in range(27):
            off = (tap // 9, tap // 3 % 3, tap % 3)
            for p in range(8):
                at = (p // 4, p // 2 % 2, p % 2)
                pos = [2 * bit[d] - 1 + off[d] + at[d] for d in range(3)]
                x, y, z = pos
                out_z = z < 0 or z > 3
                if out_z and (z < 0) != (core == 1):
                    continue
                if x < 0 or x > 3:
                    base = rxm if x < 0 else rxp
                    if y < 0 or y > 3:
                        side = 0 if y < 0 else 1
                        row = 16 + (12 + side if out_z else 4 + 4 * side + z)
                    else:
                        row = 16 + y if out_z else 4 * y + z
                    row = base + row
                elif y < 0 or y > 3:
                    row = (rym if y < 0 else ryp) + (16 + x if out_z else 4 * x + z)
                elif out_z:
                    row = rz + 4 * y + x
                else:
                    own = [pos[d] - 2 * bit[d] for d in range(3)]
                    if min(own) < 0 or max(own) > 1:
                        continue
                    row = pooled + 4 * own[0] + 2 * own[1] + own[2]
                table[combo, 8 * tap + p, row] = 1.0
    return table


class Window:
    def __init__(self, info, rz, rym, ryp):
        px, py, pz, kz = bits(info)
        self.pz, self.rz, self.rym, self.ryp = pz, rz, rym, ryp
        self.z0 = pl.ds(start16(pz), 16)
        self.z1 = pl.ds(start16(1 - pz), 16)
        self.xs = pl.ds(start16(px), 16)
        self.ys = pl.ds(start16(py), 16)
        self.xlo, self.xhi, self.ylo, self.yhi = px == 0, px == 1, py == 0, py == 1
        self.on_low = (pz == 0) & (kz == 1)
        self.on_high = (pz == 1) & (kz == 0)
        self.row16 = lax.broadcasted_iota(jnp.int32, (16, 16, 64), 1)
        self.z_row = lax.broadcasted_iota(jnp.int32, (9, 16, 128), 1)

    def edge(self, block):
        return jnp.sum(jnp.where(self.row16[: block.shape[0]] == 15 * self.pz, block.astype(F32), 0.0), axis=1)

    def edge1(self, ref, i):
        return self.edge(ref[i : i + 1, self.z1, :])

    def low_of(self, e, h):
        return keep(self.pz == 1, e) + keep(self.on_low, h)

    def high_of(self, e, h):
        return keep(self.pz == 0, e) + keep(self.on_high, h)

    def offsets(self, evens, odds, first, last, zl, zh):
        left = jnp.concatenate([first[None], odds], axis=0)
        right = jnp.concatenate([evens, last[None]], axis=0)
        tile = jnp.concatenate([left, right], axis=2)
        wide = tile.astype(F32)
        down = jnp.where(self.z_row == 0, zl, pltpu.roll(wide, 1, 1)).astype(BF)
        up = jnp.where(self.z_row == 15, zh, pltpu.roll(wide, 15, 1)).astype(BF)
        return down, tile, up


def one(ref, i, j):
    return ref[i].astype(F32)[j : j + 1]


def interior(info, lat, rz, rym, ryp, taps, raw, scene, columns, weight):
    nought = jnp.zeros((64, 64), BF)
    for tap in range(9):
        ox, oz = tap // 3, tap % 3
        for a in range(4):
            left = nought if a == 3 else taps[9 * ox + 3 * a + oz]
            right = nought if a == 0 else taps[9 * ox + 3 * a - 3 + oz]
            weight[256 * tap + 64 * a : 256 * tap + 64 * a + 64] = jnp.concatenate([left, right], axis=1)
    w = Window(info, rz, rym, ryp)
    y_low = keep(w.ylo, rym[w.xs, w.z0, :])
    y_high = keep(w.yhi, ryp[w.xs, w.z0, :])
    e_low = keep(w.ylo, w.edge(rym[w.xs, w.z1, :]))
    e_high = keep(w.yhi, w.edge(ryp[w.xs, w.z1, :]))
    h_low = jnp.where(w.ylo, rym[32, w.xs, :], rz[15, w.xs, :]).astype(F32)
    h_high = jnp.where(w.yhi, ryp[32, w.xs, :], rz[16, w.xs, :]).astype(F32)
    h_mid = rz[w.ys, w.xs, :].astype(F32)

    def packed(of):
        rows = [of(e_low, h_low)] + [of(jnp.zeros((16, 64), F32), h_mid[y]) for y in range(16)]
        rows.append(of(e_high, h_high))
        return [jnp.concatenate([rows[2 * k], rows[2 * k + 1]], axis=1) for k in range(9)]

    below, above = packed(w.low_of), packed(w.high_of)
    inner = [None] * 3
    for x in range(16):
        zl = jnp.concatenate([below[k][x : x + 1][None] for k in range(9)], axis=0)
        zh = jnp.concatenate([above[k][x : x + 1][None] for k in range(9)], axis=0)
        planes = w.offsets(lat[x, :, 0], lat[x, :, 1], y_low[x], y_high[x], zl, zh)
        for oz, plane in enumerate(planes):
            scene[oz, x] = plane
            wide = plane.astype(F32)
            inner[oz] = wide if x == 0 else inner[oz] + wide
    for oz in range(3):
        columns[oz] = jnp.sum(inner[oz], axis=1)
    for first, count in ((1, 4), (5, 4), (9, 4), (13, 2)):
        pieces = []
        for tap in range(9):
            ox, oz = tap // 3, tap % 3
            for dk in range(2):
                at = first + ox - 1
                pieces.append(scene[oz, at : at + count, dk : dk + 8].reshape(128 * count, 128))
        value = jnp.dot(jnp.concatenate(pieces, axis=1), weight[...], preferred_element_type=F32)
        raw[(first - 1) * 128 : (first - 1 + count) * 128] = value


def forward(
    info, near_low, near_high, raw, columns, rz, rym, ryp, rxm_in, rxp_in, pooled, weight,
    coarse_weight, temb, time_weight, tables, act, ends, patch_out, stats,
    shift, table, arrived, rxm, rxp
):
    px, py, pz, kz = bits(info)
    fetch = pltpu.make_async_copy(tables.at[8 * px + 4 * py + 2 * pz + kz], table, arrived)
    fetch.start()
    for ref, out in ((rxm_in, rxm), (rxp_in, rxp)):
        open_message(ref, out)
    w = Window(info, rz, rym, ryp)
    nought = jnp.zeros((16, 64), BF)

    def sides(rx, out, inner):
        first = jnp.where(
            out,
            jnp.where(w.ylo, rx[33, w.z0, :], rx[15, w.z0, :]),
            jnp.where(w.ylo, rym[inner, w.z0, :], nought),
        )
        last = jnp.where(
            out,
            jnp.where(w.yhi, rx[34, w.z0, :], rx[16, w.z0, :]),
            jnp.where(w.yhi, ryp[inner, w.z0, :], nought),
        )
        return first, last

    def side_columns(rx, out, inner, of):
        half = rz[w.ys, 0:16, :] if inner < 16 else rz[w.ys, 16:32, :]
        inner_h = jnp.sum(jnp.where(w.row16 == inner % 16, half.astype(F32), 0.0), axis=1)
        e_mid = keep(out, w.edge(rx[w.ys, w.z1, :]))
        hh = jnp.where(out, rx[32, w.ys, :].astype(F32), inner_h)
        e_first = jnp.where(
            out,
            jnp.where(w.ylo, w.edge1(rx, 33), w.edge1(rx, 15)),
            keep(w.ylo, w.edge1(rym, inner)),
        )
        h_first = jnp.where(
            out,
            jnp.where(w.ylo, one(rx, 35, 0), one(rx, 32, 15)),
            jnp.where(w.ylo, one(rym, 32, inner), one(rz, 15, inner)),
        )
        e_last = jnp.where(
            out,
            jnp.where(w.yhi, w.edge1(rx, 34), w.edge1(rx, 16)),
            keep(w.yhi, w.edge1(ryp, inner)),
        )
        h_last = jnp.where(
            out,
            jnp.where(w.yhi, one(rx, 35, 1), one(rx, 32, 16)),
            jnp.where(w.yhi, one(ryp, 32, inner), one(rz, 16, inner)),
        )
        mid = of(e_mid, hh)
        rows = [of(e_first, h_first)] + [mid[y : y + 1] for y in range(16)] + [of(e_last, h_last)]
        return [jnp.concatenate([rows[2 * k], rows[2 * k + 1]], axis=1)[None] for k in range(9)]

    for e, rx, out, inner in ((0, rxm, w.xlo, 15), (1, rxp, w.xhi, 16)):
        zl = jnp.concatenate(side_columns(rx, out, inner, w.low_of), axis=0)
        zh = jnp.concatenate(side_columns(rx, out, inner, w.high_of), axis=0)
        first, last = sides(rx, out, inner)
        plane = keep(out, rx[w.ys, w.z0, :]).reshape(8, 2, 16, 64)
        for oz, tile in enumerate(w.offsets(plane[:, 0], plane[:, 1], first, last, zl, zh)):
            ends[e, oz] = tile

    source = jnp.concatenate(
        [pooled[...], rz[32, 0:16, :], rym[33], ryp[33], rxm[35, 16:32, :], rxm[36, 0:16, :], rxp[35, 16:32, :], rxp[36, 0:16, :]],
        axis=0,
    )
    fetch.wait()
    taps = jnp.dot(table[...], source, preferred_element_type=F32)
    patch = jnp.concatenate([taps[8 * t : 8 * t + 8] for t in range(27)], axis=1)
    patch_out[...] = jnp.concatenate([patch, patch], axis=0).astype(BF)
    coarse = jnp.dot(patch_out[...], coarse_weight[...], preferred_element_type=F32)
    coarse = coarse.astype(BF).astype(F32)
    coarse = jnp.concatenate([coarse, coarse], axis=1)
    time_bias = lax.dot_general(
        jnp.broadcast_to(temb[...], (8, 256)),
        time_weight[...].astype(F32),
        (((1,), (1,)), ((), ())),
        preferred_element_type=F32,
        precision=lax.Precision.HIGHEST,
    )[:1]
    time_bias = jnp.concatenate([time_bias, time_bias], axis=1)
    z_half = lax.broadcasted_iota(jnp.int32, (16, 128), 0) < 8
    added = []
    for q in range(4):
        added.append(jnp.where(z_half, coarse[2 * q : 2 * q + 1], coarse[2 * q + 1 : 2 * q + 2]) + time_bias)

    pieces = []
    for tap in range(9):
        ox, oz = tap // 3, tap % 3
        low = ends[0, oz] if ox == 0 else near_low[oz, ox - 1]
        high = ends[1, oz] if ox == 2 else near_high[oz, ox]
        for dk in range(2):
            pieces.append(jnp.concatenate([low[dk : dk + 8], high[dk : dk + 8]], axis=0).reshape(256, 128))
    edges = jnp.dot(jnp.concatenate(pieces, axis=1), weight[...], preferred_element_type=F32)

    total = jnp.zeros((1, 128), F32)
    squares = jnp.zeros((1, 128), F32)
    for x in range(16):
        if x == 0:
            value = edges[:128]
        elif x == 15:
            value = edges[128:]
        else:
            value = raw[(x - 1) * 128 : x * 128]
        value = value.reshape(2, 4, 16, 128)
        a = x // 8
        value = jnp.concatenate([(value[b] + added[2 * a + b][None])[None] for b in range(2)], axis=0).reshape(128, 128)
        act[x * 128 : x * 128 + 128] = value
        total = total + jnp.sum(value, axis=0, keepdims=True)
        squares = squares + jnp.sum(value * value, axis=0, keepdims=True)
    shift[...] = jnp.zeros(shift.shape, F32)

    def place(tap, slot, value):
        row = SHIFT_LANE + 2 * (tap // 4 + slot)
        u = tap % 4
        shift[u // 2, row : row + 1, 64 * (u % 2) : 64 * (u % 2) + 64] = value

    for oz in range(3):
        inner = columns[oz]
        planes = (ends[0, oz], near_low[oz, 0], near_high[oz, 1], ends[1, oz])
        outer = [jnp.sum(plane.astype(F32), axis=1) for plane in planes]
        for ox, part in enumerate((inner + outer[0] - outer[2], inner, inner - outer[1] + outer[3])):
            all_columns = jnp.sum(part, axis=0, keepdims=True)
            whole = all_columns[:, :64] + all_columns[:, 64:]
            y0, y1 = part[0:1, :64], part[0:1, 64:]
            y16, y17 = part[8:9, :64], part[8:9, 64:]
            for oy, window in enumerate((whole - y16 - y17, whole - y0 - y17, whole - y0 - y1)):
                place(9 * ox + 3 * oy + oz, 0, window)
    for t in range(27):
        place(t, 7, 512.0 * jnp.sum(taps[8 * t : 8 * t + 8], axis=0, keepdims=True))

    lane = lax.broadcasted_iota(jnp.int32, (1, 128), 1)
    pairs = pair_sum(squares + pltpu.roll(squares, 64, 1))
    row = jnp.where(lane < 64, total + pltpu.roll(total, 64, 1), jnp.where(lane % 2 == 0, pairs, 0.0))
    for u in range(2):
        stats[128 * u : 128 * u + 128] = shift[u].T + row


def turn(info, scene, ends, turned_out, turned, sent):
    for oz in range(3):
        for xp in range(18):
            for dk in range(2):
                tile = scene[oz, xp - 1, dk : dk + 8] if 1 <= xp <= 16 else ends[xp // 17, oz, dk : dk + 8]
                turned[oz, 128 * dk : 128 * dk + 128, 128 * xp : 128 * xp + 128] = tile.reshape(128, 128).T
        pltpu.make_async_copy(turned.at[oz], turned_out.at[oz], sent.at[oz]).start()
    for oz in range(3):
        pltpu.make_async_copy(turned.at[oz], turned_out.at[oz], sent.at[oz]).wait()


def pair_sum(row):
    lane = lax.broadcasted_iota(jnp.int32, row.shape, 1)
    return row + jnp.where(lane % 2 == 0, pltpu.roll(row, 127, 1), pltpu.roll(row, 1, 1))


def halves(row):
    lane = lax.broadcasted_iota(jnp.int32, row.shape, 1)
    other = pltpu.roll(row, 64, 1)
    return jnp.where(lane < 64, row, other), jnp.where(lane < 64, other, row)


def moments(gathered, count):
    row = jnp.sum(gathered[...], axis=0, keepdims=True)
    sums, upper = halves(row)
    lane = lax.broadcasted_iota(jnp.int32, row.shape, 1)
    squares = jnp.where(lane % 2 == 0, upper, pltpu.roll(upper, 1, 1))
    mean = pair_sum(sums) / count
    var = squares / count - mean * mean
    return row, sums, mean, 1.0 / jnp.sqrt(var + EPS)


def backward(voxels):
    count = float(voxels * GROUP)
    scale = 1.0 / (voxels * 64)

    def kernel(
        info, gathered, target, gain, bias, weight, weight_t, patch, stats, act_in, turned_in,
        payload, other, predicted_out, cotangent, act, turned, predicted, fetched, sent, shown_sent
    ):
        def chunk(n):
            rows = (pl.ds(0, 512), pl.ds(512, 1536))[n]
            return pltpu.make_async_copy(act_in.at[rows], act.at[rows], fetched.at[n])

        def show(n):
            part = (pl.ds(0, 4), pl.ds(4, 12))[n]
            return pltpu.make_async_copy(predicted.at[part], predicted_out.at[part], shown_sent.at[n])

        whole = pltpu.make_async_copy(turned_in, turned, fetched.at[2])
        for n in range(2):
            chunk(n).start()
        kz = lax.axis_index("cz")
        _, _, mean, rstd = moments(gathered, count)
        gains = jnp.zeros((1, 128), F32)
        biases = jnp.zeros((1, 128), F32)
        lost = jnp.zeros((1, 128), F32)
        outer = jnp.zeros((128, 128), F32)
        cells = [[None] * 4, [None] * 4]
        for x in range(0, 16, 2):
            rows = slice(x * 128, x * 128 + 256)
            if x == 0:
                chunk(0).wait()
                whole.start()
            if x == 4:
                show(0).start()
                chunk(1).wait()
            normalized = (act[rows] - mean) * rstd
            shifted = normalized * gain[...] + bias[...]
            sigma = jax.nn.sigmoid(shifted)
            hidden = (shifted * sigma).astype(BF)
            output = jnp.dot(hidden, weight[...], preferred_element_type=F32)
            goal = jnp.concatenate([target[x : x + 2, :, 0], target[x : x + 2, :, 1]], axis=3)
            residue = output - goal.reshape(256, 128).astype(F32)
            shown = output.astype(BF).reshape(2, 8, 16, 128)
            predicted[x : x + 2, :, 0] = shown[..., :64]
            predicted[x : x + 2, :, 1] = shown[..., 64:]
            upstream = (2.0 * scale * residue).astype(BF)
            back = jnp.dot(upstream, weight_t[...], preferred_element_type=F32)
            value = back * sigma * (1.0 + shifted * (1.0 - sigma))
            gains = gains + jnp.sum(value * normalized, axis=0, keepdims=True)
            biases = biases + jnp.sum(value, axis=0, keepdims=True)
            lost = lost + jnp.sum(residue * residue, axis=0, keepdims=True)
            outer = outer + lax.dot_general(hidden, upstream, (((0,), (0,)), ((), ())), preferred_element_type=F32)
            value = value * (gain[...] * rstd)
            narrow = [value.astype(BF), normalized.astype(BF)]
            cotangent[rows, :128] = jnp.concatenate([part[:, :64] for part in narrow], axis=1)
            cotangent[rows, 128:] = jnp.concatenate([part[:, 64:] for part in narrow], axis=1)
            for part, wide in enumerate((value, normalized)):
                planes = wide.reshape(2, 2, 4, 16, 128)
                for b in range(2):
                    q = 2 * (x // 8) + b
                    cell = jnp.sum(planes[:, b], axis=(0, 1))
                    old = cells[part][q]
                    cells[part][q] = cell if old is None else old + cell

        def store(tap, slot, value):
            u = tap % 4
            half = jnp.where(kz == u // 2, 0, 1)
            payload.at[half][pl.ds(1024 * (u % 2) + slot + tap // 4, 64, stride=16), :] = value

        rows = []
        for q in range(4):
            for c in range(2):
                sums = [jnp.sum(cells[p][q][8 * c : 8 * c + 8], axis=0, keepdims=True) for p in range(2)]
                rows.append(jnp.concatenate([r[:, :64] + r[:, 64:] for r in sums], axis=1))
        rows = jnp.concatenate(rows, axis=0)
        high = rows.astype(BF)
        split = jnp.concatenate([high.astype(F32), rows - high.astype(F32)], axis=0).astype(BF)
        coarse = lax.dot_general(patch[...], split, (((0,), (0,)), ((), ())), preferred_element_type=F32)
        for t in range(27):
            store(t, 7, coarse[64 * t : 64 * t + 64])
        show(1).start()
        whole.wait()
        for ox in range(3):
            windows = turned[:, :, 128 * ox : 128 * ox + 2048].reshape(768, 2048)
            products = jnp.dot(windows, cotangent[...], preferred_element_type=F32)
            for oz in range(3):
                product = products[256 * oz : 256 * oz + 256]
                for oy in range(3):
                    value = product[64 * oy : 64 * oy + 64, :128] + product[64 * oy + 64 : 64 * oy + 128, 128:]
                    store(9 * ox + 3 * oy + oz, 0, value)
        nought = jnp.zeros((64, 64), F32)
        store(27, 0, jnp.concatenate([outer[:64, :64] + outer[64:, 64:], nought], axis=1))
        loss = jnp.broadcast_to(jnp.sum(lost, axis=1, keepdims=True), (64, 128))
        high = loss.astype(BF).astype(F32)
        lane = lax.broadcasted_iota(jnp.int32, (64, 128), 1)
        split = jnp.where(lane == 2 * kz, high, jnp.where(lane == 2 * kz + 1, loss - high, 0.0))
        store(27, 7, split)
        lane = lax.broadcasted_iota(jnp.int32, (1, 128), 1)
        row = jnp.where(lane < 64, gains + pltpu.roll(gains, 64, 1), biases + pltpu.roll(biases, 64, 1))
        wide = jnp.broadcast_to(row, (128, 128))
        for half in range(2):
            payload.at[half][pl.ds(14, 128, stride=16), :] = wide
            slot = jnp.where(kz == half, 0, 1)
            payload.at[slot][pl.ds(15, 128, stride=16), :] = stats[128 * half : 128 * half + 128]
        copy = pltpu.make_async_copy(payload.at[1, pl.ds(0, 2048)], other, sent)
        copy.start()
        for n in range(2):
            show(n).wait()
        copy.wait()

    return kernel


def slopes(norms, gain, count):
    grad_gain, grad_bias = halves(norms)
    return pair_sum(gain * grad_bias) / count, pair_sum(gain * grad_gain) / count


def pair_add(voxels):
    total_count = float(voxels * GROUP)
    count = float(2 * 4096 * GROUP)

    def kernel(info, mine, other, gathered, gain, out):
        _, _, _, rstd = moments(gathered, total_count)
        total = (mine[0, 0:2048] + other[...]).reshape(-1, 16, 128)
        m1, m2 = slopes(total[0, 14:15], gain[...], count)
        row = lax.broadcasted_iota(jnp.int32, total.shape, 1)
        lane = lax.broadcasted_iota(jnp.int32, total.shape, 2)
        picked = (lane == SHIFT_LANE + 2 * row) & (row < 14)
        ones = jnp.sum(jnp.where(picked, total[:, 15:16], 0.0), axis=2, keepdims=True)
        centred = total - (m1 * rstd)[None] * ones - (m2 * rstd)[None] * pltpu.roll(total, 64, 2)
        total = jnp.where((lane < 64) & (row < 14), centred, total)
        lost = pltpu.roll(total - total.astype(BF).astype(F32), 1, 1)
        out[...] = jnp.where(row == 15, lost, total).astype(BF)

    return kernel


def combine(voxels):
    count = float(voxels * GROUP)
    pair_count = float(2 * 4096 * GROUP)

    def kernel(info, pieces, gathered, gain, temb, copies, grad_time, gain_out, bias_out):
        _, sums, mean, rstd = moments(gathered, count)
        value = pieces[...].astype(F32)
        chips = value.shape[0]
        seen = value[:, 14] + value[:, 15]
        norms = jnp.sum(seen, axis=0, keepdims=True)
        grad_gain, grad_bias = halves(norms)
        gain_out[...] = grad_gain[:, :64]
        bias_out[...] = grad_bias[:, :64]
        m1, m2 = slopes(norms, gain[...], count)
        centred = (sums - voxels * mean) * rstd
        act_sum = rstd * (gain[...] * grad_bias - voxels * m1 - m2 * centred)
        column = jnp.broadcast_to(act_sum, (128, 128)).T[:64]
        grad_time[...] = jnp.concatenate([column, column], axis=1) * temb[...]
        own1, own2 = slopes(seen, gain[...], pair_count)
        delta1, delta2 = (own1 - m1) * rstd, (own2 - m2) * rstd
        ones = gathered[0:chips] + gathered[chips : 2 * chips]
        back = lax.dot_general(
            ones, delta1, (((0,), (0,)), ((), ())), preferred_element_type=F32, precision=lax.Precision.HIGHEST
        )
        back = [back[SHIFT_LANE + 2 * r : SHIFT_LANE + 2 * r + 1] for r in range(14)]
        back = jnp.concatenate(back + [jnp.zeros((2, 128), F32)], axis=0)
        total = jnp.sum(value + delta2[:, None] * pltpu.roll(value, 64, 2), axis=0) + back
        lane = lax.broadcasted_iota(jnp.int32, (7, 128), 1)
        both = jnp.where(lane < 64, total[:7], pltpu.roll(total[7:14], 64, 1))
        lost = both[6:7] - both[6:7].astype(BF).astype(F32)
        piece = jnp.concatenate([both, lost], axis=0).astype(BF)
        copies[...] = jnp.broadcast_to(piece[None], copies.shape)

    return kernel


def spread(scale, info, near, far, conv, coarse, out, loss, rows):
    kz = lax.axis_index("cz")
    rows[pl.ds(pl.multiple_of(1024 * kz, 1024), 1024), :] = near[...].astype(F32).reshape(1024, 128)
    rows[pl.ds(pl.multiple_of(1024 * (1 - kz), 1024), 1024), :] = far[...].astype(F32).reshape(1024, 128)
    for tap in range(28):
        tile = rows[pl.ds(512 * (tap % 4) + tap // 4, 64, stride=8), :]
        if tap < 27:
            conv[tap] = tile[:, :64]
            coarse[tap] = tile[:, 64:]
        else:
            out[...] = tile[:, :64]
            parts = tile[0:1] + rows[2048 - 512 + 7 : 2048 - 512 + 8, :]
            lane = lax.broadcasted_iota(jnp.int32, (1, 128), 1)
            whole = jnp.sum(jnp.where((lane >= 64) & (lane < 68), parts, 0.0), axis=1, keepdims=True)
            loss[...] = whole * scale


def exchange(rows):
    out = lax.all_to_all(rows.reshape(rows.shape[0], 1, 128), ("cz",) + CHIPS, 0, 0, tiled=True)
    return out.reshape(rows.shape)


def neighbours(down, up, axis):
    ends = lax.axis_size(axis) - 1
    before = lax.ppermute(up, axis, [(i, i + 1) for i in range(ends)])
    after = lax.ppermute(down, axis, [(i + 1, i) for i in range(ends)])
    return before, after


def time_embedding(timestep, width):
    halfway = width // 2
    indices = jnp.arange(halfway).astype(F32)
    freqs = jnp.exp(indices * (-math.log(10000.0) / halfway))
    angles = timestep[0].astype(F32) * freqs
    return jnp.concatenate([jnp.sin(angles), jnp.cos(angles)])


def twice(row):
    return jnp.concatenate([row, row]).reshape(1, 128)


def diagonal(square):
    nought = jnp.zeros_like(square)
    return jnp.block([[square, nought], [nought, square]])


def shards(latents, target, block_coords, timestep, conv_weight, coarse_weight, out_weight, time_weight, norm_gain, norm_bias):
    devices = lax.axis_size("bx") * lax.axis_size("by") * lax.axis_size("cz")
    voxels = devices * 4096
    info = block_coords
    lat = latents[0]
    lat_pairs = lat.reshape(16, 8, 2, 16, 64)

    mz, pooled = call(z_message, [message(Z_TILES), like((16, 64), BF)], [info, lat])
    rz = lax.ppermute(mz, "cz", [(0, 1), (1, 0)])
    out = message(Y_TILES)
    down, up = call(
        y_messages, [out, out], [info, lat, lat, rz, pooled], [plane(Z_TILES)], [face_spec(1, 0), face_spec(1, 15)]
    )
    rym, ryp = neighbours(down, up, "by")
    out = message(X_TILES)
    planes = [like((32 + tiles, 32, 64), BF) for tiles in (Z_TILES, Y_TILES, Y_TILES)]
    down, up, rz, rym, ryp = call(
        x_messages,
        [out, out] + planes,
        [info, lat, lat, rz, rym, ryp, pooled],
        (),
        [face_spec(0, 0), face_spec(0, 15)],
    )
    rxm, rxp = neighbours(down, up, "bx")

    temb = time_embedding(timestep, time_weight.shape[0]).reshape(1, -1)
    raw, scene, columns, taps = call(
        interior,
        [like((1792, 128), F32), like((3, 16, 9, 16, 128), BF), like((3, 9, 128), F32), like((2304, 128), BF)],
        [info, lat_pairs, rz, rym, ryp, conv_weight],
    )
    pair = (3, 2, 9, 16, 128)
    tables = jnp.asarray(coarse_table(), BF)
    act, ends, patch, stats = call(
        forward,
        [pltpu.HBM((2048, 128), F32), like((2, 3, 9, 16, 128), BF), like((16, 1728), BF), like((devices, 128), F32)],
        [info, scene, scene, raw, columns, rz, rym, ryp, rxm, rxp, pooled, taps]
        + [coarse_weight.reshape(1728, 64), temb, time_weight.T, tables],
        [pltpu.VMEM((2, 128, 128), F32), pltpu.VMEM((224, 160), BF), pltpu.SemaphoreType.DMA]
        + [plane(X_TILES), plane(X_TILES)],
        [pl.BlockSpec(pair, lambda i: (0, 0, 0, 0, 0)), pl.BlockSpec(pair, lambda i: (0, 7, 0, 0, 0))],
        far_args=1,
    )
    first = exchange(stats)
    (turned,) = call(
        turn,
        [pltpu.HBM((3, 256, 18 * 128), BF)],
        [info, scene, ends],
        [pltpu.VMEM((3, 256, 18 * 128), BF), pltpu.SemaphoreType.DMA((3,))],
        far_outs=1,
    )
    gain, bias = twice(norm_gain), twice(norm_bias)
    weights = [diagonal(out_weight), diagonal(out_weight.T)]
    payload, other, predicted = call(
        backward(voxels),
        [like((2, 2064, 128), F32), like((2048, 128), F32), pltpu.HBM((16, 8, 2, 16, 64), BF)],
        [info, first, target.reshape(16, 8, 2, 16, 64), gain, bias] + weights + [patch, stats, in_hbm(act), in_hbm(turned)],
        [
            pltpu.VMEM((2048, 256), BF),
            pltpu.VMEM((2048, 128), F32),
            pltpu.VMEM((3, 256, 18 * 128), BF),
            pltpu.VMEM((16, 8, 2, 16, 64), BF),
            pltpu.SemaphoreType.DMA((3,)),
            pltpu.SemaphoreType.DMA,
            pltpu.SemaphoreType.DMA((2,)),
        ],
        far_args=2,
        far_outs=2,
    )
    swap = [(0, 1), (1, 0)]
    chips = devices // 2
    other = lax.ppermute(other, "cz", swap)
    (pieces,) = call(pair_add(voxels), [like((chips, 16, 128), BF)], [info, payload, other, first, gain])
    pieces = lax.all_to_all(pieces, CHIPS, 0, 0, tiled=True)
    copies, grad_time, grad_gain, grad_bias = call(
        combine(voxels),
        [like((chips, 8, 128), BF), like((64, 256), F32), like((1, 64), F32), like((1, 64), F32)],
        [info, pieces, first, gain, temb],
    )
    near = lax.all_to_all(copies, CHIPS, 0, 0, tiled=True)
    far = lax.ppermute(near, "cz", swap)
    grad_conv, grad_coarse, grad_out, loss = call(
        functools.partial(spread, 1.0 / (voxels * 64)),
        [like((27, 64, 64), F32), like((27, 64, 64), F32), like((64, 64), F32), like((1, 1), F32)],
        [info, near, far],
        [pltpu.VMEM((2056, 128), F32)],
    )
    return (
        predicted.reshape(latents.shape),
        loss.reshape(1),
        grad_conv,
        grad_coarse,
        grad_out,
        grad_time.T,
        grad_gain.reshape(64),
        grad_bias.reshape(64),
    )


def solution(mesh):
    blocks = P(ALL, None, None, None, None)
    return jax.shard_map(
        shards,
        mesh=mesh,
        in_specs=(blocks, blocks, P(ALL, None)) + (P(),) * 7,
        out_specs=(blocks,) + (P(),) * 7,
        check_vma=False,
    )
```
